32 devices in a mesh: dp: 4 (over y, x), seq: 8 (over z, core).
Axes of the slice: x: 2, y: 2, z: 4, core: 2. Of those that a mesh axis runs over, the one named last changes fastest.
Arguments:
- byte_ids: int32 [4, 4096], P('dp', 'seq'), may hold values from 0 to 255
- embedding: bfloat16 [256, 1024], replicated, may hold values from -6 to 6
- cotangent: bfloat16 [4, 4096, 1024], P('dp', 'seq'), may hold values from -6 to 6
- norm_gain: float32 [1024], replicated, may hold values from 0.5 to 1.5
- input_projection_weight: bfloat16 [1024, 4096], replicated, may hold values from -0.1875 to 0.1875
- conv_weight: float32 [4, 2048], replicated, may hold values from -3 to 3
- conv_bias: float32 [2048], replicated, may hold values from -3 to 3
- select_weight: bfloat16 [2048, 96], replicated, may hold values from -0.125 to 0.125
- step_weight: bfloat16 [64, 2048], replicated, may hold values from -0.75 to 0.75
- step_bias: float32 [2048], replicated, may hold values from -7 to -3
- decay_log: float32 [16, 2048], replicated, may hold values from -5 to 1
- skip_gain: float32 [2048], replicated, may hold values from 0.5 to 1.5
- output_projection_weight: bfloat16 [2048, 1024], replicated, may hold values from -0.5 to 0.5
Outputs:
- output: bfloat16 [4, 4096, 1024], P('dp', 'seq')
- d_inputs: float32 [4, 4096, 1024], P('dp', 'seq')
- d_embedding: float32 [256, 1024], replicated
- d_norm_gain: float32 [1024], replicated
- d_input_weight: float32 [1024, 4096], replicated
- d_conv_weight: float32 [4, 2048], replicated
- d_conv_bias: float32 [2048], replicated
- d_select_weight: float32 [2048, 96], replicated
- d_step_weight: float32 [64, 2048], replicated
- d_step_bias: float32 [2048], replicated
- d_decay_log: float32 [16, 2048], replicated
- d_skip_gain: float32 [2048], replicated
- d_output_weight: float32 [2048, 1024], replicated
The draws below stay inside these ranges and needn't reach their ends.
All inputs are finite; a program needn't handle non-finite values.
Results may differ from the reference program's by a relative error of at most 0.0087.
The reference program's roundings to bfloat16 on the way count: a program that leaves them out, or rounds other values in their place, can miss the bound.
Values may be sent and summed in bfloat16 or wider, within the bound.
A program may use at most 192 MiB of HBM per device.

```python
import math
import jax
import jax.numpy as jnp
import numpy as np
from jax import lax

D = 1024
E = 2048
N = 16
R = 64
CONV = 4
VOCAB = 256
BLOCK = 16
SEQS = 4
LENGTH = 4096


def with_ends(values, stream_key, least, largest):
    spot = [jax.random.randint(jax.random.fold_in(stream_key, axis), (), 0, length) for axis, length in enumerate(values.shape)]
    widest = values.shape.index(max(values.shape))
    next_to = spot[:widest] + [(spot[widest] + 1) % values.shape[widest]] + spot[widest + 1:]
    return values.at[tuple(spot)].set(least).at[tuple(next_to)].set(largest)


def block_levels(own_key, dims, shards, smallest, largest):
    def one(position, parts):
        heights = jax.random.uniform(jax.random.fold_in(jax.random.fold_in(own_key, 6), position), (parts,), jnp.float32, smallest / len(shards), largest / len(shards))
        return jnp.repeat(jnp.exp(heights), dims[position] // parts).reshape((-1,) + (1,) * (len(dims) - position - 1))

    factor_of = one(*shards[0])
    for cut in shards[1:]:
        factor_of = factor_of * one(*cut)
    return factor_of


def rank_bounds(number_of, slope):
    weights = [(1 << 20) // math.isqrt(grade ** slope) + 1 for grade in range(1, number_of + 1)]
    scale = 1 + sum(weights) // (1 << 30)
    return np.cumsum(np.array([max(1, weight // scale) for weight in weights]))


def ranked_ids(own_key, extent, number_of, skew):
    listing = rank_bounds(number_of, skew)
    pick = jax.random.randint(jax.random.fold_in(own_key, 1), extent, 0, int(listing[number_of - 1]))
    rank = jnp.searchsorted(jnp.asarray(listing, jnp.int32), pick, side="right")
    return jax.random.permutation(jax.random.fold_in(own_key, 2), number_of)[rank].astype(jnp.int32)


def centred(own_key, extent, deviation, bound, shards=(), held_as=jnp.bfloat16):
    values = jax.random.normal(own_key, extent, jnp.float32) * deviation
    if len(shards) > 0:
        values = block_levels(own_key, extent, shards, -0.22, 0.18) * values
    return jnp.clip(values, min=-bound, max=bound).astype(held_as)


def setup_inputs(seed: int = 0) -> dict:
    key_list = jax.random.split(jax.random.key(seed), 14)
    byte_ids = with_ends(ranked_ids(key_list[0], (SEQS, LENGTH), VOCAB, 2), jax.random.fold_in(key_list[0], 3), 0, VOCAB - 1).astype(jnp.int32)
    embedding = centred(key_list[1], (VOCAB, D), 1.0, 6.0)
    cotangent = centred(key_list[2], (SEQS, LENGTH, D), 1.0, 6.0, ((0, 4), (1, 8)))
    norm_gain = jnp.clip(1.0 + 0.1 * jax.random.normal(key_list[3], (D,), jnp.float32), 0.5, 1.5)
    input_projection_weight = centred(key_list[4], (D, 2 * E), D ** -0.5, 0.1875)
    conv_weight = centred(key_list[5], (CONV, E), CONV ** -0.5, 3.0, (), jnp.float32)
    conv_bias = centred(key_list[6], (E,), 0.5, 3.0, (), jnp.float32)
    select_weight = centred(key_list[7], (E, R + 2 * N), E ** -0.5, 0.125)
    step_weight = centred(key_list[8], (R, E), R ** -0.5, 0.75)
    step_bias = jnp.clip(jax.random.uniform(key_list[9], (E,), jnp.float32, -7.0, -3.0), -7.0, -3.0)
    decay_log = jnp.clip(jax.random.uniform(key_list[10], (N, E), jnp.float32, -5.0, 1.0), -5.0, 1.0)
    skip_gain = jnp.clip(jax.random.uniform(key_list[11], (E,), jnp.float32, 0.5, 1.5), 0.5, 1.5)
    output_projection_weight = centred(key_list[12], (E, D), (E // 16) ** -0.5, 0.5)
    return dict(byte_ids=byte_ids, embedding=embedding, cotangent=cotangent, norm_gain=norm_gain, input_projection_weight=input_projection_weight, conv_weight=conv_weight, conv_bias=conv_bias, select_weight=select_weight, step_weight=step_weight, step_bias=step_bias, decay_log=decay_log, skip_gain=skip_gain, output_projection_weight=output_projection_weight)


@jax.custom_vjp
def lower_result(v):
    return lax.optimization_barrier(v.astype(jnp.bfloat16)).astype(jnp.float32)

@jax.custom_vjp
def lower_backward(v):
    return v

def low_keep(v):
    return (lower_result(v), None)

def low_pass(kept, grad):
    return (grad,)

def back_keep(v):
    return (v, None)

def back_low(kept, grad):
    return (lower_result(grad),)
lower_result.defvjp(low_keep, low_pass)
lower_backward.defvjp(back_keep, back_low)
EPS = 1e-05

def selective(delta, active, inject, readout, rates):
    count = delta.shape[0]

    def advance(state, packed):
        delta_now, active_now, inject_now, readout_now = packed
        factor = jnp.exp(delta_now[:, None, :] * rates)
        state = factor * state + (delta_now * active_now)[:, None, :] * inject_now[:, :, None]
        return (state, lax.optimization_barrier(jnp.sum(readout_now[:, :, None] * state, axis=1)))

    def block_pass(state, packed):
        return lax.scan(advance, state, packed)

    def arrange(array):
        moved = jnp.swapaxes(array, 0, 1)
        return moved.reshape((LENGTH // BLOCK, BLOCK) + moved.shape[1:])
    start = jnp.zeros((count, N, E), jnp.float32)
    unused, result = lax.scan(jax.checkpoint(block_pass), start, (arrange(delta), arrange(active), arrange(inject), arrange(readout)))
    return jnp.swapaxes(result.reshape((LENGTH,) + result.shape[2:]), 0, 1)

def forward(block_inputs, norm_gain, input_projection_weight, conv_weight, conv_bias, select_weight, step_weight, step_bias, decay_log, skip_gain, output_projection_weight):
    highest_precision = lax.Precision.HIGHEST
    scale = lax.rsqrt(lax.optimization_barrier(jnp.mean(block_inputs * block_inputs, axis=-1, keepdims=True)) + EPS)
    normed_input = lower_result(block_inputs * scale * norm_gain)
    inner_and_gate = lower_backward(lower_result(jnp.einsum('htu,uc->htc', normed_input, input_projection_weight, precision=highest_precision)))
    front = inner_and_gate[:, :, :E]
    gate = inner_and_gate[:, :, E:]
    padded = jnp.pad(front, ((0, 0), (CONV - 1, 0), (0, 0)))
    mixed = conv_bias + conv_weight[0] * padded[:, 0:LENGTH]
    for place in range(1, CONV):
        mixed = mixed + conv_weight[place] * padded[:, place:place + LENGTH]
    active = lower_result(jax.nn.silu(mixed))
    select = lower_backward(lower_result(jnp.einsum('sle,ef->slf', active, select_weight, precision=highest_precision)))
    lowrank = select[:, :, :R]
    inject = select[:, :, R:R + N]
    readout = select[:, :, R + N:]
    pre = lower_backward(jnp.einsum('slr,re->sle', lowrank, step_weight, precision=highest_precision)) + step_bias
    delta = jax.nn.softplus(pre)
    rates = -jnp.exp(decay_log)
    scanned = selective(delta, active, inject, readout, rates) + skip_gain * active
    gated_output = lower_result(scanned * jax.nn.silu(gate))
    return block_inputs + jnp.einsum('qzw,wp->qzp', gated_output, output_projection_weight, precision=highest_precision)

def reference(byte_ids, embedding, cotangent, norm_gain, input_projection_weight, conv_weight, conv_bias, select_weight, step_weight, step_bias, decay_log, skip_gain, output_projection_weight):
    table = embedding.astype(jnp.float32)
    weights = (norm_gain, input_projection_weight.astype(jnp.float32), conv_weight, conv_bias, select_weight.astype(jnp.float32), step_weight.astype(jnp.float32), step_bias, decay_log, skip_gain, output_projection_weight.astype(jnp.float32))
    group = 1
    for candidate in range(1, SEQS + 1):
        if SEQS % candidate == 0 and candidate * LENGTH <= 4096:
            group = candidate
    ids_grouped = byte_ids.reshape(SEQS // group, group, LENGTH)
    cot_grouped = cotangent.astype(jnp.float32).reshape(SEQS // group, group, LENGTH, D)

    def one_group(totals, packed):
        ids_now, cot_now = packed
        block_inputs, pull_table = jax.vjp(lambda source: source[ids_now], table)
        result, pull = jax.vjp(forward, block_inputs, *weights)
        grads = pull(cot_now)
        table_grad = pull_table(grads[0])[0]
        fresh = (table_grad,) + tuple(grads[1:])
        totals = tuple((total + extra for total, extra in zip(totals, fresh)))
        return (totals, (result.astype(jnp.bfloat16), grads[0]))
    start = (jnp.zeros_like(table),) + tuple((jnp.zeros_like(weight) for weight in weights))
    totals, (outputs, d_inputs) = lax.scan(one_group, start, (ids_grouped, cot_grouped))
    output = outputs.reshape(SEQS, LENGTH, D)
    d_inputs = d_inputs.reshape(SEQS, LENGTH, D)
    return (output, d_inputs, totals[0], totals[1], totals[2], totals[3], totals[4], totals[5], totals[6], totals[7], totals[8], totals[9], totals[10])
```

```python
import functools
import math

import jax
import jax.numpy as jnp
from jax import lax
from jax.experimental import pallas as pl
from jax.experimental.pallas import tpu as pltpu
from jax.sharding import PartitionSpec as P

EPS = 1e-05
LANES = 128
SUB = 8
LOG2E = math.log2(math.e)
LN2 = math.log(2.0)
F32 = jnp.float32
BF16 = jnp.bfloat16


def passed_along(value, axis, by):
    peers = lax.axis_size(axis)
    pairs = [(i, i + by) for i in range(peers) if 0 <= i + by < peers]
    return lax.ppermute(value, axis, pairs)


def silu_slope(value):
    sigma = jax.nn.sigmoid(value)
    return sigma * (1.0 + value * (1.0 - sigma))


def contract_rows(left, right):
    return lax.dot_general(
        left, right, (((0,), (0,)), ((), ())), preferred_element_type=F32
    )


def contract_cols(left, right):
    return lax.dot_general(
        left, right, (((1,), (1,)), ((), ())), preferred_element_type=F32
    )


def to_spans(array):
    rows = array.shape[0]
    return array.reshape(SUB, rows // SUB, -1).swapaxes(0, 1).reshape(rows, -1)


def from_spans(array):
    rows = array.shape[0]
    return array.reshape(rows // SUB, SUB, -1).swapaxes(0, 1).reshape(rows, -1)


def sublane(shape):
    return lax.broadcasted_iota(jnp.int32, shape, len(shape) - 2)


def shift_up(value, by, fill, reverse):
    place = sublane(value.shape)
    if reverse:
        moved = pltpu.roll(value, SUB - by, value.ndim - 2)
        return jnp.where(place < SUB - by, moved, fill)
    moved = pltpu.roll(value, by, value.ndim - 2)
    return jnp.where(place >= by, moved, fill)


def expand_columns(select, first, states):
    width = select.shape[1]
    shape = (width, states * LANES)
    source = lax.broadcasted_iota(jnp.int32, shape, 0)
    target = lax.broadcasted_iota(jnp.int32, shape, 1) // LANES + first
    spread = (source == target).astype(F32).astype(BF16)
    return jnp.dot(select, spread, preferred_element_type=F32)


def scaled_rates(decay_ref, rate_scr, states):
    rates = -jnp.exp(decay_ref[...]) * LOG2E
    for n in range(states):
        rate_scr[n] = jnp.broadcast_to(rates[n : n + 1], (SUB, LANES))


def ends_kernel(
    rank, states, pre_ref, active_ref, grad_ref, select_ref, decay_ref,
    sums_ref, ahead_ref, behind_ref, end_ref, message_ref,
    inject_scr, readout_scr, rate_scr, delta_scr, drive_scr,
):
    rows = pre_ref.shape[0]
    steps = rows // SUB

    @pl.when(pl.program_id(0) == 0)
    def _():
        inject_scr[...] = expand_columns(select_ref[...], rank, states)
        readout_scr[...] = expand_columns(select_ref[...], rank + states, states)

    scaled_rates(decay_ref, rate_scr, states)
    delta = jax.nn.softplus(pre_ref[...])
    delta_scr[...] = delta
    drive_scr[...] = delta * active_ref[...].astype(F32)
    unroll = 2

    def body(i, carry):
        total, state, message, decay = carry
        state, message, decay = list(state), list(message), list(decay)
        for u in range(unroll):
            here = pl.ds(pl.multiple_of((i * unroll + u) * SUB, SUB), SUB)
            d, drive, g = delta_scr[here, :], drive_scr[here, :], grad_ref[here, :]
            total = total + d
            for n in range(states):
                cols = pl.ds(n * LANES, LANES)
                factor = jnp.exp2(d * rate_scr[n])
                state[n] = factor * state[n] + drive * inject_scr[here, cols]
                decay[n] = decay[n] * factor
                message[n] = message[n] + decay[n] * (g * readout_scr[here, cols])
        return total, tuple(state), tuple(message), tuple(decay)

    zero = jnp.zeros((SUB, LANES), F32)
    total, state, message, decay = lax.fori_loop(
        0, steps // unroll, body,
        (zero, (zero,) * states, (zero,) * states, (jnp.ones((SUB, LANES), F32),) * states),
    )
    sums_ref[...] = total
    for n in range(states):
        for value, out, edge, reverse in (
            (state[n], ahead_ref, end_ref, False), (message[n], behind_ref, message_ref, True)
        ):
            factor = decay[n]
            for by in (1, 2, 4):
                value = value + factor * shift_up(value, by, 0.0, reverse)
                factor = factor * shift_up(factor, by, 1.0, reverse)
            out[n] = shift_up(value, 1, 0.0, reverse)
            last = 0 if reverse else SUB - 1
            edge[n : n + 1, :] = value[last : last + 1]


def scan_kernel(
    rank, states, pre_ref, active_ref, gate_ref, graded_ref, select_ref, decay_ref, skip_ref,
    ahead_ref, behind_ref, start_ref, incoming_ref,
    gated_ref, dgate_ref, dprelow_ref, dactive_ref, drate_ref, dbias_ref, dskip_ref, dselect_ref,
    inject_scr, readout_scr, rate_scr, delta_scr, drive_scr, grad_scr, scanned_scr,
    state_scr, factor_scr, dread_scr, dinject_scr,
):
    rows = pre_ref.shape[0]
    steps = rows // SUB

    @pl.when(pl.program_id(0) == 0)
    def _():
        inject_scr[...] = expand_columns(select_ref[...], rank, states)
        readout_scr[...] = expand_columns(select_ref[...], rank + states, states)
        dread_scr[...] = jnp.zeros_like(dread_scr)
        dinject_scr[...] = jnp.zeros_like(dinject_scr)

    scaled_rates(decay_ref, rate_scr, states)
    delta = jax.nn.softplus(pre_ref[...])
    delta_scr[...] = delta
    drive_scr[...] = delta * active_ref[...].astype(F32)
    gate = gate_ref[...].astype(F32)
    grad_scr[...] = graded_ref[...] * (gate * jax.nn.sigmoid(gate))
    total = jnp.zeros((SUB, LANES), F32)
    for j in range(steps):
        total = total + delta_scr[j * SUB : (j + 1) * SUB]
    before, after = total, total
    for by in (1, 2, 4):
        before = before + shift_up(before, by, 0.0, False)
        after = after + shift_up(after, by, 0.0, True)
    before, after = before - total, after - total
    unroll = 2
    begin = []
    for n in range(states):
        reach = jnp.exp2(before * rate_scr[n])
        begin.append(ahead_ref[n] + reach * start_ref[n : n + 1, :])
        state_scr[n] = begin[-1]

    def forward(i, state):
        state = list(state)
        for u in range(unroll):
            j = i * unroll + u
            here = pl.ds(pl.multiple_of(j * SUB, SUB), SUB)
            d, drive, g = delta_scr[here, :], drive_scr[here, :], grad_scr[here, :]
            sums = [None] * 4
            for n in range(states):
                cols = pl.ds(n * LANES, LANES)
                factor = jnp.exp2(d * rate_scr[n])
                factor_scr[j * states + n] = factor
                state[n] = factor * state[n] + drive * inject_scr[here, cols]
                state_scr[(j + 1) * states + n] = state[n]
                dread_scr[here, cols] += g * state[n]
                term = readout_scr[here, cols] * state[n]
                sums[n % 4] = term if sums[n % 4] is None else sums[n % 4] + term
            scanned_scr[here, :] = (sums[0] + sums[1]) + (sums[2] + sums[3])
        return tuple(state)

    lax.fori_loop(0, steps // unroll, forward, tuple(begin))

    active = active_ref[...].astype(F32)
    skip = skip_ref[...]
    gate = gate_ref[...].astype(F32)
    sigma = jax.nn.sigmoid(gate)
    scanned = scanned_scr[...] + skip * active
    gated_ref[...] = (scanned * (gate * sigma)).astype(BF16)
    dgate_ref[...] = (
        graded_ref[...] * scanned * (sigma * (1.0 + gate * (1.0 - sigma)))
    ).astype(BF16)
    dskip_ref[...] = jnp.sum(grad_scr[...] * active, axis=0, keepdims=True)

    adjoint0, zeros = [], (jnp.zeros((SUB, LANES), F32),) * states
    for n in range(states):
        reach = jnp.exp2(after * rate_scr[n])
        adjoint0.append(behind_ref[n] + reach * incoming_ref[n : n + 1, :])

    def backward(i, carry):
        adjoint, total = list(carry[0]), list(carry[1])
        for u in range(unroll):
            j = steps - 1 - (i * unroll + u)
            here = pl.ds(pl.multiple_of(j * SUB, SUB), SUB)
            d, drive, g = delta_scr[here, :], drive_scr[here, :], grad_scr[here, :]
            dsum, weighted = [None] * 4, [None] * 4
            for n in range(states):
                cols = pl.ds(n * LANES, LANES)
                whole = adjoint[n] + g * readout_scr[here, cols]
                adjoint[n] = factor_scr[j * states + n] * whole
                through = adjoint[n] * state_scr[j * states + n]
                total[n] = total[n] + through * d
                dinject_scr[here, cols] += whole * drive
                term = through * rate_scr[n]
                dsum[n % 4] = term if dsum[n % 4] is None else dsum[n % 4] + term
                term = whole * inject_scr[here, cols]
                weighted[n % 4] = term if weighted[n % 4] is None else weighted[n % 4] + term
            weight = (weighted[0] + weighted[1]) + (weighted[2] + weighted[3])
            dsums = (dsum[0] + dsum[1]) + (dsum[2] + dsum[3])
            dactive_ref[here, :] = d * weight
            scanned_scr[here, :] = dsums * LN2
            grad_scr[here, :] = weight
        return tuple(adjoint), tuple(total)

    dskipped = skip * grad_scr[...]
    unused, total = lax.fori_loop(0, steps // unroll, backward, (tuple(adjoint0), zeros))
    dactive_ref[...] = dactive_ref[...] + skip * (graded_ref[...] * (gate * sigma))
    dpre = (scanned_scr[...] + active * grad_scr[...]) * jax.nn.sigmoid(pre_ref[...])
    dprelow_ref[...] = dpre.astype(BF16)
    dbias_ref[...] = jnp.sum(dpre, axis=0, keepdims=True)
    for n in range(states):
        drate_ref[n : n + 1, :] = (
            jnp.sum(total[n], axis=0, keepdims=True) * rate_scr[n, 0:1] * LN2
        )

    @pl.when(pl.program_id(0) == pl.num_programs(0) - 1)
    def _():
        shape = (states * LANES, 2 * states)
        for first, scr in ((0, dinject_scr), (states, dread_scr)):
            gather = (
                lax.broadcasted_iota(jnp.int32, shape, 0) // LANES + first
                == lax.broadcasted_iota(jnp.int32, shape, 1)
            ).astype(F32).astype(BF16)
            high = scr[...].astype(BF16)
            low = (scr[...] - high.astype(F32)).astype(BF16)
            part = jnp.dot(high, gather, preferred_element_type=F32) + jnp.dot(
                low, gather, preferred_element_type=F32
            )
            if first == 0:
                dselect_ref[...] = part
            else:
                dselect_ref[...] += part


def run_ends(pre, active, grad, select, decay_log, rank):
    rows, inner = pre.shape
    states = decay_log.shape[0]
    tall = pl.BlockSpec((rows, LANES), lambda e: (0, e))
    return pl.pallas_call(
        functools.partial(ends_kernel, rank, states),
        grid=(inner // LANES,),
        in_specs=[
            tall, tall, tall,
            pl.BlockSpec(select.shape, lambda e: (0, 0)),
            pl.BlockSpec((states, LANES), lambda e: (0, e)),
        ],
        out_specs=[
            pl.BlockSpec((SUB, LANES), lambda e: (0, e)),
            pl.BlockSpec((states, SUB, LANES), lambda e: (0, 0, e)),
            pl.BlockSpec((states, SUB, LANES), lambda e: (0, 0, e)),
            pl.BlockSpec((states, LANES), lambda e: (0, e)),
            pl.BlockSpec((states, LANES), lambda e: (0, e)),
        ],
        out_shape=[
            jax.ShapeDtypeStruct((SUB, inner), F32),
            jax.ShapeDtypeStruct((states, SUB, inner), F32),
            jax.ShapeDtypeStruct((states, SUB, inner), F32),
            jax.ShapeDtypeStruct((states, inner), F32),
            jax.ShapeDtypeStruct((states, inner), F32),
        ],
        scratch_shapes=[
            pltpu.VMEM((rows, states * LANES), F32),
            pltpu.VMEM((rows, states * LANES), F32),
            pltpu.VMEM((states, SUB, LANES), F32),
            pltpu.VMEM((rows, LANES), F32),
            pltpu.VMEM((rows, LANES), F32),
        ],
        compiler_params=pltpu.CompilerParams(vmem_limit_bytes=48 << 20),
        name="span_ends",
    )(pre, active, grad, select, decay_log)


def run_scan(pre, active, gate, graded, select, decay_log, skip, ahead, behind, start, incoming, rank):
    rows, inner = pre.shape
    states = decay_log.shape[0]
    tall = pl.BlockSpec((rows, LANES), lambda e: (0, e))
    line = pl.BlockSpec((1, LANES), lambda e: (0, e))
    table = pl.BlockSpec((states, LANES), lambda e: (0, e))
    cube = pl.BlockSpec((states, SUB, LANES), lambda e: (0, 0, e))
    wide = pltpu.VMEM((rows, states * LANES), F32)
    thin = pltpu.VMEM((rows, LANES), F32)
    return pl.pallas_call(
        functools.partial(scan_kernel, rank, states),
        grid=(inner // LANES,),
        in_specs=[
            tall, tall, tall, tall,
            pl.BlockSpec(select.shape, lambda e: (0, 0)),
            table, line, cube, cube, table, table,
        ],
        out_specs=[
            tall, tall, tall, tall, table, line, line,
            pl.BlockSpec((rows, 2 * states), lambda e: (0, 0)),
        ],
        out_shape=[
            jax.ShapeDtypeStruct((rows, inner), BF16),
            jax.ShapeDtypeStruct((rows, inner), BF16),
            jax.ShapeDtypeStruct((rows, inner), BF16),
            jax.ShapeDtypeStruct((rows, inner), F32),
            jax.ShapeDtypeStruct((states, inner), F32),
            jax.ShapeDtypeStruct((1, inner), F32),
            jax.ShapeDtypeStruct((1, inner), F32),
            jax.ShapeDtypeStruct((rows, 2 * states), F32),
        ],
        scratch_shapes=[
            wide, wide,
            pltpu.VMEM((states, SUB, LANES), F32),
            thin, thin, thin, thin,
            pltpu.VMEM(((rows // SUB + 1) * states, SUB, LANES), F32),
            pltpu.VMEM((rows // SUB * states, SUB, LANES), F32),
            wide, wide,
        ],
        compiler_params=pltpu.CompilerParams(vmem_limit_bytes=56 << 20),
        name="span_scan",
    )(pre, active, gate, graded, select, decay_log, skip, ahead, behind, start, incoming)


def carried(sums, ends, rates, ahead):
    count = sums.shape[0]
    me = lax.axis_index("seq")
    one = jnp.arange(count)[:, None]
    two = jnp.arange(count)[None, :]
    if ahead:
        between = (two > one) & (two < me)
        used = jnp.arange(count) < me
    else:
        between = (two < one) & (two > me)
        used = jnp.arange(count) > me
    gaps = jnp.sum(jnp.where(between[:, :, None], sums[None], 0.0), axis=1)
    reach = jnp.exp(gaps[:, None, :] * rates[None])
    return jnp.sum(jnp.where(used[:, None, None], reach * ends, 0.0), axis=0)


def on_device(
    byte_ids,
    embedding,
    cotangent,
    norm_gain,
    input_projection_weight,
    conv_weight,
    conv_bias,
    select_weight,
    step_weight,
    step_bias,
    decay_log,
    skip_gain,
    output_projection_weight,
):
    count, stretch = byte_ids.shape
    vocab, width = embedding.shape
    kernel, inner = conv_weight.shape
    states = decay_log.shape[0]
    rank = step_weight.shape[0]
    rows = count * stretch
    halo = kernel - 1
    ids = to_spans(byte_ids.reshape(rows, 1))
    one_hot = ids == jnp.arange(vocab, dtype=jnp.int32)[None, :]
    block_inputs = jnp.dot(one_hot.astype(BF16), embedding, preferred_element_type=F32)
    scale = lax.rsqrt(jnp.mean(block_inputs * block_inputs, axis=1, keepdims=True) + EPS)
    normed_input = (block_inputs * scale * norm_gain).astype(BF16)
    front = jnp.dot(
        normed_input, input_projection_weight[:, :inner], preferred_element_type=F32
    ).astype(BF16)
    gate = jnp.dot(
        normed_input, input_projection_weight[:, inner:], preferred_element_type=F32
    ).astype(BF16)
    last = front[rows - halo * SUB :].reshape(halo, SUB, inner)
    tail = passed_along(last[:, SUB - 1], "seq", 1)
    earlier = jnp.concatenate([tail[:, None], last[:, : SUB - 1]], axis=1)
    extended = jnp.concatenate([earlier.reshape(halo * SUB, inner), front], axis=0).astype(F32)
    mixed = conv_bias + conv_weight[0] * extended[:rows]
    for place in range(1, kernel):
        mixed = mixed + conv_weight[place] * extended[place * SUB : place * SUB + rows]
    active = jax.nn.silu(mixed).astype(BF16)
    select = jnp.dot(active, select_weight, preferred_element_type=F32).astype(BF16)
    lowrank = select[:, :rank]
    pre = jnp.dot(lowrank, step_weight, preferred_element_type=F32) + step_bias
    rates = -jnp.exp(decay_log)
    upstream = to_spans(cotangent.reshape(rows, width))
    graded = contract_cols(upstream, output_projection_weight)
    gate_real = gate.astype(F32)
    grad = graded * jax.nn.silu(gate_real)

    sums, ahead, behind, end, message = run_ends(pre, active, grad, select, decay_log, rank)
    all_sums = lax.all_gather(jnp.sum(sums, axis=0), "seq")
    all_ends = lax.all_gather(jnp.stack([end, message]), "seq")
    start = carried(all_sums, all_ends[:, 0], rates, True)
    incoming = carried(all_sums, all_ends[:, 1], rates, False)
    gated, d_gate, d_pre_low, d_active, d_decay_log, d_step_bias, d_skip_gain, d_pair = run_scan(
        pre, active, gate, graded, select, decay_log, skip_gain.reshape(1, inner),
        ahead, behind, start, incoming, rank,
    )

    result = block_inputs + jnp.dot(gated, output_projection_weight, preferred_element_type=F32)
    output = from_spans(result.astype(BF16)).reshape(count, stretch, width)
    d_output_weight = contract_rows(gated, upstream)
    d_step_weight = contract_rows(lowrank, d_pre_low)
    d_lowrank = contract_cols(d_pre_low, step_weight)
    d_select = jnp.concatenate([d_lowrank, d_pair], axis=1).astype(BF16)
    d_select_weight = contract_rows(active, d_select)
    d_mixed = (d_active + contract_cols(d_select, select_weight)) * silu_slope(mixed)
    d_conv_bias = jnp.sum(d_mixed, axis=0)
    d_conv_weight = jnp.stack(
        [
            jnp.sum(d_mixed * extended[place * SUB : place * SUB + rows], axis=0)
            for place in range(kernel)
        ]
    )
    first = d_mixed[: halo * SUB].reshape(halo, SUB, inner)
    after = passed_along(first[:, 0], "seq", -1)
    later = jnp.concatenate([first[:, 1:], after[:, None]], axis=1)
    spread = jnp.concatenate([d_mixed, later.reshape(halo * SUB, inner)], axis=0)
    d_front = conv_weight[halo] * spread[:rows]
    for place in range(1, kernel):
        d_front = d_front + conv_weight[halo - place] * spread[place * SUB : place * SUB + rows]
    d_both = jnp.concatenate([d_front.astype(BF16), d_gate], axis=1)
    d_input_weight = contract_rows(normed_input, d_both)
    d_normed = contract_cols(d_both, input_projection_weight)
    d_norm_gain = jnp.sum(d_normed * block_inputs * scale, axis=0)
    scaled = norm_gain * d_normed
    cubed = scale * scale * scale
    d_inputs = (
        upstream.astype(F32)
        + scale * scaled
        - block_inputs * cubed * jnp.mean(scaled * block_inputs, axis=1, keepdims=True)
    )
    high = d_inputs.astype(BF16)
    low = (d_inputs - high.astype(F32)).astype(BF16)
    hot = one_hot.astype(BF16)
    d_embedding = contract_rows(hot, high) + contract_rows(hot, low)
    everywhere = ("dp", "seq")
    large = [
        lax.psum(part.astype(BF16), everywhere).astype(F32)
        for part in (d_output_weight, d_input_weight, d_embedding)
    ]
    small = lax.psum(
        (
            d_norm_gain,
            d_conv_weight,
            d_conv_bias,
            d_select_weight,
            d_step_weight,
            d_step_bias.reshape(inner),
            d_decay_log,
            d_skip_gain.reshape(inner),
        ),
        everywhere,
    )
    return (
        output,
        from_spans(d_inputs).reshape(count, stretch, width),
        large[2],
        small[0],
        large[1],
        small[1],
        small[2],
        small[3],
        small[4],
        small[5],
        small[6],
        small[7],
        large[0],
    )


def solution(mesh):
    placed = (P("dp", "seq"), P(), P("dp", "seq", None)) + (P(),) * 10
    return jax.shard_map(
        on_device,
        mesh=mesh,
        in_specs=placed,
        out_specs=(P("dp", "seq", None), P("dp", "seq", None)) + (P(),) * 11,
        check_vma=False,
    )
```

```python
import functools
import math

import jax
import jax.numpy as jnp
from jax import lax
from jax.experimental import pallas as pl
from jax.experimental.pallas import tpu as pltpu
from jax.sharding import PartitionSpec as P

EPS = 1e-05
LANES = 128
SUB = 8
LOG2E = math.log2(math.e)
LN2 = math.log(2.0)
F32 = jnp.float32
BF16 = jnp.bfloat16
MESH = pl.DeviceIdType.MESH


def passed_along(value, axis, by):
    peers = lax.axis_size(axis)
    pairs = [(i, i + by) for i in range(peers) if 0 <= i + by < peers]
    return lax.ppermute(value, axis, pairs)


def silu_slope(value):
    sigma = jax.nn.sigmoid(value)
    return sigma * (1.0 + value * (1.0 - sigma))


def contract_rows(left, right):
    return lax.dot_general(
        left, right, (((0,), (0,)), ((), ())), preferred_element_type=F32
    )


def contract_cols(left, right):
    return lax.dot_general(
        left, right, (((1,), (1,)), ((), ())), preferred_element_type=F32
    )


def to_spans(array):
    rows = array.shape[0]
    return array.reshape(SUB, rows // SUB, -1).swapaxes(0, 1).reshape(rows, -1)


def from_spans(array):
    rows = array.shape[0]
    return array.reshape(rows // SUB, SUB, -1).swapaxes(0, 1).reshape(rows, -1)


def sublane(shape):
    return lax.broadcasted_iota(jnp.int32, shape, len(shape) - 2)


def shift_up(value, by, fill, reverse):
    place = sublane(value.shape)
    if reverse:
        moved = pltpu.roll(value, SUB - by, value.ndim - 2)
        return jnp.where(place < SUB - by, moved, fill)
    moved = pltpu.roll(value, by, value.ndim - 2)
    return jnp.where(place >= by, moved, fill)


def expand_columns(select, first, states):
    width = select.shape[1]
    shape = (width, states * LANES)
    source = lax.broadcasted_iota(jnp.int32, shape, 0)
    target = lax.broadcasted_iota(jnp.int32, shape, 1) // LANES + first
    spread = (source == target).astype(F32).astype(BF16)
    return jnp.dot(select, spread, preferred_element_type=F32)


def scaled_rates(decay_ref, rate_scr, states):
    rates = -jnp.exp(decay_ref[...]) * LOG2E
    for n in range(states):
        rate_scr[n] = jnp.broadcast_to(rates[n : n + 1], (SUB, LANES))


def ends_kernel(
    rank, states, pre_ref, active_ref, grad_ref, select_ref, decay_ref,
    sums_ref, ahead_ref, behind_ref, end_ref, message_ref,
    inject_scr, readout_scr, rate_scr, delta_scr, drive_scr,
):
    rows = pre_ref.shape[0]
    steps = rows // SUB

    @pl.when(pl.program_id(0) == 0)
    def _():
        inject_scr[...] = expand_columns(select_ref[...], rank, states)
        readout_scr[...] = expand_columns(select_ref[...], rank + states, states)

    scaled_rates(decay_ref, rate_scr, states)
    delta = jax.nn.softplus(pre_ref[...])
    delta_scr[...] = delta
    drive_scr[...] = delta * active_ref[...].astype(F32)
    unroll = 2

    def body(i, carry):
        total, state, message, decay = carry
        state, message, decay = list(state), list(message), list(decay)
        for u in range(unroll):
            here = pl.ds(pl.multiple_of((i * unroll + u) * SUB, SUB), SUB)
            d, drive, g = delta_scr[here, :], drive_scr[here, :], grad_ref[here, :]
            total = total + d
            for n in range(states):
                cols = pl.ds(n * LANES, LANES)
                factor = jnp.exp2(d * rate_scr[n])
                state[n] = factor * state[n] + drive * inject_scr[here, cols]
                decay[n] = decay[n] * factor
                message[n] = message[n] + decay[n] * (g * readout_scr[here, cols])
        return total, tuple(state), tuple(message), tuple(decay)

    zero = jnp.zeros((SUB, LANES), F32)
    total, state, message, decay = lax.fori_loop(
        0, steps // unroll, body,
        (zero, (zero,) * states, (zero,) * states, (jnp.ones((SUB, LANES), F32),) * states),
    )
    sums_ref[...] = total
    for n in range(states):
        for value, out, edge, reverse in (
            (state[n], ahead_ref, end_ref, False), (message[n], behind_ref, message_ref, True)
        ):
            factor = decay[n]
            for by in (1, 2, 4):
                value = value + factor * shift_up(value, by, 0.0, reverse)
                factor = factor * shift_up(factor, by, 1.0, reverse)
            out[n] = shift_up(value, 1, 0.0, reverse)
            last = 0 if reverse else SUB - 1
            edge[n : n + 1, :] = value[last : last + 1]


def scan_kernel(
    rank, states, pre_ref, active_ref, gate_ref, graded_ref, select_ref, decay_ref, skip_ref,
    ahead_ref, behind_ref, start_ref, incoming_ref,
    gated_ref, dgate_ref, dprelow_ref, dactive_ref, drate_ref, dbias_ref, dskip_ref, dselect_ref,
    inject_scr, readout_scr, rate_scr, delta_scr, drive_scr, grad_scr, scanned_scr,
    state_scr, factor_scr, dread_scr, dinject_scr,
):
    rows = pre_ref.shape[0]
    steps = rows // SUB

    @pl.when(pl.program_id(0) == 0)
    def _():
        inject_scr[...] = expand_columns(select_ref[...], rank, states)
        readout_scr[...] = expand_columns(select_ref[...], rank + states, states)
        dread_scr[...] = jnp.zeros_like(dread_scr)
        dinject_scr[...] = jnp.zeros_like(dinject_scr)

    scaled_rates(decay_ref, rate_scr, states)
    delta = jax.nn.softplus(pre_ref[...])
    delta_scr[...] = delta
    drive_scr[...] = delta * active_ref[...].astype(F32)
    gate = gate_ref[...].astype(F32)
    grad_scr[...] = graded_ref[...] * (gate * jax.nn.sigmoid(gate))
    total = jnp.zeros((SUB, LANES), F32)
    for j in range(steps):
        total = total + delta_scr[j * SUB : (j + 1) * SUB]
    before, after = total, total
    for by in (1, 2, 4):
        before = before + shift_up(before, by, 0.0, False)
        after = after + shift_up(after, by, 0.0, True)
    before, after = before - total, after - total
    unroll = 2
    begin = []
    for n in range(states):
        reach = jnp.exp2(before * rate_scr[n])
        begin.append(ahead_ref[n] + reach * start_ref[n : n + 1, :])
        state_scr[n] = begin[-1]

    def forward(i, state):
        state = list(state)
        for u in range(unroll):
            j = i * unroll + u
            here = pl.ds(pl.multiple_of(j * SUB, SUB), SUB)
            d, drive, g = delta_scr[here, :], drive_scr[here, :], grad_scr[here, :]
            sums = [None] * 4
            for n in range(states):
                cols = pl.ds(n * LANES, LANES)
                factor = jnp.exp2(d * rate_scr[n])
                factor_scr[j * states + n] = factor
                state[n] = factor * state[n] + drive * inject_scr[here, cols]
                state_scr[(j + 1) * states + n] = state[n]
                dread_scr[here, cols] += g * state[n]
                term = readout_scr[here, cols] * state[n]
                sums[n % 4] = term if sums[n % 4] is None else sums[n % 4] + term
            scanned_scr[here, :] = (sums[0] + sums[1]) + (sums[2] + sums[3])
        return tuple(state)

    lax.fori_loop(0, steps // unroll, forward, tuple(begin))

    active = active_ref[...].astype(F32)
    skip = skip_ref[...]
    gate = gate_ref[...].astype(F32)
    sigma = jax.nn.sigmoid(gate)
    scanned = scanned_scr[...] + skip * active
    gated_ref[...] = (scanned * (gate * sigma)).astype(BF16)
    dgate_ref[...] = (
        graded_ref[...] * scanned * (sigma * (1.0 + gate * (1.0 - sigma)))
    ).astype(BF16)
    dskip_ref[...] = jnp.sum(grad_scr[...] * active, axis=0, keepdims=True)

    adjoint0, zeros = [], (jnp.zeros((SUB, LANES), F32),) * states
    for n in range(states):
        reach = jnp.exp2(after * rate_scr[n])
        adjoint0.append(behind_ref[n] + reach * incoming_ref[n : n + 1, :])

    def backward(i, carry):
        adjoint, total = list(carry[0]), list(carry[1])
        for u in range(unroll):
            j = steps - 1 - (i * unroll + u)
            here = pl.ds(pl.multiple_of(j * SUB, SUB), SUB)
            d, drive, g = delta_scr[here, :], drive_scr[here, :], grad_scr[here, :]
            dsum, weighted = [None] * 4, [None] * 4
            for n in range(states):
                cols = pl.ds(n * LANES, LANES)
                whole = adjoint[n] + g * readout_scr[here, cols]
                adjoint[n] = factor_scr[j * states + n] * whole
                through = adjoint[n] * state_scr[j * states + n]
                total[n] = total[n] + through * d
                dinject_scr[here, cols] += whole * drive
                term = through * rate_scr[n]
                dsum[n % 4] = term if dsum[n % 4] is None else dsum[n % 4] + term
                term = whole * inject_scr[here, cols]
                weighted[n % 4] = term if weighted[n % 4] is None else weighted[n % 4] + term
            weight = (weighted[0] + weighted[1]) + (weighted[2] + weighted[3])
            dsums = (dsum[0] + dsum[1]) + (dsum[2] + dsum[3])
            dactive_ref[here, :] = d * weight
            scanned_scr[here, :] = dsums * LN2
            grad_scr[here, :] = weight
        return tuple(adjoint), tuple(total)

    dskipped = skip * grad_scr[...]
    unused, total = lax.fori_loop(0, steps // unroll, backward, (tuple(adjoint0), zeros))
    dactive_ref[...] = dactive_ref[...] + skip * (graded_ref[...] * (gate * sigma))
    dpre = (scanned_scr[...] + active * grad_scr[...]) * jax.nn.sigmoid(pre_ref[...])
    dprelow_ref[...] = dpre.astype(BF16)
    dbias_ref[...] = jnp.sum(dpre, axis=0, keepdims=True)
    for n in range(states):
        drate_ref[n : n + 1, :] = (
            jnp.sum(total[n], axis=0, keepdims=True) * rate_scr[n, 0:1] * LN2
        )

    @pl.when(pl.program_id(0) == pl.num_programs(0) - 1)
    def _():
        shape = (states * LANES, 2 * states)
        for first, scr in ((0, dinject_scr), (states, dread_scr)):
            gather = (
                lax.broadcasted_iota(jnp.int32, shape, 0) // LANES + first
                == lax.broadcasted_iota(jnp.int32, shape, 1)
            ).astype(F32).astype(BF16)
            high = scr[...].astype(BF16)
            low = (scr[...] - high.astype(F32)).astype(BF16)
            part = jnp.dot(high, gather, preferred_element_type=F32) + jnp.dot(
                low, gather, preferred_element_type=F32
            )
            if first == 0:
                dselect_ref[...] = part
            else:
                dselect_ref[...] += part


def run_ends(pre, active, grad, select, decay_log, rank):
    rows, inner = pre.shape
    states = decay_log.shape[0]
    tall = pl.BlockSpec((rows, LANES), lambda e: (0, e))
    return pl.pallas_call(
        functools.partial(ends_kernel, rank, states),
        grid=(inner // LANES,),
        in_specs=[
            tall, tall, tall,
            pl.BlockSpec(select.shape, lambda e: (0, 0)),
            pl.BlockSpec((states, LANES), lambda e: (0, e)),
        ],
        out_specs=[
            pl.BlockSpec((SUB, LANES), lambda e: (0, e)),
            pl.BlockSpec((states, SUB, LANES), lambda e: (0, 0, e)),
            pl.BlockSpec((states, SUB, LANES), lambda e: (0, 0, e)),
            pl.BlockSpec((states, LANES), lambda e: (0, e)),
            pl.BlockSpec((states, LANES), lambda e: (0, e)),
        ],
        out_shape=[
            jax.ShapeDtypeStruct((SUB, inner), F32),
            jax.ShapeDtypeStruct((states, SUB, inner), F32),
            jax.ShapeDtypeStruct((states, SUB, inner), F32),
            jax.ShapeDtypeStruct((states, inner), F32),
            jax.ShapeDtypeStruct((states, inner), F32),
        ],
        scratch_shapes=[
            pltpu.VMEM((rows, states * LANES), F32),
            pltpu.VMEM((rows, states * LANES), F32),
            pltpu.VMEM((states, SUB, LANES), F32),
            pltpu.VMEM((rows, LANES), F32),
            pltpu.VMEM((rows, LANES), F32),
        ],
        compiler_params=pltpu.CompilerParams(vmem_limit_bytes=48 << 20),
        name="span_ends",
    )(pre, active, grad, select, decay_log)


def run_scan(pre, active, gate, graded, select, decay_log, skip, ahead, behind, start, incoming, rank):
    rows, inner = pre.shape
    states = decay_log.shape[0]
    tall = pl.BlockSpec((rows, LANES), lambda e: (0, e))
    line = pl.BlockSpec((1, LANES), lambda e: (0, e))
    table = pl.BlockSpec((states, LANES), lambda e: (0, e))
    cube = pl.BlockSpec((states, SUB, LANES), lambda e: (0, 0, e))
    wide = pltpu.VMEM((rows, states * LANES), F32)
    thin = pltpu.VMEM((rows, LANES), F32)
    return pl.pallas_call(
        functools.partial(scan_kernel, rank, states),
        grid=(inner // LANES,),
        in_specs=[
            tall, tall, tall, tall,
            pl.BlockSpec(select.shape, lambda e: (0, 0)),
            table, line, cube, cube, table, table,
        ],
        out_specs=[
            tall, tall, tall, tall, table, line, line,
            pl.BlockSpec((rows, 2 * states), lambda e: (0, 0)),
        ],
        out_shape=[
            jax.ShapeDtypeStruct((rows, inner), BF16),
            jax.ShapeDtypeStruct((rows, inner), BF16),
            jax.ShapeDtypeStruct((rows, inner), BF16),
            jax.ShapeDtypeStruct((rows, inner), F32),
            jax.ShapeDtypeStruct((states, inner), F32),
            jax.ShapeDtypeStruct((1, inner), F32),
            jax.ShapeDtypeStruct((1, inner), F32),
            jax.ShapeDtypeStruct((rows, 2 * states), F32),
        ],
        scratch_shapes=[
            wide, wide,
            pltpu.VMEM((states, SUB, LANES), F32),
            thin, thin, thin, thin,
            pltpu.VMEM(((rows // SUB + 1) * states, SUB, LANES), F32),
            pltpu.VMEM((rows // SUB * states, SUB, LANES), F32),
            wide, wide,
        ],
        compiler_params=pltpu.CompilerParams(vmem_limit_bytes=56 << 20),
        name="span_scan",
    )(pre, active, gate, graded, select, decay_log, skip, ahead, behind, start, incoming)


def bit_of(index, step):
    return (index // step) % 2

def other(axis, step):
    place = lax.axis_index(axis)
    place = place + step * (1 - 2 * bit_of(place, step))
    if axis == "dp":
        return (place, lax.axis_index("seq"))
    return (lax.axis_index("dp"), place)

CORE, X, Y, Z, ZZ = ("seq", 1), ("dp", 1), ("dp", 2), ("seq", 2), ("seq", 4)

class Exchange:
    def __init__(self, acc, out, landing, extra, send_sem, recv_sem, rows, window, seq):
        self.acc, self.out, self.landing, self.extra = acc, out, landing, extra
        self.send_sem, self.recv_sem = send_sem, recv_sem
        self.rows, self.window = rows, window
        self.more = [("seq", step) for step in (8 << i for i in range(12)) if step < seq]
        self.orders = ((CORE, X, Y, Z, ZZ), (CORE, Y, X, Z, ZZ))
        self.halvings = 5
        self.phases = 2 * self.halvings + len(self.more)
        quarter = rows // 4
        core = bit_of(lax.axis_index("seq"), 1)
        self.core_base = core * (rows // 2)
        self.kept = []
        for s, order in enumerate(self.orders):
            base, size = core * (rows // 2) + s * quarter, quarter
            spans = [(base, size)]
            for axis, step in order[1:]:
                size = size // 2
                base = base + bit_of(lax.axis_index(axis), step) * size
                spans.append((base, size))
            self.kept.append(spans)

    def partners(self):
        return [other(*link) for link in (CORE, X, Y, Z, ZZ)] + [other(*link) for link in self.more]

    def greet(self):
        barrier = pltpu.get_barrier_semaphore()
        partners = self.partners()
        for device in partners:
            pl.semaphore_signal(barrier, inc=1, device_id=device, device_id_type=MESH)
        pl.semaphore_wait(barrier, len(partners))

    def sent(self, s, level):
        base, size = self.kept[s][level]
        axis, step = self.orders[s][level]
        before = self.kept[s][level - 1][0]
        mine = bit_of(lax.axis_index(axis), step)
        return before + (1 - mine) * size, size

    def span(self, ref, k, base, size):
        return ref.at[k, pl.ds(pl.multiple_of(base, 16), size), :]

    def copies(self, k, p):
        w = lax.rem(k, self.window)
        rows, levels, more = self.rows, self.halvings, len(self.more)
        out = []
        def copy(s, src, dst, link):
            return pltpu.make_async_remote_copy(
                src_ref=src, dst_ref=dst, send_sem=self.send_sem.at[w, p, s], recv_sem=self.recv_sem.at[w, p, s],
                device_id=other(*link), device_id_type=MESH)
        if p == 0:
            src = self.span(self.acc, k, rows // 2 - self.core_base, rows // 2)
            return [copy(0, src, self.landing.at[w, pl.ds(0, rows // 2), :], CORE)]
        if p == levels * 2 + more - 1:
            half = self.span(self.out, k, self.core_base, rows // 2)
            return [copy(0, half, half, CORE)]
        for s in range(2):
            if p < levels:
                base, size = self.sent(s, p)
                dst = self.landing.at[w, pl.ds(self.land(p, s), size), :]
                out.append(copy(s, self.span(self.acc, k, base, size), dst, self.orders[s][p]))
            elif p < levels + more:
                base, size = self.kept[s][-1]
                dst = self.extra.at[w, p - levels, pl.ds(s * size, size), :]
                out.append(copy(s, self.span(self.acc, k, base, size), dst, self.more[p - levels]))
            else:
                level = 2 * levels + more - 1 - p
                piece = self.span(self.out, k, *self.kept[s][level])
                out.append(copy(s, piece, piece, self.orders[s][level]))
        return out

    def land(self, p, s):
        size = self.rows // 4 >> p
        start = self.rows // 2 + sum(2 * (self.rows // 4 >> q) for q in range(1, p))
        return start + s * size

    def add(self, k, base, source, first, size, target):
        step = math.gcd(size, 128)
        w = lax.rem(k, self.window)
        def body(i, _):
            here = pl.ds(pl.multiple_of(base + i * step, 16), step)
            there = pl.ds(pl.multiple_of(first + i * step, 16), step)
            target[k, here, :] = (self.acc[k, here, :].astype(F32) + source(w, there).astype(F32)).astype(BF16)
            return 0
        lax.fori_loop(0, size // step, body, 0)

    def finish(self, k, p):
        for copy in self.copies(k, p):
            copy.wait()
        levels, more = self.halvings, len(self.more)
        target = self.out if p == levels + more - 1 else self.acc
        landed = lambda w, there: self.landing[w, there, :]
        if p == 0:
            self.add(k, self.core_base, landed, 0, self.rows // 2, self.acc)
        elif p < levels:
            for s in range(2):
                base, size = self.kept[s][p]
                self.add(k, base, landed, self.land(p, s), size, target)
        elif p < levels + more:
            for s in range(2):
                base, size = self.kept[s][-1]
                self.add(k, base, lambda w, there: self.extra[w, p - levels, there, :], s * size, size, target)

    def advance(self, k, p):
        if p > 0:
            self.finish(k, p - 1)
        if p < self.phases:
            for copy in self.copies(k, p):
                copy.start()

def scratch(chunks, rows, window, seq):
    more = len([1 for i in range(12) if (8 << i) < seq])
    phases = 10 + more
    return [
        pltpu.VMEM((chunks, rows, LANES), BF16),
        pltpu.VMEM((chunks, rows, LANES), BF16),
        pltpu.VMEM((window, rows, LANES), BF16),
        pltpu.VMEM((window, max(more, 1), rows // 32, LANES), BF16),
        pltpu.SemaphoreType.DMA((window, phases, 2)),
        pltpu.SemaphoreType.DMA((window, phases, 2)),
    ]

def blocks(shape, rows):
    height, width = shape
    pieces = []
    at = 0
    for b in range(width // LANES):
        for r in range(0, height, rows):
            size = min(rows, height - r)
            pieces.append((at // rows, r, b * LANES, at % rows, size))
            at += size
    assert at % rows == 0
    return at // rows, pieces

def sum_kernel(rows, window, seq, shapes, gap, *refs):
    n = len(shapes)
    ins, outs = refs[:n], refs[n:2*n]
    acc, out, landing, extra, send_sem, recv_sem, load_sem, store_sem = refs[2 * n :]
    ex = Exchange(acc, out, landing, extra, send_sem, recv_sem, rows, window, seq)
    count = acc.shape[0]
    loads, stores = {}, {}
    first = 0
    for i, shape in enumerate(shapes):
        used, pieces = blocks(shape, rows)
        for j, (c, r, lane, at, size) in enumerate(pieces):
            hbm = lambda ref: ref.at[pl.ds(r, size), pl.ds(lane, LANES)]
            vm = acc.at[first + c, pl.ds(at, size), :]
            done = out.at[first + c, pl.ds(at, size), :]
            loads.setdefault(first + c, []).append(pltpu.make_async_copy(hbm(ins[i]), vm, load_sem.at[first + c]))
            stores.setdefault(first + c, []).append(pltpu.make_async_copy(done, hbm(outs[i]), store_sem.at[first + c]))
        first += used
    for c in range(count):
        for copy in loads[c]:
            copy.start()
    ex.greet()
    whole = lambda c, ref, sem: pltpu.make_async_copy(ref.at[c], ref.at[c], sem)
    def slot(t, _):
        for p in range(ex.phases, -1, -1):
            k = t - p * gap
            @pl.when((k >= 0) & (k < count))
            def _():
                if p == 0:
                    whole(k, acc, load_sem.at[k]).wait()
                ex.advance(k, p)
                if p == ex.phases:
                    for c in range(count):
                        @pl.when(k == c)
                        def _():
                            for copy in stores[c]:
                                copy.start()
        return 0
    lax.fori_loop(0, count + ex.phases * gap, slot, 0)
    def done(c, _):
        whole(c, out, store_sem.at[c]).wait()
        return 0
    lax.fori_loop(0, count, done, 0)

def sum_everywhere(arrays, seq, rows=2048, window=22, collective_id=0, gap=2):
    shapes = [a.shape for a in arrays]
    count = sum(blocks(s, rows)[0] for s in shapes)
    hbm = pl.BlockSpec(memory_space=pltpu.HBM)
    return pl.pallas_call(
        functools.partial(sum_kernel, rows, window, seq, shapes, gap),
        out_shape=[jax.ShapeDtypeStruct(s, BF16) for s in shapes],
        in_specs=[hbm] * len(arrays), out_specs=[hbm] * len(arrays),
        scratch_shapes=scratch(count, rows, window, seq) + [pltpu.SemaphoreType.DMA((count,)), pltpu.SemaphoreType.DMA((count,))],
        compiler_params=pltpu.CompilerParams(collective_id=collective_id, has_side_effects=True, vmem_limit_bytes=60 << 20),
        name="sum_everywhere",
    )(*arrays)


def carried(sums, ends, rates, ahead):
    count = sums.shape[0]
    me = lax.axis_index("seq")
    one = jnp.arange(count)[:, None]
    two = jnp.arange(count)[None, :]
    if ahead:
        between = (two > one) & (two < me)
        used = jnp.arange(count) < me
    else:
        between = (two < one) & (two > me)
        used = jnp.arange(count) > me
    gaps = jnp.sum(jnp.where(between[:, :, None], sums[None], 0.0), axis=1)
    reach = jnp.exp(gaps[:, None, :] * rates[None])
    return jnp.sum(jnp.where(used[:, None, None], reach * ends, 0.0), axis=0)


def on_device(
    byte_ids,
    embedding,
    cotangent,
    norm_gain,
    input_projection_weight,
    conv_weight,
    conv_bias,
    select_weight,
    step_weight,
    step_bias,
    decay_log,
    skip_gain,
    output_projection_weight,
):
    count, stretch = byte_ids.shape
    vocab, width = embedding.shape
    kernel, inner = conv_weight.shape
    states = decay_log.shape[0]
    rank = step_weight.shape[0]
    rows = count * stretch
    halo = kernel - 1
    ids = to_spans(byte_ids.reshape(rows, 1))
    one_hot = ids == jnp.arange(vocab, dtype=jnp.int32)[None, :]
    block_inputs = jnp.dot(one_hot.astype(BF16), embedding, preferred_element_type=F32)
    scale = lax.rsqrt(jnp.mean(block_inputs * block_inputs, axis=1, keepdims=True) + EPS)
    normed_input = (block_inputs * scale * norm_gain).astype(BF16)
    front = jnp.dot(
        normed_input, input_projection_weight[:, :inner], preferred_element_type=F32
    ).astype(BF16)
    gate = jnp.dot(
        normed_input, input_projection_weight[:, inner:], preferred_element_type=F32
    ).astype(BF16)
    last = front[rows - halo * SUB :].reshape(halo, SUB, inner)
    tail = passed_along(last[:, SUB - 1], "seq", 1)
    earlier = jnp.concatenate([tail[:, None], last[:, : SUB - 1]], axis=1)
    extended = jnp.concatenate([earlier.reshape(halo * SUB, inner), front], axis=0).astype(F32)
    mixed = conv_bias + conv_weight[0] * extended[:rows]
    for place in range(1, kernel):
        mixed = mixed + conv_weight[place] * extended[place * SUB : place * SUB + rows]
    active = jax.nn.silu(mixed).astype(BF16)
    select = jnp.dot(active, select_weight, preferred_element_type=F32).astype(BF16)
    lowrank = select[:, :rank]
    pre = jnp.dot(lowrank, step_weight, preferred_element_type=F32) + step_bias
    rates = -jnp.exp(decay_log)
    upstream = to_spans(cotangent.reshape(rows, width))
    graded = contract_cols(upstream, output_projection_weight)
    gate_real = gate.astype(F32)
    grad = graded * jax.nn.silu(gate_real)

    sums, ahead, behind, end, message = run_ends(pre, active, grad, select, decay_log, rank)
    all_sums = lax.all_gather(jnp.sum(sums, axis=0), "seq")
    all_ends = lax.all_gather(jnp.stack([end, message]), "seq")
    start = carried(all_sums, all_ends[:, 0], rates, True)
    incoming = carried(all_sums, all_ends[:, 1], rates, False)
    gated, d_gate, d_pre_low, d_active, d_decay_log, d_step_bias, d_skip_gain, d_pair = run_scan(
        pre, active, gate, graded, select, decay_log, skip_gain.reshape(1, inner),
        ahead, behind, start, incoming, rank,
    )

    result = block_inputs + jnp.dot(gated, output_projection_weight, preferred_element_type=F32)
    output = from_spans(result.astype(BF16)).reshape(count, stretch, width)
    d_output_weight = contract_rows(gated, upstream)
    d_step_weight = contract_rows(lowrank, d_pre_low)
    d_lowrank = contract_cols(d_pre_low, step_weight)
    d_select = jnp.concatenate([d_lowrank, d_pair], axis=1).astype(BF16)
    d_select_weight = contract_rows(active, d_select)
    d_mixed = (d_active + contract_cols(d_select, select_weight)) * silu_slope(mixed)
    d_conv_bias = jnp.sum(d_mixed, axis=0)
    d_conv_weight = jnp.stack(
        [
            jnp.sum(d_mixed * extended[place * SUB : place * SUB + rows], axis=0)
            for place in range(kernel)
        ]
    )
    first = d_mixed[: halo * SUB].reshape(halo, SUB, inner)
    after = passed_along(first[:, 0], "seq", -1)
    later = jnp.concatenate([first[:, 1:], after[:, None]], axis=1)
    spread = jnp.concatenate([d_mixed, later.reshape(halo * SUB, inner)], axis=0)
    d_front = conv_weight[halo] * spread[:rows]
    for place in range(1, kernel):
        d_front = d_front + conv_weight[halo - place] * spread[place * SUB : place * SUB + rows]
    d_both = jnp.concatenate([d_front.astype(BF16), d_gate], axis=1)
    d_input_weight = contract_rows(normed_input, d_both)
    d_normed = contract_cols(d_both, input_projection_weight)
    d_norm_gain = jnp.sum(d_normed * block_inputs * scale, axis=0)
    scaled = norm_gain * d_normed
    cubed = scale * scale * scale
    d_inputs = (
        upstream.astype(F32)
        + scale * scaled
        - block_inputs * cubed * jnp.mean(scaled * block_inputs, axis=1, keepdims=True)
    )
    high = d_inputs.astype(BF16)
    low = (d_inputs - high.astype(F32)).astype(BF16)
    hot = one_hot.astype(BF16)
    d_embedding = contract_rows(hot, high) + contract_rows(hot, low)
    small = (
        d_norm_gain,
        d_conv_weight,
        d_conv_bias,
        d_select_weight,
        d_step_weight,
        d_step_bias,
        d_decay_log,
        d_skip_gain,
    )
    flat = jnp.concatenate([part.astype(BF16).reshape(-1) for part in small])
    unit = 2048 * LANES
    flat = jnp.pad(flat, (0, -flat.size % unit)).reshape(-1, LANES)
    d_input_sum, d_output_sum, d_embedding_sum, flat = (
        part.astype(F32)
        for part in sum_everywhere(
            [d_input_weight.astype(BF16), d_output_weight.astype(BF16), d_embedding.astype(BF16), flat],
            lax.axis_size("seq"),
        )
    )
    flat = flat.reshape(-1)
    sums, at = [], 0
    shapes = [norm_gain, conv_weight, conv_bias, select_weight, step_weight, step_bias, decay_log, skip_gain]
    for like in shapes:
        sums.append(flat[at : at + like.size].reshape(like.shape))
        at += like.size
    return (
        output,
        from_spans(d_inputs).reshape(count, stretch, width),
        d_embedding_sum,
        sums[0],
        d_input_sum,
        sums[1],
        sums[2],
        sums[3],
        sums[4],
        sums[5],
        sums[6],
        sums[7],
        d_output_sum,
    )


def solution(mesh):
    placed = (P("dp", "seq"), P(), P("dp", "seq", None)) + (P(),) * 10
    return jax.shard_map(
        on_device,
        mesh=mesh,
        in_specs=placed,
        out_specs=(P("dp", "seq", None), P("dp", "seq", None)) + (P(),) * 11,
        check_vma=False,
    )
```

```python
import functools
import math

import jax
import jax.numpy as jnp
from jax import lax
from jax.experimental import pallas as pl
from jax.experimental.pallas import tpu as pltpu
from jax.sharding import PartitionSpec as P

EPS = 1e-05
LANES = 128
SUB = 8
LOG2E = math.log2(math.e)
LN2 = math.log(2.0)
F32 = jnp.float32
BF16 = jnp.bfloat16
MESH = pl.DeviceIdType.MESH


def passed_along(value, axis, by):
    peers = lax.axis_size(axis)
    pairs = [(i, i + by) for i in range(peers) if 0 <= i + by < peers]
    return lax.ppermute(value, axis, pairs)


def silu_slope(value):
    sigma = jax.nn.sigmoid(value)
    return sigma * (1.0 + value * (1.0 - sigma))


def contract_rows(left, right):
    return lax.dot_general(
        left, right, (((0,), (0,)), ((), ())), preferred_element_type=F32
    )


def contract_cols(left, right):
    return lax.dot_general(
        left, right, (((1,), (1,)), ((), ())), preferred_element_type=F32
    )


def to_spans(array):
    rows = array.shape[0]
    return array.reshape(SUB, rows // SUB, -1).swapaxes(0, 1).reshape(rows, -1)


def from_spans(array):
    rows = array.shape[0]
    return array.reshape(rows // SUB, SUB, -1).swapaxes(0, 1).reshape(rows, -1)


def sublane(shape):
    return lax.broadcasted_iota(jnp.int32, shape, len(shape) - 2)


def shift_up(value, by, fill, reverse):
    place = sublane(value.shape)
    if reverse:
        moved = pltpu.roll(value, SUB - by, value.ndim - 2)
        return jnp.where(place < SUB - by, moved, fill)
    moved = pltpu.roll(value, by, value.ndim - 2)
    return jnp.where(place >= by, moved, fill)


def expand_columns(select, first, states):
    width = select.shape[1]
    shape = (width, states * LANES)
    source = lax.broadcasted_iota(jnp.int32, shape, 0)
    target = lax.broadcasted_iota(jnp.int32, shape, 1) // LANES + first
    spread = (source == target).astype(F32).astype(BF16)
    return jnp.dot(select, spread, preferred_element_type=F32)


def tree_sum(value):
    while value.shape[0] > 1:
        half = value.shape[0] // 2
        value = value[:half] + value[half:]
    return value[0]


def early_chunks(inner, phases):
    slots = 2 * (inner // LANES)
    return min((slots - 4 - phases) // 2 + 1, inner // LANES) // 2 * 2


class Prefix:
    states = 16

    def __init__(self, totals, landing, start, incoming, gaps, rates, send_sem, recv_sem, rounds):
        self.totals, self.landing, self.start, self.incoming, self.gaps = totals, landing, start, incoming, gaps
        self.rates, self.send_sem, self.recv_sem, self.rounds = rates, send_sem, recv_sem, rounds

    def copy(self, e, r):
        return pltpu.make_async_remote_copy(
            src_ref=self.totals.at[e], dst_ref=self.landing.at[e, r],
            send_sem=self.send_sem.at[e, r], recv_sem=self.recv_sem.at[e, r],
            device_id=other("seq", 1 << r), device_id_type=MESH,
        )

    def advance(self, e, r):
        if r > 0:
            self.copy(e, r - 1).wait()
            self.merge(e, r - 1)
        if r < self.rounds:
            self.copy(e, r).start()

    def merge(self, e, r):
        n = self.rates.shape[1]
        rates = self.rates[e]
        later = bit_of(lax.axis_index("seq"), 1 << r) == 1
        end, message, total = self.totals[e, :n], self.totals[e, n : 2 * n], self.totals[e, 2 * n : 2 * n + 1]
        end2, message2 = self.landing[e, r, :n], self.landing[e, r, n : 2 * n]
        total2 = self.landing[e, r, 2 * n : 2 * n + 1]

        @pl.when(later)
        def _():
            gap = self.gaps[e, 0:1]
            self.start[e] = self.start[e] + jnp.exp2(gap * rates) * end2
            self.gaps[e, 0:1] = gap + total2

        @pl.when(jnp.logical_not(later))
        def _():
            gap = self.gaps[e, 1:2]
            self.incoming[e] = self.incoming[e] + jnp.exp2(gap * rates) * message2
            self.gaps[e, 1:2] = gap + total2

        if r < self.rounds - 1:
            reach, reach2 = jnp.exp2(total * rates), jnp.exp2(total2 * rates)
            self.totals[e, :n] = jnp.where(later, end + reach * end2, end2 + reach2 * end)
            self.totals[e, n : 2 * n] = jnp.where(later, message2 + reach2 * message, message + reach * message2)
            self.totals[e, 2 * n : 2 * n + 1] = total + total2


def scan_kernel(
    rank, states, chunk, rounds, seq,
    pre_ref, active_ref, gate_ref, graded_ref, select_ref, decay_ref, skip_ref, normed_ref, upstream_ref,
    gated_ref, dgate_ref, dprelow_ref, dactive_ref, drate_ref, dbias_ref, dskip_ref, dselect_ref,
    gate_sum, out_sum, gate_part, out_part,
    inject_scr, readout_scr, dread_scr, dinject_scr, state_scr, factor_scr,
    rates_scr, rate_scr, delta_scr, drive_scr, grad_scr, scan_scr, weight_scr,
    ahead_scr, behind_scr, sums_scr, gated_scr, dgated_scr,
    totals, totals_in, start_scr, incoming_scr, gaps_scr, prefix_send, prefix_recv,
    acc, out, landing, extra, send_sem, recv_sem, store_sem,
):
    rows = pre_ref.shape[0]
    steps = rows // SUB
    step = pl.program_id(0)
    tiles = pl.num_programs(0) // 2
    count = 2 * rates_scr.shape[0] // 2
    width = upstream_ref.shape[1]
    tile = lax.rem(step, tiles)
    prefix = Prefix(
        totals, totals_in, start_scr, incoming_scr, gaps_scr, rates_scr, prefix_send, prefix_recv, rounds
    )
    ex = Exchange(acc, out, landing, extra, send_sem, recv_sem, chunk, landing.shape[0], seq)
    early = early_chunks(count * LANES, ex.phases)
    half, unroll = states // 2, 8
    halves = [pl.ds(0, half), pl.ds(half, half)]

    def stores(k, kind):
        pair, final = k // 2, kind < 2
        at = pair - (0 if final else early // 2)
        source = (out if final else acc).at[k]
        copies = []
        if kind % 2 == 0:
            target = gate_sum if final else gate_part
            for side in range(2):
                lanes = pl.ds(pl.multiple_of(at * 2 * LANES + side * LANES, LANES), LANES)
                copies.append((source.at[pl.ds(side * width, width), :], target.at[:, lanes]))
        else:
            target = out_sum if final else out_part
            tall = pl.ds(pl.multiple_of(at * 2 * LANES, 2 * LANES), 2 * LANES)
            for b in range(width // LANES):
                copies.append((
                    source.at[pl.ds(b * 2 * LANES, 2 * LANES), :], target.at[tall, pl.ds(b * LANES, LANES)]
                ))
        for source, target in copies:
            pltpu.make_async_copy(source, target, store_sem.at[k]).start()

    def store(k):
        for kind in range(4):
            fits = (lax.rem(k, 2) == kind % 2) & ((k < early) if kind < 2 else (k >= early))

            @pl.when(fits)
            def _():
                stores(k, kind)

    @pl.when(step == 0)
    def _():
        for first, scr in ((rank, inject_scr), (rank + states, readout_scr)):
            wide = expand_columns(select_ref[...], first, states)
            for n in range(states):
                scr[:, n] = wide[:, n * LANES : (n + 1) * LANES].reshape(steps, SUB, LANES)
        dread_scr[...] = jnp.zeros_like(dread_scr)
        dinject_scr[...] = jnp.zeros_like(dinject_scr)
        start_scr[...] = jnp.zeros_like(start_scr)
        incoming_scr[...] = jnp.zeros_like(incoming_scr)
        gaps_scr[...] = jnp.zeros_like(gaps_scr)
        for e in range(count):
            rates_scr[e] = -jnp.exp(decay_ref[:, e * LANES : (e + 1) * LANES]) * LOG2E
        ex.greet()

    rates = rates_scr[tile]
    for n in range(states):
        rate_scr[n] = jnp.broadcast_to(rates[n : n + 1], (SUB, LANES))
    flat = lambda value: value.reshape(steps, SUB, LANES)
    active = active_ref[...].astype(F32)
    delta = jax.nn.softplus(pre_ref[...])
    delta_scr[...] = flat(delta)
    drive_scr[...] = flat(delta * active)
    gate = gate_ref[...].astype(F32)
    sigma = jax.nn.sigmoid(gate)
    grad_scr[...] = flat(graded_ref[...] * (gate * sigma))
    zero = jnp.zeros((half, SUB, LANES), F32)

    @pl.when(step < tiles)
    def _():
        total = jnp.sum(delta_scr[...], axis=0)
        sums_scr[tile] = total
        whole = jnp.sum(total, axis=0, keepdims=True)
        totals[tile, 2 * states :] = jnp.broadcast_to(whole, (SUB, LANES))
        for h, part in enumerate(halves):

            def ends(i, carry):
                state, message, decay = carry
                for u in range(unroll):
                    j = i * unroll + u
                    factor = jnp.exp2(delta_scr[j][None] * rate_scr[part])
                    state = factor * state + drive_scr[j][None] * inject_scr[j, part]
                    decay = decay * factor
                    message = message + decay * (grad_scr[j][None] * readout_scr[j, part])
                return state, message, decay

            state, message, decay = lax.fori_loop(0, steps // unroll, ends, (zero, zero, zero + 1.0))
            for value, kept, at, reverse in (
                (state, ahead_scr, h * half, False), (message, behind_scr, states + h * half, True)
            ):
                factor = decay
                for by in (1, 2, 4):
                    value = value + factor * shift_up(value, by, 0.0, reverse)
                    factor = factor * shift_up(factor, by, 1.0, reverse)
                kept[tile, part] = shift_up(value, 1, 0.0, reverse)
                last = 0 if reverse else SUB - 1
                for n in range(half):
                    totals[tile, at + n : at + n + 1] = value[n, last : last + 1]

    def spread(table):
        return jnp.concatenate(
            [jnp.broadcast_to(table[n : n + 1], (1, SUB, LANES)) for n in range(states)], axis=0
        )

    @pl.when(step >= tiles)
    def _():
        c = step - tiles
        total = sums_scr[tile]
        before, after = total, total
        for by in (1, 2, 4):
            before = before + shift_up(before, by, 0.0, False)
            after = after + shift_up(after, by, 0.0, True)
        before, after = before - total, after - total
        state_scr[0] = ahead_scr[tile] + jnp.exp2(before[None] * rate_scr[...]) * spread(start_scr[tile])

        def forward(i, state):
            for u in range(unroll // 2):
                j = i * (unroll // 2) + u
                factor = jnp.exp2(delta_scr[j][None] * rate_scr[...])
                factor_scr[j] = factor
                state = factor * state + drive_scr[j][None] * inject_scr[j]
                state_scr[j + 1] = state
                dread_scr[j] += grad_scr[j][None] * state
                scan_scr[j] = tree_sum(readout_scr[j] * state)
            return state

        lax.fori_loop(0, steps // (unroll // 2), forward, state_scr[0])
        for p in range(ex.phases - 1 + ex.phases % 2, 0, -2):
            k = c - (3 + p) // 2

            @pl.when((k >= 0) & (k < early))
            def _():
                ex.advance(k, p)
                if p == ex.phases:
                    store(k)

        active = active_ref[...].astype(F32)
        skip = skip_ref[...]
        gate = gate_ref[...].astype(F32)
        sigma = jax.nn.sigmoid(gate)
        graded = graded_ref[...]
        scanned = scan_scr[...].reshape(rows, LANES) + skip * active
        gated = (scanned * (gate * sigma)).astype(BF16)
        gated_ref[...] = gated
        dgate = (graded * scanned * (sigma * (1.0 + gate * (1.0 - sigma)))).astype(BF16)
        dgate_ref[...] = dgate
        dskip_ref[...] = jnp.sum(graded * (gate * sigma) * active, axis=0, keepdims=True)
        odd = lax.rem(c, 2)

        @pl.when(odd == 0)
        def _():
            gated_scr[:, :LANES] = gated
            dgated_scr[:, :LANES] = dgate

        @pl.when(odd == 1)
        def _():
            gated_scr[:, LANES:] = gated
            dgated_scr[:, LANES:] = dgate

        adjoint0 = behind_scr[tile] + jnp.exp2(after[None] * rate_scr[...]) * spread(incoming_scr[tile])
        state_scr[steps] = adjoint0
        for h, part in enumerate(halves):

            def backward(i, carry):
                adjoint, total = carry
                for u in range(unroll):
                    j = steps - 1 - (i * unroll + u)
                    d, g = delta_scr[j], grad_scr[j]
                    whole = adjoint + g[None] * readout_scr[j, part]
                    adjoint = factor_scr[j, part] * whole
                    through = adjoint * state_scr[j, part]
                    total = total + through * d[None]
                    dinject_scr[j, part] += whole * drive_scr[j][None]
                    one = tree_sum(through * rate_scr[part])
                    two = tree_sum(whole * inject_scr[j, part])
                    scan_scr[j] = scan_scr[j] + one if h else one
                    weight_scr[j] = weight_scr[j] + two if h else two
                return adjoint, total

            unused, total = lax.fori_loop(0, steps // unroll, backward, (state_scr[steps, part], zero))
            for n in range(half):
                at = h * half + n
                drate_ref[at : at + 1, :] = (
                    jnp.sum(total[n], axis=0, keepdims=True) * rate_scr[at, 0:1] * LN2
                )
        weight = weight_scr[...].reshape(rows, LANES)
        delta = delta_scr[...].reshape(rows, LANES)
        active = active_ref[...].astype(F32)
        dactive_ref[...] = delta * weight + skip_ref[...] * grad_scr[...].reshape(rows, LANES)
        dpre = (scan_scr[...].reshape(rows, LANES) * LN2 + active * weight) * jax.nn.sigmoid(pre_ref[...])
        dprelow_ref[...] = dpre.astype(BF16)
        dbias_ref[...] = jnp.sum(dpre, axis=0, keepdims=True)

        @pl.when(odd == 1)
        def _():
            pair = c // 2
            block = chunk // 8

            def gates(i, _):
                here = pl.ds(pl.multiple_of(i * block, block), block)
                part = jnp.dot(normed_ref[here, :], dgated_scr[...], preferred_element_type=F32).astype(BF16)
                acc[2 * pair, here, :] = part[:, :LANES]
                acc[2 * pair, pl.ds(pl.multiple_of(width + i * block, block), block), :] = part[:, LANES:]
                return 0

            lax.fori_loop(0, width // block, gates, 0)
            for b in range(width // (2 * LANES)):
                part = contract_rows(gated_scr[...], upstream_ref[:, b * 2 * LANES : (b + 1) * 2 * LANES]).astype(BF16)
                for side in range(2):
                    at = (2 * b + side) * 2 * LANES
                    acc[2 * pair + 1, at : at + 2 * LANES, :] = part[:, side * LANES : (side + 1) * LANES]

            @pl.when(2 * pair >= early)
            def _():
                store(2 * pair)
                store(2 * pair + 1)

    @pl.when(step >= tiles)
    def _():
        c = step - tiles
        for p in range(ex.phases - ex.phases % 2, -1, -2):
            k = c - 1 - p // 2

            @pl.when((k >= 0) & (k < early))
            def _():
                ex.advance(k, p)
                if p == ex.phases:
                    store(k)

    for r in range(rounds, -1, -1):
        e = step - 2 * r

        @pl.when((e >= 0) & (e < tiles))
        def _():
            prefix.advance(e, r)

    @pl.when(step == 2 * tiles - 1)
    def _():
        ones = jnp.ones((LANES, LANES), BF16)
        for first, scr in ((0, dinject_scr), (states, dread_scr)):
            for n in range(states):
                value = scr[:, n].reshape(rows, LANES)
                high = value.astype(BF16)
                low = (value - high.astype(F32)).astype(BF16)
                part = jnp.dot(high, ones, preferred_element_type=F32) + jnp.dot(
                    low, ones, preferred_element_type=F32
                )
                dselect_ref[:, first + n : first + n + 1] = part[:, first + n : first + n + 1]

        def done(k, _):
            pltpu.make_async_copy(acc.at[k], acc.at[k], store_sem.at[k]).wait()
            return 0

        lax.fori_loop(0, count, done, 0)


def run_scan(pre, active, gate, graded, select, decay_log, skip, normed, upstream, rank, seq):
    rows, inner = pre.shape
    states = decay_log.shape[0]
    width = upstream.shape[1]
    chunk = 2 * width
    tiles, steps = inner // LANES, rows // SUB
    rounds = seq.bit_length() - 1
    phases = 10 + max(rounds - 3, 0)
    early = early_chunks(inner, phases)
    first = early * LANES
    tall = pl.BlockSpec((rows, LANES), lambda i: (0, lax.rem(i, tiles)))
    line = pl.BlockSpec((1, LANES), lambda i: (0, lax.rem(i, tiles)))
    late = lambda shape: pl.BlockSpec(shape, lambda i: (0, lax.max(i - tiles, 0)))
    whole = lambda a: pl.BlockSpec(a.shape, lambda i: (0, 0), pipeline_mode=pl.Buffered(1))
    hbm = pl.BlockSpec(memory_space=pltpu.HBM)
    wide = pltpu.VMEM((steps, states, SUB, LANES), F32)
    thin = pltpu.VMEM((steps, SUB, LANES), F32)
    cube = pltpu.VMEM((tiles, states, SUB, LANES), F32)
    small = pltpu.VMEM((tiles, states, LANES), F32)
    pair = pltpu.VMEM((rows, 2 * LANES), BF16)
    buffers = scratch(tiles, chunk, early, seq)
    buffers[1] = pltpu.VMEM((early, chunk, LANES), BF16)
    return pl.pallas_call(
        functools.partial(scan_kernel, rank, states, chunk, rounds, seq),
        grid=(2 * tiles,),
        in_specs=[
            tall, tall, tall, tall, whole(select), whole(decay_log), line, whole(normed), whole(upstream),
        ],
        out_specs=[
            late((rows, LANES)), late((rows, LANES)), late((rows, LANES)), late((rows, LANES)),
            late((states, LANES)), late((1, LANES)), late((1, LANES)),
            pl.BlockSpec((rows, 2 * states), lambda i: (0, 0)), hbm, hbm, hbm, hbm,
        ],
        out_shape=[
            jax.ShapeDtypeStruct((rows, inner), BF16),
            jax.ShapeDtypeStruct((rows, inner), BF16),
            jax.ShapeDtypeStruct((rows, inner), BF16),
            jax.ShapeDtypeStruct((rows, inner), F32),
            jax.ShapeDtypeStruct((states, inner), F32),
            jax.ShapeDtypeStruct((1, inner), F32),
            jax.ShapeDtypeStruct((1, inner), F32),
            jax.ShapeDtypeStruct((rows, 2 * states), F32),
            jax.ShapeDtypeStruct((width, first), BF16),
            jax.ShapeDtypeStruct((first, width), BF16),
            jax.ShapeDtypeStruct((width, inner - first), BF16),
            jax.ShapeDtypeStruct((inner - first, width), BF16),
        ],
        scratch_shapes=[
            wide, wide, wide, wide,
            pltpu.VMEM((steps + 1, states, SUB, LANES), F32), wide,
            small, pltpu.VMEM((states, SUB, LANES), F32), thin, thin, thin, thin, thin,
            cube, cube, pltpu.VMEM((tiles, SUB, LANES), F32), pair, pair,
            pltpu.VMEM((tiles, 2 * states + SUB, LANES), F32),
            pltpu.VMEM((tiles, rounds, 2 * states + SUB, LANES), F32),
            small, small, pltpu.VMEM((tiles, SUB, LANES), F32),
            pltpu.SemaphoreType.DMA((tiles, rounds)), pltpu.SemaphoreType.DMA((tiles, rounds)),
        ]
        + buffers
        + [pltpu.SemaphoreType.DMA((tiles,))],
        compiler_params=pltpu.CompilerParams(
            collective_id=1, has_side_effects=True, vmem_limit_bytes=62 << 20
        ),
        name="span_scan",
    )(pre, active, gate, graded, select, decay_log, skip, normed, upstream)


def bit_of(index, step):
    return (index // step) % 2

def other(axis, step):
    place = lax.axis_index(axis)
    place = place + step * (1 - 2 * bit_of(place, step))
    if axis == "dp":
        return (place, lax.axis_index("seq"))
    return (lax.axis_index("dp"), place)

CORE, X, Y, Z, ZZ = ("seq", 1), ("dp", 1), ("dp", 2), ("seq", 2), ("seq", 4)

class Exchange:
    def __init__(self, acc, out, landing, extra, send_sem, recv_sem, rows, window, seq):
        self.acc, self.out, self.landing, self.extra = acc, out, landing, extra
        self.send_sem, self.recv_sem = send_sem, recv_sem
        self.rows, self.window = rows, window
        self.more = [("seq", step) for step in (8 << i for i in range(12)) if step < seq]
        self.orders = ((CORE, X, Y, Z, ZZ), (CORE, Y, X, Z, ZZ))
        self.halvings = 5
        self.phases = 2 * self.halvings + len(self.more)
        quarter = rows // 4
        core = bit_of(lax.axis_index("seq"), 1)
        self.core_base = core * (rows // 2)
        self.kept = []
        for s, order in enumerate(self.orders):
            base, size = core * (rows // 2) + s * quarter, quarter
            spans = [(base, size)]
            for axis, step in order[1:]:
                size = size // 2
                base = base + bit_of(lax.axis_index(axis), step) * size
                spans.append((base, size))
            self.kept.append(spans)

    def partners(self):
        return [other(*link) for link in (CORE, X, Y, Z, ZZ)] + [other(*link) for link in self.more]

    def greet(self):
        barrier = pltpu.get_barrier_semaphore()
        partners = self.partners()
        for device in partners:
            pl.semaphore_signal(barrier, inc=1, device_id=device, device_id_type=MESH)
        pl.semaphore_wait(barrier, len(partners))

    def sent(self, s, level):
        base, size = self.kept[s][level]
        axis, step = self.orders[s][level]
        before = self.kept[s][level - 1][0]
        mine = bit_of(lax.axis_index(axis), step)
        return before + (1 - mine) * size, size

    def span(self, ref, k, base, size):
        return ref.at[k, pl.ds(pl.multiple_of(base, 16), size), :]

    def copies(self, k, p):
        w = lax.rem(k, self.window)
        rows, levels, more = self.rows, self.halvings, len(self.more)
        out = []
        def copy(s, src, dst, link):
            return pltpu.make_async_remote_copy(
                src_ref=src, dst_ref=dst, send_sem=self.send_sem.at[w, p, s], recv_sem=self.recv_sem.at[w, p, s],
                device_id=other(*link), device_id_type=MESH)
        if p == 0:
            src = self.span(self.acc, k, rows // 2 - self.core_base, rows // 2)
            return [copy(0, src, self.landing.at[w, pl.ds(0, rows // 2), :], CORE)]
        if p == levels * 2 + more - 1:
            half = self.span(self.out, k, self.core_base, rows // 2)
            return [copy(0, half, half, CORE)]
        for s in range(2):
            if p < levels:
                base, size = self.sent(s, p)
                dst = self.landing.at[w, pl.ds(self.land(p, s), size), :]
                out.append(copy(s, self.span(self.acc, k, base, size), dst, self.orders[s][p]))
            elif p < levels + more:
                base, size = self.kept[s][-1]
                dst = self.extra.at[w, p - levels, pl.ds(s * size, size), :]
                out.append(copy(s, self.span(self.acc, k, base, size), dst, self.more[p - levels]))
            else:
                level = 2 * levels + more - 1 - p
                piece = self.span(self.out, k, *self.kept[s][level])
                out.append(copy(s, piece, piece, self.orders[s][level]))
        return out

    def land(self, p, s):
        size = self.rows // 4 >> p
        start = self.rows // 2 + sum(2 * (self.rows // 4 >> q) for q in range(1, p))
        return start + s * size

    def add(self, k, base, source, first, size, target):
        step = math.gcd(size, 128)
        w = lax.rem(k, self.window)
        def body(i, _):
            here = pl.ds(pl.multiple_of(base + i * step, 16), step)
            there = pl.ds(pl.multiple_of(first + i * step, 16), step)
            target[k, here, :] = (self.acc[k, here, :].astype(F32) + source(w, there).astype(F32)).astype(BF16)
            return 0
        lax.fori_loop(0, size // step, body, 0)

    def finish(self, k, p):
        for copy in self.copies(k, p):
            copy.wait()
        levels, more = self.halvings, len(self.more)
        target = self.out if p == levels + more - 1 else self.acc
        landed = lambda w, there: self.landing[w, there, :]
        if p == 0:
            self.add(k, self.core_base, landed, 0, self.rows // 2, self.acc)
        elif p < levels:
            for s in range(2):
                base, size = self.kept[s][p]
                self.add(k, base, landed, self.land(p, s), size, target)
        elif p < levels + more:
            for s in range(2):
                base, size = self.kept[s][-1]
                self.add(k, base, lambda w, there: self.extra[w, p - levels, there, :], s * size, size, target)

    def advance(self, k, p):
        if p > 0:
            self.finish(k, p - 1)
        if p < self.phases:
            for copy in self.copies(k, p):
                copy.start()

def scratch(chunks, rows, window, seq):
    more = len([1 for i in range(12) if (8 << i) < seq])
    phases = 10 + more
    return [
        pltpu.VMEM((chunks, rows, LANES), BF16),
        pltpu.VMEM((chunks, rows, LANES), BF16),
        pltpu.VMEM((window, rows, LANES), BF16),
        pltpu.VMEM((window, max(more, 1), rows // 32, LANES), BF16),
        pltpu.SemaphoreType.DMA((window, phases, 2)),
        pltpu.SemaphoreType.DMA((window, phases, 2)),
    ]

def blocks(shape, rows):
    height, width = shape
    pieces = []
    at = 0
    for b in range(width // LANES):
        r = 0
        while r < height:
            size = min(height - r, rows - at % rows)
            pieces.append((at // rows, r, b * LANES, at % rows, size))
            at += size
            r += size
    assert at % rows == 0
    return at // rows, pieces


def sum_kernel(rows, window, seq, shapes, gap, *refs):
    n = len(shapes)
    ins, outs = refs[:n], refs[n:2*n]
    acc, out, landing, extra, send_sem, recv_sem, load_sem, store_sem = refs[2 * n :]
    ex = Exchange(acc, out, landing, extra, send_sem, recv_sem, rows, window, seq)
    count = acc.shape[0]
    loads, stores = {}, {}
    first = 0
    for i, shape in enumerate(shapes):
        used, pieces = blocks(shape, rows)
        for j, (c, r, lane, at, size) in enumerate(pieces):
            hbm = lambda ref: ref.at[pl.ds(r, size), pl.ds(lane, LANES)]
            vm = acc.at[first + c, pl.ds(at, size), :]
            done = out.at[first + c, pl.ds(at, size), :]
            loads.setdefault(first + c, []).append(pltpu.make_async_copy(hbm(ins[i]), vm, load_sem.at[first + c]))
            stores.setdefault(first + c, []).append(pltpu.make_async_copy(done, hbm(outs[i]), store_sem.at[first + c]))
        first += used
    for c in range(count):
        for copy in loads[c]:
            copy.start()
    ex.greet()
    whole = lambda c, ref, sem: pltpu.make_async_copy(ref.at[c], ref.at[c], sem)
    def slot(t, _):
        for p in range(ex.phases, -1, -1):
            k = t - p * gap
            @pl.when((k >= 0) & (k < count))
            def _():
                if p == 0:
                    whole(k, acc, load_sem.at[k]).wait()
                ex.advance(k, p)
                if p == ex.phases:
                    for c in range(count):
                        @pl.when(k == c)
                        def _():
                            for copy in stores[c]:
                                copy.start()
        return 0
    lax.fori_loop(0, count + ex.phases * gap, slot, 0)
    def done(c, _):
        whole(c, out, store_sem.at[c]).wait()
        return 0
    lax.fori_loop(0, count, done, 0)

def sum_everywhere(arrays, seq, rows=2048, window=22, collective_id=0, gap=2):
    shapes = [a.shape for a in arrays]
    count = sum(blocks(s, rows)[0] for s in shapes)
    hbm = pl.BlockSpec(memory_space=pltpu.HBM)
    return pl.pallas_call(
        functools.partial(sum_kernel, rows, window, seq, shapes, gap),
        out_shape=[jax.ShapeDtypeStruct(s, BF16) for s in shapes],
        in_specs=[hbm] * len(arrays), out_specs=[hbm] * len(arrays),
        scratch_shapes=scratch(count, rows, window, seq) + [pltpu.SemaphoreType.DMA((count,)), pltpu.SemaphoreType.DMA((count,))],
        compiler_params=pltpu.CompilerParams(collective_id=collective_id, has_side_effects=True, vmem_limit_bytes=60 << 20),
        name="sum_everywhere",
    )(*arrays)


def on_device(
    byte_ids,
    embedding,
    cotangent,
    norm_gain,
    input_projection_weight,
    conv_weight,
    conv_bias,
    select_weight,
    step_weight,
    step_bias,
    decay_log,
    skip_gain,
    output_projection_weight,
):
    count, stretch = byte_ids.shape
    vocab, width = embedding.shape
    kernel, inner = conv_weight.shape
    states = decay_log.shape[0]
    rank = step_weight.shape[0]
    rows = count * stretch
    halo = kernel - 1
    ids = to_spans(byte_ids.reshape(rows, 1))
    one_hot = ids == jnp.arange(vocab, dtype=jnp.int32)[None, :]
    block_inputs = jnp.dot(one_hot.astype(BF16), embedding, preferred_element_type=F32)
    scale = lax.rsqrt(jnp.mean(block_inputs * block_inputs, axis=1, keepdims=True) + EPS)
    normed_input = (block_inputs * scale * norm_gain).astype(BF16)
    front = jnp.dot(
        normed_input, input_projection_weight[:, :inner], preferred_element_type=F32
    ).astype(BF16)
    gate = jnp.dot(
        normed_input, input_projection_weight[:, inner:], preferred_element_type=F32
    ).astype(BF16)
    last = front[rows - halo * SUB :].reshape(halo, SUB, inner)
    tail = passed_along(last[:, SUB - 1], "seq", 1)
    earlier = jnp.concatenate([tail[:, None], last[:, : SUB - 1]], axis=1)
    extended = jnp.concatenate([earlier.reshape(halo * SUB, inner), front], axis=0).astype(F32)
    mixed = conv_bias + conv_weight[0] * extended[:rows]
    for place in range(1, kernel):
        mixed = mixed + conv_weight[place] * extended[place * SUB : place * SUB + rows]
    active = jax.nn.silu(mixed).astype(BF16)
    select = jnp.dot(active, select_weight, preferred_element_type=F32).astype(BF16)
    lowrank = select[:, :rank]
    pre = jnp.dot(lowrank, step_weight, preferred_element_type=F32) + step_bias
    upstream = to_spans(cotangent.reshape(rows, width))
    graded = contract_cols(upstream, output_projection_weight)
    (
        gated, d_gate, d_pre_low, d_active, d_decay_log, d_step_bias, d_skip_gain, d_pair,
        gate_sum, out_sum, gate_part, out_part,
    ) = run_scan(
        pre, active, gate, graded, select, decay_log, skip_gain.reshape(1, inner),
        normed_input.T, upstream, rank, lax.axis_size("seq"),
    )

    result = block_inputs + jnp.dot(gated, output_projection_weight, preferred_element_type=F32)
    output = from_spans(result.astype(BF16)).reshape(count, stretch, width)
    d_step_weight = contract_rows(lowrank, d_pre_low)
    d_lowrank = contract_cols(d_pre_low, step_weight)
    d_select = jnp.concatenate([d_lowrank, d_pair], axis=1).astype(BF16)
    d_select_weight = contract_rows(active, d_select)
    d_mixed = (d_active + contract_cols(d_select, select_weight)) * silu_slope(mixed)
    d_conv_bias = jnp.sum(d_mixed, axis=0)
    d_conv_weight = jnp.stack(
        [
            jnp.sum(d_mixed * extended[place * SUB : place * SUB + rows], axis=0)
            for place in range(kernel)
        ]
    )
    first = d_mixed[: halo * SUB].reshape(halo, SUB, inner)
    after = passed_along(first[:, 0], "seq", -1)
    later = jnp.concatenate([first[:, 1:], after[:, None]], axis=1)
    spread = jnp.concatenate([d_mixed, later.reshape(halo * SUB, inner)], axis=0)
    d_front = conv_weight[halo] * spread[:rows]
    for place in range(1, kernel):
        d_front = d_front + conv_weight[halo - place] * spread[place * SUB : place * SUB + rows]
    d_front = d_front.astype(BF16)
    d_both = jnp.concatenate([d_front, d_gate], axis=1)
    d_front_weight = contract_rows(normed_input, d_front)
    d_normed = contract_cols(d_both, input_projection_weight)
    d_norm_gain = jnp.sum(d_normed * block_inputs * scale, axis=0)
    scaled = norm_gain * d_normed
    cubed = scale * scale * scale
    d_inputs = (
        upstream.astype(F32)
        + scale * scaled
        - block_inputs * cubed * jnp.mean(scaled * block_inputs, axis=1, keepdims=True)
    )
    high = d_inputs.astype(BF16)
    low = (d_inputs - high.astype(F32)).astype(BF16)
    hot = one_hot.astype(BF16)
    d_embedding = contract_rows(hot, high) + contract_rows(hot, low)
    small = (
        d_norm_gain,
        d_conv_weight,
        d_conv_bias,
        d_select_weight,
        d_step_weight,
        d_step_bias,
        d_decay_log,
        d_skip_gain,
    )
    flat = jnp.concatenate([part.astype(BF16).reshape(-1) for part in small])
    unit = 2048 * LANES
    flat = jnp.pad(flat, (0, -flat.size % unit)).reshape(-1, LANES)
    front_sum, gate_rest, out_rest, embedding_sum, flat = sum_everywhere(
        [d_front_weight.astype(BF16), gate_part, out_part, d_embedding.astype(BF16), flat], lax.axis_size("seq")
    )
    d_input_sum = jnp.concatenate([front_sum, gate_sum, gate_rest], axis=1).astype(F32)
    d_output_sum = jnp.concatenate([out_sum, out_rest], axis=0).astype(F32)
    d_embedding_sum = embedding_sum.astype(F32)
    flat = flat.astype(F32)
    flat = flat.reshape(-1)
    sums, at = [], 0
    shapes = [norm_gain, conv_weight, conv_bias, select_weight, step_weight, step_bias, decay_log, skip_gain]
    for like in shapes:
        sums.append(flat[at : at + like.size].reshape(like.shape))
        at += like.size
    return (
        output,
        from_spans(d_inputs).reshape(count, stretch, width),
        d_embedding_sum,
        sums[0],
        d_input_sum,
        sums[1],
        sums[2],
        sums[3],
        sums[4],
        sums[5],
        sums[6],
        sums[7],
        d_output_sum,
    )


def solution(mesh):
    placed = (P("dp", "seq"), P(), P("dp", "seq", None)) + (P(),) * 10
    return jax.shard_map(
        on_device,
        mesh=mesh,
        in_specs=placed,
        out_specs=(P("dp", "seq", None), P("dp", "seq", None)) + (P(),) * 11,
        check_vma=False,
    )
```

```python
import functools
import math

import jax
import jax.numpy as jnp
from jax import lax
from jax.experimental import pallas as pl
from jax.experimental.pallas import tpu as pltpu
from jax.sharding import PartitionSpec as P

EPS = 1e-05
LANES = 128
SUB = 8
LOG2E = math.log2(math.e)
LN2 = math.log(2.0)
F32 = jnp.float32
BF16 = jnp.bfloat16
MESH = pl.DeviceIdType.MESH


def passed_along(value, axis, by):
    peers = lax.axis_size(axis)
    pairs = [(i, i + by) for i in range(peers) if 0 <= i + by < peers]
    return lax.ppermute(value, axis, pairs)


def silu_slope(value):
    sigma = jax.nn.sigmoid(value)
    return sigma * (1.0 + value * (1.0 - sigma))


def contract_rows(left, right):
    return lax.dot_general(
        left, right, (((0,), (0,)), ((), ())), preferred_element_type=F32
    )


def contract_cols(left, right):
    return lax.dot_general(
        left, right, (((1,), (1,)), ((), ())), preferred_element_type=F32
    )


def to_spans(array):
    rows = array.shape[0]
    return array.reshape(SUB, rows // SUB, -1).swapaxes(0, 1).reshape(rows, -1)


def from_spans(array):
    rows = array.shape[0]
    return array.reshape(rows // SUB, SUB, -1).swapaxes(0, 1).reshape(rows, -1)


def sublane(shape):
    return lax.broadcasted_iota(jnp.int32, shape, len(shape) - 2)


def shift_up(value, by, fill, reverse):
    place = sublane(value.shape)
    if reverse:
        moved = pltpu.roll(value, SUB - by, value.ndim - 2)
        return jnp.where(place < SUB - by, moved, fill)
    moved = pltpu.roll(value, by, value.ndim - 2)
    return jnp.where(place >= by, moved, fill)


def expand_columns(select, first, states):
    width = select.shape[1]
    shape = (width, states * LANES)
    source = lax.broadcasted_iota(jnp.int32, shape, 0)
    target = lax.broadcasted_iota(jnp.int32, shape, 1) // LANES + first
    spread = (source == target).astype(F32).astype(BF16)
    return jnp.dot(select, spread, preferred_element_type=F32)


def tree_sum(value):
    while value.shape[0] > 1:
        half = value.shape[0] // 2
        value = value[:half] + value[half:]
    return value[0]


def slot_of(k, p):
    return 3 * k + 5 + 2 * p


def turns(phases, place):
    return [(p, (place - 5 - 2 * p) // 3) for p in range(phases, -1, -1) if (place - 5 - 2 * p) % 3 == 0]


def done_early(tiles, phases):
    return sum(slot_of(k, phases) < 3 * tiles for k in range(tiles))


def next_phase(k, tiles):
    return next(p for p in range(1000) if slot_of(k, p) >= 3 * tiles)


class Prefix:
    def __init__(self, totals, landing, start, incoming, gaps, rates, send_sem, recv_sem, rounds):
        self.totals, self.landing, self.start, self.incoming, self.gaps = totals, landing, start, incoming, gaps
        self.rates, self.send_sem, self.recv_sem, self.rounds = rates, send_sem, recv_sem, rounds

    def copy(self, e, r):
        return pltpu.make_async_remote_copy(
            src_ref=self.totals.at[e], dst_ref=self.landing.at[e, r],
            send_sem=self.send_sem.at[e, r], recv_sem=self.recv_sem.at[e, r],
            device_id=other("seq", 1 << r), device_id_type=MESH,
        )

    def advance(self, e, r):
        if r > 0:
            self.copy(e, r - 1).wait()
            self.merge(e, r - 1)
        if r < self.rounds:
            self.copy(e, r).start()

    def merge(self, e, r):
        n = self.rates.shape[1]
        rates = self.rates[e]
        later = bit_of(lax.axis_index("seq"), 1 << r) == 1
        end, message, total = self.totals[e, :n], self.totals[e, n : 2 * n], self.totals[e, 2 * n : 2 * n + 1]
        end2, message2 = self.landing[e, r, :n], self.landing[e, r, n : 2 * n]
        total2 = self.landing[e, r, 2 * n : 2 * n + 1]

        @pl.when(later)
        def _():
            gap = self.gaps[e, 0:1]
            self.start[e] = self.start[e] + jnp.exp2(gap * rates) * end2
            self.gaps[e, 0:1] = gap + total2

        @pl.when(jnp.logical_not(later))
        def _():
            gap = self.gaps[e, 1:2]
            self.incoming[e] = self.incoming[e] + jnp.exp2(gap * rates) * message2
            self.gaps[e, 1:2] = gap + total2

        if r < self.rounds - 1:
            reach, reach2 = jnp.exp2(total * rates), jnp.exp2(total2 * rates)
            self.totals[e, :n] = jnp.where(later, end + reach * end2, end2 + reach2 * end)
            self.totals[e, n : 2 * n] = jnp.where(later, message2 + reach2 * message, message + reach * message2)
            self.totals[e, 2 * n : 2 * n + 1] = total + total2


def scan_kernel(
    rank, states, chunk, rounds, seq,
    pre_ref, active_ref, gate_ref, graded_ref, select_ref, decay_ref, skip_ref, normed_ref, upstream_ref,
    gated_ref, dgate_ref, dprelow_ref, dactive_ref, drate_ref, dbias_ref, dskip_ref, dselect_ref,
    gate_sum, out_sum, handed,
    inject_scr, readout_scr, dread_scr, dinject_scr, state_scr, factor_scr,
    rates_scr, rate_scr, delta_scr, drive_scr, grad_scr, scan_scr, weight_scr,
    ahead_scr, behind_scr, sums_scr, gated_scr, dgated_scr,
    totals, totals_in, start_scr, incoming_scr, gaps_scr, prefix_send, prefix_recv,
    acc, out, landing, extra, send_sem, recv_sem, store_sem,
):
    rows = pre_ref.shape[0]
    steps = rows // SUB
    step = pl.program_id(0)
    tiles = pl.num_programs(0) // 2
    count = 2 * rates_scr.shape[0] // 2
    width = upstream_ref.shape[1]
    tile = lax.rem(step, tiles)
    prefix = Prefix(
        totals, totals_in, start_scr, incoming_scr, gaps_scr, rates_scr, prefix_send, prefix_recv, rounds
    )
    ex = Exchange(acc, out, landing, extra, send_sem, recv_sem, chunk, landing.shape[0], seq)
    early = done_early(count, ex.phases)
    half, unroll = states // 2, 8
    halves = [pl.ds(0, half), pl.ds(half, half)]

    def store(k):
        pair = k // 2

        @pl.when(lax.rem(k, 2) == 0)
        def _():
            store_lanes(out.at[k], gate_sum, pair, store_sem.at[k])

        @pl.when(lax.rem(k, 2) == 1)
        def _():
            store_rows(out.at[k], out_sum, pair, store_sem.at[k])

    def take_turns(place):
        c = step - tiles
        for p, shift in turns(ex.phases, place):
            k = c + shift

            @pl.when(k >= 0)
            def _():
                ex.advance(k, p)
                if p == ex.phases:
                    store(k)

    @pl.when(step == 0)
    def _():
        for first, scr in ((rank, inject_scr), (rank + states, readout_scr)):
            wide = expand_columns(select_ref[...], first, states)
            for n in range(states):
                scr[:, n] = wide[:, n * LANES : (n + 1) * LANES].reshape(steps, SUB, LANES)
        dread_scr[...] = jnp.zeros_like(dread_scr)
        dinject_scr[...] = jnp.zeros_like(dinject_scr)
        start_scr[...] = jnp.zeros_like(start_scr)
        incoming_scr[...] = jnp.zeros_like(incoming_scr)
        gaps_scr[...] = jnp.zeros_like(gaps_scr)
        for e in range(count):
            rates_scr[e] = -jnp.exp(decay_ref[:, e * LANES : (e + 1) * LANES]) * LOG2E
        ex.greet()

    rates = rates_scr[tile]
    for n in range(states):
        rate_scr[n] = jnp.broadcast_to(rates[n : n + 1], (SUB, LANES))
    flat = lambda value: value.reshape(steps, SUB, LANES)
    active = active_ref[...].astype(F32)
    delta = jax.nn.softplus(pre_ref[...])
    delta_scr[...] = flat(delta)
    drive_scr[...] = flat(delta * active)
    gate = gate_ref[...].astype(F32)
    sigma = jax.nn.sigmoid(gate)
    grad_scr[...] = flat(graded_ref[...] * (gate * sigma))
    zero = jnp.zeros((half, SUB, LANES), F32)

    @pl.when(step < tiles)
    def _():
        total = jnp.sum(delta_scr[...], axis=0)
        sums_scr[tile] = total
        whole = jnp.sum(total, axis=0, keepdims=True)
        totals[tile, 2 * states :] = jnp.broadcast_to(whole, (SUB, LANES))
        for h, part in enumerate(halves):

            def ends(i, carry):
                state, message, decay = carry
                for u in range(unroll):
                    j = i * unroll + u
                    factor = jnp.exp2(delta_scr[j][None] * rate_scr[part])
                    state = factor * state + drive_scr[j][None] * inject_scr[j, part]
                    decay = decay * factor
                    message = message + decay * (grad_scr[j][None] * readout_scr[j, part])
                return state, message, decay

            state, message, decay = lax.fori_loop(0, steps // unroll, ends, (zero, zero, zero + 1.0))
            for value, kept, at, reverse in (
                (state, ahead_scr, h * half, False), (message, behind_scr, states + h * half, True)
            ):
                factor = decay
                for by in (1, 2, 4):
                    value = value + factor * shift_up(value, by, 0.0, reverse)
                    factor = factor * shift_up(factor, by, 1.0, reverse)
                kept[tile, part] = shift_up(value, 1, 0.0, reverse)
                last = 0 if reverse else SUB - 1
                for n in range(half):
                    totals[tile, at + n : at + n + 1] = value[n, last : last + 1]

    def spread(table):
        return jnp.concatenate(
            [jnp.broadcast_to(table[n : n + 1], (1, SUB, LANES)) for n in range(states)], axis=0
        )

    @pl.when(step >= tiles)
    def _():
        c = step - tiles
        total = sums_scr[tile]
        before, after = total, total
        for by in (1, 2, 4):
            before = before + shift_up(before, by, 0.0, False)
            after = after + shift_up(after, by, 0.0, True)
        before, after = before - total, after - total
        state_scr[0] = ahead_scr[tile] + jnp.exp2(before[None] * rate_scr[...]) * spread(start_scr[tile])

        def forward(i, state):
            for u in range(unroll // 2):
                j = i * (unroll // 2) + u
                factor = jnp.exp2(delta_scr[j][None] * rate_scr[...])
                factor_scr[j] = factor
                state = factor * state + drive_scr[j][None] * inject_scr[j]
                state_scr[j + 1] = state
                dread_scr[j] += grad_scr[j][None] * state
                scan_scr[j] = tree_sum(readout_scr[j] * state)
            return state

        lax.fori_loop(0, steps // (unroll // 2), forward, state_scr[0])
        take_turns(0)
        active = active_ref[...].astype(F32)
        skip = skip_ref[...]
        gate = gate_ref[...].astype(F32)
        sigma = jax.nn.sigmoid(gate)
        graded = graded_ref[...]
        scanned = scan_scr[...].reshape(rows, LANES) + skip * active
        gated = (scanned * (gate * sigma)).astype(BF16)
        gated_ref[...] = gated
        dgate = (graded * scanned * (sigma * (1.0 + gate * (1.0 - sigma)))).astype(BF16)
        dgate_ref[...] = dgate
        dskip_ref[...] = jnp.sum(graded * (gate * sigma) * active, axis=0, keepdims=True)
        odd = lax.rem(c, 2)

        @pl.when(odd == 0)
        def _():
            gated_scr[:, :LANES] = gated
            dgated_scr[:, :LANES] = dgate

        @pl.when(odd == 1)
        def _():
            gated_scr[:, LANES:] = gated
            dgated_scr[:, LANES:] = dgate

        adjoint0 = behind_scr[tile] + jnp.exp2(after[None] * rate_scr[...]) * spread(incoming_scr[tile])
        state_scr[steps] = adjoint0
        for h, part in enumerate(halves):

            def backward(i, carry):
                adjoint, total = carry
                for u in range(unroll):
                    j = steps - 1 - (i * unroll + u)
                    d, g = delta_scr[j], grad_scr[j]
                    whole = adjoint + g[None] * readout_scr[j, part]
                    adjoint = factor_scr[j, part] * whole
                    through = adjoint * state_scr[j, part]
                    total = total + through * d[None]
                    dinject_scr[j, part] += whole * drive_scr[j][None]
                    one = tree_sum(through * rate_scr[part])
                    two = tree_sum(whole * inject_scr[j, part])
                    scan_scr[j] = scan_scr[j] + one if h else one
                    weight_scr[j] = weight_scr[j] + two if h else two
                return adjoint, total

            unused, total = lax.fori_loop(0, steps // unroll, backward, (state_scr[steps, part], zero))
            for n in range(half):
                at = h * half + n
                drate_ref[at : at + 1, :] = (
                    jnp.sum(total[n], axis=0, keepdims=True) * rate_scr[at, 0:1] * LN2
                )
            if h == 0:
                take_turns(1)
        weight = weight_scr[...].reshape(rows, LANES)
        delta = delta_scr[...].reshape(rows, LANES)
        active = active_ref[...].astype(F32)
        dactive_ref[...] = delta * weight + skip_ref[...] * grad_scr[...].reshape(rows, LANES)
        dpre = (scan_scr[...].reshape(rows, LANES) * LN2 + active * weight) * jax.nn.sigmoid(pre_ref[...])
        dprelow_ref[...] = dpre.astype(BF16)
        dbias_ref[...] = jnp.sum(dpre, axis=0, keepdims=True)

        @pl.when(odd == 1)
        def _():
            pair = c // 2
            part = jnp.dot(normed_ref[...], dgated_scr[...], preferred_element_type=F32).astype(BF16)
            acc[2 * pair, :width, :] = part[:, :LANES]
            acc[2 * pair, width:, :] = part[:, LANES:]
            turned = gated_scr[...].T
            for b in range(width // (2 * LANES)):
                part = jnp.dot(
                    turned, upstream_ref[:, b * 2 * LANES : (b + 1) * 2 * LANES], preferred_element_type=F32
                ).astype(BF16)
                for side in range(2):
                    at = (2 * b + side) * 2 * LANES
                    acc[2 * pair + 1, at : at + 2 * LANES, :] = part[:, side * LANES : (side + 1) * LANES]

        take_turns(2)

    for r in range(rounds, -1, -1):
        e = step - 2 * r

        @pl.when((e >= 0) & (e < tiles))
        def _():
            prefix.advance(e, r)

    @pl.when(step == 2 * tiles - 1)
    def _():
        ones = jnp.ones((LANES, LANES), BF16)
        for first, scr in ((0, dinject_scr), (states, dread_scr)):
            for n in range(states):
                value = scr[:, n].reshape(rows, LANES)
                high = value.astype(BF16)
                low = (value - high.astype(F32)).astype(BF16)
                part = jnp.dot(high, ones, preferred_element_type=F32) + jnp.dot(
                    low, ones, preferred_element_type=F32
                )
                dselect_ref[:, first + n : first + n + 1] = part[:, first + n : first + n + 1]

        slots = 3 * count
        for k in range(count):
            for p in range(ex.phases):
                if slots - 2 <= slot_of(k, p) < slots:
                    ex.finish(k, p)
        sizes = []
        for k in range(early, count):
            sizes.append(0)
            for ref, base, size in ex.state(k, next_phase(k, count)):
                here = pl.ds(pl.multiple_of(base, 16), size)
                sizes[-1] += size
                pltpu.make_async_copy(ref.at[k, here, :], handed.at[k - early, here, :], store_sem.at[k]).start()
        for k in range(early):
            wait_rows(out.at[k], store_sem.at[k])
        for k in range(early, count):
            wait_rows(acc.at[k, pl.ds(0, sizes[k - early]), :], store_sem.at[k])


def run_scan(pre, active, gate, graded, select, decay_log, skip, normed, upstream, rank, seq):
    rows, inner = pre.shape
    states = decay_log.shape[0]
    width = upstream.shape[1]
    chunk = 2 * width
    tiles, steps = inner // LANES, rows // SUB
    rounds = seq.bit_length() - 1
    phases = 10 + max(rounds - 3, 0)
    early = done_early(tiles, phases)
    first = early * LANES
    tall = pl.BlockSpec((rows, LANES), lambda i: (0, lax.rem(i, tiles)))
    line = pl.BlockSpec((1, LANES), lambda i: (0, lax.rem(i, tiles)))
    late = lambda shape: pl.BlockSpec(shape, lambda i: (0, lax.max(i - tiles, 0)))
    whole = lambda a: pl.BlockSpec(a.shape, lambda i: (0, 0), pipeline_mode=pl.Buffered(1))
    hbm = pl.BlockSpec(memory_space=pltpu.HBM)
    wide = pltpu.VMEM((steps, states, SUB, LANES), F32)
    thin = pltpu.VMEM((steps, SUB, LANES), F32)
    cube = pltpu.VMEM((tiles, states, SUB, LANES), F32)
    small = pltpu.VMEM((tiles, states, LANES), F32)
    pair = pltpu.VMEM((rows, 2 * LANES), BF16)
    buffers = scratch(tiles, chunk, 3 * tiles // 4, seq)
    buffers[1] = pltpu.VMEM((3 * tiles // 4, chunk, LANES), BF16)
    return pl.pallas_call(
        functools.partial(scan_kernel, rank, states, chunk, rounds, seq),
        grid=(2 * tiles,),
        in_specs=[
            tall, tall, tall, tall, whole(select), whole(decay_log), line, whole(normed), whole(upstream),
        ],
        out_specs=[
            late((rows, LANES)), late((rows, LANES)), late((rows, LANES)), late((rows, LANES)),
            late((states, LANES)), late((1, LANES)), late((1, LANES)),
            pl.BlockSpec((rows, 2 * states), lambda i: (0, 0)), hbm, hbm, hbm,
        ],
        out_shape=[
            jax.ShapeDtypeStruct((rows, inner), BF16),
            jax.ShapeDtypeStruct((rows, inner), BF16),
            jax.ShapeDtypeStruct((rows, inner), BF16),
            jax.ShapeDtypeStruct((rows, inner), F32),
            jax.ShapeDtypeStruct((states, inner), F32),
            jax.ShapeDtypeStruct((1, inner), F32),
            jax.ShapeDtypeStruct((1, inner), F32),
            jax.ShapeDtypeStruct((rows, 2 * states), F32),
            jax.ShapeDtypeStruct((width, first), BF16),
            jax.ShapeDtypeStruct((first, width), BF16),
            jax.ShapeDtypeStruct((tiles - early, chunk, LANES), BF16),
        ],
        scratch_shapes=[
            wide, wide, wide, wide,
            pltpu.VMEM((steps + 1, states, SUB, LANES), F32), wide,
            small, pltpu.VMEM((states, SUB, LANES), F32), thin, thin, thin, thin, thin,
            cube, cube, pltpu.VMEM((tiles, SUB, LANES), F32), pair, pair,
            pltpu.VMEM((tiles, 2 * states + SUB, LANES), F32),
            pltpu.VMEM((tiles, rounds, 2 * states + SUB, LANES), F32),
            small, small, pltpu.VMEM((tiles, SUB, LANES), F32),
            pltpu.SemaphoreType.DMA((tiles, rounds)), pltpu.SemaphoreType.DMA((tiles, rounds)),
        ]
        + buffers
        + [pltpu.SemaphoreType.DMA((tiles,))],
        compiler_params=pltpu.CompilerParams(
            collective_id=1, has_side_effects=True, vmem_limit_bytes=62 << 20
        ),
        name="span_scan",
    )(pre, active, gate, graded, select, decay_log, skip, normed, upstream)


def bit_of(index, step):
    return (index // step) % 2

def other(axis, step):
    place = lax.axis_index(axis)
    place = place + step * (1 - 2 * bit_of(place, step))
    if axis == "dp":
        return (place, lax.axis_index("seq"))
    return (lax.axis_index("dp"), place)

CORE, X, Y, Z, ZZ = ("seq", 1), ("dp", 1), ("dp", 2), ("seq", 2), ("seq", 4)

def wait_rows(rows, sem):
    pltpu.make_async_copy(rows, rows, sem).wait()


def store_lanes(source, target, pair, sem):
    width = target.shape[0]
    for side in range(2):
        lanes = pl.ds(pl.multiple_of((2 * pair + side) * LANES, LANES), LANES)
        pltpu.make_async_copy(source.at[pl.ds(side * width, width), :], target.at[:, lanes], sem).start()


def store_rows(source, target, pair, sem):
    tall = 2 * LANES
    rows = pl.ds(pl.multiple_of(pair * tall, tall), tall)
    for b in range(target.shape[1] // LANES):
        pltpu.make_async_copy(
            source.at[pl.ds(b * tall, tall), :], target.at[rows, pl.ds(b * LANES, LANES)], sem
        ).start()


class Exchange:
    def __init__(self, acc, out, landing, extra, send_sem, recv_sem, rows, window, seq):
        self.acc, self.out, self.landing, self.extra = acc, out, landing, extra
        self.send_sem, self.recv_sem = send_sem, recv_sem
        self.rows, self.window = rows, window
        self.more = [("seq", step) for step in (8 << i for i in range(12)) if step < seq]
        self.orders = ((CORE, X, Y, Z, ZZ), (CORE, Y, X, Z, ZZ))
        self.halvings = 5
        self.phases = 2 * self.halvings + len(self.more)
        quarter = rows // 4
        core = bit_of(lax.axis_index("seq"), 1)
        self.core_base = core * (rows // 2)
        self.kept = []
        for s, order in enumerate(self.orders):
            base, size = core * (rows // 2) + s * quarter, quarter
            spans = [(base, size)]
            for axis, step in order[1:]:
                size = size // 2
                base = base + bit_of(lax.axis_index(axis), step) * size
                spans.append((base, size))
            self.kept.append(spans)

    def partners(self):
        return [other(*link) for link in (CORE, X, Y, Z, ZZ)] + [other(*link) for link in self.more]

    def greet(self):
        barrier = pltpu.get_barrier_semaphore()
        partners = self.partners()
        for device in partners:
            pl.semaphore_signal(barrier, inc=1, device_id=device, device_id_type=MESH)
        pl.semaphore_wait(barrier, len(partners))

    def sent(self, s, level):
        base, size = self.kept[s][level]
        axis, step = self.orders[s][level]
        before = self.kept[s][level - 1][0]
        mine = bit_of(lax.axis_index(axis), step)
        return before + (1 - mine) * size, size

    def span(self, ref, k, base, size):
        return ref.at[k, pl.ds(pl.multiple_of(base, 16), size), :]

    def copies(self, k, p):
        w = lax.rem(k, self.window)
        rows, levels, more = self.rows, self.halvings, len(self.more)
        out = []
        def copy(s, src, dst, link):
            return pltpu.make_async_remote_copy(
                src_ref=src, dst_ref=dst, send_sem=self.send_sem.at[w, p, s], recv_sem=self.recv_sem.at[w, p, s],
                device_id=other(*link), device_id_type=MESH)
        if p == 0:
            src = self.span(self.acc, k, rows // 2 - self.core_base, rows // 2)
            return [copy(0, src, self.landing.at[w, pl.ds(0, rows // 2), :], CORE)]
        if p == levels * 2 + more - 1:
            half = self.span(self.out, k, self.core_base, rows // 2)
            return [copy(0, half, half, CORE)]
        for s in range(2):
            if p < levels:
                base, size = self.sent(s, p)
                dst = self.landing.at[w, pl.ds(self.land(p, s), size), :]
                out.append(copy(s, self.span(self.acc, k, base, size), dst, self.orders[s][p]))
            elif p < levels + more:
                base, size = self.kept[s][-1]
                dst = self.extra.at[w, p - levels, pl.ds(s * size, size), :]
                out.append(copy(s, self.span(self.acc, k, base, size), dst, self.more[p - levels]))
            else:
                level = 2 * levels + more - 1 - p
                piece = self.span(self.out, k, *self.kept[s][level])
                out.append(copy(s, piece, piece, self.orders[s][level]))
        return out

    def land(self, p, s):
        size = self.rows // 4 >> p
        start = self.rows // 2 + sum(2 * (self.rows // 4 >> q) for q in range(1, p))
        return start + s * size

    def add(self, k, base, source, first, size, target):
        step = math.gcd(size, 128)
        w = lax.rem(k, self.window)
        def body(i, _):
            here = pl.ds(pl.multiple_of(base + i * step, 16), step)
            there = pl.ds(pl.multiple_of(first + i * step, 16), step)
            target[k, here, :] = (self.acc[k, here, :].astype(F32) + source(w, there).astype(F32)).astype(BF16)
            return 0
        lax.fori_loop(0, size // step, body, 0)

    def finish(self, k, p):
        for copy in self.copies(k, p):
            copy.wait()
        levels, more = self.halvings, len(self.more)
        target = self.out if p == levels + more - 1 else self.acc
        landed = lambda w, there: self.landing[w, there, :]
        if p == 0:
            self.add(k, self.core_base, landed, 0, self.rows // 2, self.acc)
        elif p < levels:
            for s in range(2):
                base, size = self.kept[s][p]
                self.add(k, base, landed, self.land(p, s), size, target)
        elif p < levels + more:
            for s in range(2):
                base, size = self.kept[s][-1]
                self.add(k, base, lambda w, there: self.extra[w, p - levels, there, :], s * size, size, target)

    def start(self, k, p):
        for copy in self.copies(k, p):
            copy.start()

    def advance(self, k, p):
        if p > 0:
            self.finish(k, p - 1)
        if p < self.phases:
            self.start(k, p)

    def state(self, k, p):
        levels, more, rows = self.halvings, len(self.more), self.rows
        if p == 0:
            return [(self.acc, 0, rows)]
        if p == self.phases:
            return [(self.out, 0, rows)]
        sending = p < levels + more
        level = min(p - 1, levels - 1) if sending else 2 * levels + more - 1 - p
        spans = [(self.core_base, rows // 2)] if level == 0 else [self.kept[s][level] for s in range(2)]
        return [(self.acc if sending else self.out, base, size) for base, size in spans]

def scratch(chunks, rows, window, seq):
    more = len([1 for i in range(12) if (8 << i) < seq])
    phases = 10 + more
    return [
        pltpu.VMEM((chunks, rows, LANES), BF16),
        pltpu.VMEM((chunks, rows, LANES), BF16),
        pltpu.VMEM((window, rows, LANES), BF16),
        pltpu.VMEM((window, max(more, 1), rows // 32, LANES), BF16),
        pltpu.SemaphoreType.DMA((window, phases, 2)),
        pltpu.SemaphoreType.DMA((window, phases, 2)),
    ]

def tail_kernel(
    rank, states, chunk, seq,
    dprelow_ref, select_ref, dpair_ref, step_weight_ref, normed_ref, upstream_ref, inputs_ref, scale_ref, ids_ref,
    gain_ref, dactive_first_ref, mixed_first_ref, select_weight_ref, halo_ref, drate_ref, dbias_ref, dskip_ref,
    dactive_ref, mixed_ref, front_ref, active_ref, select_tile_ref, conv_ref, front_weight_ref, gate_weight_ref,
    dgate_ref, gated_ref, out_weight_ref, handed,
    output_ref, dinputs_ref, front_sum, gate_rest, out_rest, embedding_sum, wide_sum, mixed_sum,
    dselect_scr, first_scr, after_scr, spread_scr, extended_scr, dnormed_scr, result_scr, misc_scr, gain_scr,
    acc, out, landing, extra, send_sem, recv_sem, load_sem, store_sem, first_send, first_recv,
):
    step = pl.program_id(0)
    rows, width = upstream_ref.shape
    across = width // LANES
    inner = dprelow_ref.shape[1]
    tiles, pairs = inner // LANES, inner // (2 * LANES)
    tall = 2 * LANES
    kernel = conv_ref.shape[0]
    halo = kernel - 1
    vocab = embedding_sum.shape[0]
    ex = Exchange(acc, out, landing, extra, send_sem, recv_sem, chunk, landing.shape[0], seq)
    early = done_early(tiles, ex.phases)
    old = tiles - early
    embedding_at, wide_at, mixed_at = (old + pairs + i for i in range(3))
    count = old + pairs + 3
    place = lax.axis_index("seq")
    here_dp = lax.axis_index("dp")

    def add(scr, value):
        for b in range(across):
            scr[b] += value[:, b * LANES : (b + 1) * LANES]

    def put(scr, here, value):
        for b in range(across):
            scr[b, here, :] = value[:, b * LANES : (b + 1) * LANES]

    def take(scr, here):
        return jnp.concatenate([scr[b, here, :] for b in range(across)], axis=1)

    def first_copy():
        return pltpu.make_async_remote_copy(
            src_ref=first_scr, dst_ref=after_scr, send_sem=first_send, recv_sem=first_recv,
            device_id=(here_dp, lax.rem(place + seq - 1, seq)), device_id_type=MESH,
        )

    def greet():
        barrier = pltpu.get_barrier_semaphore()
        partners = ex.partners()
        for device in partners:
            pl.semaphore_signal(barrier, inc=1, device_id=device, device_id_type=MESH)
        for there, by in ((place > 0, -1), (place < seq - 1, 1)):

            @pl.when(there)
            def _():
                pl.semaphore_signal(barrier, inc=1, device_id=(here_dp, place + by), device_id_type=MESH)

        neighbours = 2 - (place == 0).astype(jnp.int32) - (place == seq - 1).astype(jnp.int32)
        pl.semaphore_wait(barrier, len(partners) + neighbours)

    def store(k):
        pair = (k + early) // 2

        @pl.when((k < old) & (lax.rem(k + early, 2) == 0))
        def _():
            store_lanes(out.at[k], gate_rest, pair - early // 2, store_sem.at[k])

        @pl.when((k < old) & (lax.rem(k + early, 2) == 1))
        def _():
            store_rows(out.at[k], out_rest, pair - early // 2, store_sem.at[k])

        @pl.when((k >= old) & (k < embedding_at))
        def _():
            store_lanes(out.at[k], front_sum, k - old, store_sem.at[k])

        @pl.when(k == embedding_at)
        def _():
            for b in range(width // LANES):
                pltpu.make_async_copy(
                    out.at[k, pl.ds(b * vocab, vocab), :], embedding_sum.at[:, pl.ds(b * LANES, LANES)], store_sem.at[k]
                ).start()

        @pl.when(k == wide_at)
        def _():
            pltpu.make_async_copy(out.at[k], wide_sum, store_sem.at[k]).start()

        @pl.when(k == mixed_at)
        def _():
            pltpu.make_async_copy(out.at[k], mixed_sum, store_sem.at[k]).start()

    def old_turns():
        for spot in range(3):
            slot = 3 * (tiles + step) + spot
            for p, shift in turns(ex.phases, spot):
                k = tiles + step + shift - early

                @pl.when((k >= 0) & (k < old))
                def _():
                    if p > 0:

                        @pl.when(slot >= 3 * tiles + 2)
                        def _():
                            ex.finish(k, p - 1)

                    if p < ex.phases:
                        ex.start(k, p)
                    else:
                        store(k)

    def new_turns():
        for p in range(ex.phases, -1, -1):
            k = old + step - 2 * p

            @pl.when((k >= old) & (k < count))
            def _():
                ex.advance(k, p)
                if p == ex.phases:
                    store(k)

    @pl.when(step == 0)
    def _():
        sizes = []
        for k in range(old):
            sizes.append(0)
            for ref, base, size in ex.state(k, next_phase(k + early, tiles)):
                here = pl.ds(pl.multiple_of(base, 16), size)
                sizes[-1] += size
                pltpu.make_async_copy(handed.at[k, here, :], ref.at[k, here, :], load_sem.at[k]).start()
        greet()
        dlow = contract_cols(dprelow_ref[...], step_weight_ref[...])
        dselect_scr[...] = jnp.concatenate([dlow, dpair_ref[...]], axis=1).astype(BF16)
        some = contract_cols(dselect_scr[: halo * SUB], select_weight_ref[...])
        some = (dactive_first_ref[...] + some) * silu_slope(mixed_first_ref[...])
        for i in range(halo):
            first_scr[i : i + 1, :] = some[i * SUB : i * SUB + 1, :]
        first_scr[halo:, :] = jnp.zeros((SUB - halo, inner), F32)

        @pl.when(place > 0)
        def _():
            first_copy().start()

        dnormed_scr[...] = jnp.zeros_like(dnormed_scr)
        result_scr[...] = jnp.zeros_like(result_scr)
        misc_scr[...] = jnp.zeros_like(misc_scr)
        misc_scr[kernel + 1 : kernel + 2, :] = dbias_ref[...]
        misc_scr[kernel + 2 : kernel + 3, :] = dskip_ref[...]
        acc[wide_at] = jnp.zeros_like(acc[wide_at])
        acc[mixed_at] = jnp.zeros_like(acc[mixed_at])
        for b in range(tiles):
            at = rank * tiles + b * states
            acc[mixed_at, at : at + states, :] = drate_ref[:, b * LANES : (b + 1) * LANES].astype(BF16)
        for k in range(old):
            wait_rows(acc.at[k, pl.ds(0, sizes[k]), :], load_sem.at[k])

    old_turns()

    @pl.when(step < pairs)
    def _():
        add(result_scr, jnp.dot(gated_ref[...], out_weight_ref[...], preferred_element_type=F32))
        add(dnormed_scr, contract_cols(dgate_ref[...], gate_weight_ref[...]))
        lanes = pl.ds(pl.multiple_of(step * tall, tall), tall)
        mixed = mixed_ref[...]
        back = contract_cols(dselect_scr[...], select_tile_ref[...])
        dmixed = (dactive_ref[...] + back) * silu_slope(mixed)
        spread_scr[:rows] = dmixed
        extended_scr[: halo * SUB] = halo_ref[...].astype(F32)
        extended_scr[halo * SUB :] = front_ref[...].astype(F32)
        misc_scr[kernel : kernel + 1, lanes] = jnp.sum(dmixed, axis=0, keepdims=True)
        for i in range(kernel):
            misc_scr[i : i + 1, lanes] = jnp.sum(
                dmixed * extended_scr[i * SUB : i * SUB + rows], axis=0, keepdims=True
            )
        wide = contract_rows(active_ref[...], dselect_scr[...]).astype(BF16)
        acc[wide_at, pl.ds(pl.multiple_of(step * tall, tall), tall), : wide.shape[1]] = wide
        part = contract_rows(select_ref[:, :rank], dprelow_ref[:, lanes]).astype(BF16)
        for side in range(2):
            at = pl.ds(pl.multiple_of((2 * step + side) * rank, rank), rank)
            acc[mixed_at, at, :] = part[:, side * LANES : (side + 1) * LANES]

        @pl.when(step == 0)
        def _():
            @pl.when(place > 0)
            def _():
                first_copy().wait_send()

            @pl.when(place < seq - 1)
            def _():
                first_copy().wait_recv()

            @pl.when(place == seq - 1)
            def _():
                after_scr[...] = jnp.zeros_like(after_scr)

        sub = lax.broadcasted_iota(jnp.int32, (SUB, tall), 0)
        for i in range(halo):
            own = pltpu.roll(spread_scr[i * SUB : (i + 1) * SUB, :], SUB - 1, 0)
            spread_scr[rows + i * SUB : rows + (i + 1) * SUB] = jnp.where(
                sub < SUB - 1, own, after_scr[i : i + 1, lanes]
            )
        dfront = conv_ref[halo : halo + 1] * spread_scr[:rows]
        for i in range(1, kernel):
            dfront = dfront + conv_ref[halo - i : halo - i + 1] * spread_scr[i * SUB : i * SUB + rows]
        dfront = dfront.astype(BF16)
        part = jnp.dot(normed_ref[...], dfront, preferred_element_type=F32).astype(BF16)
        acc[old + step, :width, :] = part[:, :LANES]
        acc[old + step, width:, :] = part[:, LANES:]
        add(dnormed_scr, contract_cols(dfront, front_weight_ref[...]))

    @pl.when(step == pairs)
    def _():
        part = rows // SUB

        def norms(i, total):
            here = pl.ds(pl.multiple_of(i * part, part), part)
            dnormed, inputs, scale = take(dnormed_scr, here), inputs_ref[here, :], scale_ref[here, :]
            scaled = gain_ref[...] * dnormed
            mean = jnp.sum(scaled * inputs, axis=1, keepdims=True) * (1.0 / width)
            put(
                dnormed_scr, here,
                upstream_ref[here, :].astype(F32) + scale * scaled - inputs * (scale * scale * scale * mean),
            )
            put(result_scr, here, take(result_scr, here) + inputs)
            return total + jnp.sum((dnormed * inputs * scale).reshape(-1, SUB, width), axis=0)

        total = lax.fori_loop(0, SUB, norms, jnp.zeros((SUB, width), F32))
        gain_scr[...] = jnp.sum(total, axis=0, keepdims=True)
        hot = (ids_ref[...] == lax.broadcasted_iota(jnp.int32, (rows, vocab), 1)).astype(F32).astype(BF16)
        for b in range(width // tall):
            value = jnp.concatenate([dnormed_scr[2 * b], dnormed_scr[2 * b + 1]], axis=1)
            high = value.astype(BF16)
            low = (value - high.astype(F32)).astype(BF16)
            whole = (contract_rows(hot, high) + contract_rows(hot, low)).astype(BF16)
            for side in range(2):
                at = (2 * b + side) * vocab
                acc[embedding_at, at : at + vocab, :] = whole[:, side * LANES : (side + 1) * LANES]
        at = (rank + states) * tiles
        for b in range(tiles):
            acc[mixed_at, at + b * 16 : at + (b + 1) * 16, :] = misc_scr[:, b * LANES : (b + 1) * LANES].astype(BF16)
        at = (rank + states + 16) * tiles
        for b in range(width // LANES):
            acc[mixed_at, at + b * 16 : at + (b + 1) * 16, :] = jnp.broadcast_to(
                gain_scr[:, b * LANES : (b + 1) * LANES], (16, LANES)
            ).astype(BF16)

    @pl.when(step == pairs + 1)
    def _():
        span = rows // SUB
        for i in range(SUB):
            for b in range(across):
                lanes, every = slice(b * LANES, (b + 1) * LANES), pl.ds(i, span, stride=SUB)
                dinputs_ref[i * span : (i + 1) * span, lanes] = dnormed_scr[b, every, :]
                output_ref[i * span : (i + 1) * span, lanes] = result_scr[b, every, :].astype(BF16)

    new_turns()

    @pl.when(step == pl.num_programs(0) - 1)
    def _():
        for k in range(count):
            wait_rows(out.at[k], store_sem.at[k])


def run_tail(
    d_pre_low, select, d_pair, step_weight, normed, upstream, inputs, scale, ids, gain, d_active, mixed, select_weight,
    halo, d_rate, d_bias, d_skip, front, active, conv_weight, input_weight, d_gate, gated, output_weight, handed, vocab, seq,
):
    rows, inner = front.shape
    width = inputs.shape[1]
    rank, states = step_weight.shape[0], d_rate.shape[0]
    chunk = 2 * width
    tiles, pairs, tall = inner // LANES, inner // (2 * LANES), 2 * LANES
    phases = 10 + max(seq.bit_length() - 4, 0)
    early = done_early(tiles, phases)
    count = tiles - early + pairs + 3
    some = halo.shape[0]
    at = lambda i: lax.min(i, pairs - 1)
    whole = lambda a: pl.BlockSpec(a.shape, lambda i: (0, 0), pipeline_mode=pl.Buffered(1))
    first = pl.BlockSpec((some, inner), lambda i: (0, 0), pipeline_mode=pl.Buffered(1))
    tile = lambda height: pl.BlockSpec((height, tall), lambda i: (0, at(i)))
    high = lambda wide: pl.BlockSpec((tall, wide), lambda i: (at(i), 0))
    hbm = pl.BlockSpec(memory_space=pltpu.HBM)
    fixed = pl.BlockSpec((rows, width), lambda i: (0, 0))
    rest = (tiles - early) * LANES
    return pl.pallas_call(
        functools.partial(tail_kernel, rank, states, chunk, seq),
        grid=(pairs + 3 + 2 * phases,),
        in_specs=[
            whole(d_pre_low), whole(select), whole(d_pair), whole(step_weight), whole(normed), whole(upstream),
            whole(inputs), whole(scale), whole(ids), whole(gain), first, first, whole(select_weight), tile(some),
            whole(d_rate), whole(d_bias), whole(d_skip), tile(rows), tile(rows), tile(rows), tile(rows),
            high(select_weight.shape[1]), tile(conv_weight.shape[0]), tile(width),
            pl.BlockSpec((width, tall), lambda i: (0, at(i) + pairs)), tile(rows), tile(rows), high(width), hbm,
        ],
        out_specs=[fixed, fixed, hbm, hbm, hbm, hbm, hbm, hbm],
        out_shape=[
            jax.ShapeDtypeStruct((rows, width), BF16),
            jax.ShapeDtypeStruct((rows, width), F32),
            jax.ShapeDtypeStruct((width, inner), BF16),
            jax.ShapeDtypeStruct((width, rest), BF16),
            jax.ShapeDtypeStruct((rest, width), BF16),
            jax.ShapeDtypeStruct((vocab, width), BF16),
            jax.ShapeDtypeStruct((chunk, LANES), BF16),
            jax.ShapeDtypeStruct((chunk, LANES), BF16),
        ],
        scratch_shapes=[
            pltpu.VMEM(select.shape, BF16),
            pltpu.VMEM((SUB, inner), F32), pltpu.VMEM((SUB, inner), F32),
            pltpu.VMEM((rows + some, tall), F32), pltpu.VMEM((rows + some, tall), F32),
            pltpu.VMEM((width // LANES, rows, LANES), F32), pltpu.VMEM((width // LANES, rows, LANES), F32),
            pltpu.VMEM((16, inner), F32), pltpu.VMEM((1, width), F32),
        ]
        + scratch(count, chunk, count, seq)
        + [
            pltpu.SemaphoreType.DMA((count,)), pltpu.SemaphoreType.DMA((count,)),
            pltpu.SemaphoreType.DMA, pltpu.SemaphoreType.DMA,
        ],
        compiler_params=pltpu.CompilerParams(
            collective_id=2, has_side_effects=True, vmem_limit_bytes=62 << 20
        ),
        name="span_tail",
    )(
        d_pre_low, select, d_pair, step_weight, normed, upstream, inputs, scale, ids, gain, d_active, mixed,
        select_weight, halo, d_rate, d_bias, d_skip, d_active, mixed, front, active, select_weight, conv_weight,
        input_weight, input_weight, d_gate, gated, output_weight, handed,
    )


def on_device(
    byte_ids,
    embedding,
    cotangent,
    norm_gain,
    input_projection_weight,
    conv_weight,
    conv_bias,
    select_weight,
    step_weight,
    step_bias,
    decay_log,
    skip_gain,
    output_projection_weight,
):
    count, stretch = byte_ids.shape
    vocab, width = embedding.shape
    kernel, inner = conv_weight.shape
    states = decay_log.shape[0]
    rank = step_weight.shape[0]
    rows = count * stretch
    halo = kernel - 1
    ids = to_spans(byte_ids.reshape(rows, 1))
    one_hot = ids == jnp.arange(vocab, dtype=jnp.int32)[None, :]
    block_inputs = jnp.dot(one_hot.astype(BF16), embedding, preferred_element_type=F32)
    scale = lax.rsqrt(jnp.mean(block_inputs * block_inputs, axis=1, keepdims=True) + EPS)
    normed_input = (block_inputs * scale * norm_gain).astype(BF16)
    front = jnp.dot(
        normed_input, input_projection_weight[:, :inner], preferred_element_type=F32
    ).astype(BF16)
    gate = jnp.dot(
        normed_input, input_projection_weight[:, inner:], preferred_element_type=F32
    ).astype(BF16)
    last = front[rows - halo * SUB :].reshape(halo, SUB, inner)
    tail = passed_along(last[:, SUB - 1], "seq", 1)
    earlier = jnp.concatenate([tail[:, None], last[:, : SUB - 1]], axis=1).reshape(halo * SUB, inner)
    extended = jnp.concatenate([earlier, front], axis=0).astype(F32)
    mixed = conv_bias + conv_weight[0] * extended[:rows]
    for place in range(1, kernel):
        mixed = mixed + conv_weight[place] * extended[place * SUB : place * SUB + rows]
    active = jax.nn.silu(mixed).astype(BF16)
    select = jnp.dot(active, select_weight, preferred_element_type=F32).astype(BF16)
    lowrank = select[:, :rank]
    pre = jnp.dot(lowrank, step_weight, preferred_element_type=F32) + step_bias
    upstream = to_spans(cotangent.reshape(rows, width))
    graded = contract_cols(upstream, output_projection_weight)
    seq = lax.axis_size("seq")
    turned = normed_input.T
    (
        gated, d_gate, d_pre_low, d_active, d_rate, d_bias, d_skip, d_pair, gate_sum, out_sum, handed
    ) = run_scan(
        pre, active, gate, graded, select, decay_log, skip_gain.reshape(1, inner), turned, upstream, rank, seq
    )
    output, d_inputs, front_sum, gate_rest, out_rest, embedding_sum, wide_sum, mixed_sum = run_tail(
        d_pre_low, select, d_pair, step_weight, turned, upstream, block_inputs, scale, ids, norm_gain.reshape(1, width),
        d_active, mixed, select_weight, earlier, d_rate, d_bias, d_skip, front, active, conv_weight,
        input_projection_weight, d_gate, gated, output_projection_weight, handed, vocab, seq,
    )
    tiles = inner // LANES

    def unpacked(first, height, blocks):
        part = mixed_sum[first : first + height * blocks].astype(F32).reshape(blocks, height, LANES)
        return part.swapaxes(0, 1).reshape(height, blocks * LANES)

    at = (rank + states) * tiles
    misc = unpacked(at, 16, tiles)
    return (
        output.reshape(count, stretch, width),
        d_inputs.reshape(count, stretch, width),
        embedding_sum.astype(F32),
        unpacked(at + 16 * tiles, 16, width // LANES)[0],
        jnp.concatenate([front_sum, gate_sum, gate_rest], axis=1).astype(F32),
        misc[:kernel],
        misc[kernel],
        wide_sum[:, : select_weight.shape[1]].astype(F32),
        unpacked(0, rank, tiles),
        misc[kernel + 1],
        unpacked(rank * tiles, states, tiles),
        misc[kernel + 2],
        jnp.concatenate([out_sum, out_rest], axis=0).astype(F32),
    )


def solution(mesh):
    placed = (P("dp", "seq"), P(), P("dp", "seq", None)) + (P(),) * 10
    return jax.shard_map(
        on_device,
        mesh=mesh,
        in_specs=placed,
        out_specs=(P("dp", "seq", None), P("dp", "seq", None)) + (P(),) * 11,
        check_vma=False,
    )
```

```python
import functools
import math

import jax
import jax.numpy as jnp
from jax import lax
from jax.experimental import pallas as pl
from jax.experimental.pallas import tpu as pltpu
from jax.sharding import PartitionSpec as P

EPS = 1e-05
LANES = 128
SUB = 8
LOG2E = math.log2(math.e)
LN2 = math.log(2.0)
F32 = jnp.float32
BF16 = jnp.bfloat16
MESH = pl.DeviceIdType.MESH


def passed_along(value, axis, by):
    peers = lax.axis_size(axis)
    pairs = [(i, i + by) for i in range(peers) if 0 <= i + by < peers]
    return lax.ppermute(value, axis, pairs)


def silu_slope(value):
    sigma = jax.nn.sigmoid(value)
    return sigma * (1.0 + value * (1.0 - sigma))


def contract_rows(left, right):
    return lax.dot_general(
        left, right, (((0,), (0,)), ((), ())), preferred_element_type=F32
    )


def contract_cols(left, right):
    return lax.dot_general(
        left, right, (((1,), (1,)), ((), ())), preferred_element_type=F32
    )


def to_spans(array):
    rows = array.shape[0]
    return array.reshape(SUB, rows // SUB, -1).swapaxes(0, 1).reshape(rows, -1)


def from_spans(array):
    rows = array.shape[0]
    return array.reshape(rows // SUB, SUB, -1).swapaxes(0, 1).reshape(rows, -1)


def sublane(shape):
    return lax.broadcasted_iota(jnp.int32, shape, len(shape) - 2)


def shift_up(value, by, fill, reverse):
    place = sublane(value.shape)
    if reverse:
        moved = pltpu.roll(value, SUB - by, value.ndim - 2)
        return jnp.where(place < SUB - by, moved, fill)
    moved = pltpu.roll(value, by, value.ndim - 2)
    return jnp.where(place >= by, moved, fill)


def expand_columns(select, first, states):
    width = select.shape[1]
    shape = (width, states * LANES)
    source = lax.broadcasted_iota(jnp.int32, shape, 0)
    target = lax.broadcasted_iota(jnp.int32, shape, 1) // LANES + first
    spread = (source == target).astype(F32).astype(BF16)
    return jnp.dot(select, spread, preferred_element_type=F32)


def tree_sum(value):
    while value.shape[0] > 1:
        half = value.shape[0] // 2
        value = value[:half] + value[half:]
    return value[0]


def slot_of(k, p):
    return 2 * k + 3 + 2 * p


def turns(phases, place):
    return [(p, (place - 3 - 2 * p) // 2) for p in range(phases, -1, -1) if (place - 3 - 2 * p) % 2 == 0]


def done_early(tiles, phases):
    return sum(slot_of(k, phases) < 2 * tiles for k in range(tiles))


def next_phase(k, tiles):
    return next(p for p in range(1000) if slot_of(k, p) >= 2 * tiles)


class Prefix:
    def __init__(self, totals, landing, start, incoming, gaps, rates, send_sem, recv_sem, rounds):
        self.totals, self.landing, self.start, self.incoming, self.gaps = totals, landing, start, incoming, gaps
        self.rates, self.send_sem, self.recv_sem, self.rounds = rates, send_sem, recv_sem, rounds

    def copy(self, e, r):
        return pltpu.make_async_remote_copy(
            src_ref=self.totals.at[e], dst_ref=self.landing.at[e, r],
            send_sem=self.send_sem.at[e, r], recv_sem=self.recv_sem.at[e, r],
            device_id=other("seq", 1 << r), device_id_type=MESH,
        )

    def advance(self, e, r):
        if r > 0:
            self.copy(e, r - 1).wait()
            self.merge(e, r - 1)
        if r < self.rounds:
            self.copy(e, r).start()

    def merge(self, e, r):
        n = self.rates.shape[1]
        rates = self.rates[e]
        later = bit_of(lax.axis_index("seq"), 1 << r) == 1
        end, message, total = self.totals[e, :n], self.totals[e, n : 2 * n], self.totals[e, 2 * n : 2 * n + 1]
        end2, message2 = self.landing[e, r, :n], self.landing[e, r, n : 2 * n]
        total2 = self.landing[e, r, 2 * n : 2 * n + 1]

        @pl.when(later)
        def _():
            gap = self.gaps[e, 0:1]
            self.start[e] = self.start[e] + jnp.exp2(gap * rates) * end2
            self.gaps[e, 0:1] = gap + total2

        @pl.when(jnp.logical_not(later))
        def _():
            gap = self.gaps[e, 1:2]
            self.incoming[e] = self.incoming[e] + jnp.exp2(gap * rates) * message2
            self.gaps[e, 1:2] = gap + total2

        if r < self.rounds - 1:
            reach, reach2 = jnp.exp2(total * rates), jnp.exp2(total2 * rates)
            self.totals[e, :n] = jnp.where(later, end + reach * end2, end2 + reach2 * end)
            self.totals[e, n : 2 * n] = jnp.where(later, message2 + reach2 * message, message + reach * message2)
            self.totals[e, 2 * n : 2 * n + 1] = total + total2


def scan_kernel(
    rank, states, chunk, rounds, seq,
    pre_now, active_now, gate_now, graded_now, pre_ref, active_ref, gate_ref, graded_ref,
    select_ref, decay_ref, skip_ref, normed_ref, upstream_ref,
    gated_ref, dgate_ref, dprelow_ref, dactive_ref, drate_ref, dbias_ref, dskip_ref, dselect_ref,
    gate_sum, out_sum, handed,
    inject_scr, readout_scr, dread_scr, dinject_scr, state_scr, factor_scr,
    rates_scr, rate_scr, delta_scr, drive_scr, grad_scr, sigma_scr, scan_scr, weight_scr,
    ahead_scr, behind_scr, sums_scr, gated_scr, dgated_scr,
    totals, totals_in, start_scr, incoming_scr, gaps_scr, prefix_send, prefix_recv,
    acc, out, landing, extra, send_sem, recv_sem, store_sem,
):
    rows = pre_ref.shape[0]
    steps = rows // SUB
    step = pl.program_id(0)
    count = rates_scr.shape[0]
    lag = rounds + 1
    width = upstream_ref.shape[1]
    prefix = Prefix(
        totals, totals_in, start_scr, incoming_scr, gaps_scr, rates_scr, prefix_send, prefix_recv, rounds
    )
    ex = Exchange(acc, out, landing, extra, send_sem, recv_sem, chunk, landing.shape[0], seq)
    early = done_early(count, ex.phases)
    half, unroll = states // 2, 8
    halves = [pl.ds(0, half), pl.ds(half, half)]

    def store(k):
        pair = k // 2

        @pl.when(lax.rem(k, 2) == 0)
        def _():
            store_lanes(out.at[k], gate_sum, pair, store_sem.at[k])

        @pl.when(lax.rem(k, 2) == 1)
        def _():
            store_rows(out.at[k], out_sum, pair, store_sem.at[k])

    def take_turns(place):
        c = step - lag
        for p, shift in turns(ex.phases, place):
            k = c + shift

            @pl.when(k >= 0)
            def _():
                ex.advance(k, p)
                if p == ex.phases:
                    store(k)

    @pl.when(step == 0)
    def _():
        for first, scr in ((rank, inject_scr), (rank + states, readout_scr)):
            for n in range(0, states, 2):
                wide = expand_columns(select_ref[...], first + n, 2)
                for side in range(2):
                    scr[:, n + side] = wide[:, side * LANES : (side + 1) * LANES].reshape(steps, SUB, LANES)
        dread_scr[...] = jnp.zeros_like(dread_scr)
        dinject_scr[...] = jnp.zeros_like(dinject_scr)
        start_scr[...] = jnp.zeros_like(start_scr)
        incoming_scr[...] = jnp.zeros_like(incoming_scr)
        gaps_scr[...] = jnp.zeros_like(gaps_scr)
        for e in range(count):
            rates_scr[e] = -jnp.exp(decay_ref[:, e * LANES : (e + 1) * LANES]) * LOG2E
        ex.greet()

    flat = lambda value: value.reshape(steps, SUB, LANES)
    zero = jnp.zeros((half, SUB, LANES), F32)

    def prepare(tile, pre_ref, active_ref, gate_ref, graded_ref):
        rates = rates_scr[tile]
        for n in range(states):
            rate_scr[n] = jnp.broadcast_to(rates[n : n + 1], (SUB, LANES))
        delta = jax.nn.softplus(pre_ref[...])
        delta_scr[...] = flat(delta)
        drive_scr[...] = flat(delta * active_ref[...].astype(F32))
        gate = gate_ref[...].astype(F32)
        sigma = jax.nn.sigmoid(gate)
        sigma_scr[...] = flat(sigma)
        grad_scr[...] = flat(graded_ref[...] * (gate * sigma))

    @pl.when(step < count)
    def _():
        tile = step
        prepare(tile, pre_now, active_now, gate_now, graded_now)
        total = jnp.sum(delta_scr[...], axis=0)
        sums_scr[tile] = total
        whole = jnp.sum(total, axis=0, keepdims=True)
        totals[tile, 2 * states :] = jnp.broadcast_to(whole, (SUB, LANES))
        for h, part in enumerate(halves):

            def ends(i, carry):
                state, message, decay = carry
                for u in range(unroll):
                    j = i * unroll + u
                    factor = jnp.exp2(delta_scr[j][None] * rate_scr[part])
                    state = factor * state + drive_scr[j][None] * inject_scr[j, part]
                    decay = decay * factor
                    message = message + decay * (grad_scr[j][None] * readout_scr[j, part])
                return state, message, decay

            state, message, decay = lax.fori_loop(0, steps // unroll, ends, (zero, zero, zero + 1.0))
            for value, kept, at, reverse in (
                (state, ahead_scr, h * half, False), (message, behind_scr, states + h * half, True)
            ):
                factor = decay
                for by in (1, 2, 4):
                    value = value + factor * shift_up(value, by, 0.0, reverse)
                    factor = factor * shift_up(factor, by, 1.0, reverse)
                kept[tile, part] = shift_up(value, 1, 0.0, reverse)
                last = 0 if reverse else SUB - 1
                for n in range(half):
                    totals[tile, at + n : at + n + 1] = value[n, last : last + 1]

    def spread(table):
        return jnp.concatenate(
            [jnp.broadcast_to(table[n : n + 1], (1, SUB, LANES)) for n in range(states)], axis=0
        )

    @pl.when(step >= lag)
    def _():
        c = step - lag
        tile = c
        prepare(tile, pre_ref, active_ref, gate_ref, graded_ref)
        total = sums_scr[tile]
        before, after = total, total
        for by in (1, 2, 4):
            before = before + shift_up(before, by, 0.0, False)
            after = after + shift_up(after, by, 0.0, True)
        before, after = before - total, after - total
        state_scr[0] = ahead_scr[tile] + jnp.exp2(before[None] * rate_scr[...]) * spread(start_scr[tile])

        def forward(i, state):
            for u in range(unroll // 2):
                j = i * (unroll // 2) + u
                factor = jnp.exp2(delta_scr[j][None] * rate_scr[...])
                factor_scr[j] = factor
                state = factor * state + drive_scr[j][None] * inject_scr[j]
                state_scr[j + 1] = state
                dread_scr[j] += grad_scr[j][None] * state
                scan_scr[j] = tree_sum(readout_scr[j] * state)
            return state

        lax.fori_loop(0, steps // (unroll // 2), forward, state_scr[0])
        take_turns(0)
        active = active_ref[...].astype(F32)
        skip = skip_ref[...]
        gate = gate_ref[...].astype(F32)
        sigma = sigma_scr[...].reshape(rows, LANES)
        graded = graded_ref[...]
        scanned = scan_scr[...].reshape(rows, LANES) + skip * active
        gated = (scanned * (gate * sigma)).astype(BF16)
        gated_ref[...] = gated
        dgate = (graded * scanned * (sigma * (1.0 + gate * (1.0 - sigma)))).astype(BF16)
        dgate_ref[...] = dgate
        dskip_ref[...] = jnp.sum(graded * (gate * sigma) * active, axis=0, keepdims=True)
        odd = lax.rem(c, 2)

        @pl.when(odd == 0)
        def _():
            gated_scr[:, :LANES] = gated
            dgated_scr[:, :LANES] = dgate

        @pl.when(odd == 1)
        def _():
            gated_scr[:, LANES:] = gated
            dgated_scr[:, LANES:] = dgate

        adjoint0 = behind_scr[tile] + jnp.exp2(after[None] * rate_scr[...]) * spread(incoming_scr[tile])
        state_scr[steps] = adjoint0
        for h, part in enumerate(halves):

            def backward(i, carry):
                adjoint, total = carry
                for u in range(unroll):
                    j = steps - 1 - (i * unroll + u)
                    d, g = delta_scr[j], grad_scr[j]
                    whole = adjoint + g[None] * readout_scr[j, part]
                    adjoint = factor_scr[j, part] * whole
                    through = adjoint * state_scr[j, part]
                    total = total + through * d[None]
                    dinject_scr[j, part] += whole * drive_scr[j][None]
                    one = tree_sum(through * rate_scr[part])
                    two = tree_sum(whole * inject_scr[j, part])
                    scan_scr[j] = scan_scr[j] + one if h else one
                    weight_scr[j] = weight_scr[j] + two if h else two
                return adjoint, total

            unused, total = lax.fori_loop(0, steps // unroll, backward, (state_scr[steps, part], zero))
            for n in range(half):
                at = h * half + n
                drate_ref[at : at + 1, :] = (
                    jnp.sum(total[n], axis=0, keepdims=True) * rate_scr[at, 0:1] * LN2
                )
        weight = weight_scr[...].reshape(rows, LANES)
        delta = delta_scr[...].reshape(rows, LANES)
        active = active_ref[...].astype(F32)
        dactive_ref[...] = delta * weight + skip_ref[...] * grad_scr[...].reshape(rows, LANES)
        dpre = (scan_scr[...].reshape(rows, LANES) * LN2 + active * weight) * jax.nn.sigmoid(pre_ref[...])
        dprelow_ref[...] = dpre.astype(BF16)
        dbias_ref[...] = jnp.sum(dpre, axis=0, keepdims=True)

        @pl.when(odd == 1)
        def _():
            pair = c // 2
            part = jnp.dot(normed_ref[...], dgated_scr[...], preferred_element_type=F32).astype(BF16)
            acc[2 * pair, :width, :] = part[:, :LANES]
            acc[2 * pair, width:, :] = part[:, LANES:]
            turned = gated_scr[...].T
            for b in range(width // (2 * LANES)):
                part = jnp.dot(
                    turned, upstream_ref[:, b * 2 * LANES : (b + 1) * 2 * LANES], preferred_element_type=F32
                ).astype(BF16)
                for side in range(2):
                    at = (2 * b + side) * 2 * LANES
                    acc[2 * pair + 1, at : at + 2 * LANES, :] = part[:, side * LANES : (side + 1) * LANES]

        take_turns(1)

    for r in range(rounds, -1, -1):
        e = step - r

        @pl.when((e >= 0) & (e < count))
        def _():
            prefix.advance(e, r)

    @pl.when(step == count + lag - 1)
    def _():
        shape = (2 * LANES, 2 * states)
        from_lane = lax.broadcasted_iota(jnp.int32, shape, 0) // LANES
        to_column = lax.broadcasted_iota(jnp.int32, shape, 1)
        whole = jnp.zeros((rows, 2 * states), F32)
        for first, scr in ((0, dinject_scr), (states, dread_scr)):
            for n in range(0, states, 2):
                ones = (from_lane + (first + n) == to_column).astype(F32).astype(BF16)
                value = jnp.concatenate([scr[:, n + side].reshape(rows, LANES) for side in range(2)], axis=1)
                high = value.astype(BF16)
                low = (value - high.astype(F32)).astype(BF16)
                whole = whole + jnp.dot(high, ones, preferred_element_type=F32)
                whole = whole + jnp.dot(low, ones, preferred_element_type=F32)
        dselect_ref[...] = whole

        slots = 2 * count
        for k in range(count):
            for p in range(ex.phases):
                if slot_of(k, p) in (slots - 1, slots - 2):
                    ex.finish(k, p)
        sizes = []
        for k in range(early, count):
            sizes.append(0)
            for ref, base, size in ex.state(k, next_phase(k, count)):
                here = pl.ds(pl.multiple_of(base, 16), size)
                sizes[-1] += size
                pltpu.make_async_copy(ref.at[k, here, :], handed.at[k - early, here, :], store_sem.at[k]).start()
        for k in range(early):
            wait_rows(out.at[k], store_sem.at[k])
        for k in range(early, count):
            wait_rows(acc.at[k, pl.ds(0, sizes[k - early]), :], store_sem.at[k])


def run_scan(pre, active, gate, graded, select, decay_log, skip, normed, upstream, rank, seq):
    rows, inner = pre.shape
    states = decay_log.shape[0]
    width = upstream.shape[1]
    chunk = 2 * width
    tiles, steps = inner // LANES, rows // SUB
    rounds = seq.bit_length() - 1
    phases = 8 + max(rounds - 3, 0)
    early = done_early(tiles, phases)
    gates, outs = (early + 1) // 2 * 2 * LANES, early // 2 * 2 * LANES
    lag = rounds + 1
    now = pl.BlockSpec((rows, LANES), lambda i: (0, lax.min(i, tiles - 1)))
    late = lambda shape: pl.BlockSpec(shape, lambda i: (0, lax.max(i - lag, 0)))
    tall, line = late((rows, LANES)), late((1, LANES))
    whole = lambda a: pl.BlockSpec(a.shape, lambda i: (0, 0), pipeline_mode=pl.Buffered(1))
    hbm = pl.BlockSpec(memory_space=pltpu.HBM)
    wide = pltpu.VMEM((steps, states, SUB, LANES), F32)
    thin = pltpu.VMEM((steps, SUB, LANES), F32)
    cube = pltpu.VMEM((tiles, states, SUB, LANES), F32)
    small = pltpu.VMEM((tiles, states, LANES), F32)
    pair = pltpu.VMEM((rows, 2 * LANES), BF16)
    buffers = scratch(tiles, chunk, tiles // 2, seq)
    buffers[1] = pltpu.VMEM((3 * tiles // 4, chunk, LANES), BF16)
    return pl.pallas_call(
        functools.partial(scan_kernel, rank, states, chunk, rounds, seq),
        grid=(tiles + lag,),
        in_specs=[
            now, now, now, now, tall, tall, tall, tall, whole(select), whole(decay_log), line, whole(normed), whole(upstream),
        ],
        out_specs=[
            late((rows, LANES)), late((rows, LANES)), late((rows, LANES)), late((rows, LANES)),
            late((states, LANES)), late((1, LANES)), late((1, LANES)),
            pl.BlockSpec((rows, 2 * states), lambda i: (0, 0)), hbm, hbm, hbm,
        ],
        out_shape=[
            jax.ShapeDtypeStruct((rows, inner), BF16),
            jax.ShapeDtypeStruct((rows, inner), BF16),
            jax.ShapeDtypeStruct((rows, inner), BF16),
            jax.ShapeDtypeStruct((rows, inner), F32),
            jax.ShapeDtypeStruct((states, inner), F32),
            jax.ShapeDtypeStruct((1, inner), F32),
            jax.ShapeDtypeStruct((1, inner), F32),
            jax.ShapeDtypeStruct((rows, 2 * states), F32),
            jax.ShapeDtypeStruct((width, gates), BF16),
            jax.ShapeDtypeStruct((outs, width), BF16),
            jax.ShapeDtypeStruct((tiles - early, chunk, LANES), BF16),
        ],
        scratch_shapes=[
            wide, wide, wide, wide,
            pltpu.VMEM((steps + 1, states, SUB, LANES), F32), wide,
            small, pltpu.VMEM((states, SUB, LANES), F32), thin, thin, thin, thin, thin, thin,
            cube, cube, pltpu.VMEM((tiles, SUB, LANES), F32), pair, pair,
            pltpu.VMEM((tiles, 2 * states + SUB, LANES), F32),
            pltpu.VMEM((tiles, rounds, 2 * states + SUB, LANES), F32),
            small, small, pltpu.VMEM((tiles, SUB, LANES), F32),
            pltpu.SemaphoreType.DMA((tiles, rounds)), pltpu.SemaphoreType.DMA((tiles, rounds)),
        ]
        + buffers
        + [pltpu.SemaphoreType.DMA((tiles,))],
        compiler_params=pltpu.CompilerParams(
            collective_id=1, has_side_effects=True, vmem_limit_bytes=62 << 20
        ),
        name="span_scan",
    )(pre, active, gate, graded, pre, active, gate, graded, select, decay_log, skip, normed, upstream)


def bit_of(index, step):
    return (index // step) % 2

def other(axis, step):
    place = lax.axis_index(axis)
    place = place + step * (1 - 2 * bit_of(place, step))
    if axis == "dp":
        return (place, lax.axis_index("seq"))
    return (lax.axis_index("dp"), place)

CORE, X, Y = ("seq", 1), ("dp", 1), ("dp", 2)

def wait_rows(rows, sem):
    pltpu.make_async_copy(rows, rows, sem).wait()


def store_lanes(source, target, pair, sem):
    width = target.shape[0]
    for side in range(2):
        lanes = pl.ds(pl.multiple_of((2 * pair + side) * LANES, LANES), LANES)
        pltpu.make_async_copy(source.at[pl.ds(side * width, width), :], target.at[:, lanes], sem).start()


def store_rows(source, target, pair, sem):
    tall = 2 * LANES
    rows = pl.ds(pl.multiple_of(pair * tall, tall), tall)
    for b in range(target.shape[1] // LANES):
        pltpu.make_async_copy(
            source.at[pl.ds(b * tall, tall), :], target.at[rows, pl.ds(b * LANES, LANES)], sem
        ).start()


class Exchange:
    levels = 4

    def __init__(self, acc, out, landing, extra, send_sem, recv_sem, rows, window, seq):
        self.acc, self.out, self.landing, self.extra = acc, out, landing, extra
        self.send_sem, self.recv_sem = send_sem, recv_sem
        self.rows, self.window = rows, window
        self.more = [("seq", 8 << i) for i in range(12) if (8 << i) < seq]
        self.orders = ((CORE, X, Y), (CORE, Y, X))
        self.back = self.levels + len(self.more)
        self.phases = self.back + self.levels
        place = lax.axis_index("seq")
        self.quarter = (place // 2) % 4
        self.core_base = bit_of(place, 1) * (rows // 2)
        self.kept = []
        for s, order in enumerate(self.orders):
            base, size = self.core_base + s * (rows // 4), rows // 4
            spans = [(base, size)]
            for axis, step in order[1:]:
                size = size // 2
                base = base + bit_of(lax.axis_index(axis), step) * size
                spans.append((base, size))
            size = size // 4
            spans.append((base + self.quarter * size, size))
            self.kept.append(spans)

    def partners(self):
        links = [CORE, X, Y] + self.more
        return [other(*link) for link in links] + [self.along(i) for i in range(1, 4)]

    def greet(self):
        barrier = pltpu.get_barrier_semaphore()
        partners = self.partners()
        for device in partners:
            pl.semaphore_signal(barrier, inc=1, device_id=device, device_id_type=MESH)
        pl.semaphore_wait(barrier, len(partners))

    def along(self, i):
        place = lax.axis_index("seq")
        return (lax.axis_index("dp"), place + 2 * (lax.rem(self.quarter + i, 4) - self.quarter))

    def span(self, ref, k, base, size):
        return ref.at[k, pl.ds(pl.multiple_of(base, 16), size), :]

    def land(self, p):
        rows = self.rows
        return [0, rows // 2, rows // 2 + rows // 4, rows // 2 + rows // 4 + rows // 8][p]

    def rows_of(self, p):
        rows, last = self.rows, self.phases - 1
        if self.levels <= p < self.back:
            return rows // 32
        return [rows // 2, rows // 4, rows // 8, 6 * rows // 64][min(p, last - p)]

    def copies(self, k, p):
        w = lax.rem(k, self.window)
        rows = self.rows
        if p == 0:
            return [(self.span(self.acc, k, rows // 2 - self.core_base, rows // 2),
                     self.landing.at[w, pl.ds(0, rows // 2), :], other(*CORE))]
        if p == self.phases - 1:
            half = self.span(self.out, k, self.core_base, rows // 2)
            return [(half, half, other(*CORE))]
        found = []
        for s in range(2):
            if p < self.levels - 1:
                size = self.kept[s][p][1]
                axis, step = self.orders[s][p]
                base = self.kept[s][p - 1][0] + (1 - bit_of(lax.axis_index(axis), step)) * size
                target = self.landing.at[w, pl.ds(self.land(p) + s * size, size), :]
                found.append((self.span(self.acc, k, base, size), target, other(axis, step)))
            elif p == self.levels - 1:
                first, size = self.kept[s][p - 1][0], self.kept[s][p][1]
                for i in range(1, 4):
                    base = first + lax.rem(self.quarter + i, 4) * size
                    target = self.landing.at[w, pl.ds(self.land(p) + (3 * s + i - 1) * size, size), :]
                    found.append((self.span(self.acc, k, base, size), target, self.along(i)))
            elif p < self.back:
                base, size = self.kept[s][-1]
                target = self.extra.at[w, p - self.levels, pl.ds(s * size, size), :]
                found.append((self.span(self.acc, k, base, size), target, other(*self.more[p - self.levels])))
            else:
                level = self.phases - 1 - p
                piece = self.span(self.out, k, *self.kept[s][level])
                devices = [self.along(i) for i in range(1, 4)] if level == 3 else [other(*self.orders[s][level])]
                found += [(piece, piece, device) for device in devices]
        return found

    def add(self, k, base, size, sources, target):
        step = min(size, 256)

        def body(i, _):
            here = pl.ds(pl.multiple_of(base + i * step, 16), step)
            total = self.acc[k, here, :].astype(F32)
            for ref, index, first in sources:
                there = pl.ds(pl.multiple_of(first + i * step, 16), step)
                total = total + ref[index + (there,)].astype(F32)
            target[k, here, :] = total.astype(BF16)
            return 0

        lax.fori_loop(0, size // step, body, 0)

    def finish(self, k, p):
        w = lax.rem(k, self.window)
        rows = self.acc.at[k, pl.ds(0, self.rows_of(p)), :]
        copy = pltpu.make_async_remote_copy(
            src_ref=rows, dst_ref=rows, send_sem=self.send_sem.at[w, p], recv_sem=self.recv_sem.at[w, p],
            device_id=other(*CORE), device_id_type=MESH,
        )
        copy.wait_send()
        copy.wait_recv()
        target = self.out if p == self.back - 1 else self.acc
        if p == 0:
            self.add(k, self.core_base, self.rows // 2, [(self.landing, (w,), 0)], target)
        elif p < self.back:
            for s in range(2):
                base, size = self.kept[s][min(p, self.levels - 1)]
                if p < self.levels - 1:
                    sources = [(self.landing, (w,), self.land(p) + s * size)]
                elif p < self.levels:
                    sources = [(self.landing, (w,), self.land(p) + (3 * s + i) * size) for i in range(3)]
                else:
                    sources = [(self.extra, (w, p - self.levels), s * size)]
                self.add(k, base, size, sources, target)

    def start(self, k, p):
        w = lax.rem(k, self.window)
        for source, target, device in self.copies(k, p):
            pltpu.make_async_remote_copy(
                src_ref=source, dst_ref=target, send_sem=self.send_sem.at[w, p], recv_sem=self.recv_sem.at[w, p],
                device_id=device, device_id_type=MESH,
            ).start()

    def advance(self, k, p):
        if p > 0:
            self.finish(k, p - 1)
        if p < self.phases:
            self.start(k, p)

    def state(self, k, p):
        rows = self.rows
        if p == 0:
            return [(self.acc, 0, rows)]
        if p == self.phases:
            return [(self.out, 0, rows)]
        level = min(p - 1, self.levels - 1) if p < self.back else self.phases - 1 - p
        spans = [(self.core_base, rows // 2)] if level == 0 else [self.kept[s][level] for s in range(2)]
        return [(self.acc if p < self.back else self.out, base, size) for base, size in spans]


def scratch(chunks, rows, window, seq):
    more = len([1 for i in range(12) if (8 << i) < seq])
    return [
        pltpu.VMEM((chunks, rows, LANES), BF16),
        pltpu.VMEM((chunks, rows, LANES), BF16),
        pltpu.VMEM((window, rows, LANES), BF16),
        pltpu.VMEM((window, max(more, 1), rows // 32, LANES), BF16),
        pltpu.SemaphoreType.DMA((window, 8 + more)),
        pltpu.SemaphoreType.DMA((window, 8 + more)),
    ]


def tail_kernel(
    rank, states, chunk, seq,
    dprelow_ref, select_ref, dpair_ref, step_weight_ref, normed_ref, upstream_ref, inputs_ref, scale_ref, ids_ref,
    gain_ref, dactive_first_ref, mixed_first_ref, select_weight_ref, halo_ref, drate_ref, dbias_ref, dskip_ref,
    dactive_ref, mixed_ref, front_ref, active_ref, select_tile_ref, conv_ref, front_weight_ref, gate_weight_ref,
    dgate_ref, gated_ref, out_weight_ref, handed,
    output_ref, dinputs_ref, front_sum, gate_rest, out_rest, embedding_sum, wide_sum, mixed_sum,
    dselect_scr, first_scr, after_scr, spread_scr, extended_scr, dnormed_scr, result_scr, misc_scr, gain_scr,
    acc, out, landing, extra, send_sem, recv_sem, load_sem, store_sem, first_send, first_recv,
):
    step = pl.program_id(0)
    rows, width = upstream_ref.shape
    across = width // LANES
    inner = dprelow_ref.shape[1]
    tiles, pairs = inner // LANES, inner // (2 * LANES)
    tall = 2 * LANES
    kernel = conv_ref.shape[0]
    halo = kernel - 1
    vocab = embedding_sum.shape[0]
    ex = Exchange(acc, out, landing, extra, send_sem, recv_sem, chunk, landing.shape[0], seq)
    early = done_early(tiles, ex.phases)
    old = tiles - early
    embedding_at, wide_at, mixed_at = (old + pairs + i for i in range(3))
    count = old + pairs + 3
    place = lax.axis_index("seq")
    here_dp = lax.axis_index("dp")

    def add(scr, value):
        for b in range(across):
            scr[b] += value[:, b * LANES : (b + 1) * LANES]

    def put(scr, here, value):
        for b in range(across):
            scr[b, here, :] = value[:, b * LANES : (b + 1) * LANES]

    def take(scr, here):
        return jnp.concatenate([scr[b, here, :] for b in range(across)], axis=1)

    def first_copy():
        return pltpu.make_async_remote_copy(
            src_ref=first_scr, dst_ref=after_scr, send_sem=first_send, recv_sem=first_recv,
            device_id=(here_dp, lax.rem(place + seq - 1, seq)), device_id_type=MESH,
        )

    def greet():
        barrier = pltpu.get_barrier_semaphore()
        partners = ex.partners()
        for device in partners:
            pl.semaphore_signal(barrier, inc=1, device_id=device, device_id_type=MESH)
        for there, by in ((place > 0, -1), (place < seq - 1, 1)):

            @pl.when(there)
            def _():
                pl.semaphore_signal(barrier, inc=1, device_id=(here_dp, place + by), device_id_type=MESH)

        neighbours = 2 - (place == 0).astype(jnp.int32) - (place == seq - 1).astype(jnp.int32)
        pl.semaphore_wait(barrier, len(partners) + neighbours)

    def store(k):
        pair = (k + early) // 2

        @pl.when((k < old) & (lax.rem(k + early, 2) == 0))
        def _():
            store_lanes(out.at[k], gate_rest, pair - (early + 1) // 2, store_sem.at[k])

        @pl.when((k < old) & (lax.rem(k + early, 2) == 1))
        def _():
            store_rows(out.at[k], out_rest, pair - early // 2, store_sem.at[k])

        @pl.when((k >= old) & (k < embedding_at))
        def _():
            store_lanes(out.at[k], front_sum, k - old, store_sem.at[k])

        @pl.when(k == embedding_at)
        def _():
            for b in range(width // LANES):
                pltpu.make_async_copy(
                    out.at[k, pl.ds(b * vocab, vocab), :], embedding_sum.at[:, pl.ds(b * LANES, LANES)], store_sem.at[k]
                ).start()

        @pl.when(k == wide_at)
        def _():
            pltpu.make_async_copy(out.at[k], wide_sum, store_sem.at[k]).start()

        @pl.when(k == mixed_at)
        def _():
            pltpu.make_async_copy(out.at[k], mixed_sum, store_sem.at[k]).start()

    def old_turns(spot):
        slot = 2 * (tiles + step) + spot
        for p, shift in turns(ex.phases, spot):
            k = tiles + step + shift - early

            @pl.when((k >= 0) & (k < old))
            def _():
                if p > 0:

                    @pl.when(slot > 2 * tiles + 1)
                    def _():
                        ex.finish(k, p - 1)

                if p < ex.phases:
                    ex.start(k, p)
                else:
                    store(k)

    def new_turns(turn):
        for p in range(ex.phases, -1, -1):
            k = old + turn - 2 * p

            @pl.when((k >= old) & (k < count))
            def _():
                ex.advance(k, p)
                if p == ex.phases:
                    store(k)

    @pl.when(step == 0)
    def _():
        sizes = []
        for k in range(old):
            sizes.append(0)
            for ref, base, size in ex.state(k, next_phase(k + early, tiles)):
                here = pl.ds(pl.multiple_of(base, 16), size)
                sizes[-1] += size
                pltpu.make_async_copy(handed.at[k, here, :], ref.at[k, here, :], load_sem.at[k]).start()
        greet()
        dlow = contract_cols(dprelow_ref[...], step_weight_ref[...])
        dselect_scr[...] = jnp.concatenate([dlow, dpair_ref[...]], axis=1).astype(BF16)
        some = jnp.dot(dselect_scr[: halo * SUB], select_weight_ref[...], preferred_element_type=F32)
        some = (dactive_first_ref[...] + some) * silu_slope(mixed_first_ref[...])
        for i in range(halo):
            first_scr[i : i + 1, :] = some[i * SUB : i * SUB + 1, :]
        first_scr[halo:, :] = jnp.zeros((SUB - halo, inner), F32)

        @pl.when(place > 0)
        def _():
            first_copy().start()

        dnormed_scr[...] = jnp.zeros_like(dnormed_scr)
        result_scr[...] = jnp.zeros_like(result_scr)
        misc_scr[...] = jnp.zeros_like(misc_scr)
        misc_scr[kernel + 1 : kernel + 2, :] = dbias_ref[...]
        misc_scr[kernel + 2 : kernel + 3, :] = dskip_ref[...]
        acc[wide_at] = jnp.zeros_like(acc[wide_at])
        acc[mixed_at] = jnp.zeros_like(acc[mixed_at])
        for b in range(tiles):
            at = rank * tiles + b * states
            acc[mixed_at, at : at + states, :] = drate_ref[:, b * LANES : (b + 1) * LANES].astype(BF16)
        for k in range(old):
            wait_rows(acc.at[k, pl.ds(0, sizes[k]), :], load_sem.at[k])

    old_turns(0)

    @pl.when(step < pairs)
    def _():
        add(result_scr, jnp.dot(gated_ref[...], out_weight_ref[...], preferred_element_type=F32))
        add(dnormed_scr, contract_cols(dgate_ref[...], gate_weight_ref[...]))
        lanes = pl.ds(pl.multiple_of(step * tall, tall), tall)
        mixed = mixed_ref[...]
        back = jnp.dot(dselect_scr[...], select_tile_ref[...], preferred_element_type=F32)
        dmixed = (dactive_ref[...] + back) * silu_slope(mixed)
        spread_scr[:rows] = dmixed
        extended_scr[: halo * SUB] = halo_ref[...].astype(F32)
        extended_scr[halo * SUB :] = front_ref[...].astype(F32)
        misc_scr[kernel : kernel + 1, lanes] = jnp.sum(dmixed, axis=0, keepdims=True)
        for i in range(kernel):
            misc_scr[i : i + 1, lanes] = jnp.sum(
                dmixed * extended_scr[i * SUB : i * SUB + rows], axis=0, keepdims=True
            )
        wide = contract_rows(dselect_scr[...], active_ref[...]).astype(BF16)
        columns = wide.shape[0]
        for side in range(2):
            at = pl.ds(pl.multiple_of((2 * step + side) * columns, columns), columns)
            acc[wide_at, at, :] = wide[:, side * LANES : (side + 1) * LANES]
        part = contract_rows(select_ref[:, :rank], dprelow_ref[:, lanes]).astype(BF16)
        for side in range(2):
            at = pl.ds(pl.multiple_of((2 * step + side) * rank, rank), rank)
            acc[mixed_at, at, :] = part[:, side * LANES : (side + 1) * LANES]

        @pl.when(step == 0)
        def _():
            @pl.when(place > 0)
            def _():
                first_copy().wait_send()

            @pl.when(place < seq - 1)
            def _():
                first_copy().wait_recv()

            @pl.when(place == seq - 1)
            def _():
                after_scr[...] = jnp.zeros_like(after_scr)

        sub = lax.broadcasted_iota(jnp.int32, (SUB, tall), 0)
        for i in range(halo):
            own = pltpu.roll(spread_scr[i * SUB : (i + 1) * SUB, :], SUB - 1, 0)
            spread_scr[rows + i * SUB : rows + (i + 1) * SUB] = jnp.where(
                sub < SUB - 1, own, after_scr[i : i + 1, lanes]
            )
        dfront = conv_ref[halo : halo + 1] * spread_scr[:rows]
        for i in range(1, kernel):
            dfront = dfront + conv_ref[halo - i : halo - i + 1] * spread_scr[i * SUB : i * SUB + rows]
        dfront = dfront.astype(BF16)
        part = jnp.dot(normed_ref[...], dfront, preferred_element_type=F32).astype(BF16)
        acc[old + step, :width, :] = part[:, :LANES]
        acc[old + step, width:, :] = part[:, LANES:]
        add(dnormed_scr, contract_cols(dfront, front_weight_ref[...]))

    @pl.when(step == pairs)
    def _():
        part = rows // SUB

        def norms(i, total):
            here = pl.ds(pl.multiple_of(i * part, part), part)
            dnormed, inputs, scale = take(dnormed_scr, here), inputs_ref[here, :], scale_ref[here, :]
            scaled = gain_ref[...] * dnormed
            mean = jnp.sum(scaled * inputs, axis=1, keepdims=True) * (1.0 / width)
            put(
                dnormed_scr, here,
                upstream_ref[here, :].astype(F32) + scale * scaled - inputs * (scale * scale * scale * mean),
            )
            put(result_scr, here, take(result_scr, here) + inputs)
            return total + jnp.sum((dnormed * inputs * scale).reshape(-1, SUB, width), axis=0)

        total = lax.fori_loop(0, SUB, norms, jnp.zeros((SUB, width), F32))
        gain_scr[...] = jnp.sum(total, axis=0, keepdims=True)
        hot = (ids_ref[...] == lax.broadcasted_iota(jnp.int32, (rows, vocab), 1)).astype(F32).astype(BF16)
        for b in range(width // tall):
            value = jnp.concatenate([dnormed_scr[2 * b], dnormed_scr[2 * b + 1]], axis=1)
            high = value.astype(BF16)
            low = (value - high.astype(F32)).astype(BF16)
            whole = (contract_rows(hot, high) + contract_rows(hot, low)).astype(BF16)
            for side in range(2):
                at = (2 * b + side) * vocab
                acc[embedding_at, at : at + vocab, :] = whole[:, side * LANES : (side + 1) * LANES]
        at = (rank + states) * tiles
        for b in range(tiles):
            acc[mixed_at, at + b * 16 : at + (b + 1) * 16, :] = misc_scr[:, b * LANES : (b + 1) * LANES].astype(BF16)
        at = (rank + states + 16) * tiles
        for b in range(width // LANES):
            acc[mixed_at, at + b * 16 : at + (b + 1) * 16, :] = jnp.broadcast_to(
                gain_scr[:, b * LANES : (b + 1) * LANES], (16, LANES)
            ).astype(BF16)

    @pl.when(step == pairs + 1)
    def _():
        span = rows // SUB
        for i in range(SUB):
            for b in range(across):
                lanes, every = slice(b * LANES, (b + 1) * LANES), pl.ds(i, span, stride=SUB)
                dinputs_ref[i * span : (i + 1) * span, lanes] = dnormed_scr[b, every, :]
                output_ref[i * span : (i + 1) * span, lanes] = result_scr[b, every, :].astype(BF16)

    old_turns(1)
    new_turns(step)

    @pl.when(step == pl.num_programs(0) - 1)
    def _():
        def rest(turn, _):
            new_turns(turn)
            return 0

        lax.fori_loop(pairs + 3, pairs + 3 + 2 * ex.phases, rest, 0)
        for k in range(count):
            wait_rows(out.at[k], store_sem.at[k])


def run_tail(
    d_pre_low, select, d_pair, step_weight, normed, upstream, inputs, scale, ids, gain, d_active, mixed, select_weight,
    halo, d_rate, d_bias, d_skip, front, active, conv_weight, input_weight, d_gate, gated, output_weight, handed, vocab, seq,
):
    rows, inner = front.shape
    width = inputs.shape[1]
    rank, states = step_weight.shape[0], d_rate.shape[0]
    chunk = 2 * width
    tiles, pairs, tall = inner // LANES, inner // (2 * LANES), 2 * LANES
    phases = 8 + max(seq.bit_length() - 4, 0)
    early = done_early(tiles, phases)
    count = tiles - early + pairs + 3
    some = halo.shape[0]
    at = lambda i: lax.min(i, pairs - 1)
    whole = lambda a: pl.BlockSpec(a.shape, lambda i: (0, 0), pipeline_mode=pl.Buffered(1))
    first = pl.BlockSpec((some, inner), lambda i: (0, 0), pipeline_mode=pl.Buffered(1))
    tile = lambda height: pl.BlockSpec((height, tall), lambda i: (0, at(i)))
    high = lambda wide: pl.BlockSpec((tall, wide), lambda i: (at(i), 0))
    hbm = pl.BlockSpec(memory_space=pltpu.HBM)
    fixed = pl.BlockSpec((rows, width), lambda i: (0, 0))
    gates, outs = inner - (early + 1) // 2 * tall, inner - early // 2 * tall
    return pl.pallas_call(
        functools.partial(tail_kernel, rank, states, chunk, seq),
        grid=(pairs + 3,),
        in_specs=[
            whole(d_pre_low), whole(select), whole(d_pair), whole(step_weight), whole(normed), whole(upstream),
            whole(inputs), whole(scale), whole(ids), whole(gain), first, first, whole(select_weight), tile(some),
            whole(d_rate), whole(d_bias), whole(d_skip), tile(rows), tile(rows), tile(rows), tile(rows),
            tile(select_weight.shape[0]), tile(conv_weight.shape[0]), tile(width),
            pl.BlockSpec((width, tall), lambda i: (0, at(i) + pairs)), tile(rows), tile(rows), high(width), hbm,
        ],
        out_specs=[fixed, fixed, hbm, hbm, hbm, hbm, hbm, hbm],
        out_shape=[
            jax.ShapeDtypeStruct((rows, width), BF16),
            jax.ShapeDtypeStruct((rows, width), F32),
            jax.ShapeDtypeStruct((width, inner), BF16),
            jax.ShapeDtypeStruct((width, gates), BF16),
            jax.ShapeDtypeStruct((outs, width), BF16),
            jax.ShapeDtypeStruct((vocab, width), BF16),
            jax.ShapeDtypeStruct((chunk, LANES), BF16),
            jax.ShapeDtypeStruct((chunk, LANES), BF16),
        ],
        scratch_shapes=[
            pltpu.VMEM(select.shape, BF16),
            pltpu.VMEM((SUB, inner), F32), pltpu.VMEM((SUB, inner), F32),
            pltpu.VMEM((rows + some, tall), F32), pltpu.VMEM((rows + some, tall), F32),
            pltpu.VMEM((width // LANES, rows, LANES), F32), pltpu.VMEM((width // LANES, rows, LANES), F32),
            pltpu.VMEM((16, inner), F32), pltpu.VMEM((1, width), F32),
        ]
        + scratch(count, chunk, 8, seq)
        + [
            pltpu.SemaphoreType.DMA((count,)), pltpu.SemaphoreType.DMA((count,)),
            pltpu.SemaphoreType.DMA, pltpu.SemaphoreType.DMA,
        ],
        compiler_params=pltpu.CompilerParams(
            collective_id=2, has_side_effects=True, vmem_limit_bytes=62 << 20
        ),
        name="span_tail",
    )(
        d_pre_low, select, d_pair, step_weight, normed, upstream, inputs, scale, ids, gain, d_active, mixed,
        select_weight, halo, d_rate, d_bias, d_skip, d_active, mixed, front, active, select_weight, conv_weight,
        input_weight, input_weight, d_gate, gated, output_weight, handed,
    )


def widen_kernel(
    rank, states, columns, outs,
    front_ref, gate_ref, gate_rest_ref, out_ref, out_rest_ref, embedding_ref, wide_ref, mixed_ref,
    input_to, output_to, embedding_to, select_to, step_to, decay_to, conv_to, gain_to, *line_to,
):
    step = pl.program_id(0)
    inner, gates = front_ref.shape[1], gate_ref.shape[1]
    input_to[:, :inner] = front_ref[...].astype(F32)
    input_to[:, inner : inner + gates] = gate_ref[...].astype(F32)
    input_to[:, inner + gates :] = gate_rest_ref[...].astype(F32)

    @pl.when(step < outs)
    def _():
        output_to[...] = out_ref[...].astype(F32)

    @pl.when(step >= outs)
    def _():
        output_to[...] = out_rest_ref[...].astype(F32)

    embedding_to[...] = embedding_ref[...].astype(F32)

    @pl.when(step == 0)
    def _():
        for source, whole in (
            (wide_ref, ((select_to, columns),)),
            (mixed_ref, ((step_to, rank), (decay_to, states), (conv_to, 16), (gain_to, 16))),
        ):
            at = 0
            for to, height in whole:
                for b in range(to.shape[1] // LANES):
                    part = source[at : at + height, :].astype(F32)
                    lanes = slice(b * LANES, (b + 1) * LANES)
                    to[:, lanes] = part[: to.shape[0]]
                    if to is conv_to:
                        for i, line in enumerate(line_to):
                            line[:, lanes] = part[to.shape[0] + i : to.shape[0] + i + 1]
                    at += height


def run_widen(front, gate, gate_rest, out, out_rest, embedding, wide, mixed, rank, states, columns, kernel):
    width, inner = front.shape
    tall = 2 * LANES
    tiles, outs = inner // tall, out.shape[0] // tall
    vocab = embedding.shape[0]
    lines = lambda a: pl.BlockSpec((width // tiles, a.shape[1]), lambda i: (i, 0))
    thin = pl.BlockSpec((vocab // tiles, width), lambda i: (i, 0))
    fixed = lambda shape: pl.BlockSpec(shape, lambda i: (0, 0))
    shapes = [
        (width, 2 * inner), (inner, width), (vocab, width), (columns, inner), (rank, inner), (states, inner), (kernel, inner),
        (1, width), (1, inner), (1, inner), (1, inner),
    ]
    return pl.pallas_call(
        functools.partial(widen_kernel, rank, states, columns, outs),
        grid=(tiles,),
        in_specs=[
            lines(front), lines(gate), lines(gate_rest),
            pl.BlockSpec((tall, width), lambda i: (lax.min(i, outs - 1), 0)),
            pl.BlockSpec((tall, width), lambda i: (lax.max(i - outs, 0), 0)),
            thin, fixed(wide.shape), fixed(mixed.shape),
        ],
        out_specs=[
            pl.BlockSpec((width // tiles, 2 * inner), lambda i: (i, 0)),
            pl.BlockSpec((tall, width), lambda i: (i, 0)), thin,
        ]
        + [fixed(shape) for shape in shapes[3:]],
        out_shape=[jax.ShapeDtypeStruct(shape, F32) for shape in shapes],
        compiler_params=pltpu.CompilerParams(vmem_limit_bytes=62 << 20),
        name="sums_to_float32",
    )(front, gate, gate_rest, out, out_rest, embedding, wide, mixed)


def on_device(
    byte_ids,
    embedding,
    cotangent,
    norm_gain,
    input_projection_weight,
    conv_weight,
    conv_bias,
    select_weight,
    step_weight,
    step_bias,
    decay_log,
    skip_gain,
    output_projection_weight,
):
    count, stretch = byte_ids.shape
    vocab, width = embedding.shape
    kernel, inner = conv_weight.shape
    states = decay_log.shape[0]
    rank = step_weight.shape[0]
    rows = count * stretch
    halo = kernel - 1
    ids = to_spans(byte_ids.reshape(rows, 1))
    one_hot = ids == jnp.arange(vocab, dtype=jnp.int32)[None, :]
    block_inputs = jnp.dot(one_hot.astype(BF16), embedding, preferred_element_type=F32)
    scale = lax.rsqrt(jnp.mean(block_inputs * block_inputs, axis=1, keepdims=True) + EPS)
    normed_input = (block_inputs * scale * norm_gain).astype(BF16)
    front = jnp.dot(
        normed_input, input_projection_weight[:, :inner], preferred_element_type=F32
    ).astype(BF16)
    gate = jnp.dot(
        normed_input, input_projection_weight[:, inner:], preferred_element_type=F32
    ).astype(BF16)
    last = front[rows - halo * SUB :].reshape(halo, SUB, inner)
    tail = passed_along(last[:, SUB - 1], "seq", 1)
    earlier = jnp.concatenate([tail[:, None], last[:, : SUB - 1]], axis=1).reshape(halo * SUB, inner)
    extended = jnp.concatenate([earlier, front], axis=0).astype(F32)
    mixed = conv_bias + conv_weight[0] * extended[:rows]
    for place in range(1, kernel):
        mixed = mixed + conv_weight[place] * extended[place * SUB : place * SUB + rows]
    active = jax.nn.silu(mixed).astype(BF16)
    select = jnp.dot(active, select_weight, preferred_element_type=F32).astype(BF16)
    lowrank = select[:, :rank]
    pre = jnp.dot(lowrank, step_weight, preferred_element_type=F32) + step_bias
    upstream = to_spans(cotangent.reshape(rows, width))
    graded = contract_cols(upstream, output_projection_weight)
    seq = lax.axis_size("seq")
    turned = normed_input.T
    (
        gated, d_gate, d_pre_low, d_active, d_rate, d_bias, d_skip, d_pair, gate_sum, out_sum, handed
    ) = run_scan(
        pre, active, gate, graded, select, decay_log, skip_gain.reshape(1, inner), turned, upstream, rank, seq
    )
    output, d_inputs, front_sum, gate_rest, out_rest, embedding_sum, wide_sum, mixed_sum = run_tail(
        d_pre_low, select, d_pair, step_weight, turned, upstream, block_inputs, scale, ids, norm_gain.reshape(1, width),
        d_active, mixed, select_weight.T, earlier, d_rate, d_bias, d_skip, front, active, conv_weight,
        input_projection_weight, d_gate, gated, output_projection_weight, handed, vocab, seq,
    )
    (
        d_input_weight, d_output_weight, d_embedding, d_select_weight, d_step_weight, d_decay_log, d_conv_weight,
        d_norm_gain, d_conv_bias, d_step_bias, d_skip_gain,
    ) = run_widen(
        front_sum, gate_sum, gate_rest, out_sum, out_rest, embedding_sum, wide_sum, mixed_sum, rank, states,
        select_weight.shape[1], kernel,
    )
    return (
        output.reshape(count, stretch, width),
        d_inputs.reshape(count, stretch, width),
        d_embedding,
        d_norm_gain[0],
        d_input_weight,
        d_conv_weight,
        d_conv_bias[0],
        d_select_weight.T,
        d_step_weight,
        d_step_bias[0],
        d_decay_log,
        d_skip_gain[0],
        d_output_weight,
    )


def solution(mesh):
    placed = (P("dp", "seq"), P(), P("dp", "seq", None)) + (P(),) * 10
    return jax.shard_map(
        on_device,
        mesh=mesh,
        in_specs=placed,
        out_specs=(P("dp", "seq", None), P("dp", "seq", None)) + (P(),) * 11,
        check_vma=False,
    )
```

```python
import functools
import math

import jax
import jax.numpy as jnp
from jax import lax
from jax.experimental import pallas as pl
from jax.experimental.pallas import tpu as pltpu
from jax.sharding import PartitionSpec as P

EPS = 1e-05
LANES = 128
SUB = 8
LOG2E = math.log2(math.e)
LN2 = math.log(2.0)
F32 = jnp.float32
BF16 = jnp.bfloat16
MESH = pl.DeviceIdType.MESH


def silu_slope(value):
    sigma = jax.nn.sigmoid(value)
    return sigma * (1.0 + value * (1.0 - sigma))


def contract_rows(left, right):
    return lax.dot_general(
        left, right, (((0,), (0,)), ((), ())), preferred_element_type=F32
    )


def contract_cols(left, right):
    return lax.dot_general(
        left, right, (((1,), (1,)), ((), ())), preferred_element_type=F32
    )


def sublane(shape):
    return lax.broadcasted_iota(jnp.int32, shape, len(shape) - 2)


def shift_up(value, by, fill, reverse):
    place = sublane(value.shape)
    if reverse:
        moved = pltpu.roll(value, SUB - by, value.ndim - 2)
        return jnp.where(place < SUB - by, moved, fill)
    moved = pltpu.roll(value, by, value.ndim - 2)
    return jnp.where(place >= by, moved, fill)


def expand_columns(select, first, states):
    width = select.shape[1]
    shape = (width, states * LANES)
    source = lax.broadcasted_iota(jnp.int32, shape, 0)
    target = lax.broadcasted_iota(jnp.int32, shape, 1) // LANES + first
    spread = (source == target).astype(F32).astype(BF16)
    return jnp.dot(select, spread, preferred_element_type=F32)


def tree_sum(value):
    while value.shape[0] > 1:
        half = value.shape[0] // 2
        value = value[:half] + value[half:]
    return value[0]


def front_kernel(
    seq,
    ids_ref, embedding_ref, cotangent_ref, gain_ref, front_weight_ref, gate_weight_ref, out_weight_ref, conv_ref,
    conv_bias_ref, select_weight_ref,
    inputs_ref, scale_ref, normed_ref, turned_ref, upstream_ref, hot_ref, front_ref, halo_ref, mixed_ref, active_ref,
    gate_ref, graded_ref, select_ref,
    last_scr, extended_scr, total_scr, send_sem, recv_sem,
):
    step = pl.program_id(0)
    rows, width = upstream_ref.shape
    span = rows // SUB
    vocab = embedding_ref.shape[0]
    kernel = conv_ref.shape[0]
    halo = kernel - 1
    place = lax.axis_index("seq")

    def there(by):
        return (lax.axis_index("dp"), place + by)

    def copy():
        return pltpu.make_async_remote_copy(
            src_ref=ids_ref.at[:, pl.ds(rows - LANES, LANES)], dst_ref=last_scr, send_sem=send_sem, recv_sem=recv_sem,
            device_id=there(1), device_id_type=MESH,
        )

    def norm(inputs):
        scale = lax.rsqrt(jnp.sum(inputs * inputs, axis=1, keepdims=True) * (1.0 / width) + EPS)
        return scale, (inputs * scale * gain_ref[...]).astype(BF16)

    def hot_of(ids):
        shape = (vocab, ids.shape[1])
        return (lax.broadcasted_iota(jnp.int32, shape, 0) == ids).astype(F32).astype(BF16)

    @pl.when(step == 0)
    def _():
        barrier = pltpu.get_barrier_semaphore()

        @pl.when(place > 0)
        def _():
            pl.semaphore_signal(barrier, inc=1, device_id=there(-1), device_id_type=MESH)

        @pl.when(place == 0)
        def _():
            last_scr[...] = jnp.full(last_scr.shape, -1, jnp.int32)

        row = lax.broadcasted_iota(jnp.int32, (rows, rows), 0)
        position = lax.broadcasted_iota(jnp.int32, (rows, rows), 1)
        order = (lax.rem(row, SUB) * span + row // SUB == position).astype(F32).astype(BF16)
        upstream_ref[...] = jnp.dot(order, cotangent_ref[...], preferred_element_type=F32).astype(BF16)

        @pl.when(place < seq - 1)
        def _():
            pl.semaphore_wait(barrier, 1)
            copy().start()

        hot = contract_cols(hot_of(ids_ref[...]), order).astype(BF16)
        hot_ref[...] = hot
        inputs = contract_rows(hot, embedding_ref[...])
        inputs_ref[...] = inputs
        scale, normed = norm(inputs)
        scale_ref[...] = scale
        normed_ref[:rows] = normed
        turned_ref[...] = normed.T

        @pl.when(place < seq - 1)
        def _():
            copy().wait_send()

        @pl.when(place > 0)
        def _():
            copy().wait_recv()

        last = contract_rows(hot_of(last_scr[...]), embedding_ref[...])[LANES - 16 :]
        normed_ref[rows:] = norm(last)[1]
        total_scr[...] = jnp.zeros_like(total_scr)

    both = jnp.dot(normed_ref[...], front_weight_ref[...], preferred_element_type=F32).astype(BF16)
    front_ref[...] = both[:rows]
    both = both.astype(F32)
    extended_scr[halo * SUB :] = both[:rows]
    sub = lax.broadcasted_iota(jnp.int32, (SUB, both.shape[1]), 0)
    for i in range(halo):
        own = pltpu.roll(both[rows - (halo - i) * SUB : rows - (halo - i - 1) * SUB], 1, 0)
        before = both[rows + 16 - halo + i : rows + 16 - halo + i + 1]
        extended_scr[i * SUB : (i + 1) * SUB] = jnp.where(sub > 0, own, before)
    halo_ref[...] = extended_scr[: halo * SUB].astype(BF16)
    mixed = conv_bias_ref[...] + conv_ref[0:1] * extended_scr[:rows]
    for i in range(1, kernel):
        mixed = mixed + conv_ref[i : i + 1] * extended_scr[i * SUB : i * SUB + rows]
    mixed_ref[...] = mixed
    active = jax.nn.silu(mixed).astype(BF16)
    active_ref[...] = active
    gate_ref[...] = jnp.dot(normed_ref[:rows], gate_weight_ref[...], preferred_element_type=F32).astype(BF16)
    graded_ref[...] = contract_cols(upstream_ref[...], out_weight_ref[...])
    total_scr[...] += contract_cols(active, select_weight_ref[...])

    @pl.when(step == pl.num_programs(0) - 1)
    def _():
        select_ref[...] = total_scr[...].astype(BF16)


def run_front(
    ids, embedding, cotangent, gain, input_weight, output_weight, conv_weight, conv_bias, select_weight, seq
):
    rows, width = cotangent.shape
    inner = output_weight.shape[0]
    vocab, kernel, columns = embedding.shape[0], conv_weight.shape[0], select_weight.shape[0]
    halo = (kernel - 1) * SUB
    tall = 2 * LANES
    pairs = inner // tall
    whole = lambda a: pl.BlockSpec(a.shape, lambda i: (0, 0), pipeline_mode=pl.Buffered(1))
    tile = lambda height: pl.BlockSpec((height, tall), lambda i: (0, i))
    fixed = lambda shape: pl.BlockSpec(shape, lambda i: (0, 0))
    outs = [
        ((rows, width), F32, None), ((rows, 1), F32, None), ((rows + 16, width), BF16, None),
        ((width, rows), BF16, None), ((rows, width), BF16, None), ((vocab, rows), BF16, None),
        ((rows, inner), BF16, rows), ((halo, inner), BF16, halo), ((rows, inner), F32, rows), ((rows, inner), BF16, rows),
        ((rows, inner), BF16, rows), ((rows, inner), F32, rows), ((rows, columns), BF16, None),
    ]
    return pl.pallas_call(
        functools.partial(front_kernel, seq),
        grid=(pairs,),
        in_specs=[
            whole(ids), whole(embedding), whole(cotangent), whole(gain), tile(width),
            pl.BlockSpec((width, tall), lambda i: (0, i + pairs)), pl.BlockSpec((tall, width), lambda i: (i, 0)),
            tile(kernel), tile(1), tile(columns),
        ],
        out_specs=[fixed(shape) if height is None else tile(height) for shape, kind, height in outs],
        out_shape=[jax.ShapeDtypeStruct(shape, kind) for shape, kind, height in outs],
        scratch_shapes=[
            pltpu.VMEM((1, LANES), jnp.int32), pltpu.VMEM((rows + halo, tall), F32), pltpu.VMEM((rows, columns), F32),
            pltpu.SemaphoreType.DMA, pltpu.SemaphoreType.DMA,
        ],
        compiler_params=pltpu.CompilerParams(
            collective_id=3, has_side_effects=True, vmem_limit_bytes=62 << 20
        ),
        name="span_front",
    )(
        ids, embedding, cotangent, gain, input_weight, input_weight, output_weight, conv_weight, conv_bias, select_weight
    )


def slot_of(k, p):
    return 2 * k + 3 - k % 2 + 2 * p


def turns(phases, tile, place):
    for p in range(phases, -1, -1):
        k = tile - 1 - p
        yield k, p, (k >= 0) & (lax.rem(k + 2 * phases, 2) == 1 - place)


def begun(tiles, p):
    return sum(slot_of(k, p) < 2 * tiles for k in range(tiles))


def next_phase(k, tiles):
    return next(p for p in range(1000) if slot_of(k, p) >= 2 * tiles)


class Prefix:
    def __init__(self, totals, landing, start, incoming, gaps, rates, send_sem, recv_sem, rounds):
        self.totals, self.landing, self.start, self.incoming, self.gaps = totals, landing, start, incoming, gaps
        self.rates, self.send_sem, self.recv_sem, self.rounds = rates, send_sem, recv_sem, rounds

    def copy(self, e, r):
        return pltpu.make_async_remote_copy(
            src_ref=self.totals.at[e], dst_ref=self.landing.at[e, r],
            send_sem=self.send_sem.at[e, r], recv_sem=self.recv_sem.at[e, r],
            device_id=other("seq", 1 << r), device_id_type=MESH,
        )

    def advance(self, e, r):
        if r > 0:
            self.copy(e, r - 1).wait()
            self.merge(e, r - 1)
        if r < self.rounds:
            self.copy(e, r).start()

    def merge(self, e, r):
        n = self.rates.shape[1]
        rates = self.rates[e]
        later = bit_of(lax.axis_index("seq"), 1 << r) == 1
        end, message, total = self.totals[e, :n], self.totals[e, n : 2 * n], self.totals[e, 2 * n : 2 * n + 1]
        end2, message2 = self.landing[e, r, :n], self.landing[e, r, n : 2 * n]
        total2 = self.landing[e, r, 2 * n : 2 * n + 1]

        @pl.when(later)
        def _():
            gap = self.gaps[e, 0:1]
            self.start[e] = self.start[e] + jnp.exp2(gap * rates) * end2
            self.gaps[e, 0:1] = gap + total2

        @pl.when(jnp.logical_not(later))
        def _():
            gap = self.gaps[e, 1:2]
            self.incoming[e] = self.incoming[e] + jnp.exp2(gap * rates) * message2
            self.gaps[e, 1:2] = gap + total2

        if r < self.rounds - 1:
            reach, reach2 = jnp.exp2(total * rates), jnp.exp2(total2 * rates)
            self.totals[e, :n] = jnp.where(later, end + reach * end2, end2 + reach2 * end)
            self.totals[e, n : 2 * n] = jnp.where(later, message2 + reach2 * message, message + reach * message2)
            self.totals[e, 2 * n : 2 * n + 1] = total + total2


def scan_kernel(
    rank, states, chunk, rounds, seq,
    active_now, gate_now, graded_now, select_ref, step_weight_ref, step_bias_ref, decay_ref, skip_ref, normed_ref, upstream_ref,
    gated_ref, dgate_ref, dprelow_ref, dactive_ref, lines_ref, dselect_ref,
    gate_sum, out_sum, handed,
    inject_scr, readout_scr, dread_scr, dinject_scr, state_scr, factor_scr,
    rates_scr, rate_scr, delta_ring, drive_ring, grad_ring, silu_ring, sway_ring, active_ring, slope_ring, scan_scr, weight_scr,
    ahead_scr, behind_scr, sums_scr, gated_scr, dgated_scr,
    totals, totals_in, start_scr, incoming_scr, gaps_scr, prefix_send, prefix_recv,
    acc, out, landing, extra, send_sem, recv_sem, store_sem,
):
    rows = active_now.shape[0]
    steps = rows // SUB
    step = pl.program_id(0)
    count = rates_scr.shape[0]
    lag = delta_ring.shape[0]
    per = -(-rounds // (lag - 1))
    width = upstream_ref.shape[1]
    prefix = Prefix(
        totals, totals_in, start_scr, incoming_scr, gaps_scr, rates_scr, prefix_send, prefix_recv, rounds
    )
    ex = Exchange(acc, out, landing, extra, send_sem, recv_sem, chunk, landing.shape[0], seq)
    early = begun(count, ex.phases)
    half, unroll = states // 2, 8
    halves = [pl.ds(0, half), pl.ds(half, half)]

    def store(k):
        pair = k // 2

        @pl.when(lax.rem(k, 2) == 0)
        def _():
            store_lanes(out.at[k], gate_sum, pair, store_sem.at[k])

        @pl.when(lax.rem(k, 2) == 1)
        def _():
            store_rows(out.at[k], out_sum, pair, store_sem.at[k])

    def take_turns(place):
        for k, p, now in turns(ex.phases, step - lag, place):

            @pl.when(now)
            def _():
                ex.advance(k, p)
                if p == ex.phases:
                    store(k)

    @pl.when(step == 0)
    def _():
        for first, scr in ((rank, inject_scr), (rank + states, readout_scr)):
            for n in range(0, states, 2):
                wide = expand_columns(select_ref[...], first + n, 2)
                for side in range(2):
                    scr[:, n + side] = wide[:, side * LANES : (side + 1) * LANES].reshape(steps, SUB, LANES)
        dread_scr[...] = jnp.zeros_like(dread_scr)
        dinject_scr[...] = jnp.zeros_like(dinject_scr)
        start_scr[...] = jnp.zeros_like(start_scr)
        incoming_scr[...] = jnp.zeros_like(incoming_scr)
        gaps_scr[...] = jnp.zeros_like(gaps_scr)
        for e in range(count):
            rates_scr[e] = -jnp.exp(decay_ref[:, e * LANES : (e + 1) * LANES]) * LOG2E
        ex.greet()

    flat = lambda value: value.reshape(steps, SUB, LANES)
    zero = jnp.zeros((half, SUB, LANES), F32)

    def spread_rates(tile):
        rates = rates_scr[tile]
        for n in range(states):
            rate_scr[n] = jnp.broadcast_to(rates[n : n + 1], (SUB, LANES))

    def spread(table):
        return jnp.concatenate(
            [jnp.broadcast_to(table[n : n + 1], (1, SUB, LANES)) for n in range(states)], axis=0
        )

    @pl.when(step >= lag)
    def _():
        c = step - lag
        tile = c
        spread_rates(tile)
        slot = lax.rem(c, lag)
        delta_scr, drive_scr, grad_scr = delta_ring.at[slot], drive_ring.at[slot], grad_ring.at[slot]
        total = sums_scr[tile]
        before, after = total, total
        for by in (1, 2, 4):
            before = before + shift_up(before, by, 0.0, False)
            after = after + shift_up(after, by, 0.0, True)
        before, after = before - total, after - total
        state_scr[0] = ahead_scr[tile] + jnp.exp2(before[None] * rate_scr[...]) * spread(start_scr[tile])

        def forward(i, state):
            for u in range(unroll // 2):
                j = i * (unroll // 2) + u
                factor = jnp.exp2(delta_scr[j][None] * rate_scr[...])
                factor_scr[j] = factor
                state = factor * state + drive_scr[j][None] * inject_scr[j]
                state_scr[j + 1] = state
                dread_scr[j] += grad_scr[j][None] * state
                scan_scr[j] = tree_sum(readout_scr[j] * state)
            return state

        lax.fori_loop(0, steps // (unroll // 2), forward, state_scr[0])
        take_turns(0)
        lanes = pl.ds(pl.multiple_of(c * LANES, LANES), LANES)
        skip = skip_ref[:, lanes]
        active = active_ring[slot].reshape(rows, LANES)
        scanned = scan_scr[...].reshape(rows, LANES) + skip * active
        gated = (scanned * silu_ring[slot].reshape(rows, LANES)).astype(BF16)
        gated_ref[...] = gated
        dgate = (scanned * sway_ring[slot].reshape(rows, LANES)).astype(BF16)
        dgate_ref[...] = dgate
        lines_ref[states + 1 : states + 2, :] = jnp.sum(
            grad_scr[...].reshape(rows, LANES) * active, axis=0, keepdims=True
        )
        odd = lax.rem(c, 2)

        @pl.when(odd == 0)
        def _():
            gated_scr[:, :LANES] = gated
            dgated_scr[:, :LANES] = dgate

        @pl.when(odd == 1)
        def _():
            gated_scr[:, LANES:] = gated
            dgated_scr[:, LANES:] = dgate

        adjoint0 = behind_scr[tile] + jnp.exp2(after[None] * rate_scr[...]) * spread(incoming_scr[tile])
        state_scr[steps] = adjoint0
        for h, part in enumerate(halves):

            def backward(i, carry):
                adjoint, total = carry
                for u in range(unroll):
                    j = steps - 1 - (i * unroll + u)
                    d, g = delta_scr[j], grad_scr[j]
                    whole = adjoint + g[None] * readout_scr[j, part]
                    adjoint = factor_scr[j, part] * whole
                    through = adjoint * state_scr[j, part]
                    total = total + through * d[None]
                    dinject_scr[j, part] += whole * drive_scr[j][None]
                    one = tree_sum(through * rate_scr[part])
                    two = tree_sum(whole * inject_scr[j, part])
                    scan_scr[j] = scan_scr[j] + one if h else one
                    weight_scr[j] = weight_scr[j] + two if h else two
                return adjoint, total

            unused, total = lax.fori_loop(0, steps // unroll, backward, (state_scr[steps, part], zero))
            for n in range(half):
                at = h * half + n
                lines_ref[at : at + 1, :] = (
                    jnp.sum(total[n], axis=0, keepdims=True) * rate_scr[at, 0:1] * LN2
                )
        weight = weight_scr[...].reshape(rows, LANES)
        delta = delta_scr[...].reshape(rows, LANES)
        active = active_ring[slot].reshape(rows, LANES)
        dactive_ref[...] = delta * weight + skip_ref[:, lanes] * grad_scr[...].reshape(rows, LANES)
        dpre = (scan_scr[...].reshape(rows, LANES) * LN2 + active * weight) * slope_ring[slot].reshape(rows, LANES)
        dprelow_ref[...] = dpre.astype(BF16)
        lines_ref[states : states + 1, :] = jnp.sum(dpre, axis=0, keepdims=True)

        @pl.when(odd == 1)
        def _():
            pair = c // 2
            part = jnp.dot(normed_ref[...], dgated_scr[...], preferred_element_type=F32).astype(BF16)
            acc[2 * pair, :width, :] = part[:, :LANES]
            acc[2 * pair, width:, :] = part[:, LANES:]
            turned = gated_scr[...].T
            for b in range(width // (2 * LANES)):
                part = jnp.dot(
                    turned, upstream_ref[:, b * 2 * LANES : (b + 1) * 2 * LANES], preferred_element_type=F32
                ).astype(BF16)
                for side in range(2):
                    at = (2 * b + side) * 2 * LANES
                    acc[2 * pair + 1, at : at + 2 * LANES, :] = part[:, side * LANES : (side + 1) * LANES]

        take_turns(1)

    @pl.when(step < count)
    def _():
        tile = step
        spread_rates(tile)
        slot = lax.rem(step, lag)
        delta_scr, drive_scr, grad_scr = delta_ring.at[slot], drive_ring.at[slot], grad_ring.at[slot]
        lanes = pl.ds(pl.multiple_of(tile * LANES, LANES), LANES)
        pre = jnp.dot(select_ref[:, :rank], step_weight_ref[:, lanes], preferred_element_type=F32)
        pre = pre + step_bias_ref[:, lanes]
        small = jnp.exp(-jnp.abs(pre))
        delta = jnp.maximum(pre, 0.0) + jnp.log1p(small)
        slope_ring[slot] = flat(jnp.where(pre >= 0.0, 1.0, small) / (1.0 + small))
        delta_scr[...] = flat(delta)
        active = active_now[...].astype(F32)
        active_ring[slot] = flat(active)
        drive_scr[...] = flat(delta * active)
        gate = gate_now[...].astype(F32)
        sigma = jax.nn.sigmoid(gate)
        silu = gate * sigma
        silu_ring[slot] = flat(silu)
        graded = graded_now[...]
        grad_scr[...] = flat(graded * silu)
        sway_ring[slot] = flat(graded * (sigma * (1.0 + gate * (1.0 - sigma))))
        total = jnp.sum(delta_scr[...], axis=0)
        sums_scr[tile] = total
        whole = jnp.sum(total, axis=0, keepdims=True)
        totals[tile, 2 * states :] = jnp.broadcast_to(whole, (SUB, LANES))
        for h, part in enumerate(halves):

            def ends(i, carry):
                state, message, decay = carry
                for u in range(unroll):
                    j = i * unroll + u
                    factor = jnp.exp2(delta_scr[j][None] * rate_scr[part])
                    state = factor * state + drive_scr[j][None] * inject_scr[j, part]
                    decay = decay * factor
                    message = message + decay * (grad_scr[j][None] * readout_scr[j, part])
                return state, message, decay

            state, message, decay = lax.fori_loop(0, steps // unroll, ends, (zero, zero, zero + 1.0))
            for value, kept, at, reverse in (
                (state, ahead_scr, h * half, False), (message, behind_scr, states + h * half, True)
            ):
                factor = decay
                for by in (1, 2, 4):
                    value = value + factor * shift_up(value, by, 0.0, reverse)
                    factor = factor * shift_up(factor, by, 1.0, reverse)
                kept[tile, part] = shift_up(value, 1, 0.0, reverse)
                last = 0 if reverse else SUB - 1
                for n in range(half):
                    totals[tile, at + n : at + n + 1] = value[n, last : last + 1]

    for r in range(lag - 1, -1, -1):
        e = step - r

        @pl.when((e >= 0) & (e < count))
        def _():
            if r == 0:
                prefix.copy(e, 0).start()
            for done in range((r - 1) * per, min(r * per, rounds)) if r > 0 else ():
                prefix.advance(e, done + 1)

    @pl.when(step == count + lag - 1)
    def _():
        group = 4
        shape = (group * LANES, 2 * states)
        from_lane = lax.broadcasted_iota(jnp.int32, shape, 0) // LANES
        to_column = lax.broadcasted_iota(jnp.int32, shape, 1)
        whole = jnp.zeros((rows, 2 * states), F32)
        for first, scr in ((0, dinject_scr), (states, dread_scr)):
            for n in range(0, states, group):
                ones = (from_lane + (first + n) == to_column).astype(F32).astype(BF16)
                values = [scr[:, n + i].reshape(rows, LANES) for i in range(group)]
                highs = [value.astype(BF16) for value in values]
                lows = [(value - high.astype(F32)).astype(BF16) for value, high in zip(values, highs)]
                for parts in (highs, lows):
                    whole = whole + jnp.dot(jnp.concatenate(parts, axis=1), ones, preferred_element_type=F32)
        dselect_ref[...] = whole

        slots = 2 * count
        for k in range(count):
            for p in range(ex.phases):
                if slots - 2 <= slot_of(k, p) < slots:
                    ex.finish(k, p)
        sizes = []
        for k in range(early, count):
            sizes.append(0)
            for ref, base, size in ex.state(k, next_phase(k, count)):
                here = pl.ds(pl.multiple_of(base, 16), size)
                sizes[-1] += size
                pltpu.make_async_copy(ref.at[k, here, :], handed.at[k - early, here, :], store_sem.at[k]).start()
        for k in range(early):
            wait_rows(out.at[k], store_sem.at[k])
        for k in range(early, count):
            wait_rows(acc.at[k, pl.ds(0, sizes[k - early]), :], store_sem.at[k])


def run_scan(active, gate, graded, select, step_weight, step_bias, decay_log, skip, normed, upstream, seq):
    rows, inner = active.shape
    rank = step_weight.shape[0]
    states = decay_log.shape[0]
    width = upstream.shape[1]
    chunk = 2 * width
    tiles, steps = inner // LANES, rows // SUB
    rounds = seq.bit_length() - 1
    phases = 8 + max(rounds - 3, 0)
    early = begun(tiles, phases)
    gates, outs = (early + 1) // 2 * 2 * LANES, early // 2 * 2 * LANES
    lag = min(rounds, 3) + 1
    now = pl.BlockSpec((rows, LANES), lambda i: (0, lax.min(i, tiles - 1)))
    late = lambda shape: pl.BlockSpec(shape, lambda i: (0, lax.max(i - lag, 0)))
    whole = lambda a: pl.BlockSpec(a.shape, lambda i: (0, 0), pipeline_mode=pl.Buffered(1))
    hbm = pl.BlockSpec(memory_space=pltpu.HBM)
    wide = pltpu.VMEM((steps, states, SUB, LANES), F32)
    thin = pltpu.VMEM((steps, SUB, LANES), F32)
    cube = pltpu.VMEM((tiles, states, SUB, LANES), F32)
    small = pltpu.VMEM((tiles, states, LANES), F32)
    pair = pltpu.VMEM((rows, 2 * LANES), BF16)
    buffers = scratch(tiles, chunk, tiles // 2, seq)
    buffers[1] = pltpu.VMEM((begun(tiles, phases - 5), chunk, LANES), BF16)
    ring = pltpu.VMEM((lag, steps, SUB, LANES), F32)
    return pl.pallas_call(
        functools.partial(scan_kernel, rank, states, chunk, rounds, seq),
        grid=(tiles + lag,),
        in_specs=[
            now, now, now, whole(select), whole(step_weight), whole(step_bias), whole(decay_log), whole(skip),
            whole(normed), whole(upstream),
        ],
        out_specs=[
            late((rows, LANES)), late((rows, LANES)), late((rows, LANES)), late((rows, LANES)),
            late((states + SUB, LANES)), pl.BlockSpec((rows, 2 * states), lambda i: (0, 0)), hbm, hbm, hbm,
        ],
        out_shape=[
            jax.ShapeDtypeStruct((rows, inner), BF16),
            jax.ShapeDtypeStruct((rows, inner), BF16),
            jax.ShapeDtypeStruct((rows, inner), BF16),
            jax.ShapeDtypeStruct((rows, inner), F32),
            jax.ShapeDtypeStruct((states + SUB, inner), F32),
            jax.ShapeDtypeStruct((rows, 2 * states), F32),
            jax.ShapeDtypeStruct((width, gates), BF16),
            jax.ShapeDtypeStruct((outs, width), BF16),
            jax.ShapeDtypeStruct((tiles - early, chunk, LANES), BF16),
        ],
        scratch_shapes=[
            wide, wide, wide, wide,
            pltpu.VMEM((steps + 1, states, SUB, LANES), F32), wide,
            small, pltpu.VMEM((states, SUB, LANES), F32), ring, ring, ring, ring, ring, ring, ring, thin, thin,
            cube, cube, pltpu.VMEM((tiles, SUB, LANES), F32), pair, pair,
            pltpu.VMEM((tiles, 2 * states + SUB, LANES), F32),
            pltpu.VMEM((tiles, rounds, 2 * states + SUB, LANES), F32),
            small, small, pltpu.VMEM((tiles, SUB, LANES), F32),
            pltpu.SemaphoreType.DMA((tiles, rounds)), pltpu.SemaphoreType.DMA((tiles, rounds)),
        ]
        + buffers
        + [pltpu.SemaphoreType.DMA((tiles,))],
        compiler_params=pltpu.CompilerParams(
            collective_id=1, has_side_effects=True, vmem_limit_bytes=62 << 20
        ),
        name="span_scan",
    )(
        active, gate, graded, select, step_weight, step_bias, decay_log, skip, normed, upstream
    )


def bit_of(index, step):
    return (index // step) % 2

def other(axis, step):
    place = lax.axis_index(axis)
    place = place + step * (1 - 2 * bit_of(place, step))
    if axis == "dp":
        return (place, lax.axis_index("seq"))
    return (lax.axis_index("dp"), place)

CORE, X, Y = ("seq", 1), ("dp", 1), ("dp", 2)

def wait_rows(rows, sem):
    pltpu.make_async_copy(rows, rows, sem).wait()


def store_lanes(source, target, pair, sem):
    width = target.shape[0]
    for side in range(2):
        lanes = pl.ds(pl.multiple_of((2 * pair + side) * LANES, LANES), LANES)
        pltpu.make_async_copy(source.at[pl.ds(side * width, width), :], target.at[:, lanes], sem).start()


def store_rows(source, target, pair, sem):
    tall = 2 * LANES
    rows = pl.ds(pl.multiple_of(pair * tall, tall), tall)
    for b in range(target.shape[1] // LANES):
        pltpu.make_async_copy(
            source.at[pl.ds(b * tall, tall), :], target.at[rows, pl.ds(b * LANES, LANES)], sem
        ).start()


class Exchange:
    levels = 4

    def __init__(self, acc, out, landing, extra, send_sem, recv_sem, rows, window, seq):
        self.acc, self.out, self.landing, self.extra = acc, out, landing, extra
        self.send_sem, self.recv_sem = send_sem, recv_sem
        self.rows, self.window = rows, window
        self.more = [("seq", 8 << i) for i in range(12) if (8 << i) < seq]
        self.orders = ((CORE, X, Y), (CORE, Y, X))
        self.back = self.levels + len(self.more)
        self.phases = self.back + self.levels
        place = lax.axis_index("seq")
        self.quarter = (place // 2) % 4
        self.core_base = bit_of(place, 1) * (rows // 2)
        self.kept = []
        for s, order in enumerate(self.orders):
            base, size = self.core_base + s * (rows // 4), rows // 4
            spans = [(base, size)]
            for axis, step in order[1:]:
                size = size // 2
                base = base + bit_of(lax.axis_index(axis), step) * size
                spans.append((base, size))
            size = size // 4
            spans.append((base + self.quarter * size, size))
            self.kept.append(spans)

    def partners(self):
        links = [CORE, X, Y] + self.more
        return [other(*link) for link in links] + [self.along(i) for i in range(1, 4)]

    def greet(self):
        barrier = pltpu.get_barrier_semaphore()
        partners = self.partners()
        for device in partners:
            pl.semaphore_signal(barrier, inc=1, device_id=device, device_id_type=MESH)
        pl.semaphore_wait(barrier, len(partners))

    def along(self, i):
        place = lax.axis_index("seq")
        return (lax.axis_index("dp"), place + 2 * (lax.rem(self.quarter + i, 4) - self.quarter))

    def span(self, ref, k, base, size):
        return ref.at[k, pl.ds(pl.multiple_of(base, 16), size), :]

    def land(self, p):
        rows = self.rows
        return [0, rows // 2, rows // 2 + rows // 4, rows // 2 + rows // 4 + rows // 8][p]

    def rows_of(self, p):
        rows, last = self.rows, self.phases - 1
        if self.levels <= p < self.back:
            return rows // 32
        return [rows // 2, rows // 4, rows // 8, 6 * rows // 64][min(p, last - p)]

    def copies(self, k, p):
        w = lax.rem(k, self.window)
        rows = self.rows
        if p == 0:
            return [(self.span(self.acc, k, rows // 2 - self.core_base, rows // 2),
                     self.landing.at[w, pl.ds(0, rows // 2), :], other(*CORE))]
        if p == self.phases - 1:
            half = self.span(self.out, k, self.core_base, rows // 2)
            return [(half, half, other(*CORE))]
        found = []
        for s in range(2):
            if p < self.levels - 1:
                size = self.kept[s][p][1]
                axis, step = self.orders[s][p]
                base = self.kept[s][p - 1][0] + (1 - bit_of(lax.axis_index(axis), step)) * size
                target = self.landing.at[w, pl.ds(self.land(p) + s * size, size), :]
                found.append((self.span(self.acc, k, base, size), target, other(axis, step)))
            elif p == self.levels - 1:
                first, size = self.kept[s][p - 1][0], self.kept[s][p][1]
                for i in range(1, 4):
                    base = first + lax.rem(self.quarter + i, 4) * size
                    target = self.landing.at[w, pl.ds(self.land(p) + (3 * s + i - 1) * size, size), :]
                    found.append((self.span(self.acc, k, base, size), target, self.along(i)))
            elif p < self.back:
                base, size = self.kept[s][-1]
                target = self.extra.at[w, p - self.levels, pl.ds(s * size, size), :]
                found.append((self.span(self.acc, k, base, size), target, other(*self.more[p - self.levels])))
            else:
                level = self.phases - 1 - p
                piece = self.span(self.out, k, *self.kept[s][level])
                devices = [self.along(i) for i in range(1, 4)] if level == 3 else [other(*self.orders[s][level])]
                found += [(piece, piece, device) for device in devices]
        return found

    def add(self, k, base, size, sources, target):
        step = min(size, 256)

        def body(i, _):
            here = pl.ds(pl.multiple_of(base + i * step, 16), step)
            total = self.acc[k, here, :].astype(F32)
            for ref, index, first in sources:
                there = pl.ds(pl.multiple_of(first + i * step, 16), step)
                total = total + ref[index + (there,)].astype(F32)
            target[k, here, :] = total.astype(BF16)
            return 0

        lax.fori_loop(0, size // step, body, 0)

    def finish(self, k, p):
        w = lax.rem(k, self.window)
        rows = self.acc.at[k, pl.ds(0, self.rows_of(p)), :]
        copy = pltpu.make_async_remote_copy(
            src_ref=rows, dst_ref=rows, send_sem=self.send_sem.at[w, p], recv_sem=self.recv_sem.at[w, p],
            device_id=other(*CORE), device_id_type=MESH,
        )
        copy.wait_send()
        copy.wait_recv()
        target = self.out if p == self.back - 1 else self.acc
        if p == 0:
            self.add(k, self.core_base, self.rows // 2, [(self.landing, (w,), 0)], target)
        elif p < self.back:
            for s in range(2):
                base, size = self.kept[s][min(p, self.levels - 1)]
                if p < self.levels - 1:
                    sources = [(self.landing, (w,), self.land(p) + s * size)]
                elif p < self.levels:
                    sources = [(self.landing, (w,), self.land(p) + (3 * s + i) * size) for i in range(3)]
                else:
                    sources = [(self.extra, (w, p - self.levels), s * size)]
                self.add(k, base, size, sources, target)

    def start(self, k, p):
        w = lax.rem(k, self.window)
        for source, target, device in self.copies(k, p):
            pltpu.make_async_remote_copy(
                src_ref=source, dst_ref=target, send_sem=self.send_sem.at[w, p], recv_sem=self.recv_sem.at[w, p],
                device_id=device, device_id_type=MESH,
            ).start()

    def advance(self, k, p):
        if p > 0:
            self.finish(k, p - 1)
        if p < self.phases:
            self.start(k, p)

    def state(self, k, p):
        rows = self.rows
        if p == 0:
            return [(self.acc, 0, rows)]
        if p == self.phases:
            return [(self.out, 0, rows)]
        level = min(p - 1, self.levels - 1) if p < self.back else self.phases - 1 - p
        spans = [(self.core_base, rows // 2)] if level == 0 else [self.kept[s][level] for s in range(2)]
        return [(self.acc if p < self.back else self.out, base, size) for base, size in spans]


def scratch(chunks, rows, window, seq):
    more = len([1 for i in range(12) if (8 << i) < seq])
    return [
        pltpu.VMEM((chunks, rows, LANES), BF16),
        pltpu.VMEM((chunks, rows, LANES), BF16),
        pltpu.VMEM((window, rows, LANES), BF16),
        pltpu.VMEM((window, max(more, 1), rows // 32, LANES), BF16),
        pltpu.SemaphoreType.DMA((window, 8 + more)),
        pltpu.SemaphoreType.DMA((window, 8 + more)),
    ]


def tail_kernel(
    rank, states, chunk, seq,
    dprelow_ref, select_ref, dpair_ref, step_weight_ref, normed_ref, upstream_ref, inputs_ref, scale_ref, hot_ref,
    gain_ref, dactive_first_ref, mixed_first_ref, select_weight_ref, halo_ref, lines_ref,
    dactive_ref, mixed_ref, front_ref, active_ref, select_tile_ref, conv_ref, front_weight_ref, gate_weight_ref,
    dgate_ref, gated_ref, out_weight_ref, handed,
    output_ref, dinputs_ref, front_sum, gate_rest, out_rest, embedding_sum, wide_sum, mixed_sum,
    dselect_scr, first_scr, after_scr, spread_scr, extended_scr, dnormed_scr, result_scr, misc_scr, gain_scr,
    acc, out, landing, extra, send_sem, recv_sem, load_sem, store_sem, first_send, first_recv,
):
    step = pl.program_id(0)
    rows, width = upstream_ref.shape
    across = width // LANES
    inner = dprelow_ref.shape[1]
    tiles, pairs = inner // LANES, inner // (2 * LANES)
    tall = 2 * LANES
    kernel = conv_ref.shape[0]
    halo = kernel - 1
    vocab = embedding_sum.shape[0]
    ex = Exchange(acc, out, landing, extra, send_sem, recv_sem, chunk, landing.shape[0], seq)
    early = begun(tiles, ex.phases)
    old = tiles - early
    embedding_at, wide_at, mixed_at = (old + pairs + i for i in range(3))
    count = old + pairs + 3
    place = lax.axis_index("seq")
    here_dp = lax.axis_index("dp")

    def add(scr, value):
        for b in range(across):
            scr[b] += value[:, b * LANES : (b + 1) * LANES]

    def put(scr, here, value):
        for b in range(across):
            scr[b, here, :] = value[:, b * LANES : (b + 1) * LANES]

    def take(scr, here):
        return jnp.concatenate([scr[b, here, :] for b in range(across)], axis=1)

    def first_copy():
        return pltpu.make_async_remote_copy(
            src_ref=first_scr, dst_ref=after_scr, send_sem=first_send, recv_sem=first_recv,
            device_id=(here_dp, lax.rem(place + seq - 1, seq)), device_id_type=MESH,
        )

    def greet():
        barrier = pltpu.get_barrier_semaphore()
        partners = ex.partners()
        for device in partners:
            pl.semaphore_signal(barrier, inc=1, device_id=device, device_id_type=MESH)
        for there, by in ((place > 0, -1), (place < seq - 1, 1)):

            @pl.when(there)
            def _():
                pl.semaphore_signal(barrier, inc=1, device_id=(here_dp, place + by), device_id_type=MESH)

        neighbours = 2 - (place == 0).astype(jnp.int32) - (place == seq - 1).astype(jnp.int32)
        pl.semaphore_wait(barrier, len(partners) + neighbours)

    def store(k):
        pair = (k + early) // 2

        @pl.when((k < old) & (lax.rem(k + early, 2) == 0))
        def _():
            store_lanes(out.at[k], gate_rest, pair - (early + 1) // 2, store_sem.at[k])

        @pl.when((k < old) & (lax.rem(k + early, 2) == 1))
        def _():
            store_rows(out.at[k], out_rest, pair - early // 2, store_sem.at[k])

        @pl.when((k >= old) & (k < embedding_at))
        def _():
            store_lanes(out.at[k], front_sum, k - old, store_sem.at[k])

        @pl.when(k == embedding_at)
        def _():
            for b in range(width // LANES):
                pltpu.make_async_copy(
                    out.at[k, pl.ds(b * vocab, vocab), :], embedding_sum.at[:, pl.ds(b * LANES, LANES)], store_sem.at[k]
                ).start()

        @pl.when(k == wide_at)
        def _():
            pltpu.make_async_copy(out.at[k], wide_sum, store_sem.at[k]).start()

        @pl.when(k == mixed_at)
        def _():
            pltpu.make_async_copy(out.at[k], mixed_sum, store_sem.at[k]).start()

    def old_turns(spot):
        for k, p, now in turns(ex.phases, tiles + step, spot):
            k = k - early

            @pl.when(now & (k >= 0) & (k < old))
            def _():
                if p > 0:

                    @pl.when(step > 0)
                    def _():
                        ex.finish(k, p - 1)

                if p < ex.phases:
                    ex.start(k, p)
                else:
                    store(k)

    def new_turns(turn):
        for p in range(ex.phases, -1, -1):
            k = old + turn - 2 * p

            @pl.when((k >= old) & (k < count))
            def _():
                ex.advance(k, p)
                if p == ex.phases:
                    store(k)

    @pl.when(step == 0)
    def _():
        sizes = []
        for k in range(old):
            sizes.append(0)
            for ref, base, size in ex.state(k, next_phase(k + early, tiles)):
                here = pl.ds(pl.multiple_of(base, 16), size)
                sizes[-1] += size
                pltpu.make_async_copy(handed.at[k, here, :], ref.at[k, here, :], load_sem.at[k]).start()
        greet()
        dlow = contract_cols(dprelow_ref[...], step_weight_ref[...])
        dselect_scr[...] = jnp.concatenate([dlow, dpair_ref[...]], axis=1).astype(BF16)
        some = jnp.dot(dselect_scr[: halo * SUB], select_weight_ref[...], preferred_element_type=F32)
        some = (dactive_first_ref[...] + some) * silu_slope(mixed_first_ref[...])
        for i in range(halo):
            first_scr[i : i + 1, :] = some[i * SUB : i * SUB + 1, :]
        first_scr[halo:, :] = jnp.zeros((SUB - halo, inner), F32)

        @pl.when(place > 0)
        def _():
            first_copy().start()

        dnormed_scr[...] = jnp.zeros_like(dnormed_scr)
        result_scr[...] = jnp.zeros_like(result_scr)
        misc_scr[...] = jnp.zeros_like(misc_scr)
        misc_scr[kernel + 1 : kernel + 3, :] = lines_ref[states : states + 2, :]
        acc[wide_at] = jnp.zeros_like(acc[wide_at])
        acc[mixed_at] = jnp.zeros_like(acc[mixed_at])
        for b in range(tiles):
            at = rank * tiles + b * states
            acc[mixed_at, at : at + states, :] = lines_ref[:states, b * LANES : (b + 1) * LANES].astype(BF16)
        for k in range(old):
            wait_rows(acc.at[k, pl.ds(0, sizes[k]), :], load_sem.at[k])

    old_turns(0)

    @pl.when(step < pairs)
    def _():
        add(result_scr, jnp.dot(gated_ref[...], out_weight_ref[...], preferred_element_type=F32))
        add(dnormed_scr, contract_cols(dgate_ref[...], gate_weight_ref[...]))

    old_turns(1)

    @pl.when(step < pairs)
    def _():
        lanes = pl.ds(pl.multiple_of(step * tall, tall), tall)
        mixed = mixed_ref[...]
        back = jnp.dot(dselect_scr[...], select_tile_ref[...], preferred_element_type=F32)
        dmixed = (dactive_ref[...] + back) * silu_slope(mixed)
        spread_scr[:rows] = dmixed
        extended_scr[: halo * SUB] = halo_ref[...].astype(F32)
        extended_scr[halo * SUB :] = front_ref[...].astype(F32)
        misc_scr[kernel : kernel + 1, lanes] = jnp.sum(dmixed, axis=0, keepdims=True)
        for i in range(kernel):
            misc_scr[i : i + 1, lanes] = jnp.sum(
                dmixed * extended_scr[i * SUB : i * SUB + rows], axis=0, keepdims=True
            )
        wide = contract_rows(dselect_scr[...], active_ref[...]).astype(BF16)
        columns = wide.shape[0]
        for side in range(2):
            at = pl.ds(pl.multiple_of((2 * step + side) * columns, columns), columns)
            acc[wide_at, at, :] = wide[:, side * LANES : (side + 1) * LANES]
        part = contract_rows(select_ref[:, :rank], dprelow_ref[:, lanes]).astype(BF16)
        for side in range(2):
            at = pl.ds(pl.multiple_of((2 * step + side) * rank, rank), rank)
            acc[mixed_at, at, :] = part[:, side * LANES : (side + 1) * LANES]

        @pl.when(step == 0)
        def _():
            @pl.when(place > 0)
            def _():
                first_copy().wait_send()

            @pl.when(place < seq - 1)
            def _():
                first_copy().wait_recv()

            @pl.when(place == seq - 1)
            def _():
                after_scr[...] = jnp.zeros_like(after_scr)

        sub = lax.broadcasted_iota(jnp.int32, (SUB, tall), 0)
        for i in range(halo):
            own = pltpu.roll(spread_scr[i * SUB : (i + 1) * SUB, :], SUB - 1, 0)
            spread_scr[rows + i * SUB : rows + (i + 1) * SUB] = jnp.where(
                sub < SUB - 1, own, after_scr[i : i + 1, lanes]
            )
        dfront = conv_ref[halo : halo + 1] * spread_scr[:rows]
        for i in range(1, kernel):
            dfront = dfront + conv_ref[halo - i : halo - i + 1] * spread_scr[i * SUB : i * SUB + rows]
        dfront = dfront.astype(BF16)
        part = jnp.dot(normed_ref[...], dfront, preferred_element_type=F32).astype(BF16)
        acc[old + step, :width, :] = part[:, :LANES]
        acc[old + step, width:, :] = part[:, LANES:]
        add(dnormed_scr, contract_cols(dfront, front_weight_ref[...]))

    @pl.when(step == pairs)
    def _():
        part = rows // SUB

        def norms(i, total):
            here = pl.ds(pl.multiple_of(i * part, part), part)
            dnormed, inputs, scale = take(dnormed_scr, here), inputs_ref[here, :], scale_ref[here, :]
            scaled = gain_ref[...] * dnormed
            mean = jnp.sum(scaled * inputs, axis=1, keepdims=True) * (1.0 / width)
            put(
                dnormed_scr, here,
                upstream_ref[here, :].astype(F32) + scale * scaled - inputs * (scale * scale * scale * mean),
            )
            put(result_scr, here, take(result_scr, here) + inputs)
            return total + jnp.sum((dnormed * inputs * scale).reshape(-1, SUB, width), axis=0)

        total = lax.fori_loop(0, SUB, norms, jnp.zeros((SUB, width), F32))
        gain_scr[...] = jnp.sum(total, axis=0, keepdims=True)
        for b in range(width // tall):
            value = jnp.concatenate([dnormed_scr[2 * b], dnormed_scr[2 * b + 1]], axis=1)
            high = value.astype(BF16)
            low = (value - high.astype(F32)).astype(BF16)
            whole = jnp.dot(hot_ref[...], high, preferred_element_type=F32)
            whole = (whole + jnp.dot(hot_ref[...], low, preferred_element_type=F32)).astype(BF16)
            for side in range(2):
                at = (2 * b + side) * vocab
                acc[embedding_at, at : at + vocab, :] = whole[:, side * LANES : (side + 1) * LANES]
        at = (rank + states) * tiles
        for b in range(tiles):
            acc[mixed_at, at + b * 16 : at + (b + 1) * 16, :] = misc_scr[:, b * LANES : (b + 1) * LANES].astype(BF16)
        at = (rank + states + 16) * tiles
        for b in range(width // LANES):
            acc[mixed_at, at + b * 16 : at + (b + 1) * 16, :] = jnp.broadcast_to(
                gain_scr[:, b * LANES : (b + 1) * LANES], (16, LANES)
            ).astype(BF16)

    @pl.when(step == pairs + 1)
    def _():
        span = rows // SUB
        for i in range(SUB):
            for b in range(across):
                lanes, every = slice(b * LANES, (b + 1) * LANES), pl.ds(i, span, stride=SUB)
                dinputs_ref[i * span : (i + 1) * span, lanes] = dnormed_scr[b, every, :]
                output_ref[i * span : (i + 1) * span, lanes] = result_scr[b, every, :].astype(BF16)

    new_turns(step)

    @pl.when(step == pl.num_programs(0) - 1)
    def _():
        def rest(turn, _):
            new_turns(turn)
            return 0

        lax.fori_loop(pairs + 3, pairs + 3 + 2 * ex.phases, rest, 0)
        for k in range(count):
            wait_rows(out.at[k], store_sem.at[k])


def run_tail(
    d_pre_low, select, d_pair, step_weight, normed, upstream, inputs, scale, ids, gain, d_active, mixed, select_weight,
    halo, lines, front, active, conv_weight, input_weight, d_gate, gated, output_weight, handed, vocab, seq,
):
    rows, inner = front.shape
    width = inputs.shape[1]
    rank, states = step_weight.shape[0], lines.shape[0] - SUB
    chunk = 2 * width
    tiles, pairs, tall = inner // LANES, inner // (2 * LANES), 2 * LANES
    phases = 8 + max(seq.bit_length() - 4, 0)
    early = begun(tiles, phases)
    count = tiles - early + pairs + 3
    some = halo.shape[0]
    at = lambda i: lax.min(i, pairs - 1)
    whole = lambda a: pl.BlockSpec(a.shape, lambda i: (0, 0), pipeline_mode=pl.Buffered(1))
    first = pl.BlockSpec((some, inner), lambda i: (0, 0), pipeline_mode=pl.Buffered(1))
    tile = lambda height: pl.BlockSpec((height, tall), lambda i: (0, at(i)))
    high = lambda wide: pl.BlockSpec((tall, wide), lambda i: (at(i), 0))
    hbm = pl.BlockSpec(memory_space=pltpu.HBM)
    fixed = pl.BlockSpec((rows, width), lambda i: (0, 0))
    gates, outs = inner - (early + 1) // 2 * tall, inner - early // 2 * tall
    return pl.pallas_call(
        functools.partial(tail_kernel, rank, states, chunk, seq),
        grid=(pairs + 3,),
        in_specs=[
            whole(d_pre_low), whole(select), whole(d_pair), whole(step_weight), whole(normed), whole(upstream),
            whole(inputs), whole(scale), whole(ids), whole(gain), first, first, whole(select_weight), tile(some),
            whole(lines), tile(rows), tile(rows), tile(rows), tile(rows),
            tile(select_weight.shape[0]), tile(conv_weight.shape[0]), tile(width),
            pl.BlockSpec((width, tall), lambda i: (0, at(i) + pairs)), tile(rows), tile(rows), high(width), hbm,
        ],
        out_specs=[fixed, fixed, hbm, hbm, hbm, hbm, hbm, hbm],
        out_shape=[
            jax.ShapeDtypeStruct((rows, width), BF16),
            jax.ShapeDtypeStruct((rows, width), F32),
            jax.ShapeDtypeStruct((width, inner), BF16),
            jax.ShapeDtypeStruct((width, gates), BF16),
            jax.ShapeDtypeStruct((outs, width), BF16),
            jax.ShapeDtypeStruct((vocab, width), BF16),
            jax.ShapeDtypeStruct((chunk, LANES), BF16),
            jax.ShapeDtypeStruct((chunk, LANES), BF16),
        ],
        scratch_shapes=[
            pltpu.VMEM(select.shape, BF16),
            pltpu.VMEM((SUB, inner), F32), pltpu.VMEM((SUB, inner), F32),
            pltpu.VMEM((rows + some, tall), F32), pltpu.VMEM((rows + some, tall), F32),
            pltpu.VMEM((width // LANES, rows, LANES), F32), pltpu.VMEM((width // LANES, rows, LANES), F32),
            pltpu.VMEM((16, inner), F32), pltpu.VMEM((1, width), F32),
        ]
        + scratch(count, chunk, 8, seq)
        + [
            pltpu.SemaphoreType.DMA((count,)), pltpu.SemaphoreType.DMA((count,)),
            pltpu.SemaphoreType.DMA, pltpu.SemaphoreType.DMA,
        ],
        compiler_params=pltpu.CompilerParams(
            collective_id=2, has_side_effects=True, vmem_limit_bytes=62 << 20
        ),
        name="span_tail",
    )(
        d_pre_low, select, d_pair, step_weight, normed, upstream, inputs, scale, ids, gain, d_active, mixed,
        select_weight, halo, lines, d_active, mixed, front, active, select_weight, conv_weight,
        input_weight, input_weight, d_gate, gated, output_weight, handed,
    )


def widen_kernel(
    rank, states, columns, outs,
    front_ref, gate_ref, gate_rest_ref, out_ref, out_rest_ref, embedding_ref, wide_ref, mixed_ref,
    input_to, output_to, embedding_to, select_to, step_to, decay_to, conv_to, gain_to, *line_to,
):
    step = pl.program_id(0)
    inner, gates = front_ref.shape[1], gate_ref.shape[1]
    input_to[:, :inner] = front_ref[...].astype(F32)
    input_to[:, inner : inner + gates] = gate_ref[...].astype(F32)
    input_to[:, inner + gates :] = gate_rest_ref[...].astype(F32)

    @pl.when(step < outs)
    def _():
        output_to[...] = out_ref[...].astype(F32)

    @pl.when(step >= outs)
    def _():
        output_to[...] = out_rest_ref[...].astype(F32)

    embedding_to[...] = embedding_ref[...].astype(F32)

    @pl.when(step == 0)
    def _():
        for source, whole in (
            (wide_ref, ((select_to, columns),)),
            (mixed_ref, ((step_to, rank), (decay_to, states), (conv_to, 16), (gain_to, 16))),
        ):
            at = 0
            for to, height in whole:
                for b in range(to.shape[1] // LANES):
                    part = source[at : at + height, :].astype(F32)
                    lanes = slice(b * LANES, (b + 1) * LANES)
                    to[:, lanes] = part[: to.shape[0]]
                    if to is conv_to:
                        for i, line in enumerate(line_to):
                            line[:, lanes] = part[to.shape[0] + i : to.shape[0] + i + 1]
                    at += height


def run_widen(front, gate, gate_rest, out, out_rest, embedding, wide, mixed, rank, states, columns, kernel):
    width, inner = front.shape
    tall = 2 * LANES
    tiles, outs = inner // tall, out.shape[0] // tall
    vocab = embedding.shape[0]
    lines = lambda a: pl.BlockSpec((width // tiles, a.shape[1]), lambda i: (i, 0))
    thin = pl.BlockSpec((vocab // tiles, width), lambda i: (i, 0))
    fixed = lambda shape: pl.BlockSpec(shape, lambda i: (0, 0))
    shapes = [
        (width, 2 * inner), (inner, width), (vocab, width), (columns, inner), (rank, inner), (states, inner), (kernel, inner),
        (1, width), (1, inner), (1, inner), (1, inner),
    ]
    return pl.pallas_call(
        functools.partial(widen_kernel, rank, states, columns, outs),
        grid=(tiles,),
        in_specs=[
            lines(front), lines(gate), lines(gate_rest),
            pl.BlockSpec((tall, width), lambda i: (lax.min(i, outs - 1), 0)),
            pl.BlockSpec((tall, width), lambda i: (lax.max(i - outs, 0), 0)),
            thin, fixed(wide.shape), fixed(mixed.shape),
        ],
        out_specs=[
            pl.BlockSpec((width // tiles, 2 * inner), lambda i: (i, 0)),
            pl.BlockSpec((tall, width), lambda i: (i, 0)), thin,
        ]
        + [fixed(shape) for shape in shapes[3:]],
        out_shape=[jax.ShapeDtypeStruct(shape, F32) for shape in shapes],
        compiler_params=pltpu.CompilerParams(vmem_limit_bytes=62 << 20),
        name="sums_to_float32",
    )(front, gate, gate_rest, out, out_rest, embedding, wide, mixed)


def on_device(
    byte_ids,
    embedding,
    cotangent,
    norm_gain,
    input_projection_weight,
    conv_weight,
    conv_bias,
    select_weight,
    step_weight,
    step_bias,
    decay_log,
    skip_gain,
    output_projection_weight,
):
    count, stretch = byte_ids.shape
    vocab, width = embedding.shape
    kernel, inner = conv_weight.shape
    states = decay_log.shape[0]
    rank = step_weight.shape[0]
    rows = count * stretch
    seq = lax.axis_size("seq")
    gain, turned_select = norm_gain.reshape(1, width), select_weight.T
    (
        block_inputs, scale, unused, turned, upstream, hot, front, earlier, mixed, active, gate, graded, select
    ) = run_front(
        byte_ids.reshape(1, rows), embedding, cotangent.reshape(rows, width), gain, input_projection_weight,
        output_projection_weight, conv_weight, conv_bias.reshape(1, inner), turned_select, seq,
    )
    (
        gated, d_gate, d_pre_low, d_active, lines, d_pair, gate_sum, out_sum, handed
    ) = run_scan(
        active, gate, graded, select, step_weight, step_bias.reshape(1, inner), decay_log, skip_gain.reshape(1, inner),
        turned, upstream, seq,
    )
    output, d_inputs, front_sum, gate_rest, out_rest, embedding_sum, wide_sum, mixed_sum = run_tail(
        d_pre_low, select, d_pair, step_weight, turned, upstream, block_inputs, scale, hot, gain,
        d_active, mixed, turned_select, earlier, lines, front, active, conv_weight,
        input_projection_weight, d_gate, gated, output_projection_weight, handed, vocab, seq,
    )
    (
        d_input_weight, d_output_weight, d_embedding, d_select_weight, d_step_weight, d_decay_log, d_conv_weight,
        d_norm_gain, d_conv_bias, d_step_bias, d_skip_gain,
    ) = run_widen(
        front_sum, gate_sum, gate_rest, out_sum, out_rest, embedding_sum, wide_sum, mixed_sum, rank, states,
        select_weight.shape[1], kernel,
    )
    return (
        output.reshape(count, stretch, width),
        d_inputs.reshape(count, stretch, width),
        d_embedding,
        d_norm_gain[0],
        d_input_weight,
        d_conv_weight,
        d_conv_bias[0],
        d_select_weight.T,
        d_step_weight,
        d_step_bias[0],
        d_decay_log,
        d_skip_gain[0],
        d_output_weight,
    )


def solution(mesh):
    placed = (P("dp", "seq"), P(), P("dp", "seq", None)) + (P(),) * 10
    return jax.shard_map(
        on_device,
        mesh=mesh,
        in_specs=placed,
        out_specs=(P("dp", "seq", None), P("dp", "seq", None)) + (P(),) * 11,
        check_vma=False,
    )
```

```python
import functools
import math

import jax
import jax.numpy as jnp
from jax import lax
from jax.experimental import pallas as pl
from jax.experimental.pallas import tpu as pltpu
from jax.sharding import PartitionSpec as P

EPS = 1e-05
LANES = 128
SUB = 8
LOG2E = math.log2(math.e)
LN2 = math.log(2.0)
F32 = jnp.float32
BF16 = jnp.bfloat16
MESH = pl.DeviceIdType.MESH


def silu_slope(value):
    sigma = jax.nn.sigmoid(value)
    return sigma * (1.0 + value * (1.0 - sigma))


def contract_rows(left, right):
    return lax.dot_general(
        left, right, (((0,), (0,)), ((), ())), preferred_element_type=F32
    )


def contract_cols(left, right):
    return lax.dot_general(
        left, right, (((1,), (1,)), ((), ())), preferred_element_type=F32
    )


def sublane(shape):
    return lax.broadcasted_iota(jnp.int32, shape, len(shape) - 2)


def shift_up(value, by, fill, reverse):
    place = sublane(value.shape)
    if reverse:
        moved = pltpu.roll(value, SUB - by, value.ndim - 2)
        return jnp.where(place < SUB - by, moved, fill)
    moved = pltpu.roll(value, by, value.ndim - 2)
    return jnp.where(place >= by, moved, fill)


def expand_columns(select, first, states):
    width = select.shape[1]
    shape = (width, states * LANES)
    source = lax.broadcasted_iota(jnp.int32, shape, 0)
    target = lax.broadcasted_iota(jnp.int32, shape, 1) // LANES + first
    spread = (source == target).astype(F32).astype(BF16)
    return jnp.dot(select, spread, preferred_element_type=F32)


def tree_sum(value):
    while value.shape[0] > 1:
        half = value.shape[0] // 2
        value = value[:half] + value[half:]
    return value[0]


def front_kernel(
    seq,
    ids_ref, embedding_ref, cotangent_ref, gain_ref, front_weight_ref, gate_weight_ref, out_weight_ref, conv_ref,
    conv_bias_ref, select_weight_ref,
    inputs_ref, scale_ref, normed_ref, turned_ref, upstream_ref, hot_ref, front_ref, halo_ref, mixed_ref, active_ref,
    gate_ref, graded_ref, select_ref,
    last_scr, extended_scr, total_scr, send_sem, recv_sem,
):
    step = pl.program_id(0)
    rows, width = upstream_ref.shape
    span = rows // SUB
    vocab = embedding_ref.shape[0]
    kernel = conv_ref.shape[0]
    halo = kernel - 1
    place = lax.axis_index("seq")

    def there(by):
        return (lax.axis_index("dp"), place + by)

    def copy():
        return pltpu.make_async_remote_copy(
            src_ref=ids_ref.at[:, pl.ds(rows - LANES, LANES)], dst_ref=last_scr, send_sem=send_sem, recv_sem=recv_sem,
            device_id=there(1), device_id_type=MESH,
        )

    def norm(inputs):
        scale = lax.rsqrt(jnp.sum(inputs * inputs, axis=1, keepdims=True) * (1.0 / width) + EPS)
        return scale, (inputs * scale * gain_ref[...]).astype(BF16)

    def hot_of(ids):
        shape = (vocab, ids.shape[1])
        return (lax.broadcasted_iota(jnp.int32, shape, 0) == ids).astype(F32).astype(BF16)

    @pl.when(step == 0)
    def _():
        barrier = pltpu.get_barrier_semaphore()

        @pl.when(place > 0)
        def _():
            pl.semaphore_signal(barrier, inc=1, device_id=there(-1), device_id_type=MESH)

        @pl.when(place == 0)
        def _():
            last_scr[...] = jnp.full(last_scr.shape, -1, jnp.int32)

        row = lax.broadcasted_iota(jnp.int32, (rows, rows), 0)
        position = lax.broadcasted_iota(jnp.int32, (rows, rows), 1)
        order = (lax.rem(row, SUB) * span + row // SUB == position).astype(F32).astype(BF16)
        upstream_ref[...] = jnp.dot(order, cotangent_ref[...], preferred_element_type=F32).astype(BF16)

        @pl.when(place < seq - 1)
        def _():
            pl.semaphore_wait(barrier, 1)
            copy().start()

        hot = contract_cols(hot_of(ids_ref[...]), order).astype(BF16)
        hot_ref[...] = hot
        inputs = contract_rows(hot, embedding_ref[...])
        inputs_ref[...] = inputs
        scale, normed = norm(inputs)
        scale_ref[...] = scale
        normed_ref[:rows] = normed
        turned_ref[...] = normed.T

        @pl.when(place < seq - 1)
        def _():
            copy().wait_send()

        @pl.when(place > 0)
        def _():
            copy().wait_recv()

        last = contract_rows(hot_of(last_scr[...]), embedding_ref[...])[LANES - 16 :]
        normed_ref[rows:] = norm(last)[1]
        total_scr[...] = jnp.zeros_like(total_scr)

    both = jnp.dot(normed_ref[...], front_weight_ref[...], preferred_element_type=F32).astype(BF16)
    front_ref[...] = both[:rows]
    both = both.astype(F32)
    extended_scr[halo * SUB :] = both[:rows]
    sub = lax.broadcasted_iota(jnp.int32, (SUB, both.shape[1]), 0)
    for i in range(halo):
        own = pltpu.roll(both[rows - (halo - i) * SUB : rows - (halo - i - 1) * SUB], 1, 0)
        before = both[rows + 16 - halo + i : rows + 16 - halo + i + 1]
        extended_scr[i * SUB : (i + 1) * SUB] = jnp.where(sub > 0, own, before)
    halo_ref[...] = extended_scr[: halo * SUB].astype(BF16)
    mixed = conv_bias_ref[...] + conv_ref[0:1] * extended_scr[:rows]
    for i in range(1, kernel):
        mixed = mixed + conv_ref[i : i + 1] * extended_scr[i * SUB : i * SUB + rows]
    mixed_ref[...] = mixed
    active = jax.nn.silu(mixed).astype(BF16)
    active_ref[...] = active
    gate_ref[...] = jnp.dot(normed_ref[:rows], gate_weight_ref[...], preferred_element_type=F32).astype(BF16)
    graded_ref[...] = contract_cols(upstream_ref[...], out_weight_ref[...])
    total_scr[...] += contract_cols(active, select_weight_ref[...])

    @pl.when(step == pl.num_programs(0) - 1)
    def _():
        select_ref[...] = total_scr[...].astype(BF16)


def run_front(
    ids, embedding, cotangent, gain, input_weight, output_weight, conv_weight, conv_bias, select_weight, seq
):
    rows, width = cotangent.shape
    inner = output_weight.shape[0]
    vocab, kernel, columns = embedding.shape[0], conv_weight.shape[0], select_weight.shape[0]
    halo = (kernel - 1) * SUB
    tall = 2 * LANES
    pairs = inner // tall
    whole = lambda a: pl.BlockSpec(a.shape, lambda i: (0, 0), pipeline_mode=pl.Buffered(1))
    tile = lambda height: pl.BlockSpec((height, tall), lambda i: (0, i))
    fixed = lambda shape: pl.BlockSpec(shape, lambda i: (0, 0))
    outs = [
        ((rows, width), F32, None), ((rows, 1), F32, None), ((rows + 16, width), BF16, None),
        ((width, rows), BF16, None), ((rows, width), BF16, None), ((vocab, rows), BF16, None),
        ((rows, inner), BF16, rows), ((halo, inner), BF16, halo), ((rows, inner), F32, rows), ((rows, inner), BF16, rows),
        ((rows, inner), BF16, rows), ((rows, inner), F32, rows), ((rows, columns), BF16, None),
    ]
    return pl.pallas_call(
        functools.partial(front_kernel, seq),
        grid=(pairs,),
        in_specs=[
            whole(ids), whole(embedding), whole(cotangent), whole(gain), tile(width),
            pl.BlockSpec((width, tall), lambda i: (0, i + pairs)), pl.BlockSpec((tall, width), lambda i: (i, 0)),
            tile(kernel), tile(1), tile(columns),
        ],
        out_specs=[fixed(shape) if height is None else tile(height) for shape, kind, height in outs],
        out_shape=[jax.ShapeDtypeStruct(shape, kind) for shape, kind, height in outs],
        scratch_shapes=[
            pltpu.VMEM((1, LANES), jnp.int32), pltpu.VMEM((rows + halo, tall), F32), pltpu.VMEM((rows, columns), F32),
            pltpu.SemaphoreType.DMA, pltpu.SemaphoreType.DMA,
        ],
        compiler_params=pltpu.CompilerParams(
            collective_id=3, has_side_effects=True, vmem_limit_bytes=62 << 20
        ),
        name="span_front",
    )(
        ids, embedding, cotangent, gain, input_weight, input_weight, output_weight, conv_weight, conv_bias, select_weight
    )


def slot_of(k, p):
    return 2 * k + 3 - k % 2 + 2 * p


def turns(phases, tile, place):
    for p in range(phases, -1, -1):
        k = tile - 1 - p
        yield k, p, (k >= 0) & (lax.rem(k + 2 * phases, 2) == 1 - place)


def begun(tiles, p):
    return sum(slot_of(k, p) < 2 * tiles for k in range(tiles))


def next_phase(k, tiles):
    return next(p for p in range(1000) if slot_of(k, p) >= 2 * tiles)


class Prefix:
    def __init__(self, totals, landing, start, incoming, gaps, rates, send_sem, recv_sem, rounds):
        self.totals, self.landing, self.start, self.incoming, self.gaps = totals, landing, start, incoming, gaps
        self.rates, self.send_sem, self.recv_sem, self.rounds = rates, send_sem, recv_sem, rounds

    def copy(self, e, r):
        return pltpu.make_async_remote_copy(
            src_ref=self.totals.at[e], dst_ref=self.landing.at[e, r],
            send_sem=self.send_sem.at[e, r], recv_sem=self.recv_sem.at[e, r],
            device_id=other("seq", 1 << r), device_id_type=MESH,
        )

    def advance(self, e, r):
        if r > 0:
            self.copy(e, r - 1).wait()
            self.merge(e, r - 1)
        if r < self.rounds:
            self.copy(e, r).start()

    def merge(self, e, r):
        n = self.rates.shape[1]
        rates = self.rates[e]
        later = bit_of(lax.axis_index("seq"), 1 << r) == 1
        end, message, total = self.totals[e, :n], self.totals[e, n : 2 * n], self.totals[e, 2 * n : 2 * n + 1]
        end2, message2 = self.landing[e, r, :n], self.landing[e, r, n : 2 * n]
        total2 = self.landing[e, r, 2 * n : 2 * n + 1]

        @pl.when(later)
        def _():
            gap = self.gaps[e, 0:1]
            self.start[e] = self.start[e] + jnp.exp2(gap * rates) * end2
            self.gaps[e, 0:1] = gap + total2

        @pl.when(jnp.logical_not(later))
        def _():
            gap = self.gaps[e, 1:2]
            self.incoming[e] = self.incoming[e] + jnp.exp2(gap * rates) * message2
            self.gaps[e, 1:2] = gap + total2

        if r < self.rounds - 1:
            reach, reach2 = jnp.exp2(total * rates), jnp.exp2(total2 * rates)
            self.totals[e, :n] = jnp.where(later, end + reach * end2, end2 + reach2 * end)
            self.totals[e, n : 2 * n] = jnp.where(later, message2 + reach2 * message, message + reach * message2)
            self.totals[e, 2 * n : 2 * n + 1] = total + total2


def scan_kernel(
    rank, states, chunk, rounds, seq,
    active_now, gate_now, graded_now, select_ref, step_weight_ref, step_bias_ref, decay_ref, skip_ref, normed_hbm, upstream_hbm,
    gated_ref, dgate_ref, dprelow_ref, dactive_ref, lines_ref, dselect_ref,
    gate_sum, out_sum, handed,
    inject_scr, readout_scr, dread_scr, dinject_scr, state_scr, factor_scr,
    rates_scr, rate_scr, delta_ring, drive_ring, grad_ring, silu_ring, sway_ring, active_ring, slope_ring, scan_scr, weight_scr,
    ahead_scr, behind_scr, sums_scr, gated_scr, dgated_scr,
    totals, totals_in, start_scr, incoming_scr, gaps_scr, prefix_send, prefix_recv,
    normed_ref, upstream_ref, late_sem,
    acc, out, landing, extra, send_sem, recv_sem, store_sem,
):
    rows = active_now.shape[0]
    steps = rows // SUB
    step = pl.program_id(0)
    count = rates_scr.shape[0]
    lag = delta_ring.shape[0]
    per = -(-rounds // (lag - 1))
    width = upstream_ref.shape[1]
    prefix = Prefix(
        totals, totals_in, start_scr, incoming_scr, gaps_scr, rates_scr, prefix_send, prefix_recv, rounds
    )
    ex = Exchange(acc, out, landing, extra, send_sem, recv_sem, chunk, landing.shape[0], seq)
    early = begun(count, ex.phases)
    half, unroll = states // 2, 8
    halves = [pl.ds(0, half), pl.ds(half, half)]

    def store(k):
        pair = k // 2

        @pl.when(lax.rem(k, 2) == 0)
        def _():
            store_lanes(out.at[k], gate_sum, pair, store_sem.at[k])

        @pl.when(lax.rem(k, 2) == 1)
        def _():
            store_rows(out.at[k], out_sum, pair, store_sem.at[k])

    def take_turns(place):
        for k, p, now in turns(ex.phases, step - lag, place):

            @pl.when(now)
            def _():
                ex.advance(k, p)
                if p == ex.phases:
                    store(k)

    late_loads = [
        pltpu.make_async_copy(source, target, late_sem.at[i])
        for i, (source, target) in enumerate(((normed_hbm, normed_ref), (upstream_hbm, upstream_ref)))
    ]

    @pl.when(step == 0)
    def _():
        ex.greet()
        for copy in late_loads:
            copy.start()
        for first, scr in ((rank, inject_scr), (rank + states, readout_scr)):
            for n in range(0, states, 2):
                wide = expand_columns(select_ref[...], first + n, 2)
                for side in range(2):
                    scr[:, n + side] = wide[:, side * LANES : (side + 1) * LANES].reshape(steps, SUB, LANES)
        dread_scr[...] = jnp.zeros_like(dread_scr)
        dinject_scr[...] = jnp.zeros_like(dinject_scr)
        start_scr[...] = jnp.zeros_like(start_scr)
        incoming_scr[...] = jnp.zeros_like(incoming_scr)
        gaps_scr[...] = jnp.zeros_like(gaps_scr)
        for e in range(count):
            rates_scr[e] = -jnp.exp(decay_ref[:, e * LANES : (e + 1) * LANES]) * LOG2E
        for copy in late_loads:
            copy.wait()
        ex.welcome()

    flat = lambda value: value.reshape(steps, SUB, LANES)
    zero = jnp.zeros((half, SUB, LANES), F32)

    def spread_rates(tile):
        rates = rates_scr[tile]
        for n in range(states):
            rate_scr[n] = jnp.broadcast_to(rates[n : n + 1], (SUB, LANES))

    def spread(table):
        return jnp.concatenate(
            [jnp.broadcast_to(table[n : n + 1], (1, SUB, LANES)) for n in range(states)], axis=0
        )

    @pl.when(step >= lag)
    def _():
        c = step - lag
        tile = c
        spread_rates(tile)
        slot = lax.rem(c, lag)
        delta_scr, drive_scr, grad_scr = delta_ring.at[slot], drive_ring.at[slot], grad_ring.at[slot]
        total = sums_scr[tile]
        before, after = total, total
        for by in (1, 2, 4):
            before = before + shift_up(before, by, 0.0, False)
            after = after + shift_up(after, by, 0.0, True)
        before, after = before - total, after - total
        state_scr[0] = ahead_scr[tile] + jnp.exp2(before[None] * rate_scr[...]) * spread(start_scr[tile])

        def forward(i, state):
            for u in range(unroll // 2):
                j = i * (unroll // 2) + u
                factor = jnp.exp2(delta_scr[j][None] * rate_scr[...])
                factor_scr[j] = factor
                state = factor * state + drive_scr[j][None] * inject_scr[j]
                state_scr[j + 1] = state
                dread_scr[j] += grad_scr[j][None] * state
                scan_scr[j] = tree_sum(readout_scr[j] * state)
            return state

        lax.fori_loop(0, steps // (unroll // 2), forward, state_scr[0])
        take_turns(0)
        lanes = pl.ds(pl.multiple_of(c * LANES, LANES), LANES)
        skip = skip_ref[:, lanes]
        active = active_ring[slot].reshape(rows, LANES)
        scanned = scan_scr[...].reshape(rows, LANES) + skip * active
        gated = (scanned * silu_ring[slot].reshape(rows, LANES)).astype(BF16)
        gated_ref[...] = gated
        dgate = (scanned * sway_ring[slot].reshape(rows, LANES)).astype(BF16)
        dgate_ref[...] = dgate
        lines_ref[states + 1 : states + 2, :] = jnp.sum(
            grad_scr[...].reshape(rows, LANES) * active, axis=0, keepdims=True
        )
        odd = lax.rem(c, 2)

        @pl.when(odd == 0)
        def _():
            gated_scr[:, :LANES] = gated
            dgated_scr[:, :LANES] = dgate

        @pl.when(odd == 1)
        def _():
            gated_scr[:, LANES:] = gated
            dgated_scr[:, LANES:] = dgate

        adjoint0 = behind_scr[tile] + jnp.exp2(after[None] * rate_scr[...]) * spread(incoming_scr[tile])
        state_scr[steps] = adjoint0
        for h, part in enumerate(halves):

            def backward(i, carry):
                adjoint, total = carry
                for u in range(unroll):
                    j = steps - 1 - (i * unroll + u)
                    d, g = delta_scr[j], grad_scr[j]
                    whole = adjoint + g[None] * readout_scr[j, part]
                    adjoint = factor_scr[j, part] * whole
                    through = adjoint * state_scr[j, part]
                    total = total + through * d[None]
                    dinject_scr[j, part] += whole * drive_scr[j][None]
                    one = tree_sum(through * rate_scr[part])
                    two = tree_sum(whole * inject_scr[j, part])
                    scan_scr[j] = scan_scr[j] + one if h else one
                    weight_scr[j] = weight_scr[j] + two if h else two
                return adjoint, total

            unused, total = lax.fori_loop(0, steps // unroll, backward, (state_scr[steps, part], zero))
            for n in range(half):
                at = h * half + n
                lines_ref[at : at + 1, :] = (
                    jnp.sum(total[n], axis=0, keepdims=True) * rate_scr[at, 0:1] * LN2
                )
        weight = weight_scr[...].reshape(rows, LANES)
        delta = delta_scr[...].reshape(rows, LANES)
        active = active_ring[slot].reshape(rows, LANES)
        dactive_ref[...] = delta * weight + skip_ref[:, lanes] * grad_scr[...].reshape(rows, LANES)
        dpre = (scan_scr[...].reshape(rows, LANES) * LN2 + active * weight) * slope_ring[slot].reshape(rows, LANES)
        dprelow_ref[...] = dpre.astype(BF16)
        lines_ref[states : states + 1, :] = jnp.sum(dpre, axis=0, keepdims=True)

        @pl.when(odd == 1)
        def _():
            pair = c // 2
            part = jnp.dot(normed_ref[...], dgated_scr[...], preferred_element_type=F32).astype(BF16)
            acc[2 * pair, :width, :] = part[:, :LANES]
            acc[2 * pair, width:, :] = part[:, LANES:]
            turned = gated_scr[...].T
            for b in range(width // (2 * LANES)):
                part = jnp.dot(
                    turned, upstream_ref[:, b * 2 * LANES : (b + 1) * 2 * LANES], preferred_element_type=F32
                ).astype(BF16)
                for side in range(2):
                    at = (2 * b + side) * 2 * LANES
                    acc[2 * pair + 1, at : at + 2 * LANES, :] = part[:, side * LANES : (side + 1) * LANES]

        take_turns(1)

    @pl.when(step < count)
    def _():
        tile = step
        spread_rates(tile)
        slot = lax.rem(step, lag)
        delta_scr, drive_scr, grad_scr = delta_ring.at[slot], drive_ring.at[slot], grad_ring.at[slot]
        lanes = pl.ds(pl.multiple_of(tile * LANES, LANES), LANES)
        pre = jnp.dot(select_ref[:, :rank], step_weight_ref[:, lanes], preferred_element_type=F32)
        pre = pre + step_bias_ref[:, lanes]
        small = jnp.exp(-jnp.abs(pre))
        delta = jnp.maximum(pre, 0.0) + jnp.log1p(small)
        slope_ring[slot] = flat(jnp.where(pre >= 0.0, 1.0, small) / (1.0 + small))
        delta_scr[...] = flat(delta)
        active = active_now[...].astype(F32)
        active_ring[slot] = flat(active)
        drive_scr[...] = flat(delta * active)
        gate = gate_now[...].astype(F32)
        sigma = jax.nn.sigmoid(gate)
        silu = gate * sigma
        silu_ring[slot] = flat(silu)
        graded = graded_now[...]
        grad_scr[...] = flat(graded * silu)
        sway_ring[slot] = flat(graded * (sigma * (1.0 + gate * (1.0 - sigma))))
        total = jnp.sum(delta_scr[...], axis=0)
        sums_scr[tile] = total
        whole = jnp.sum(total, axis=0, keepdims=True)
        totals[tile, 2 * states :] = jnp.broadcast_to(whole, (SUB, LANES))
        for h, part in enumerate(halves):

            def ends(i, carry):
                state, message, decay = carry
                for u in range(unroll):
                    j = i * unroll + u
                    factor = jnp.exp2(delta_scr[j][None] * rate_scr[part])
                    state = factor * state + drive_scr[j][None] * inject_scr[j, part]
                    decay = decay * factor
                    message = message + decay * (grad_scr[j][None] * readout_scr[j, part])
                return state, message, decay

            state, message, decay = lax.fori_loop(0, steps // unroll, ends, (zero, zero, zero + 1.0))
            for value, kept, at, reverse in (
                (state, ahead_scr, h * half, False), (message, behind_scr, states + h * half, True)
            ):
                factor = decay
                for by in (1, 2, 4):
                    value = value + factor * shift_up(value, by, 0.0, reverse)
                    factor = factor * shift_up(factor, by, 1.0, reverse)
                kept[tile, part] = shift_up(value, 1, 0.0, reverse)
                last = 0 if reverse else SUB - 1
                for n in range(half):
                    totals[tile, at + n : at + n + 1] = value[n, last : last + 1]

    for r in range(lag - 1, -1, -1):
        e = step - r

        @pl.when((e >= 0) & (e < count))
        def _():
            if r == 0:
                prefix.copy(e, 0).start()
            for done in range((r - 1) * per, min(r * per, rounds)) if r > 0 else ():
                prefix.advance(e, done + 1)

    @pl.when(step == count + lag - 1)
    def _():
        group = 4
        shape = (group * LANES, 2 * states)
        from_lane = lax.broadcasted_iota(jnp.int32, shape, 0) // LANES
        to_column = lax.broadcasted_iota(jnp.int32, shape, 1)
        whole = jnp.zeros((rows, 2 * states), F32)
        for first, scr in ((0, dinject_scr), (states, dread_scr)):
            for n in range(0, states, group):
                ones = (from_lane + (first + n) == to_column).astype(F32).astype(BF16)
                values = [scr[:, n + i].reshape(rows, LANES) for i in range(group)]
                highs = [value.astype(BF16) for value in values]
                lows = [(value - high.astype(F32)).astype(BF16) for value, high in zip(values, highs)]
                for parts in (highs, lows):
                    whole = whole + jnp.dot(jnp.concatenate(parts, axis=1), ones, preferred_element_type=F32)
        dselect_ref[...] = whole

        slots = 2 * count
        for k in range(count):
            for p in range(ex.phases):
                if slots - 2 <= slot_of(k, p) < slots:
                    ex.finish(k, p)
        sizes = []
        for k in range(early, count):
            sizes.append(0)
            for ref, base, size in ex.state(k, next_phase(k, count)):
                here = pl.ds(pl.multiple_of(base, 16), size)
                sizes[-1] += size
                pltpu.make_async_copy(ref.at[k, here, :], handed.at[k - early, here, :], store_sem.at[k]).start()
        for k in range(early):
            wait_rows(out.at[k], store_sem.at[k])
        for k in range(early, count):
            wait_rows(acc.at[k, pl.ds(0, sizes[k - early]), :], store_sem.at[k])


def run_scan(active, gate, graded, select, step_weight, step_bias, decay_log, skip, normed, upstream, seq):
    rows, inner = active.shape
    rank = step_weight.shape[0]
    states = decay_log.shape[0]
    width = upstream.shape[1]
    chunk = 2 * width
    tiles, steps = inner // LANES, rows // SUB
    rounds = seq.bit_length() - 1
    phases = 8 + max(rounds - 3, 0)
    early = begun(tiles, phases)
    gates, outs = (early + 1) // 2 * 2 * LANES, early // 2 * 2 * LANES
    lag = min(rounds, 3) + 1
    now = pl.BlockSpec((rows, LANES), lambda i: (0, lax.min(i, tiles - 1)))
    late = lambda shape: pl.BlockSpec(shape, lambda i: (0, lax.max(i - lag, 0)))
    whole = lambda a: pl.BlockSpec(a.shape, lambda i: (0, 0), pipeline_mode=pl.Buffered(1))
    hbm = pl.BlockSpec(memory_space=pltpu.HBM)
    wide = pltpu.VMEM((steps, states, SUB, LANES), F32)
    thin = pltpu.VMEM((steps, SUB, LANES), F32)
    cube = pltpu.VMEM((tiles, states, SUB, LANES), F32)
    small = pltpu.VMEM((tiles, states, LANES), F32)
    pair = pltpu.VMEM((rows, 2 * LANES), BF16)
    buffers = scratch(tiles, chunk, tiles // 2, seq)
    buffers[1] = pltpu.VMEM((begun(tiles, phases - 5), chunk, LANES), BF16)
    ring = pltpu.VMEM((lag, steps, SUB, LANES), F32)
    return pl.pallas_call(
        functools.partial(scan_kernel, rank, states, chunk, rounds, seq),
        grid=(tiles + lag,),
        in_specs=[
            now, now, now, whole(select), whole(step_weight), whole(step_bias), whole(decay_log), whole(skip),
            hbm, hbm,
        ],
        out_specs=[
            late((rows, LANES)), late((rows, LANES)), late((rows, LANES)), late((rows, LANES)),
            late((states + SUB, LANES)), pl.BlockSpec((rows, 2 * states), lambda i: (0, 0)), hbm, hbm, hbm,
        ],
        out_shape=[
            jax.ShapeDtypeStruct((rows, inner), BF16),
            jax.ShapeDtypeStruct((rows, inner), BF16),
            jax.ShapeDtypeStruct((rows, inner), BF16),
            jax.ShapeDtypeStruct((rows, inner), F32),
            jax.ShapeDtypeStruct((states + SUB, inner), F32),
            jax.ShapeDtypeStruct((rows, 2 * states), F32),
            jax.ShapeDtypeStruct((width, gates), BF16),
            jax.ShapeDtypeStruct((outs, width), BF16),
            jax.ShapeDtypeStruct((tiles - early, chunk, LANES), BF16),
        ],
        scratch_shapes=[
            wide, wide, wide, wide,
            pltpu.VMEM((steps + 1, states, SUB, LANES), F32), wide,
            small, pltpu.VMEM((states, SUB, LANES), F32), ring, ring, ring, ring, ring, ring, ring, thin, thin,
            cube, cube, pltpu.VMEM((tiles, SUB, LANES), F32), pair, pair,
            pltpu.VMEM((tiles, 2 * states + SUB, LANES), F32),
            pltpu.VMEM((tiles, rounds, 2 * states + SUB, LANES), F32),
            small, small, pltpu.VMEM((tiles, SUB, LANES), F32),
            pltpu.SemaphoreType.DMA((tiles, rounds)), pltpu.SemaphoreType.DMA((tiles, rounds)),
            pltpu.VMEM(normed.shape, BF16), pltpu.VMEM(upstream.shape, BF16), pltpu.SemaphoreType.DMA((2,)),
        ]
        + buffers
        + [pltpu.SemaphoreType.DMA((tiles,))],
        compiler_params=pltpu.CompilerParams(
            collective_id=1, has_side_effects=True, vmem_limit_bytes=62 << 20
        ),
        name="span_scan",
    )(
        active, gate, graded, select, step_weight, step_bias, decay_log, skip, normed, upstream
    )


def bit_of(index, step):
    return (index // step) % 2

def other(axis, step):
    place = lax.axis_index(axis)
    place = place + step * (1 - 2 * bit_of(place, step))
    if axis == "dp":
        return (place, lax.axis_index("seq"))
    return (lax.axis_index("dp"), place)

CORE, X, Y = ("seq", 1), ("dp", 1), ("dp", 2)

def wait_rows(rows, sem):
    pltpu.make_async_copy(rows, rows, sem).wait()


def store_lanes(source, target, pair, sem):
    width = target.shape[0]
    for side in range(2):
        lanes = pl.ds(pl.multiple_of((2 * pair + side) * LANES, LANES), LANES)
        pltpu.make_async_copy(source.at[pl.ds(side * width, width), :], target.at[:, lanes], sem).start()


def store_rows(source, target, pair, sem):
    tall = 2 * LANES
    rows = pl.ds(pl.multiple_of(pair * tall, tall), tall)
    for b in range(target.shape[1] // LANES):
        pltpu.make_async_copy(
            source.at[pl.ds(b * tall, tall), :], target.at[rows, pl.ds(b * LANES, LANES)], sem
        ).start()


class Exchange:
    levels = 4

    def __init__(self, acc, out, landing, extra, send_sem, recv_sem, rows, window, seq):
        self.acc, self.out, self.landing, self.extra = acc, out, landing, extra
        self.send_sem, self.recv_sem = send_sem, recv_sem
        self.rows, self.window = rows, window
        self.more = [("seq", 8 << i) for i in range(12) if (8 << i) < seq]
        self.orders = ((CORE, X, Y), (CORE, Y, X))
        self.back = self.levels + len(self.more)
        self.phases = self.back + self.levels
        place = lax.axis_index("seq")
        self.quarter = (place // 2) % 4
        self.core_base = bit_of(place, 1) * (rows // 2)
        self.kept = []
        for s, order in enumerate(self.orders):
            base, size = self.core_base + s * (rows // 4), rows // 4
            spans = [(base, size)]
            for axis, step in order[1:]:
                size = size // 2
                base = base + bit_of(lax.axis_index(axis), step) * size
                spans.append((base, size))
            size = size // 4
            spans.append((base + self.quarter * size, size))
            self.kept.append(spans)

    def partners(self):
        links = [CORE, X, Y] + self.more
        return [other(*link) for link in links] + [self.along(i) for i in range(1, 4)]

    def greet(self):
        for device in self.partners():
            pl.semaphore_signal(pltpu.get_barrier_semaphore(), inc=1, device_id=device, device_id_type=MESH)

    def welcome(self):
        pl.semaphore_wait(pltpu.get_barrier_semaphore(), len(self.partners()))

    def along(self, i):
        place = lax.axis_index("seq")
        return (lax.axis_index("dp"), place + 2 * (lax.rem(self.quarter + i, 4) - self.quarter))

    def span(self, ref, k, base, size):
        return ref.at[k, pl.ds(pl.multiple_of(base, 16), size), :]

    def land(self, p):
        rows = self.rows
        return [0, rows // 2, rows // 2 + rows // 4, rows // 2 + rows // 4 + rows // 8][p]

    def rows_of(self, p):
        rows, last = self.rows, self.phases - 1
        if self.levels <= p < self.back:
            return rows // 32
        return [rows // 2, rows // 4, rows // 8, 6 * rows // 64][min(p, last - p)]

    def copies(self, k, p):
        w = lax.rem(k, self.window)
        rows = self.rows
        if p == 0:
            return [(self.span(self.acc, k, rows // 2 - self.core_base, rows // 2),
                     self.landing.at[w, pl.ds(0, rows // 2), :], other(*CORE))]
        if p == self.phases - 1:
            half = self.span(self.out, k, self.core_base, rows // 2)
            return [(half, half, other(*CORE))]
        found = []
        for s in range(2):
            if p < self.levels - 1:
                size = self.kept[s][p][1]
                axis, step = self.orders[s][p]
                base = self.kept[s][p - 1][0] + (1 - bit_of(lax.axis_index(axis), step)) * size
                target = self.landing.at[w, pl.ds(self.land(p) + s * size, size), :]
                found.append((self.span(self.acc, k, base, size), target, other(axis, step)))
            elif p == self.levels - 1:
                first, size = self.kept[s][p - 1][0], self.kept[s][p][1]
                for i in range(1, 4):
                    base = first + lax.rem(self.quarter + i, 4) * size
                    target = self.landing.at[w, pl.ds(self.land(p) + (3 * s + i - 1) * size, size), :]
                    found.append((self.span(self.acc, k, base, size), target, self.along(i)))
            elif p < self.back:
                base, size = self.kept[s][-1]
                target = self.extra.at[w, p - self.levels, pl.ds(s * size, size), :]
                found.append((self.span(self.acc, k, base, size), target, other(*self.more[p - self.levels])))
            else:
                level = self.phases - 1 - p
                piece = self.span(self.out, k, *self.kept[s][level])
                devices = [self.along(i) for i in range(1, 4)] if level == 3 else [other(*self.orders[s][level])]
                found += [(piece, piece, device) for device in devices]
        return found

    def add(self, k, base, size, sources, target):
        step = min(size, 256)

        def body(i, _):
            here = pl.ds(pl.multiple_of(base + i * step, 16), step)
            total = self.acc[k, here, :].astype(F32)
            for ref, index, first in sources:
                there = pl.ds(pl.multiple_of(first + i * step, 16), step)
                total = total + ref[index + (there,)].astype(F32)
            target[k, here, :] = total.astype(BF16)
            return 0

        lax.fori_loop(0, size // step, body, 0)

    def finish(self, k, p):
        w = lax.rem(k, self.window)
        rows = self.acc.at[k, pl.ds(0, self.rows_of(p)), :]
        copy = pltpu.make_async_remote_copy(
            src_ref=rows, dst_ref=rows, send_sem=self.send_sem.at[w, p], recv_sem=self.recv_sem.at[w, p],
            device_id=other(*CORE), device_id_type=MESH,
        )
        copy.wait_send()
        copy.wait_recv()
        target = self.out if p == self.back - 1 else self.acc
        if p == 0:
            self.add(k, self.core_base, self.rows // 2, [(self.landing, (w,), 0)], target)
        elif p < self.back:
            for s in range(2):
                base, size = self.kept[s][min(p, self.levels - 1)]
                if p < self.levels - 1:
                    sources = [(self.landing, (w,), self.land(p) + s * size)]
                elif p < self.levels:
                    sources = [(self.landing, (w,), self.land(p) + (3 * s + i) * size) for i in range(3)]
                else:
                    sources = [(self.extra, (w, p - self.levels), s * size)]
                self.add(k, base, size, sources, target)

    def start(self, k, p):
        w = lax.rem(k, self.window)
        for source, target, device in self.copies(k, p):
            pltpu.make_async_remote_copy(
                src_ref=source, dst_ref=target, send_sem=self.send_sem.at[w, p], recv_sem=self.recv_sem.at[w, p],
                device_id=device, device_id_type=MESH,
            ).start()

    def advance(self, k, p):
        if p > 0:
            self.finish(k, p - 1)
        if p < self.phases:
            self.start(k, p)

    def state(self, k, p):
        rows = self.rows
        if p == 0:
            return [(self.acc, 0, rows)]
        if p == self.phases:
            return [(self.out, 0, rows)]
        level = min(p - 1, self.levels - 1) if p < self.back else self.phases - 1 - p
        spans = [(self.core_base, rows // 2)] if level == 0 else [self.kept[s][level] for s in range(2)]
        return [(self.acc if p < self.back else self.out, base, size) for base, size in spans]


def scratch(chunks, rows, window, seq):
    more = len([1 for i in range(12) if (8 << i) < seq])
    return [
        pltpu.VMEM((chunks, rows, LANES), BF16),
        pltpu.VMEM((chunks, rows, LANES), BF16),
        pltpu.VMEM((window, rows, LANES), BF16),
        pltpu.VMEM((window, max(more, 1), rows // 32, LANES), BF16),
        pltpu.SemaphoreType.DMA((window, 8 + more)),
        pltpu.SemaphoreType.DMA((window, 8 + more)),
    ]


def tail_kernel(
    rank, states, chunk, seq,
    dprelow_ref, select_ref, dpair_ref, step_weight_ref, normed_ref, upstream_hbm, inputs_hbm, scale_ref, hot_hbm,
    gain_ref, dactive_first_ref, mixed_first_ref, select_weight_ref, halo_ref, lines_ref,
    dactive_ref, mixed_ref, front_ref, active_ref, select_tile_ref, conv_ref, front_weight_ref, gate_weight_ref,
    dgate_ref, gated_ref, out_weight_ref, handed,
    output_ref, dinputs_ref, front_sum, gate_rest, out_rest, embedding_sum, wide_sum, mixed_sum,
    upstream_ref, inputs_ref, hot_ref, late_sem, dselect_scr, first_scr, after_scr, spread_scr, extended_scr, dnormed_scr, result_scr, misc_scr, gain_scr,
    acc, out, landing, extra, send_sem, recv_sem, load_sem, store_sem, first_send, first_recv,
):
    step = pl.program_id(0)
    rows, width = upstream_ref.shape
    across = width // LANES
    inner = dprelow_ref.shape[1]
    tiles, pairs = inner // LANES, inner // (2 * LANES)
    tall = 2 * LANES
    kernel = conv_ref.shape[0]
    halo = kernel - 1
    vocab = embedding_sum.shape[0]
    ex = Exchange(acc, out, landing, extra, send_sem, recv_sem, chunk, landing.shape[0], seq)
    early = begun(tiles, ex.phases)
    old = tiles - early
    embedding_at, wide_at, mixed_at = (old + pairs + i for i in range(3))
    count = old + pairs + 3
    place = lax.axis_index("seq")
    here_dp = lax.axis_index("dp")

    def add(scr, value):
        for b in range(across):
            scr[b] += value[:, b * LANES : (b + 1) * LANES]

    def put(scr, here, value):
        for b in range(across):
            scr[b, here, :] = value[:, b * LANES : (b + 1) * LANES]

    def take(scr, here):
        return jnp.concatenate([scr[b, here, :] for b in range(across)], axis=1)

    def first_copy():
        return pltpu.make_async_remote_copy(
            src_ref=first_scr, dst_ref=after_scr, send_sem=first_send, recv_sem=first_recv,
            device_id=(here_dp, lax.rem(place + seq - 1, seq)), device_id_type=MESH,
        )

    late_loads = [
        pltpu.make_async_copy(source, target, late_sem.at[i])
        for i, (source, target) in enumerate(
            ((upstream_hbm, upstream_ref), (inputs_hbm, inputs_ref), (hot_hbm, hot_ref))
        )
    ]

    def greet():
        barrier = pltpu.get_barrier_semaphore()
        ex.greet()
        for there, by in ((place > 0, -1), (place < seq - 1, 1)):

            @pl.when(there)
            def _():
                pl.semaphore_signal(barrier, inc=1, device_id=(here_dp, place + by), device_id_type=MESH)

    def welcome():
        barrier = pltpu.get_barrier_semaphore()
        neighbours = 2 - (place == 0).astype(jnp.int32) - (place == seq - 1).astype(jnp.int32)
        pl.semaphore_wait(barrier, len(ex.partners()) + neighbours)

    def store(k):
        pair = (k + early) // 2

        @pl.when((k < old) & (lax.rem(k + early, 2) == 0))
        def _():
            store_lanes(out.at[k], gate_rest, pair - (early + 1) // 2, store_sem.at[k])

        @pl.when((k < old) & (lax.rem(k + early, 2) == 1))
        def _():
            store_rows(out.at[k], out_rest, pair - early // 2, store_sem.at[k])

        @pl.when((k >= old) & (k < embedding_at))
        def _():
            store_lanes(out.at[k], front_sum, k - old, store_sem.at[k])

        @pl.when(k == embedding_at)
        def _():
            for b in range(width // LANES):
                pltpu.make_async_copy(
                    out.at[k, pl.ds(b * vocab, vocab), :], embedding_sum.at[:, pl.ds(b * LANES, LANES)], store_sem.at[k]
                ).start()

        @pl.when(k == wide_at)
        def _():
            pltpu.make_async_copy(out.at[k], wide_sum, store_sem.at[k]).start()

        @pl.when(k == mixed_at)
        def _():
            pltpu.make_async_copy(out.at[k], mixed_sum, store_sem.at[k]).start()

    def old_turns(spot):
        for k, p, now in turns(ex.phases, tiles + step, spot):
            k = k - early

            @pl.when(now & (k >= 0) & (k < old))
            def _():
                if p > 0:

                    @pl.when(step > 0)
                    def _():
                        ex.finish(k, p - 1)

                if p < ex.phases:
                    ex.start(k, p)
                else:
                    store(k)

    def new_turns(turn):
        for p in range(ex.phases, -1, -1):
            k = old + turn - 2 * p

            @pl.when((k >= old) & (k < count))
            def _():
                ex.advance(k, p)
                if p == ex.phases:
                    store(k)

    @pl.when(step == 0)
    def _():
        greet()
        sizes = []
        for k in range(old):
            sizes.append(0)
            for ref, base, size in ex.state(k, next_phase(k + early, tiles)):
                here = pl.ds(pl.multiple_of(base, 16), size)
                sizes[-1] += size
                pltpu.make_async_copy(handed.at[k, here, :], ref.at[k, here, :], load_sem.at[k]).start()
        for copy in late_loads:
            copy.start()
        dlow = contract_cols(dprelow_ref[...], step_weight_ref[...])
        dselect_scr[...] = jnp.concatenate([dlow, dpair_ref[...]], axis=1).astype(BF16)
        some = jnp.dot(dselect_scr[: halo * SUB], select_weight_ref[...], preferred_element_type=F32)
        some = (dactive_first_ref[...] + some) * silu_slope(mixed_first_ref[...])
        for i in range(halo):
            first_scr[i : i + 1, :] = some[i * SUB : i * SUB + 1, :]
        first_scr[halo:, :] = jnp.zeros((SUB - halo, inner), F32)
        welcome()

        @pl.when(place > 0)
        def _():
            first_copy().start()

        dnormed_scr[...] = jnp.zeros_like(dnormed_scr)
        result_scr[...] = jnp.zeros_like(result_scr)
        misc_scr[...] = jnp.zeros_like(misc_scr)
        misc_scr[kernel + 1 : kernel + 3, :] = lines_ref[states : states + 2, :]
        acc[wide_at] = jnp.zeros_like(acc[wide_at])
        acc[mixed_at] = jnp.zeros_like(acc[mixed_at])
        for b in range(tiles):
            at = rank * tiles + b * states
            acc[mixed_at, at : at + states, :] = lines_ref[:states, b * LANES : (b + 1) * LANES].astype(BF16)
        for k in range(old):
            wait_rows(acc.at[k, pl.ds(0, sizes[k]), :], load_sem.at[k])

    old_turns(0)

    @pl.when(step < pairs)
    def _():
        add(result_scr, jnp.dot(gated_ref[...], out_weight_ref[...], preferred_element_type=F32))
        add(dnormed_scr, contract_cols(dgate_ref[...], gate_weight_ref[...]))

    old_turns(1)

    @pl.when(step < pairs)
    def _():
        lanes = pl.ds(pl.multiple_of(step * tall, tall), tall)
        mixed = mixed_ref[...]
        back = jnp.dot(dselect_scr[...], select_tile_ref[...], preferred_element_type=F32)
        dmixed = (dactive_ref[...] + back) * silu_slope(mixed)
        spread_scr[:rows] = dmixed
        extended_scr[: halo * SUB] = halo_ref[...].astype(F32)
        extended_scr[halo * SUB :] = front_ref[...].astype(F32)
        misc_scr[kernel : kernel + 1, lanes] = jnp.sum(dmixed, axis=0, keepdims=True)
        for i in range(kernel):
            misc_scr[i : i + 1, lanes] = jnp.sum(
                dmixed * extended_scr[i * SUB : i * SUB + rows], axis=0, keepdims=True
            )
        wide = contract_rows(dselect_scr[...], active_ref[...]).astype(BF16)
        columns = wide.shape[0]
        for side in range(2):
            at = pl.ds(pl.multiple_of((2 * step + side) * columns, columns), columns)
            acc[wide_at, at, :] = wide[:, side * LANES : (side + 1) * LANES]
        part = contract_rows(select_ref[:, :rank], dprelow_ref[:, lanes]).astype(BF16)
        for side in range(2):
            at = pl.ds(pl.multiple_of((2 * step + side) * rank, rank), rank)
            acc[mixed_at, at, :] = part[:, side * LANES : (side + 1) * LANES]

        @pl.when(step == 0)
        def _():
            @pl.when(place > 0)
            def _():
                first_copy().wait_send()

            @pl.when(place < seq - 1)
            def _():
                first_copy().wait_recv()

            @pl.when(place == seq - 1)
            def _():
                after_scr[...] = jnp.zeros_like(after_scr)

        sub = lax.broadcasted_iota(jnp.int32, (SUB, tall), 0)
        for i in range(halo):
            own = pltpu.roll(spread_scr[i * SUB : (i + 1) * SUB, :], SUB - 1, 0)
            spread_scr[rows + i * SUB : rows + (i + 1) * SUB] = jnp.where(
                sub < SUB - 1, own, after_scr[i : i + 1, lanes]
            )
        dfront = conv_ref[halo : halo + 1] * spread_scr[:rows]
        for i in range(1, kernel):
            dfront = dfront + conv_ref[halo - i : halo - i + 1] * spread_scr[i * SUB : i * SUB + rows]
        dfront = dfront.astype(BF16)
        part = jnp.dot(normed_ref[...], dfront, preferred_element_type=F32).astype(BF16)
        acc[old + step, :width, :] = part[:, :LANES]
        acc[old + step, width:, :] = part[:, LANES:]
        add(dnormed_scr, contract_cols(dfront, front_weight_ref[...]))

    @pl.when(step == pairs)
    def _():
        for copy in late_loads:
            copy.wait()
        part = rows // SUB

        def norms(i, total):
            here = pl.ds(pl.multiple_of(i * part, part), part)
            dnormed, inputs, scale = take(dnormed_scr, here), inputs_ref[here, :], scale_ref[here, :]
            scaled = gain_ref[...] * dnormed
            mean = jnp.sum(scaled * inputs, axis=1, keepdims=True) * (1.0 / width)
            put(
                dnormed_scr, here,
                upstream_ref[here, :].astype(F32) + scale * scaled - inputs * (scale * scale * scale * mean),
            )
            put(result_scr, here, take(result_scr, here) + inputs)
            return total + jnp.sum((dnormed * inputs * scale).reshape(-1, SUB, width), axis=0)

        total = lax.fori_loop(0, SUB, norms, jnp.zeros((SUB, width), F32))
        gain_scr[...] = jnp.sum(total, axis=0, keepdims=True)
        for b in range(width // tall):
            value = jnp.concatenate([dnormed_scr[2 * b], dnormed_scr[2 * b + 1]], axis=1)
            high = value.astype(BF16)
            low = (value - high.astype(F32)).astype(BF16)
            whole = jnp.dot(hot_ref[...], high, preferred_element_type=F32)
            whole = (whole + jnp.dot(hot_ref[...], low, preferred_element_type=F32)).astype(BF16)
            for side in range(2):
                at = (2 * b + side) * vocab
                acc[embedding_at, at : at + vocab, :] = whole[:, side * LANES : (side + 1) * LANES]
        at = (rank + states) * tiles
        for b in range(tiles):
            acc[mixed_at, at + b * 16 : at + (b + 1) * 16, :] = misc_scr[:, b * LANES : (b + 1) * LANES].astype(BF16)
        at = (rank + states + 16) * tiles
        for b in range(width // LANES):
            acc[mixed_at, at + b * 16 : at + (b + 1) * 16, :] = jnp.broadcast_to(
                gain_scr[:, b * LANES : (b + 1) * LANES], (16, LANES)
            ).astype(BF16)

    @pl.when(step == pairs + 1)
    def _():
        span = rows // SUB
        for i in range(SUB):
            for b in range(across):
                lanes, every = slice(b * LANES, (b + 1) * LANES), pl.ds(i, span, stride=SUB)
                dinputs_ref[i * span : (i + 1) * span, lanes] = dnormed_scr[b, every, :]
                output_ref[i * span : (i + 1) * span, lanes] = result_scr[b, every, :].astype(BF16)

    new_turns(step)

    @pl.when(step == pl.num_programs(0) - 1)
    def _():
        def rest(turn, _):
            new_turns(turn)
            return 0

        lax.fori_loop(pairs + 3, pairs + 3 + 2 * ex.phases, rest, 0)
        for k in range(count):
            wait_rows(out.at[k], store_sem.at[k])


def run_tail(
    d_pre_low, select, d_pair, step_weight, normed, upstream, inputs, scale, hot, gain, d_active, mixed, select_weight,
    halo, lines, front, active, conv_weight, input_weight, d_gate, gated, output_weight, handed, vocab, seq,
):
    rows, inner = front.shape
    width = inputs.shape[1]
    rank, states = step_weight.shape[0], lines.shape[0] - SUB
    chunk = 2 * width
    tiles, pairs, tall = inner // LANES, inner // (2 * LANES), 2 * LANES
    phases = 8 + max(seq.bit_length() - 4, 0)
    early = begun(tiles, phases)
    count = tiles - early + pairs + 3
    some = halo.shape[0]
    at = lambda i: lax.min(i, pairs - 1)
    whole = lambda a: pl.BlockSpec(a.shape, lambda i: (0, 0), pipeline_mode=pl.Buffered(1))
    first = pl.BlockSpec((some, inner), lambda i: (0, 0), pipeline_mode=pl.Buffered(1))
    tile = lambda height: pl.BlockSpec((height, tall), lambda i: (0, at(i)))
    high = lambda wide: pl.BlockSpec((tall, wide), lambda i: (at(i), 0))
    hbm = pl.BlockSpec(memory_space=pltpu.HBM)
    fixed = pl.BlockSpec((rows, width), lambda i: (0, 0))
    gates, outs = inner - (early + 1) // 2 * tall, inner - early // 2 * tall
    return pl.pallas_call(
        functools.partial(tail_kernel, rank, states, chunk, seq),
        grid=(pairs + 3,),
        in_specs=[
            whole(d_pre_low), whole(select), whole(d_pair), whole(step_weight), whole(normed), hbm,
            hbm, whole(scale), hbm, whole(gain), first, first, whole(select_weight), tile(some),
            whole(lines), tile(rows), tile(rows), tile(rows), tile(rows),
            tile(select_weight.shape[0]), tile(conv_weight.shape[0]), tile(width),
            pl.BlockSpec((width, tall), lambda i: (0, at(i) + pairs)), tile(rows), tile(rows), high(width), hbm,
        ],
        out_specs=[fixed, fixed, hbm, hbm, hbm, hbm, hbm, hbm],
        out_shape=[
            jax.ShapeDtypeStruct((rows, width), BF16),
            jax.ShapeDtypeStruct((rows, width), F32),
            jax.ShapeDtypeStruct((width, inner), BF16),
            jax.ShapeDtypeStruct((width, gates), BF16),
            jax.ShapeDtypeStruct((outs, width), BF16),
            jax.ShapeDtypeStruct((vocab, width), BF16),
            jax.ShapeDtypeStruct((chunk, LANES), BF16),
            jax.ShapeDtypeStruct((chunk, LANES), BF16),
        ],
        scratch_shapes=[
            pltpu.VMEM(upstream.shape, BF16), pltpu.VMEM(inputs.shape, F32), pltpu.VMEM(hot.shape, BF16),
            pltpu.SemaphoreType.DMA((3,)),
            pltpu.VMEM(select.shape, BF16),
            pltpu.VMEM((SUB, inner), F32), pltpu.VMEM((SUB, inner), F32),
            pltpu.VMEM((rows + some, tall), F32), pltpu.VMEM((rows + some, tall), F32),
            pltpu.VMEM((width // LANES, rows, LANES), F32), pltpu.VMEM((width // LANES, rows, LANES), F32),
            pltpu.VMEM((16, inner), F32), pltpu.VMEM((1, width), F32),
        ]
        + scratch(count, chunk, 8, seq)
        + [
            pltpu.SemaphoreType.DMA((count,)), pltpu.SemaphoreType.DMA((count,)),
            pltpu.SemaphoreType.DMA, pltpu.SemaphoreType.DMA,
        ],
        compiler_params=pltpu.CompilerParams(
            collective_id=2, has_side_effects=True, vmem_limit_bytes=62 << 20
        ),
        name="span_tail",
    )(
        d_pre_low, select, d_pair, step_weight, normed, upstream, inputs, scale, hot, gain, d_active, mixed,
        select_weight, halo, lines, d_active, mixed, front, active, select_weight, conv_weight,
        input_weight, input_weight, d_gate, gated, output_weight, handed,
    )


def widen_kernel(
    rank, states, columns, parts, slots,
    front, gate, gate_rest, outs, outs_rest, output, dinputs, embedding, wide_sum, mixed_sum,
    input_to, output_weight_to, output_to, dinputs_to, *rest,
):
    small_to, scratches = rest[:9], rest[9:]
    (
        input_scr, outs_scr, wide_input, wide_outs, output_scr, dinputs_scr, embedding_ref, wide_ref, mixed_ref,
        load_sem, outs_load, store_sem, outs_store, pass_sem, small_load, small_store,
    ) = scratches[:16]
    small_scr = scratches[16:]
    small = [
        pltpu.make_async_copy(source, scr, small_load.at[i])
        for i, (source, scr) in enumerate(((embedding, embedding_ref), (wide_sum, wide_ref), (mixed_sum, mixed_ref)))
    ]
    small_out = [
        pltpu.make_async_copy(scr, to, small_store.at[i]) for i, (scr, to) in enumerate(zip(small_scr, small_to))
    ]
    passed = [
        (pltpu.make_async_copy(source, scr, pass_sem.at[i]), pltpu.make_async_copy(scr, to, pass_sem.at[i]))
        for i, (source, scr, to) in enumerate(((output, output_scr, output_to), (dinputs, dinputs_scr, dinputs_to)))
    ]
    thick, tall = input_scr.shape[0] // parts, outs_scr.shape[0] // parts
    early = outs.shape[0] // tall
    for i in range(parts):
        here, lane = pl.ds(i * thick, thick), 0
        for source in (front, gate, gate_rest):
            lanes = pl.ds(lane, source.shape[1])
            pltpu.make_async_copy(source.at[here, :], input_scr.at[here, lanes], load_sem.at[i]).start()
            lane += source.shape[1]
        source, at = (outs, i) if i < early else (outs_rest, i - early)
        there = pl.ds(i * tall, tall)
        pltpu.make_async_copy(source.at[pl.ds(at * tall, tall), :], outs_scr.at[there, :], outs_load.at[i]).start()
    for copy, unused in passed:
        copy.start()
    for copy in small:
        copy.start()

    def unpack():
        embedding_to, select_to, step_to, decay_to, conv_to, gain_to, *line_to = small_scr
        for copy in small:
            copy.wait()
        embedding_to[...] = embedding_ref[...].astype(F32)
        for source, whole in (
            (wide_ref, ((select_to, columns),)),
            (mixed_ref, ((step_to, rank), (decay_to, states), (conv_to, 16), (gain_to, 16))),
        ):
            at = 0
            for to, height in whole:
                for b in range(to.shape[1] // LANES):
                    part = source[at : at + height, :].astype(F32)
                    lanes = slice(b * LANES, (b + 1) * LANES)
                    to[:, lanes] = part[: to.shape[0]]
                    if to is conv_to:
                        for i, line in enumerate(line_to):
                            line[:, lanes] = part[to.shape[0] + i : to.shape[0] + i + 1]
                    at += height
        for copy in small_out:
            copy.start()

    for i in range(parts):
        if i == parts // 2:
            for first, second in passed:
                first.wait()
                second.start()
            unpack()
        slot = i % slots
        for narrow, wide, to, size, load, store in (
            (input_scr, wide_input, input_to, thick, load_sem, store_sem),
            (outs_scr, wide_outs, output_weight_to, tall, outs_load, outs_store),
        ):
            here, half = pl.ds(i * size, size), size // 2
            wait_rows(narrow.at[here, :], load.at[i])
            if i >= slots:
                wait_rows(wide.at[slot], store.at[slot])
            wide[slot] = narrow[here, :].astype(F32)
            for j in range(2):
                pltpu.make_async_copy(
                    wide.at[slot, pl.ds(j * half, half), :], to.at[pl.ds(i * size + j * half, half), :], store.at[slot]
                ).start()
    for slot in range(slots):
        wait_rows(wide_input.at[slot], store_sem.at[slot])
        wait_rows(wide_outs.at[slot], outs_store.at[slot])
    for unused, copy in passed:
        copy.wait()
    for copy in small_out:
        copy.wait()


def run_widen(
    front, gate, gate_rest, out, out_rest, output, d_inputs, embedding, wide, mixed, rank, states, columns, kernel
):
    width, inner = front.shape
    vocab = embedding.shape[0]
    parts, slots = inner // (2 * LANES), 4
    hbm = pl.BlockSpec(memory_space=pltpu.HBM)
    shapes = [
        (width, 2 * inner), (inner, width), output.shape, d_inputs.shape, (vocab, width), (columns, inner), (rank, inner),
        (states, inner), (kernel, inner), (1, width), (1, inner), (1, inner), (1, inner),
    ]
    return pl.pallas_call(
        functools.partial(widen_kernel, rank, states, columns, parts, slots),
        in_specs=[hbm] * 10,
        out_specs=[hbm] * len(shapes),
        out_shape=[
            jax.ShapeDtypeStruct(shape, output.dtype if i == 2 else F32) for i, shape in enumerate(shapes)
        ],
        scratch_shapes=[
            pltpu.VMEM((width, 2 * inner), BF16), pltpu.VMEM((inner, width), BF16),
            pltpu.VMEM((slots, width // parts, 2 * inner), F32), pltpu.VMEM((slots, inner // parts, width), F32),
            pltpu.VMEM(output.shape, output.dtype), pltpu.VMEM(d_inputs.shape, F32),
            pltpu.VMEM(embedding.shape, BF16), pltpu.VMEM(wide.shape, BF16), pltpu.VMEM(mixed.shape, BF16),
            pltpu.SemaphoreType.DMA((parts,)), pltpu.SemaphoreType.DMA((parts,)),
            pltpu.SemaphoreType.DMA((slots,)), pltpu.SemaphoreType.DMA((slots,)), pltpu.SemaphoreType.DMA((2,)),
            pltpu.SemaphoreType.DMA((3,)), pltpu.SemaphoreType.DMA((len(shapes) - 4,)),
        ]
        + [pltpu.VMEM(shape, F32) for shape in shapes[4:]],
        compiler_params=pltpu.CompilerParams(vmem_limit_bytes=62 << 20),
        name="sums_to_float32",
    )(front, gate, gate_rest, out, out_rest, output, d_inputs, embedding, wide, mixed)


def on_device(
    byte_ids,
    embedding,
    cotangent,
    norm_gain,
    input_projection_weight,
    conv_weight,
    conv_bias,
    select_weight,
    step_weight,
    step_bias,
    decay_log,
    skip_gain,
    output_projection_weight,
):
    count, stretch = byte_ids.shape
    vocab, width = embedding.shape
    kernel, inner = conv_weight.shape
    states = decay_log.shape[0]
    rank = step_weight.shape[0]
    rows = count * stretch
    seq = lax.axis_size("seq")
    gain, turned_select = norm_gain.reshape(1, width), select_weight.T
    (
        block_inputs, scale, unused, turned, upstream, hot, front, earlier, mixed, active, gate, graded, select
    ) = run_front(
        byte_ids.reshape(1, rows), embedding, cotangent.reshape(rows, width), gain, input_projection_weight,
        output_projection_weight, conv_weight, conv_bias.reshape(1, inner), turned_select, seq,
    )
    (
        gated, d_gate, d_pre_low, d_active, lines, d_pair, gate_sum, out_sum, handed
    ) = run_scan(
        active, gate, graded, select, step_weight, step_bias.reshape(1, inner), decay_log, skip_gain.reshape(1, inner),
        turned, upstream, seq,
    )
    output, d_inputs, front_sum, gate_rest, out_rest, embedding_sum, wide_sum, mixed_sum = run_tail(
        d_pre_low, select, d_pair, step_weight, turned, upstream, block_inputs, scale, hot, gain,
        d_active, mixed, turned_select, earlier, lines, front, active, conv_weight,
        input_projection_weight, d_gate, gated, output_projection_weight, handed, vocab, seq,
    )
    (
        d_input_weight, d_output_weight, output, d_inputs, d_embedding, d_select_weight, d_step_weight, d_decay_log, d_conv_weight,
        d_norm_gain, d_conv_bias, d_step_bias, d_skip_gain,
    ) = run_widen(
        front_sum, gate_sum, gate_rest, out_sum, out_rest, output, d_inputs, embedding_sum, wide_sum, mixed_sum, rank, states,
        select_weight.shape[1], kernel,
    )
    return (
        output.reshape(count, stretch, width),
        d_inputs.reshape(count, stretch, width),
        d_embedding,
        d_norm_gain[0],
        d_input_weight,
        d_conv_weight,
        d_conv_bias[0],
        d_select_weight.T,
        d_step_weight,
        d_step_bias[0],
        d_decay_log,
        d_skip_gain[0],
        d_output_weight,
    )


def solution(mesh):
    placed = (P("dp", "seq"), P(), P("dp", "seq", None)) + (P(),) * 10
    return jax.shard_map(
        on_device,
        mesh=mesh,
        in_specs=placed,
        out_specs=(P("dp", "seq", None), P("dp", "seq", None)) + (P(),) * 11,
        check_vma=False,
    )
```

```python
import functools
import math

import jax
import jax.numpy as jnp
from jax import lax
from jax.experimental import pallas as pl
from jax.experimental.pallas import tpu as pltpu
from jax.sharding import PartitionSpec as P

EPS = 1e-05
LANES = 128
SUB = 8
LOG2E = math.log2(math.e)
LN2 = math.log(2.0)
F32 = jnp.float32
BF16 = jnp.bfloat16
MESH = pl.DeviceIdType.MESH


def silu_slope(value):
    sigma = jax.nn.sigmoid(value)
    return sigma * (1.0 + value * (1.0 - sigma))


def contract_rows(left, right):
    return lax.dot_general(
        left, right, (((0,), (0,)), ((), ())), preferred_element_type=F32
    )


def contract_cols(left, right):
    return lax.dot_general(
        left, right, (((1,), (1,)), ((), ())), preferred_element_type=F32
    )


def sublane(shape):
    return lax.broadcasted_iota(jnp.int32, shape, len(shape) - 2)


def shift_up(value, by, fill, reverse):
    place = sublane(value.shape)
    if reverse:
        moved = pltpu.roll(value, SUB - by, value.ndim - 2)
        return jnp.where(place < SUB - by, moved, fill)
    moved = pltpu.roll(value, by, value.ndim - 2)
    return jnp.where(place >= by, moved, fill)


def expand_columns(select, first, states):
    width = select.shape[1]
    shape = (width, states * LANES)
    source = lax.broadcasted_iota(jnp.int32, shape, 0)
    target = lax.broadcasted_iota(jnp.int32, shape, 1) // LANES + first
    spread = (source == target).astype(F32).astype(BF16)
    return jnp.dot(select, spread, preferred_element_type=F32)


def tree_sum(value):
    while value.shape[0] > 1:
        half = value.shape[0] // 2
        value = value[:half] + value[half:]
    return value[0]


def front_kernel(
    seq,
    ids_ref, embedding_ref, cotangent_ref, gain_ref, front_weight_ref, gate_weight_ref, out_weight_ref, conv_ref,
    conv_bias_ref, select_weight_ref,
    inputs_ref, scale_ref, normed_ref, turned_ref, upstream_ref, hot_ref, front_ref, halo_ref, mixed_ref, active_ref,
    gate_ref, graded_ref, select_ref,
    last_scr, extended_scr, total_scr, send_sem, recv_sem,
):
    step = pl.program_id(0)
    rows, width = upstream_ref.shape
    span = rows // SUB
    vocab = embedding_ref.shape[0]
    kernel = conv_ref.shape[0]
    halo = kernel - 1
    place = lax.axis_index("seq")

    def there(by):
        return (lax.axis_index("dp"), place + by)

    def copy():
        return pltpu.make_async_remote_copy(
            src_ref=ids_ref.at[:, pl.ds(rows - LANES, LANES)], dst_ref=last_scr, send_sem=send_sem, recv_sem=recv_sem,
            device_id=there(1), device_id_type=MESH,
        )

    def norm(inputs):
        scale = lax.rsqrt(jnp.sum(inputs * inputs, axis=1, keepdims=True) * (1.0 / width) + EPS)
        return scale, (inputs * scale * gain_ref[...]).astype(BF16)

    def hot_of(ids):
        shape = (vocab, ids.shape[1])
        return (lax.broadcasted_iota(jnp.int32, shape, 0) == ids).astype(F32).astype(BF16)

    @pl.when(step == 0)
    def _():
        barrier = pltpu.get_barrier_semaphore()

        @pl.when(place > 0)
        def _():
            pl.semaphore_signal(barrier, inc=1, device_id=there(-1), device_id_type=MESH)

        @pl.when(place == 0)
        def _():
            last_scr[...] = jnp.full(last_scr.shape, -1, jnp.int32)

        row = lax.broadcasted_iota(jnp.int32, (rows, rows), 0)
        position = lax.broadcasted_iota(jnp.int32, (rows, rows), 1)
        order = (lax.rem(row, SUB) * span + row // SUB == position).astype(F32).astype(BF16)
        upstream_ref[...] = jnp.dot(order, cotangent_ref[...], preferred_element_type=F32).astype(BF16)

        @pl.when(place < seq - 1)
        def _():
            pl.semaphore_wait(barrier, 1)
            copy().start()

        hot = contract_cols(hot_of(ids_ref[...]), order).astype(BF16)
        hot_ref[...] = hot
        inputs = contract_rows(hot, embedding_ref[...])
        inputs_ref[...] = inputs
        scale, normed = norm(inputs)
        scale_ref[...] = scale
        normed_ref[:rows] = normed
        turned_ref[...] = normed.T

        @pl.when(place < seq - 1)
        def _():
            copy().wait_send()

        @pl.when(place > 0)
        def _():
            copy().wait_recv()

        last = contract_rows(hot_of(last_scr[...]), embedding_ref[...])[LANES - 16 :]
        normed_ref[rows:] = norm(last)[1]
        total_scr[...] = jnp.zeros_like(total_scr)

    both = jnp.dot(normed_ref[...], front_weight_ref[...], preferred_element_type=F32).astype(BF16)
    front_ref[...] = both[:rows]
    both = both.astype(F32)
    extended_scr[halo * SUB :] = both[:rows]
    sub = lax.broadcasted_iota(jnp.int32, (SUB, both.shape[1]), 0)
    for i in range(halo):
        own = pltpu.roll(both[rows - (halo - i) * SUB : rows - (halo - i - 1) * SUB], 1, 0)
        before = both[rows + 16 - halo + i : rows + 16 - halo + i + 1]
        extended_scr[i * SUB : (i + 1) * SUB] = jnp.where(sub > 0, own, before)
    halo_ref[...] = extended_scr[: halo * SUB]
    mixed = conv_bias_ref[...] + conv_ref[0:1] * extended_scr[:rows]
    for i in range(1, kernel):
        mixed = mixed + conv_ref[i : i + 1] * extended_scr[i * SUB : i * SUB + rows]
    mixed_ref[...] = mixed
    active = jax.nn.silu(mixed).astype(BF16)
    active_ref[...] = active
    gate_ref[...] = jnp.dot(normed_ref[:rows], gate_weight_ref[...], preferred_element_type=F32).astype(BF16)
    graded_ref[...] = contract_cols(upstream_ref[...], out_weight_ref[...])
    total_scr[...] += contract_cols(active, select_weight_ref[...])

    @pl.when(step == pl.num_programs(0) - 1)
    def _():
        select_ref[...] = total_scr[...].astype(BF16)


def run_front(
    ids, embedding, cotangent, gain, input_weight, output_weight, conv_weight, conv_bias, select_weight, seq
):
    rows, width = cotangent.shape
    inner = output_weight.shape[0]
    vocab, kernel, columns = embedding.shape[0], conv_weight.shape[0], select_weight.shape[0]
    halo = (kernel - 1) * SUB
    tall = 4 * LANES
    pairs = inner // tall
    whole = lambda a: pl.BlockSpec(a.shape, lambda i: (0, 0), pipeline_mode=pl.Buffered(1))
    tile = lambda height: pl.BlockSpec((height, tall), lambda i: (0, i))
    fixed = lambda shape: pl.BlockSpec(shape, lambda i: (0, 0))
    outs = [
        ((rows, width), F32, None), ((rows, 1), F32, None), ((rows + 16, width), BF16, None),
        ((width, rows), BF16, None), ((rows, width), BF16, None), ((vocab, rows), BF16, None),
        ((rows, inner), BF16, rows), ((halo, inner), F32, halo), ((rows, inner), F32, rows), ((rows, inner), BF16, rows),
        ((rows, inner), BF16, rows), ((rows, inner), F32, rows), ((rows, columns), BF16, None),
    ]
    return pl.pallas_call(
        functools.partial(front_kernel, seq),
        grid=(pairs,),
        in_specs=[
            whole(ids), whole(embedding), whole(cotangent), whole(gain), tile(width),
            pl.BlockSpec((width, tall), lambda i: (0, i + pairs)), pl.BlockSpec((tall, width), lambda i: (i, 0)),
            tile(kernel), tile(1), tile(columns),
        ],
        out_specs=[fixed(shape) if height is None else tile(height) for shape, kind, height in outs],
        out_shape=[jax.ShapeDtypeStruct(shape, kind) for shape, kind, height in outs],
        scratch_shapes=[
            pltpu.VMEM((1, LANES), jnp.int32), pltpu.VMEM((rows + halo, tall), F32), pltpu.VMEM((rows, columns), F32),
            pltpu.SemaphoreType.DMA, pltpu.SemaphoreType.DMA,
        ],
        compiler_params=pltpu.CompilerParams(
            collective_id=3, has_side_effects=True, vmem_limit_bytes=62 << 20
        ),
        name="span_front",
    )(
        ids, embedding, cotangent, gain, input_weight, input_weight, output_weight, conv_weight, conv_bias, select_weight
    )


def slot_of(k, p):
    return 2 * k + 3 - k % 2 + 2 * p


def turns(phases, tile, place):
    for p in range(phases, -1, -1):
        k = tile - 1 - p
        yield k, p, (k >= 0) & (lax.rem(k + 2 * phases, 2) == 1 - place)


def begun(tiles, p):
    return sum(slot_of(k, p) < 2 * tiles for k in range(tiles))


def next_phase(k, tiles):
    return next(p for p in range(1000) if slot_of(k, p) >= 2 * tiles)


class Prefix:
    def __init__(self, totals, landing, start, incoming, gaps, rates, send_sem, recv_sem, rounds):
        self.totals, self.landing, self.start, self.incoming, self.gaps = totals, landing, start, incoming, gaps
        self.rates, self.send_sem, self.recv_sem, self.rounds = rates, send_sem, recv_sem, rounds

    def copy(self, e, r):
        return pltpu.make_async_remote_copy(
            src_ref=self.totals.at[e], dst_ref=self.landing.at[e, r],
            send_sem=self.send_sem.at[e, r], recv_sem=self.recv_sem.at[e, r],
            device_id=other("seq", 1 << r), device_id_type=MESH,
        )

    def advance(self, e, r):
        if r > 0:
            self.copy(e, r - 1).wait()
            self.merge(e, r - 1)
        if r < self.rounds:
            self.copy(e, r).start()

    def merge(self, e, r):
        n = self.rates.shape[1]
        rates = self.rates[e]
        later = bit_of(lax.axis_index("seq"), 1 << r) == 1
        end, message, total = self.totals[e, :n], self.totals[e, n : 2 * n], self.totals[e, 2 * n : 2 * n + 1]
        end2, message2 = self.landing[e, r, :n], self.landing[e, r, n : 2 * n]
        total2 = self.landing[e, r, 2 * n : 2 * n + 1]

        @pl.when(later)
        def _():
            gap = self.gaps[e, 0:1]
            self.start[e] = self.start[e] + jnp.exp2(gap * rates) * end2
            self.gaps[e, 0:1] = gap + total2

        @pl.when(jnp.logical_not(later))
        def _():
            gap = self.gaps[e, 1:2]
            self.incoming[e] = self.incoming[e] + jnp.exp2(gap * rates) * message2
            self.gaps[e, 1:2] = gap + total2

        if r < self.rounds - 1:
            reach, reach2 = jnp.exp2(total * rates), jnp.exp2(total2 * rates)
            self.totals[e, :n] = jnp.where(later, end + reach * end2, end2 + reach2 * end)
            self.totals[e, n : 2 * n] = jnp.where(later, message2 + reach2 * message, message + reach * message2)
            self.totals[e, 2 * n : 2 * n + 1] = total + total2


def scan_kernel(
    rank, states, chunk, rounds, seq,
    active_now, gate_now, graded_now, select_ref, step_weight_ref, step_bias_ref, decay_ref, skip_ref, normed_hbm, upstream_hbm,
    gated_ref, dgate_ref, dprelow_ref, dactive_ref, lines_ref, dselect_ref,
    gate_sum, out_sum, handed,
    inject_scr, readout_scr, dread_scr, dinject_scr, state_scr, factor_scr,
    rates_scr, rate_scr, delta_ring, drive_ring, grad_ring, silu_ring, sway_ring, active_ring, slope_ring, scan_scr, weight_scr,
    ahead_scr, behind_scr, sums_scr, gated_scr, dgated_scr,
    totals, totals_in, start_scr, incoming_scr, gaps_scr, prefix_send, prefix_recv,
    normed_ref, upstream_ref, late_sem,
    acc, out, landing, extra, send_sem, recv_sem, store_sem,
):
    rows = active_now.shape[0]
    steps = rows // SUB
    step = pl.program_id(0)
    count = rates_scr.shape[0]
    lag = delta_ring.shape[0]
    per = -(-rounds // (lag - 1))
    width = upstream_ref.shape[1]
    prefix = Prefix(
        totals, totals_in, start_scr, incoming_scr, gaps_scr, rates_scr, prefix_send, prefix_recv, rounds
    )
    ex = Exchange(acc, out, landing, extra, send_sem, recv_sem, chunk, landing.shape[0], seq)
    early = begun(count, ex.phases)
    half, unroll = states // 2, 16
    halves = [pl.ds(0, half), pl.ds(half, half)]

    def store(k):
        pair = k // 2

        @pl.when(lax.rem(k, 2) == 0)
        def _():
            store_lanes(out.at[k], gate_sum, pair, store_sem.at[k])

        @pl.when(lax.rem(k, 2) == 1)
        def _():
            store_rows(out.at[k], out_sum, pair, store_sem.at[k])

    def take_turns(place):
        for k, p, now in turns(ex.phases, step - lag, place):

            @pl.when(now)
            def _():
                ex.advance(k, p)
                if p == ex.phases:
                    store(k)

    late_loads = [
        pltpu.make_async_copy(source, target, late_sem.at[i])
        for i, (source, target) in enumerate(((normed_hbm, normed_ref), (upstream_hbm, upstream_ref)))
    ]

    @pl.when(step == 0)
    def _():
        ex.greet()
        for copy in late_loads:
            copy.start()
        for first, scr in ((rank, inject_scr), (rank + states, readout_scr)):
            for n in range(0, states, 2):
                wide = expand_columns(select_ref[...], first + n, 2)
                for side in range(2):
                    scr[:, n + side] = wide[:, side * LANES : (side + 1) * LANES].reshape(steps, SUB, LANES)
        dread_scr[...] = jnp.zeros_like(dread_scr)
        dinject_scr[...] = jnp.zeros_like(dinject_scr)
        start_scr[...] = jnp.zeros_like(start_scr)
        incoming_scr[...] = jnp.zeros_like(incoming_scr)
        gaps_scr[...] = jnp.zeros_like(gaps_scr)
        for e in range(count):
            rates_scr[e] = -jnp.exp(decay_ref[:, e * LANES : (e + 1) * LANES]) * LOG2E
        for copy in late_loads:
            copy.wait()
        ex.welcome()

    flat = lambda value: value.reshape(steps, SUB, LANES)
    zero = jnp.zeros((half, SUB, LANES), F32)

    def spread_rates(tile):
        rates = rates_scr[tile]
        for n in range(states):
            rate_scr[n] = jnp.broadcast_to(rates[n : n + 1], (SUB, LANES))

    def spread(table):
        return jnp.concatenate(
            [jnp.broadcast_to(table[n : n + 1], (1, SUB, LANES)) for n in range(states)], axis=0
        )

    @pl.when(step >= lag)
    def _():
        c = step - lag
        tile = c
        spread_rates(tile)
        slot = lax.rem(c, lag)
        delta_scr, drive_scr, grad_scr = delta_ring.at[slot], drive_ring.at[slot], grad_ring.at[slot]
        total = sums_scr[tile]
        before, after = total, total
        for by in (1, 2, 4):
            before = before + shift_up(before, by, 0.0, False)
            after = after + shift_up(after, by, 0.0, True)
        before, after = before - total, after - total
        state_scr[0] = ahead_scr[tile] + jnp.exp2(before[None] * rate_scr[...]) * spread(start_scr[tile])

        def forward(i, state):
            for u in range(unroll // 2):
                j = i * (unroll // 2) + u
                factor = jnp.exp2(delta_scr[j][None] * rate_scr[...])
                factor_scr[j] = factor
                state = factor * state + drive_scr[j][None] * inject_scr[j]
                state_scr[j + 1] = state
                dread_scr[j] += grad_scr[j][None] * state
                scan_scr[j] = tree_sum(readout_scr[j] * state)
            return state

        lax.fori_loop(0, steps // (unroll // 2), forward, state_scr[0])
        take_turns(0)
        lanes = pl.ds(pl.multiple_of(c * LANES, LANES), LANES)
        skip = skip_ref[:, lanes]
        active = active_ring[slot].reshape(rows, LANES)
        scanned = scan_scr[...].reshape(rows, LANES) + skip * active
        gated = (scanned * silu_ring[slot].reshape(rows, LANES)).astype(BF16)
        gated_ref[...] = gated
        dgate = (scanned * sway_ring[slot].reshape(rows, LANES)).astype(BF16)
        dgate_ref[...] = dgate
        lines_ref[states + 1 : states + 2, :] = jnp.sum(
            grad_scr[...].reshape(rows, LANES) * active, axis=0, keepdims=True
        )
        odd = lax.rem(c, 2)

        @pl.when(odd == 0)
        def _():
            gated_scr[:, :LANES] = gated
            dgated_scr[:, :LANES] = dgate

        @pl.when(odd == 1)
        def _():
            gated_scr[:, LANES:] = gated
            dgated_scr[:, LANES:] = dgate

        adjoint0 = behind_scr[tile] + jnp.exp2(after[None] * rate_scr[...]) * spread(incoming_scr[tile])
        state_scr[steps] = adjoint0
        for h, part in enumerate(halves):

            def backward(i, carry):
                adjoint, total = carry
                for u in range(unroll):
                    j = steps - 1 - (i * unroll + u)
                    d, g = delta_scr[j], grad_scr[j]
                    whole = adjoint + g[None] * readout_scr[j, part]
                    adjoint = factor_scr[j, part] * whole
                    through = adjoint * state_scr[j, part]
                    total = total + through * d[None]
                    dinject_scr[j, part] += whole * drive_scr[j][None]
                    one = tree_sum(through * rate_scr[part])
                    two = tree_sum(whole * inject_scr[j, part])
                    scan_scr[j] = scan_scr[j] + one if h else one
                    weight_scr[j] = weight_scr[j] + two if h else two
                return adjoint, total

            unused, total = lax.fori_loop(0, steps // unroll, backward, (state_scr[steps, part], zero))
            for n in range(half):
                at = h * half + n
                lines_ref[at : at + 1, :] = (
                    jnp.sum(total[n], axis=0, keepdims=True) * rate_scr[at, 0:1] * LN2
                )
        weight = weight_scr[...].reshape(rows, LANES)
        delta = delta_scr[...].reshape(rows, LANES)
        active = active_ring[slot].reshape(rows, LANES)
        dactive_ref[...] = delta * weight + skip_ref[:, lanes] * grad_scr[...].reshape(rows, LANES)
        dpre = (scan_scr[...].reshape(rows, LANES) * LN2 + active * weight) * slope_ring[slot].reshape(rows, LANES)
        dprelow_ref[...] = dpre.astype(BF16)
        lines_ref[states : states + 1, :] = jnp.sum(dpre, axis=0, keepdims=True)

        @pl.when(odd == 1)
        def _():
            pair = c // 2
            part = jnp.dot(normed_ref[...], dgated_scr[...], preferred_element_type=F32).astype(BF16)
            acc[2 * pair, :width, :] = part[:, :LANES]
            acc[2 * pair, width:, :] = part[:, LANES:]
            turned = gated_scr[...].T
            for b in range(width // (2 * LANES)):
                part = jnp.dot(
                    turned, upstream_ref[:, b * 2 * LANES : (b + 1) * 2 * LANES], preferred_element_type=F32
                ).astype(BF16)
                for side in range(2):
                    at = (2 * b + side) * 2 * LANES
                    acc[2 * pair + 1, at : at + 2 * LANES, :] = part[:, side * LANES : (side + 1) * LANES]

        take_turns(1)

    @pl.when(step < count)
    def _():
        tile = step
        spread_rates(tile)
        slot = lax.rem(step, lag)
        delta_scr, drive_scr, grad_scr = delta_ring.at[slot], drive_ring.at[slot], grad_ring.at[slot]
        lanes = pl.ds(pl.multiple_of(tile * LANES, LANES), LANES)
        pre = jnp.dot(select_ref[:, :rank], step_weight_ref[:, lanes], preferred_element_type=F32)
        pre = pre + step_bias_ref[:, lanes]
        small = jnp.exp(-jnp.abs(pre))
        delta = jnp.maximum(pre, 0.0) + jnp.log1p(small)
        slope_ring[slot] = flat(jnp.where(pre >= 0.0, 1.0, small) / (1.0 + small))
        delta_scr[...] = flat(delta)
        active = active_now[...].astype(F32)
        active_ring[slot] = flat(active)
        drive_scr[...] = flat(delta * active)
        gate = gate_now[...].astype(F32)
        sigma = jax.nn.sigmoid(gate)
        silu = gate * sigma
        silu_ring[slot] = flat(silu)
        graded = graded_now[...]
        grad_scr[...] = flat(graded * silu)
        sway_ring[slot] = flat(graded * (sigma * (1.0 + gate * (1.0 - sigma))))
        total = jnp.sum(delta_scr[...], axis=0)
        sums_scr[tile] = total
        whole = jnp.sum(total, axis=0, keepdims=True)
        totals[tile, 2 * states :] = jnp.broadcast_to(whole, (SUB, LANES))
        for h, part in enumerate(halves):

            def ends(i, carry):
                state, message, decay = carry
                for u in range(unroll):
                    j = i * unroll + u
                    factor = jnp.exp2(delta_scr[j][None] * rate_scr[part])
                    state = factor * state + drive_scr[j][None] * inject_scr[j, part]
                    decay = decay * factor
                    message = message + decay * (grad_scr[j][None] * readout_scr[j, part])
                return state, message, decay

            state, message, decay = lax.fori_loop(0, steps // unroll, ends, (zero, zero, zero + 1.0))
            for value, kept, at, reverse in (
                (state, ahead_scr, h * half, False), (message, behind_scr, states + h * half, True)
            ):
                factor = decay
                for by in (1, 2, 4):
                    value = value + factor * shift_up(value, by, 0.0, reverse)
                    factor = factor * shift_up(factor, by, 1.0, reverse)
                kept[tile, part] = shift_up(value, 1, 0.0, reverse)
                last = 0 if reverse else SUB - 1
                for n in range(half):
                    totals[tile, at + n : at + n + 1] = value[n, last : last + 1]

    for r in range(lag - 1, -1, -1):
        e = step - r

        @pl.when((e >= 0) & (e < count))
        def _():
            if r == 0:
                prefix.copy(e, 0).start()
            for done in range((r - 1) * per, min(r * per, rounds)) if r > 0 else ():
                prefix.advance(e, done + 1)

    @pl.when(step == count + lag - 1)
    def _():
        group = 4
        shape = (group * LANES, 2 * states)
        from_lane = lax.broadcasted_iota(jnp.int32, shape, 0) // LANES
        to_column = lax.broadcasted_iota(jnp.int32, shape, 1)
        whole = jnp.zeros((rows, 2 * states), F32)
        for first, scr in ((0, dinject_scr), (states, dread_scr)):
            for n in range(0, states, group):
                ones = (from_lane + (first + n) == to_column).astype(F32).astype(BF16)
                values = [scr[:, n + i].reshape(rows, LANES) for i in range(group)]
                highs = [value.astype(BF16) for value in values]
                lows = [(value - high.astype(F32)).astype(BF16) for value, high in zip(values, highs)]
                for parts in (highs, lows):
                    whole = whole + jnp.dot(jnp.concatenate(parts, axis=1), ones, preferred_element_type=F32)
        dselect_ref[...] = whole

        slots = 2 * count
        for k in range(count):
            for p in range(ex.phases):
                if slots - 2 <= slot_of(k, p) < slots:
                    ex.finish(k, p)
        sizes = []
        for k in range(early, count):
            sizes.append(0)
            for ref, base, size in ex.state(k, next_phase(k, count)):
                here = pl.ds(pl.multiple_of(base, 16), size)
                sizes[-1] += size
                pltpu.make_async_copy(ref.at[k, here, :], handed.at[k - early, here, :], store_sem.at[k]).start()
        for k in range(early):
            wait_rows(out.at[k], store_sem.at[k])
        for k in range(early, count):
            wait_rows(acc.at[k, pl.ds(0, sizes[k - early]), :], store_sem.at[k])


def run_scan(active, gate, graded, select, step_weight, step_bias, decay_log, skip, normed, upstream, seq):
    rows, inner = active.shape
    rank = step_weight.shape[0]
    states = decay_log.shape[0]
    width = upstream.shape[1]
    chunk = 2 * width
    tiles, steps = inner // LANES, rows // SUB
    rounds = seq.bit_length() - 1
    phases = 8 + max(rounds - 3, 0)
    early = begun(tiles, phases)
    gates, outs = (early + 1) // 2 * 2 * LANES, early // 2 * 2 * LANES
    lag = min(rounds, 3) + 1
    now = pl.BlockSpec((rows, LANES), lambda i: (0, lax.min(i, tiles - 1)))
    late = lambda shape: pl.BlockSpec(shape, lambda i: (0, lax.max(i - lag, 0)))
    whole = lambda a: pl.BlockSpec(a.shape, lambda i: (0, 0), pipeline_mode=pl.Buffered(1))
    hbm = pl.BlockSpec(memory_space=pltpu.HBM)
    wide = pltpu.VMEM((steps, states, SUB, LANES), F32)
    thin = pltpu.VMEM((steps, SUB, LANES), F32)
    cube = pltpu.VMEM((tiles, states, SUB, LANES), F32)
    small = pltpu.VMEM((tiles, states, LANES), F32)
    pair = pltpu.VMEM((rows, 2 * LANES), BF16)
    buffers = scratch(tiles, chunk, tiles // 2, seq)
    buffers[1] = pltpu.VMEM((begun(tiles, phases - 5), chunk, LANES), BF16)
    ring = pltpu.VMEM((lag, steps, SUB, LANES), F32)
    return pl.pallas_call(
        functools.partial(scan_kernel, rank, states, chunk, rounds, seq),
        grid=(tiles + lag,),
        in_specs=[
            now, now, now, whole(select), whole(step_weight), whole(step_bias), whole(decay_log), whole(skip),
            hbm, hbm,
        ],
        out_specs=[
            late((rows, LANES)), late((rows, LANES)), late((rows, LANES)), late((rows, LANES)),
            late((states + SUB, LANES)), pl.BlockSpec((rows, 2 * states), lambda i: (0, 0)), hbm, hbm, hbm,
        ],
        out_shape=[
            jax.ShapeDtypeStruct((rows, inner), BF16),
            jax.ShapeDtypeStruct((rows, inner), BF16),
            jax.ShapeDtypeStruct((rows, inner), BF16),
            jax.ShapeDtypeStruct((rows, inner), F32),
            jax.ShapeDtypeStruct((states + SUB, inner), F32),
            jax.ShapeDtypeStruct((rows, 2 * states), F32),
            jax.ShapeDtypeStruct((width, gates), BF16),
            jax.ShapeDtypeStruct((outs, width), BF16),
            jax.ShapeDtypeStruct((tiles - early, chunk, LANES), BF16),
        ],
        scratch_shapes=[
            wide, wide, wide, wide,
            pltpu.VMEM((steps + 1, states, SUB, LANES), F32), wide,
            small, pltpu.VMEM((states, SUB, LANES), F32), ring, ring, ring, ring, ring, ring, ring, thin, thin,
            cube, cube, pltpu.VMEM((tiles, SUB, LANES), F32), pair, pair,
            pltpu.VMEM((tiles, 2 * states + SUB, LANES), F32),
            pltpu.VMEM((tiles, rounds, 2 * states + SUB, LANES), F32),
            small, small, pltpu.VMEM((tiles, SUB, LANES), F32),
            pltpu.SemaphoreType.DMA((tiles, rounds)), pltpu.SemaphoreType.DMA((tiles, rounds)),
            pltpu.VMEM(normed.shape, BF16), pltpu.VMEM(upstream.shape, BF16), pltpu.SemaphoreType.DMA((2,)),
        ]
        + buffers
        + [pltpu.SemaphoreType.DMA((tiles,))],
        compiler_params=pltpu.CompilerParams(
            collective_id=1, has_side_effects=True, vmem_limit_bytes=62 << 20
        ),
        name="span_scan",
    )(
        active, gate, graded, select, step_weight, step_bias, decay_log, skip, normed, upstream
    )


def bit_of(index, step):
    return (index // step) % 2

def other(axis, step):
    place = lax.axis_index(axis)
    place = place + step * (1 - 2 * bit_of(place, step))
    if axis == "dp":
        return (place, lax.axis_index("seq"))
    return (lax.axis_index("dp"), place)

CORE, X, Y = ("seq", 1), ("dp", 1), ("dp", 2)

def wait_rows(rows, sem):
    pltpu.make_async_copy(rows, rows, sem).wait()


def store_lanes(source, target, pair, sem):
    width = target.shape[0]
    for side in range(2):
        lanes = pl.ds(pl.multiple_of((2 * pair + side) * LANES, LANES), LANES)
        pltpu.make_async_copy(source.at[pl.ds(side * width, width), :], target.at[:, lanes], sem).start()


def store_rows(source, target, pair, sem):
    tall = 2 * LANES
    rows = pl.ds(pl.multiple_of(pair * tall, tall), tall)
    for b in range(target.shape[1] // LANES):
        pltpu.make_async_copy(
            source.at[pl.ds(b * tall, tall), :], target.at[rows, pl.ds(b * LANES, LANES)], sem
        ).start()


class Exchange:
    levels = 4

    def __init__(self, acc, out, landing, extra, send_sem, recv_sem, rows, window, seq):
        self.acc, self.out, self.landing, self.extra = acc, out, landing, extra
        self.send_sem, self.recv_sem = send_sem, recv_sem
        self.rows, self.window = rows, window
        self.more = [("seq", 8 << i) for i in range(12) if (8 << i) < seq]
        self.orders = ((CORE, X, Y), (CORE, Y, X))
        self.back = self.levels + len(self.more)
        self.phases = self.back + self.levels
        place = lax.axis_index("seq")
        self.quarter = (place // 2) % 4
        self.core_base = bit_of(place, 1) * (rows // 2)
        self.kept = []
        for s, order in enumerate(self.orders):
            base, size = self.core_base + s * (rows // 4), rows // 4
            spans = [(base, size)]
            for axis, step in order[1:]:
                size = size // 2
                base = base + bit_of(lax.axis_index(axis), step) * size
                spans.append((base, size))
            size = size // 4
            spans.append((base + self.quarter * size, size))
            self.kept.append(spans)

    def partners(self):
        links = [CORE, X, Y] + self.more
        return [other(*link) for link in links] + [self.along(i) for i in range(1, 4)]

    def greet(self):
        for device in self.partners():
            pl.semaphore_signal(pltpu.get_barrier_semaphore(), inc=1, device_id=device, device_id_type=MESH)

    def welcome(self):
        pl.semaphore_wait(pltpu.get_barrier_semaphore(), len(self.partners()))

    def along(self, i):
        place = lax.axis_index("seq")
        return (lax.axis_index("dp"), place + 2 * (lax.rem(self.quarter + i, 4) - self.quarter))

    def span(self, ref, k, base, size):
        return ref.at[k, pl.ds(pl.multiple_of(base, 16), size), :]

    def land(self, p):
        rows = self.rows
        return [0, rows // 2, rows // 2 + rows // 4, rows // 2 + rows // 4 + rows // 8][p]

    def rows_of(self, p):
        rows, last = self.rows, self.phases - 1
        if self.levels <= p < self.back:
            return rows // 32
        return [rows // 2, rows // 4, rows // 8, 6 * rows // 64][min(p, last - p)]

    def copies(self, k, p):
        w = lax.rem(k, self.window)
        rows = self.rows
        if p == 0:
            return [(self.span(self.acc, k, rows // 2 - self.core_base, rows // 2),
                     self.landing.at[w, pl.ds(0, rows // 2), :], other(*CORE))]
        if p == self.phases - 1:
            half = self.span(self.out, k, self.core_base, rows // 2)
            return [(half, half, other(*CORE))]
        found = []
        for s in range(2):
            if p < self.levels - 1:
                size = self.kept[s][p][1]
                axis, step = self.orders[s][p]
                base = self.kept[s][p - 1][0] + (1 - bit_of(lax.axis_index(axis), step)) * size
                target = self.landing.at[w, pl.ds(self.land(p) + s * size, size), :]
                found.append((self.span(self.acc, k, base, size), target, other(axis, step)))
            elif p == self.levels - 1:
                first, size = self.kept[s][p - 1][0], self.kept[s][p][1]
                for i in range(1, 4):
                    base = first + lax.rem(self.quarter + i, 4) * size
                    target = self.landing.at[w, pl.ds(self.land(p) + (3 * s + i - 1) * size, size), :]
                    found.append((self.span(self.acc, k, base, size), target, self.along(i)))
            elif p < self.back:
                base, size = self.kept[s][-1]
                target = self.extra.at[w, p - self.levels, pl.ds(s * size, size), :]
                found.append((self.span(self.acc, k, base, size), target, other(*self.more[p - self.levels])))
            else:
                level = self.phases - 1 - p
                piece = self.span(self.out, k, *self.kept[s][level])
                devices = [self.along(i) for i in range(1, 4)] if level == 3 else [other(*self.orders[s][level])]
                found += [(piece, piece, device) for device in devices]
        return found

    def add(self, k, base, size, sources, target):
        step = min(size, 256)

        def body(i, _):
            here = pl.ds(pl.multiple_of(base + i * step, 16), step)
            total = self.acc[k, here, :].astype(F32)
            for ref, index, first in sources:
                there = pl.ds(pl.multiple_of(first + i * step, 16), step)
                total = total + ref[index + (there,)].astype(F32)
            target[k, here, :] = total.astype(BF16)
            return 0

        lax.fori_loop(0, size // step, body, 0)

    def finish(self, k, p):
        w = lax.rem(k, self.window)
        rows = self.acc.at[k, pl.ds(0, self.rows_of(p)), :]
        copy = pltpu.make_async_remote_copy(
            src_ref=rows, dst_ref=rows, send_sem=self.send_sem.at[w, p], recv_sem=self.recv_sem.at[w, p],
            device_id=other(*CORE), device_id_type=MESH,
        )
        copy.wait_send()
        copy.wait_recv()
        target = self.out if p == self.back - 1 else self.acc
        if p == 0:
            self.add(k, self.core_base, self.rows // 2, [(self.landing, (w,), 0)], target)
        elif p < self.back:
            for s in range(2):
                base, size = self.kept[s][min(p, self.levels - 1)]
                if p < self.levels - 1:
                    sources = [(self.landing, (w,), self.land(p) + s * size)]
                elif p < self.levels:
                    sources = [(self.landing, (w,), self.land(p) + (3 * s + i) * size) for i in range(3)]
                else:
                    sources = [(self.extra, (w, p - self.levels), s * size)]
                self.add(k, base, size, sources, target)

    def start(self, k, p):
        w = lax.rem(k, self.window)
        for source, target, device in self.copies(k, p):
            pltpu.make_async_remote_copy(
                src_ref=source, dst_ref=target, send_sem=self.send_sem.at[w, p], recv_sem=self.recv_sem.at[w, p],
                device_id=device, device_id_type=MESH,
            ).start()

    def advance(self, k, p):
        if p > 0:
            self.finish(k, p - 1)
        if p < self.phases:
            self.start(k, p)

    def state(self, k, p):
        rows = self.rows
        if p == 0:
            return [(self.acc, 0, rows)]
        if p == self.phases:
            return [(self.out, 0, rows)]
        level = min(p - 1, self.levels - 1) if p < self.back else self.phases - 1 - p
        spans = [(self.core_base, rows // 2)] if level == 0 else [self.kept[s][level] for s in range(2)]
        return [(self.acc if p < self.back else self.out, base, size) for base, size in spans]


def scratch(chunks, rows, window, seq):
    more = len([1 for i in range(12) if (8 << i) < seq])
    return [
        pltpu.VMEM((chunks, rows, LANES), BF16),
        pltpu.VMEM((chunks, rows, LANES), BF16),
        pltpu.VMEM((window, rows, LANES), BF16),
        pltpu.VMEM((window, max(more, 1), rows // 32, LANES), BF16),
        pltpu.SemaphoreType.DMA((window, 8 + more)),
        pltpu.SemaphoreType.DMA((window, 8 + more)),
    ]


def tail_kernel(
    rank, states, chunk, seq,
    dprelow_ref, select_ref, dpair_ref, step_weight_ref, normed_ref, upstream_hbm, inputs_hbm, scale_ref, hot_hbm,
    gain_ref, dactive_first_ref, mixed_first_ref, select_weight_ref, halo_ref, lines_ref,
    dactive_ref, mixed_ref, front_ref, active_ref, select_tile_ref, conv_ref, front_weight_ref, gate_weight_ref,
    dgate_ref, gated_ref, out_weight_ref, handed,
    output_ref, dinputs_ref, front_sum, gate_rest, out_rest, embedding_sum, wide_sum, mixed_sum,
    upstream_ref, inputs_ref, hot_ref, late_sem, dselect_scr, first_scr, after_scr, spread_scr, extended_scr, dnormed_scr, result_scr, misc_scr, gain_scr,
    acc, out, landing, extra, send_sem, recv_sem, load_sem, store_sem, first_send, first_recv,
):
    step = pl.program_id(0)
    rows, width = upstream_ref.shape
    across = width // LANES
    inner = dprelow_ref.shape[1]
    tiles, pairs = inner // LANES, inner // (2 * LANES)
    tall = 2 * LANES
    kernel = conv_ref.shape[0]
    halo = kernel - 1
    vocab = embedding_sum.shape[0]
    ex = Exchange(acc, out, landing, extra, send_sem, recv_sem, chunk, landing.shape[0], seq)
    early = begun(tiles, ex.phases)
    old = tiles - early
    embedding_at, wide_at, mixed_at = (old + pairs + i for i in range(3))
    count = old + pairs + 3
    place = lax.axis_index("seq")
    here_dp = lax.axis_index("dp")

    def add(scr, value):
        for b in range(across):
            scr[b] += value[:, b * LANES : (b + 1) * LANES]

    def put(scr, here, value):
        for b in range(across):
            scr[b, here, :] = value[:, b * LANES : (b + 1) * LANES]

    def take(scr, here):
        return jnp.concatenate([scr[b, here, :] for b in range(across)], axis=1)

    def first_copy():
        return pltpu.make_async_remote_copy(
            src_ref=first_scr, dst_ref=after_scr, send_sem=first_send, recv_sem=first_recv,
            device_id=(here_dp, lax.rem(place + seq - 1, seq)), device_id_type=MESH,
        )

    late_loads = [
        pltpu.make_async_copy(source, target, late_sem.at[i])
        for i, (source, target) in enumerate(
            ((upstream_hbm, upstream_ref), (inputs_hbm, inputs_ref), (hot_hbm, hot_ref))
        )
    ]

    def greet():
        barrier = pltpu.get_barrier_semaphore()
        ex.greet()
        for there, by in ((place > 0, -1), (place < seq - 1, 1)):

            @pl.when(there)
            def _():
                pl.semaphore_signal(barrier, inc=1, device_id=(here_dp, place + by), device_id_type=MESH)

    def welcome():
        barrier = pltpu.get_barrier_semaphore()
        neighbours = 2 - (place == 0).astype(jnp.int32) - (place == seq - 1).astype(jnp.int32)
        pl.semaphore_wait(barrier, len(ex.partners()) + neighbours)

    def store(k):
        pair = (k + early) // 2

        @pl.when((k < old) & (lax.rem(k + early, 2) == 0))
        def _():
            store_lanes(out.at[k], gate_rest, pair - (early + 1) // 2, store_sem.at[k])

        @pl.when((k < old) & (lax.rem(k + early, 2) == 1))
        def _():
            store_rows(out.at[k], out_rest, pair - early // 2, store_sem.at[k])

        @pl.when((k >= old) & (k < embedding_at))
        def _():
            store_lanes(out.at[k], front_sum, k - old, store_sem.at[k])

        @pl.when(k == embedding_at)
        def _():
            for b in range(width // LANES):
                pltpu.make_async_copy(
                    out.at[k, pl.ds(b * vocab, vocab), :], embedding_sum.at[:, pl.ds(b * LANES, LANES)], store_sem.at[k]
                ).start()

        @pl.when(k == wide_at)
        def _():
            pltpu.make_async_copy(out.at[k], wide_sum, store_sem.at[k]).start()

        @pl.when(k == mixed_at)
        def _():
            pltpu.make_async_copy(out.at[k], mixed_sum, store_sem.at[k]).start()

    def old_turns(spot):
        for k, p, now in turns(ex.phases, tiles + step, spot):
            k = k - early

            @pl.when(now & (k >= 0) & (k < old))
            def _():
                if p > 0:

                    @pl.when(step > 0)
                    def _():
                        ex.finish(k, p - 1)

                if p < ex.phases:
                    ex.start(k, p)
                else:
                    store(k)

    def new_turns(turn):
        for p in range(ex.phases, -1, -1):
            k = old + turn - 2 * p

            @pl.when((k >= old) & (k < count))
            def _():
                ex.advance(k, p)
                if p == ex.phases:
                    store(k)

    @pl.when(step == 0)
    def _():
        greet()
        sizes = []
        for k in range(old):
            sizes.append(0)
            for ref, base, size in ex.state(k, next_phase(k + early, tiles)):
                here = pl.ds(pl.multiple_of(base, 16), size)
                sizes[-1] += size
                pltpu.make_async_copy(handed.at[k, here, :], ref.at[k, here, :], load_sem.at[k]).start()
        for copy in late_loads:
            copy.start()
        dlow = contract_cols(dprelow_ref[...], step_weight_ref[...])
        dselect_scr[...] = jnp.concatenate([dlow, dpair_ref[...]], axis=1).astype(BF16)
        some = jnp.dot(dselect_scr[: (halo + 1) * SUB], select_weight_ref[...], preferred_element_type=F32)
        some = (dactive_first_ref[...] + some[: halo * SUB]) * silu_slope(mixed_first_ref[...])
        for i in range(halo):
            first_scr[i : i + 1, :] = some[i * SUB : i * SUB + 1, :]
        first_scr[halo:, :] = jnp.zeros((SUB - halo, inner), F32)
        welcome()

        @pl.when(place > 0)
        def _():
            first_copy().start()

        dnormed_scr[...] = jnp.zeros_like(dnormed_scr)
        result_scr[...] = jnp.zeros_like(result_scr)
        misc_scr[...] = jnp.zeros_like(misc_scr)
        misc_scr[kernel + 1 : kernel + 3, :] = lines_ref[states : states + 2, :]
        acc[wide_at] = jnp.zeros_like(acc[wide_at])
        acc[mixed_at] = jnp.zeros_like(acc[mixed_at])
        for b in range(tiles):
            at = rank * tiles + b * states
            acc[mixed_at, at : at + states, :] = lines_ref[:states, b * LANES : (b + 1) * LANES].astype(BF16)
        for k in range(old):
            wait_rows(acc.at[k, pl.ds(0, sizes[k]), :], load_sem.at[k])

    old_turns(0)

    @pl.when(step < pairs)
    def _():
        add(result_scr, jnp.dot(gated_ref[...], out_weight_ref[...], preferred_element_type=F32))
        add(dnormed_scr, contract_cols(dgate_ref[...], gate_weight_ref[...]))

    old_turns(1)

    @pl.when(step < pairs)
    def _():
        lanes = pl.ds(pl.multiple_of(step * tall, tall), tall)
        mixed = mixed_ref[...]
        back = jnp.dot(dselect_scr[...], select_tile_ref[...], preferred_element_type=F32)
        dmixed = (dactive_ref[...] + back) * silu_slope(mixed)
        spread_scr[:rows] = dmixed
        extended_scr[: halo * SUB] = halo_ref[...]
        extended_scr[halo * SUB :] = front_ref[...].astype(F32)
        misc_scr[kernel : kernel + 1, lanes] = jnp.sum(dmixed, axis=0, keepdims=True)
        for i in range(kernel):
            misc_scr[i : i + 1, lanes] = jnp.sum(
                dmixed * extended_scr[i * SUB : i * SUB + rows], axis=0, keepdims=True
            )
        wide = contract_rows(dselect_scr[...], active_ref[...]).astype(BF16)
        columns = wide.shape[0]
        for side in range(2):
            at = pl.ds(pl.multiple_of((2 * step + side) * columns, columns), columns)
            acc[wide_at, at, :] = wide[:, side * LANES : (side + 1) * LANES]
        part = contract_rows(select_ref[:, :rank], dprelow_ref[:, lanes]).astype(BF16)
        for side in range(2):
            at = pl.ds(pl.multiple_of((2 * step + side) * rank, rank), rank)
            acc[mixed_at, at, :] = part[:, side * LANES : (side + 1) * LANES]

        @pl.when(step == 0)
        def _():
            @pl.when(place > 0)
            def _():
                first_copy().wait_send()

            @pl.when(place < seq - 1)
            def _():
                first_copy().wait_recv()

            @pl.when(place == seq - 1)
            def _():
                after_scr[...] = jnp.zeros_like(after_scr)

        sub = lax.broadcasted_iota(jnp.int32, (SUB, tall), 0)
        for i in range(halo):
            own = pltpu.roll(spread_scr[i * SUB : (i + 1) * SUB, :], SUB - 1, 0)
            spread_scr[rows + i * SUB : rows + (i + 1) * SUB] = jnp.where(
                sub < SUB - 1, own, after_scr[i : i + 1, lanes]
            )
        dfront = conv_ref[halo : halo + 1] * spread_scr[:rows]
        for i in range(1, kernel):
            dfront = dfront + conv_ref[halo - i : halo - i + 1] * spread_scr[i * SUB : i * SUB + rows]
        dfront = dfront.astype(BF16)
        part = jnp.dot(normed_ref[...], dfront, preferred_element_type=F32).astype(BF16)
        acc[old + step, :width, :] = part[:, :LANES]
        acc[old + step, width:, :] = part[:, LANES:]
        add(dnormed_scr, contract_cols(dfront, front_weight_ref[...]))

    @pl.when(step == pairs)
    def _():
        for copy in late_loads:
            copy.wait()
        part = rows // SUB

        def norms(i, total):
            here = pl.ds(pl.multiple_of(i * part, part), part)
            dnormed, inputs, scale = take(dnormed_scr, here), inputs_ref[here, :], scale_ref[here, :]
            scaled = gain_ref[...] * dnormed
            mean = jnp.sum(scaled * inputs, axis=1, keepdims=True) * (1.0 / width)
            put(
                dnormed_scr, here,
                upstream_ref[here, :].astype(F32) + scale * scaled - inputs * (scale * scale * scale * mean),
            )
            put(result_scr, here, take(result_scr, here) + inputs)
            return total + jnp.sum((dnormed * inputs * scale).reshape(-1, SUB, width), axis=0)

        total = lax.fori_loop(0, SUB, norms, jnp.zeros((SUB, width), F32))
        gain_scr[...] = jnp.sum(total, axis=0, keepdims=True)
        for b in range(width // tall):
            value = jnp.concatenate([dnormed_scr[2 * b], dnormed_scr[2 * b + 1]], axis=1)
            high = value.astype(BF16)
            low = (value - high.astype(F32)).astype(BF16)
            whole = jnp.dot(hot_ref[...], high, preferred_element_type=F32)
            whole = (whole + jnp.dot(hot_ref[...], low, preferred_element_type=F32)).astype(BF16)
            for side in range(2):
                at = (2 * b + side) * vocab
                acc[embedding_at, at : at + vocab, :] = whole[:, side * LANES : (side + 1) * LANES]
        at = (rank + states) * tiles
        for b in range(tiles):
            acc[mixed_at, at + b * 16 : at + (b + 1) * 16, :] = misc_scr[:, b * LANES : (b + 1) * LANES].astype(BF16)
        at = (rank + states + 16) * tiles
        for b in range(width // LANES):
            acc[mixed_at, at + b * 16 : at + (b + 1) * 16, :] = jnp.broadcast_to(
                gain_scr[:, b * LANES : (b + 1) * LANES], (16, LANES)
            ).astype(BF16)

    @pl.when(step == pairs + 1)
    def _():
        span = rows // SUB
        for i in range(SUB):
            for b in range(across):
                lanes, every = slice(b * LANES, (b + 1) * LANES), pl.ds(i, span, stride=SUB)
                dinputs_ref[i * span : (i + 1) * span, lanes] = dnormed_scr[b, every, :]
                output_ref[i * span : (i + 1) * span, lanes] = result_scr[b, every, :].astype(BF16)

    new_turns(step)

    @pl.when(step == pl.num_programs(0) - 1)
    def _():
        def rest(turn, _):
            new_turns(turn)
            return 0

        lax.fori_loop(pairs + 3, pairs + 3 + 2 * ex.phases, rest, 0)
        for k in range(count):
            wait_rows(out.at[k], store_sem.at[k])


def run_tail(
    d_pre_low, select, d_pair, step_weight, normed, upstream, inputs, scale, hot, gain, d_active, mixed, select_weight,
    halo, lines, front, active, conv_weight, input_weight, d_gate, gated, output_weight, handed, vocab, seq,
):
    rows, inner = front.shape
    width = inputs.shape[1]
    rank, states = step_weight.shape[0], lines.shape[0] - SUB
    chunk = 2 * width
    tiles, pairs, tall = inner // LANES, inner // (2 * LANES), 2 * LANES
    phases = 8 + max(seq.bit_length() - 4, 0)
    early = begun(tiles, phases)
    count = tiles - early + pairs + 3
    some = halo.shape[0]
    at = lambda i: lax.min(i, pairs - 1)
    whole = lambda a: pl.BlockSpec(a.shape, lambda i: (0, 0), pipeline_mode=pl.Buffered(1))
    first = pl.BlockSpec((some, inner), lambda i: (0, 0), pipeline_mode=pl.Buffered(1))
    tile = lambda height: pl.BlockSpec((height, tall), lambda i: (0, at(i)))
    high = lambda wide: pl.BlockSpec((tall, wide), lambda i: (at(i), 0))
    hbm = pl.BlockSpec(memory_space=pltpu.HBM)
    fixed = pl.BlockSpec((rows, width), lambda i: (0, 0))
    gates, outs = inner - (early + 1) // 2 * tall, inner - early // 2 * tall
    return pl.pallas_call(
        functools.partial(tail_kernel, rank, states, chunk, seq),
        grid=(pairs + 3,),
        in_specs=[
            whole(d_pre_low), whole(select), whole(d_pair), whole(step_weight), whole(normed), hbm,
            hbm, whole(scale), hbm, whole(gain), first, first, whole(select_weight), tile(some),
            whole(lines), tile(rows), tile(rows), tile(rows), tile(rows),
            tile(select_weight.shape[0]), tile(conv_weight.shape[0]), tile(width),
            pl.BlockSpec((width, tall), lambda i: (0, at(i) + pairs)), tile(rows), tile(rows), high(width), hbm,
        ],
        out_specs=[fixed, fixed, hbm, hbm, hbm, hbm, hbm, hbm],
        out_shape=[
            jax.ShapeDtypeStruct((rows, width), BF16),
            jax.ShapeDtypeStruct((rows, width), F32),
            jax.ShapeDtypeStruct((width, inner), BF16),
            jax.ShapeDtypeStruct((width, gates), BF16),
            jax.ShapeDtypeStruct((outs, width), BF16),
            jax.ShapeDtypeStruct((vocab, width), BF16),
            jax.ShapeDtypeStruct((chunk, LANES), BF16),
            jax.ShapeDtypeStruct((chunk, LANES), BF16),
        ],
        scratch_shapes=[
            pltpu.VMEM(upstream.shape, BF16), pltpu.VMEM(inputs.shape, F32), pltpu.VMEM(hot.shape, BF16),
            pltpu.SemaphoreType.DMA((3,)),
            pltpu.VMEM(select.shape, BF16),
            pltpu.VMEM((SUB, inner), F32), pltpu.VMEM((SUB, inner), F32),
            pltpu.VMEM((rows + some, tall), F32), pltpu.VMEM((rows + some, tall), F32),
            pltpu.VMEM((width // LANES, rows, LANES), F32), pltpu.VMEM((width // LANES, rows, LANES), F32),
            pltpu.VMEM((16, inner), F32), pltpu.VMEM((1, width), F32),
        ]
        + scratch(count, chunk, 8, seq)
        + [
            pltpu.SemaphoreType.DMA((count,)), pltpu.SemaphoreType.DMA((count,)),
            pltpu.SemaphoreType.DMA, pltpu.SemaphoreType.DMA,
        ],
        compiler_params=pltpu.CompilerParams(
            collective_id=2, has_side_effects=True, vmem_limit_bytes=62 << 20
        ),
        name="span_tail",
    )(
        d_pre_low, select, d_pair, step_weight, normed, upstream, inputs, scale, hot, gain, d_active, mixed,
        select_weight, halo, lines, d_active, mixed, front, active, select_weight, conv_weight,
        input_weight, input_weight, d_gate, gated, output_weight, handed,
    )


def widen_kernel(
    rank, states, columns, parts, slots,
    front, gate, gate_rest, outs, outs_rest, output, dinputs, embedding, wide_sum, mixed_sum,
    input_to, output_weight_to, output_to, dinputs_to, *rest,
):
    small_to, scratches = rest[:9], rest[9:]
    (
        input_scr, outs_scr, wide_input, wide_outs, output_scr, dinputs_scr, embedding_ref, wide_ref, mixed_ref,
        load_sem, outs_load, store_sem, outs_store, pass_sem, small_load, small_store,
    ) = scratches[:16]
    small_scr = scratches[16:]
    small = [
        pltpu.make_async_copy(source, scr, small_load.at[i])
        for i, (source, scr) in enumerate(((embedding, embedding_ref), (wide_sum, wide_ref), (mixed_sum, mixed_ref)))
    ]
    small_out = [
        pltpu.make_async_copy(scr, to, small_store.at[i]) for i, (scr, to) in enumerate(zip(small_scr, small_to))
    ]
    passed = [
        (pltpu.make_async_copy(source, scr, pass_sem.at[i]), pltpu.make_async_copy(scr, to, pass_sem.at[i]))
        for i, (source, scr, to) in enumerate(((output, output_scr, output_to), (dinputs, dinputs_scr, dinputs_to)))
    ]
    thick, tall = input_scr.shape[0] // parts, outs_scr.shape[0] // parts
    early = outs.shape[0] // tall
    for i in range(parts):
        here, lane = pl.ds(i * thick, thick), 0
        for source in (front, gate, gate_rest):
            lanes = pl.ds(lane, source.shape[1])
            pltpu.make_async_copy(source.at[here, :], input_scr.at[here, lanes], load_sem.at[i]).start()
            lane += source.shape[1]
        source, at = (outs, i) if i < early else (outs_rest, i - early)
        there = pl.ds(i * tall, tall)
        pltpu.make_async_copy(source.at[pl.ds(at * tall, tall), :], outs_scr.at[there, :], outs_load.at[i]).start()
    for copy, unused in passed:
        copy.start()
    for copy in small:
        copy.start()

    def unpack():
        embedding_to, select_to, step_to, decay_to, conv_to, gain_to, *line_to = small_scr
        for copy in small:
            copy.wait()
        embedding_to[...] = embedding_ref[...].astype(F32)
        for source, whole in (
            (wide_ref, ((select_to, columns),)),
            (mixed_ref, ((step_to, rank), (decay_to, states), (conv_to, 16), (gain_to, 16))),
        ):
            at = 0
            for to, height in whole:
                for b in range(to.shape[1] // LANES):
                    part = source[at : at + height, :].astype(F32)
                    lanes = slice(b * LANES, (b + 1) * LANES)
                    to[:, lanes] = part[: to.shape[0]]
                    if to is conv_to:
                        for i, line in enumerate(line_to):
                            line[:, lanes] = part[to.shape[0] + i : to.shape[0] + i + 1]
                    at += height
        for copy in small_out:
            copy.start()

    for i in range(parts):
        if i == parts // 2:
            for first, second in passed:
                first.wait()
                second.start()
            unpack()
        slot = i % slots
        for narrow, wide, to, size, load, store in (
            (input_scr, wide_input, input_to, thick, load_sem, store_sem),
            (outs_scr, wide_outs, output_weight_to, tall, outs_load, outs_store),
        ):
            here, half = pl.ds(i * size, size), size // 2
            wait_rows(narrow.at[here, :], load.at[i])
            if i >= slots:
                wait_rows(wide.at[slot], store.at[slot])
            wide[slot] = narrow[here, :].astype(F32)
            for j in range(2):
                pltpu.make_async_copy(
                    wide.at[slot, pl.ds(j * half, half), :], to.at[pl.ds(i * size + j * half, half), :], store.at[slot]
                ).start()
    for slot in range(slots):
        wait_rows(wide_input.at[slot], store_sem.at[slot])
        wait_rows(wide_outs.at[slot], outs_store.at[slot])
    for unused, copy in passed:
        copy.wait()
    for copy in small_out:
        copy.wait()


def run_widen(
    front, gate, gate_rest, out, out_rest, output, d_inputs, embedding, wide, mixed, rank, states, columns, kernel
):
    width, inner = front.shape
    vocab = embedding.shape[0]
    parts, slots = inner // (2 * LANES), 4
    hbm = pl.BlockSpec(memory_space=pltpu.HBM)
    shapes = [
        (width, 2 * inner), (inner, width), output.shape, d_inputs.shape, (vocab, width), (columns, inner), (rank, inner),
        (states, inner), (kernel, inner), (1, width), (1, inner), (1, inner), (1, inner),
    ]
    return pl.pallas_call(
        functools.partial(widen_kernel, rank, states, columns, parts, slots),
        in_specs=[hbm] * 10,
        out_specs=[hbm] * len(shapes),
        out_shape=[
            jax.ShapeDtypeStruct(shape, output.dtype if i == 2 else F32) for i, shape in enumerate(shapes)
        ],
        scratch_shapes=[
            pltpu.VMEM((width, 2 * inner), BF16), pltpu.VMEM((inner, width), BF16),
            pltpu.VMEM((slots, width // parts, 2 * inner), F32), pltpu.VMEM((slots, inner // parts, width), F32),
            pltpu.VMEM(output.shape, output.dtype), pltpu.VMEM(d_inputs.shape, F32),
            pltpu.VMEM(embedding.shape, BF16), pltpu.VMEM(wide.shape, BF16), pltpu.VMEM(mixed.shape, BF16),
            pltpu.SemaphoreType.DMA((parts,)), pltpu.SemaphoreType.DMA((parts,)),
            pltpu.SemaphoreType.DMA((slots,)), pltpu.SemaphoreType.DMA((slots,)), pltpu.SemaphoreType.DMA((2,)),
            pltpu.SemaphoreType.DMA((3,)), pltpu.SemaphoreType.DMA((len(shapes) - 4,)),
        ]
        + [pltpu.VMEM(shape, F32) for shape in shapes[4:]],
        compiler_params=pltpu.CompilerParams(vmem_limit_bytes=62 << 20),
        name="sums_to_float32",
    )(front, gate, gate_rest, out, out_rest, output, d_inputs, embedding, wide, mixed)


def on_device(
    byte_ids,
    embedding,
    cotangent,
    norm_gain,
    input_projection_weight,
    conv_weight,
    conv_bias,
    select_weight,
    step_weight,
    step_bias,
    decay_log,
    skip_gain,
    output_projection_weight,
):
    count, stretch = byte_ids.shape
    vocab, width = embedding.shape
    kernel, inner = conv_weight.shape
    states = decay_log.shape[0]
    rank = step_weight.shape[0]
    rows = count * stretch
    seq = lax.axis_size("seq")
    gain, turned_select = norm_gain.reshape(1, width), select_weight.T
    (
        block_inputs, scale, unused, turned, upstream, hot, front, earlier, mixed, active, gate, graded, select
    ) = run_front(
        byte_ids.reshape(1, rows), embedding, cotangent.reshape(rows, width), gain, input_projection_weight,
        output_projection_weight, conv_weight, conv_bias.reshape(1, inner), turned_select, seq,
    )
    (
        gated, d_gate, d_pre_low, d_active, lines, d_pair, gate_sum, out_sum, handed
    ) = run_scan(
        active, gate, graded, select, step_weight, step_bias.reshape(1, inner), decay_log, skip_gain.reshape(1, inner),
        turned, upstream, seq,
    )
    output, d_inputs, front_sum, gate_rest, out_rest, embedding_sum, wide_sum, mixed_sum = run_tail(
        d_pre_low, select, d_pair, step_weight, turned, upstream, block_inputs, scale, hot, gain,
        d_active, mixed, turned_select, earlier, lines, front, active, conv_weight,
        input_projection_weight, d_gate, gated, output_projection_weight, handed, vocab, seq,
    )
    (
        d_input_weight, d_output_weight, output, d_inputs, d_embedding, d_select_weight, d_step_weight, d_decay_log, d_conv_weight,
        d_norm_gain, d_conv_bias, d_step_bias, d_skip_gain,
    ) = run_widen(
        front_sum, gate_sum, gate_rest, out_sum, out_rest, output, d_inputs, embedding_sum, wide_sum, mixed_sum, rank, states,
        select_weight.shape[1], kernel,
    )
    return (
        output.reshape(count, stretch, width),
        d_inputs.reshape(count, stretch, width),
        d_embedding,
        d_norm_gain[0],
        d_input_weight,
        d_conv_weight,
        d_conv_bias[0],
        d_select_weight.T,
        d_step_weight,
        d_step_bias[0],
        d_decay_log,
        d_skip_gain[0],
        d_output_weight,
    )


def solution(mesh):
    placed = (P("dp", "seq"), P(), P("dp", "seq", None)) + (P(),) * 10
    return jax.shard_map(
        on_device,
        mesh=mesh,
        in_specs=placed,
        out_specs=(P("dp", "seq", None), P("dp", "seq", None)) + (P(),) * 11,
        check_vma=False,
    )
```

```python
import functools
import math

import jax
import jax.numpy as jnp
from jax import lax
from jax.experimental import pallas as pl
from jax.experimental.pallas import tpu as pltpu
from jax.sharding import PartitionSpec as P

EPS = 1e-05
LANES = 128
SUB = 8
LOG2E = math.log2(math.e)
LN2 = math.log(2.0)
F32 = jnp.float32
BF16 = jnp.bfloat16
MESH = pl.DeviceIdType.MESH


def silu_slope(value):
    sigma = jax.nn.sigmoid(value)
    return sigma * (1.0 + value * (1.0 - sigma))


def contract_rows(left, right):
    return lax.dot_general(
        left, right, (((0,), (0,)), ((), ())), preferred_element_type=F32
    )


def contract_cols(left, right):
    return lax.dot_general(
        left, right, (((1,), (1,)), ((), ())), preferred_element_type=F32
    )


def sublane(shape):
    return lax.broadcasted_iota(jnp.int32, shape, len(shape) - 2)


def shift_up(value, by, fill, reverse):
    place = sublane(value.shape)
    if reverse:
        moved = pltpu.roll(value, SUB - by, value.ndim - 2)
        return jnp.where(place < SUB - by, moved, fill)
    moved = pltpu.roll(value, by, value.ndim - 2)
    return jnp.where(place >= by, moved, fill)


def expand_columns(select, first, states):
    width = select.shape[1]
    shape = (width, states * LANES)
    source = lax.broadcasted_iota(jnp.int32, shape, 0)
    target = lax.broadcasted_iota(jnp.int32, shape, 1) // LANES + first
    spread = (source == target).astype(F32).astype(BF16)
    return jnp.dot(select, spread, preferred_element_type=F32)


def tree_sum(value):
    while value.shape[0] > 1:
        half = value.shape[0] // 2
        value = value[:half] + value[half:]
    return value[0]


def front_kernel(
    seq,
    ids_ref, embedding_ref, cotangent_ref, gain_ref, front_weight_ref, gate_weight_ref, out_weight_ref, conv_ref,
    conv_bias_ref, select_weight_ref,
    inputs_ref, scale_ref, normed_ref, turned_ref, upstream_ref, hot_ref, front_ref, halo_ref, mixed_ref, active_ref,
    gate_ref, graded_ref, select_ref,
    last_scr, extended_scr, total_scr, send_sem, recv_sem,
):
    step = pl.program_id(0)
    rows, width = upstream_ref.shape
    span = rows // SUB
    vocab = embedding_ref.shape[0]
    kernel = conv_ref.shape[0]
    halo = kernel - 1
    place = lax.axis_index("seq")

    def there(by):
        return (lax.axis_index("dp"), place + by)

    def copy():
        return pltpu.make_async_remote_copy(
            src_ref=ids_ref.at[:, pl.ds(rows - LANES, LANES)], dst_ref=last_scr, send_sem=send_sem, recv_sem=recv_sem,
            device_id=there(1), device_id_type=MESH,
        )

    def norm(inputs):
        scale = lax.rsqrt(jnp.sum(inputs * inputs, axis=1, keepdims=True) * (1.0 / width) + EPS)
        return scale, (inputs * scale * gain_ref[...]).astype(BF16)

    def hot_of(ids):
        shape = (vocab, ids.shape[1])
        return (lax.broadcasted_iota(jnp.int32, shape, 0) == ids).astype(F32).astype(BF16)

    @pl.when(step == 0)
    def _():
        barrier = pltpu.get_barrier_semaphore()

        @pl.when(place > 0)
        def _():
            pl.semaphore_signal(barrier, inc=1, device_id=there(-1), device_id_type=MESH)

        @pl.when(place == 0)
        def _():
            last_scr[...] = jnp.full(last_scr.shape, -1, jnp.int32)

        row = lax.broadcasted_iota(jnp.int32, (rows, rows), 0)
        position = lax.broadcasted_iota(jnp.int32, (rows, rows), 1)
        order = (lax.rem(row, SUB) * span + row // SUB == position).astype(F32).astype(BF16)
        upstream_ref[...] = jnp.dot(order, cotangent_ref[...], preferred_element_type=F32).astype(BF16)

        @pl.when(place < seq - 1)
        def _():
            pl.semaphore_wait(barrier, 1)
            copy().start()

        hot = contract_cols(hot_of(ids_ref[...]), order).astype(BF16)
        hot_ref[...] = hot
        inputs = contract_rows(hot, embedding_ref[...])
        inputs_ref[...] = inputs
        scale, normed = norm(inputs)
        scale_ref[...] = scale
        normed_ref[:rows] = normed
        turned_ref[...] = normed.T

        @pl.when(place < seq - 1)
        def _():
            copy().wait_send()

        @pl.when(place > 0)
        def _():
            copy().wait_recv()

        last = contract_rows(hot_of(last_scr[...]), embedding_ref[...])[LANES - 16 :]
        normed_ref[rows:] = norm(last)[1]
        total_scr[...] = jnp.zeros_like(total_scr)

    both = jnp.dot(normed_ref[...], front_weight_ref[...], preferred_element_type=F32).astype(BF16)
    front_ref[...] = both[:rows]
    both = both.astype(F32)
    extended_scr[halo * SUB :] = both[:rows]
    sub = lax.broadcasted_iota(jnp.int32, (SUB, both.shape[1]), 0)
    for i in range(halo):
        own = pltpu.roll(both[rows - (halo - i) * SUB : rows - (halo - i - 1) * SUB], 1, 0)
        before = both[rows + 16 - halo + i : rows + 16 - halo + i + 1]
        extended_scr[i * SUB : (i + 1) * SUB] = jnp.where(sub > 0, own, before)
    halo_ref[...] = extended_scr[: halo * SUB]
    mixed = conv_bias_ref[...] + conv_ref[0:1] * extended_scr[:rows]
    for i in range(1, kernel):
        mixed = mixed + conv_ref[i : i + 1] * extended_scr[i * SUB : i * SUB + rows]
    mixed_ref[...] = mixed
    active = jax.nn.silu(mixed).astype(BF16)
    active_ref[...] = active
    gate_ref[...] = jnp.dot(normed_ref[:rows], gate_weight_ref[...], preferred_element_type=F32).astype(BF16)
    graded_ref[...] = contract_cols(upstream_ref[...], out_weight_ref[...])
    total_scr[...] += contract_cols(active, select_weight_ref[...])

    @pl.when(step == pl.num_programs(0) - 1)
    def _():
        select_ref[...] = total_scr[...].astype(BF16)


def run_front(
    ids, embedding, cotangent, gain, input_weight, output_weight, conv_weight, conv_bias, select_weight, seq
):
    rows, width = cotangent.shape
    inner = output_weight.shape[0]
    vocab, kernel, columns = embedding.shape[0], conv_weight.shape[0], select_weight.shape[0]
    halo = (kernel - 1) * SUB
    tall = 4 * LANES
    pairs = inner // tall
    whole = lambda a: pl.BlockSpec(a.shape, lambda i: (0, 0), pipeline_mode=pl.Buffered(1))
    tile = lambda height: pl.BlockSpec((height, tall), lambda i: (0, i))
    fixed = lambda shape: pl.BlockSpec(shape, lambda i: (0, 0))
    outs = [
        ((rows, width), F32, None), ((rows, 1), F32, None), ((rows + 16, width), BF16, None),
        ((width, rows), BF16, None), ((rows, width), BF16, None), ((vocab, rows), BF16, None),
        ((rows, inner), BF16, rows), ((halo, inner), F32, halo), ((rows, inner), F32, rows), ((rows, inner), BF16, rows),
        ((rows, inner), BF16, rows), ((rows, inner), F32, rows), ((rows, columns), BF16, None),
    ]
    return pl.pallas_call(
        functools.partial(front_kernel, seq),
        grid=(pairs,),
        in_specs=[
            whole(ids), whole(embedding), whole(cotangent), whole(gain), tile(width),
            pl.BlockSpec((width, tall), lambda i: (0, i + pairs)), pl.BlockSpec((tall, width), lambda i: (i, 0)),
            tile(kernel), tile(1), tile(columns),
        ],
        out_specs=[fixed(shape) if height is None else tile(height) for shape, kind, height in outs],
        out_shape=[jax.ShapeDtypeStruct(shape, kind) for shape, kind, height in outs],
        scratch_shapes=[
            pltpu.VMEM((1, LANES), jnp.int32), pltpu.VMEM((rows + halo, tall), F32), pltpu.VMEM((rows, columns), F32),
            pltpu.SemaphoreType.DMA, pltpu.SemaphoreType.DMA,
        ],
        compiler_params=pltpu.CompilerParams(
            collective_id=3, has_side_effects=True, vmem_limit_bytes=62 << 20
        ),
        name="span_front",
    )(
        ids, embedding, cotangent, gain, input_weight, input_weight, output_weight, conv_weight, conv_bias, select_weight
    )


def slot_of(k, p):
    return 2 * k + 3 - k % 2 + 2 * p


def turns(phases, tile, place):
    for p in range(phases, -1, -1):
        k = tile - 1 - p
        yield k, p, (k >= 0) & (lax.rem(k + 2 * phases, 2) == 1 - place)


def begun(tiles, p):
    return sum(slot_of(k, p) < 2 * tiles for k in range(tiles))


def next_phase(k, tiles):
    return next(p for p in range(1000) if slot_of(k, p) >= 2 * tiles)


class Prefix:
    def __init__(self, totals, landing, start, incoming, gaps, rates, send_sem, recv_sem, rounds):
        self.totals, self.landing, self.start, self.incoming, self.gaps = totals, landing, start, incoming, gaps
        self.rates, self.send_sem, self.recv_sem, self.rounds = rates, send_sem, recv_sem, rounds

    def copy(self, e, r):
        return pltpu.make_async_remote_copy(
            src_ref=self.totals.at[e], dst_ref=self.landing.at[e, r],
            send_sem=self.send_sem.at[e, r], recv_sem=self.recv_sem.at[e, r],
            device_id=other("seq", 1 << r), device_id_type=MESH,
        )

    def advance(self, e, r):
        if r > 0:
            self.copy(e, r - 1).wait()
            self.merge(e, r - 1)
        if r < self.rounds:
            self.copy(e, r).start()

    def merge(self, e, r):
        n = self.rates.shape[1]
        rates = self.rates[e]
        later = bit_of(lax.axis_index("seq"), 1 << r) == 1
        end, message, total = self.totals[e, :n], self.totals[e, n : 2 * n], self.totals[e, 2 * n : 2 * n + 1]
        end2, message2 = self.landing[e, r, :n], self.landing[e, r, n : 2 * n]
        total2 = self.landing[e, r, 2 * n : 2 * n + 1]

        @pl.when(later)
        def _():
            gap = self.gaps[e, 0:1]
            self.start[e] = self.start[e] + jnp.exp2(gap * rates) * end2
            self.gaps[e, 0:1] = gap + total2

        @pl.when(jnp.logical_not(later))
        def _():
            gap = self.gaps[e, 1:2]
            self.incoming[e] = self.incoming[e] + jnp.exp2(gap * rates) * message2
            self.gaps[e, 1:2] = gap + total2

        if r < self.rounds - 1:
            reach, reach2 = jnp.exp2(total * rates), jnp.exp2(total2 * rates)
            self.totals[e, :n] = jnp.where(later, end + reach * end2, end2 + reach2 * end)
            self.totals[e, n : 2 * n] = jnp.where(later, message2 + reach2 * message, message + reach * message2)
            self.totals[e, 2 * n : 2 * n + 1] = total + total2


def scan_kernel(
    rank, states, chunk, rounds, seq,
    active_now, gate_now, graded_now, select_ref, step_weight_ref, step_bias_ref, decay_ref, skip_ref, normed_hbm, upstream_hbm,
    gated_ref, dgate_ref, dprelow_ref, dactive_ref, lines_ref, dselect_ref,
    gate_sum, out_sum, handed,
    inject_scr, readout_scr, dread_scr, dinject_scr, state_scr, factor_scr,
    rates_scr, rate_scr, delta_ring, drive_ring, grad_ring, silu_ring, sway_ring, active_ring, slope_ring, scan_scr, weight_scr,
    ahead_scr, behind_scr, sums_scr, gated_scr, dgated_scr,
    totals, totals_in, start_scr, incoming_scr, gaps_scr, prefix_send, prefix_recv,
    normed_ref, upstream_ref, late_sem,
    acc, out, landing, extra, send_sem, recv_sem, store_sem,
):
    rows = active_now.shape[0]
    steps = rows // SUB
    step = pl.program_id(0)
    count = rates_scr.shape[0]
    lag = delta_ring.shape[0]
    per = -(-rounds // (lag - 1))
    width = upstream_ref.shape[1]
    prefix = Prefix(
        totals, totals_in, start_scr, incoming_scr, gaps_scr, rates_scr, prefix_send, prefix_recv, rounds
    )
    ex = Exchange(acc, out, landing, extra, send_sem, recv_sem, chunk, landing.shape[0], seq)
    early = begun(count, ex.phases)
    half, unroll = states // 2, 16
    halves = [pl.ds(0, half), pl.ds(half, half)]

    def store(k):
        pair = k // 2

        @pl.when(lax.rem(k, 2) == 0)
        def _():
            store_lanes(out.at[k], gate_sum, pair, store_sem.at[k])

        @pl.when(lax.rem(k, 2) == 1)
        def _():
            store_rows(out.at[k], out_sum, pair, store_sem.at[k])

    def take_turns(place):
        for k, p, now in turns(ex.phases, step - lag, place):

            @pl.when(now)
            def _():
                ex.advance(k, p)
                if p == ex.phases:
                    store(k)

    late_loads = [
        pltpu.make_async_copy(source, target, late_sem.at[i])
        for i, (source, target) in enumerate(((normed_hbm, normed_ref), (upstream_hbm, upstream_ref)))
    ]

    @pl.when(step == 0)
    def _():
        ex.greet()
        for copy in late_loads:
            copy.start()
        for first, scr in ((rank, inject_scr), (rank + states, readout_scr)):
            for n in range(0, states, 2):
                wide = expand_columns(select_ref[...], first + n, 2)
                for side in range(2):
                    scr[:, n + side] = wide[:, side * LANES : (side + 1) * LANES].reshape(steps, SUB, LANES)
        dread_scr[...] = jnp.zeros_like(dread_scr)
        dinject_scr[...] = jnp.zeros_like(dinject_scr)
        start_scr[...] = jnp.zeros_like(start_scr)
        incoming_scr[...] = jnp.zeros_like(incoming_scr)
        gaps_scr[...] = jnp.zeros_like(gaps_scr)
        for e in range(count):
            rates_scr[e] = -jnp.exp(decay_ref[:, e * LANES : (e + 1) * LANES]) * LOG2E
        for copy in late_loads:
            copy.wait()
        ex.welcome()

    flat = lambda value: value.reshape(steps, SUB, LANES)
    zero = jnp.zeros((half, SUB, LANES), F32)

    def spread_rates(tile):
        rates = rates_scr[tile]
        for n in range(states):
            rate_scr[n] = jnp.broadcast_to(rates[n : n + 1], (SUB, LANES))

    def spread(table):
        return jnp.concatenate(
            [jnp.broadcast_to(table[n : n + 1], (1, SUB, LANES)) for n in range(states)], axis=0
        )

    @pl.when(step >= lag)
    def _():
        c = step - lag
        tile = c
        spread_rates(tile)
        slot = lax.rem(c, lag)
        delta_scr, drive_scr, grad_scr = delta_ring.at[slot], drive_ring.at[slot], grad_ring.at[slot]
        total = sums_scr[tile]
        before, after = total, total
        for by in (1, 2, 4):
            before = before + shift_up(before, by, 0.0, False)
            after = after + shift_up(after, by, 0.0, True)
        before, after = before - total, after - total
        state_scr[0] = ahead_scr[tile] + jnp.exp2(before[None] * rate_scr[...]) * spread(start_scr[tile])

        def forward(i, state):
            for u in range(unroll):
                j = i * unroll + u
                factor = jnp.exp2(delta_scr[j][None] * rate_scr[...])
                factor_scr[j] = factor
                state = factor * state + drive_scr[j][None] * inject_scr[j]
                state_scr[j + 1] = state
                dread_scr[j] += grad_scr[j][None] * state
                scan_scr[j] = tree_sum(readout_scr[j] * state)
            return state

        lax.fori_loop(0, steps // unroll, forward, state_scr[0])
        take_turns(0)
        lanes = pl.ds(pl.multiple_of(c * LANES, LANES), LANES)
        skip = skip_ref[:, lanes]
        active = active_ring[slot].reshape(rows, LANES)
        scanned = scan_scr[...].reshape(rows, LANES) + skip * active
        gated = (scanned * silu_ring[slot].reshape(rows, LANES)).astype(BF16)
        gated_ref[...] = gated
        dgate = (scanned * sway_ring[slot].reshape(rows, LANES)).astype(BF16)
        dgate_ref[...] = dgate
        lines_ref[states + 1 : states + 2, :] = jnp.sum(
            grad_scr[...].reshape(rows, LANES) * active, axis=0, keepdims=True
        )
        odd = lax.rem(c, 2)

        @pl.when(odd == 0)
        def _():
            gated_scr[:, :LANES] = gated
            dgated_scr[:, :LANES] = dgate

        @pl.when(odd == 1)
        def _():
            gated_scr[:, LANES:] = gated
            dgated_scr[:, LANES:] = dgate

        adjoint0 = behind_scr[tile] + jnp.exp2(after[None] * rate_scr[...]) * spread(incoming_scr[tile])
        state_scr[steps] = adjoint0
        for h, part in enumerate(halves):

            def backward(i, carry):
                adjoint, total = carry
                for u in range(unroll):
                    j = steps - 1 - (i * unroll + u)
                    d, g = delta_scr[j], grad_scr[j]
                    whole = adjoint + g[None] * readout_scr[j, part]
                    adjoint = factor_scr[j, part] * whole
                    through = adjoint * state_scr[j, part]
                    total = total + through * d[None]
                    dinject_scr[j, part] += whole * drive_scr[j][None]
                    one = tree_sum(through * rate_scr[part])
                    two = tree_sum(whole * inject_scr[j, part])
                    scan_scr[j] = scan_scr[j] + one if h else one
                    weight_scr[j] = weight_scr[j] + two if h else two
                return adjoint, total

            unused, total = lax.fori_loop(0, steps // unroll, backward, (state_scr[steps, part], zero))
            for n in range(half):
                at = h * half + n
                lines_ref[at : at + 1, :] = (
                    jnp.sum(total[n], axis=0, keepdims=True) * rate_scr[at, 0:1] * LN2
                )
        weight = weight_scr[...].reshape(rows, LANES)
        delta = delta_scr[...].reshape(rows, LANES)
        active = active_ring[slot].reshape(rows, LANES)
        dactive_ref[...] = delta * weight + skip_ref[:, lanes] * grad_scr[...].reshape(rows, LANES)
        dpre = (scan_scr[...].reshape(rows, LANES) * LN2 + active * weight) * slope_ring[slot].reshape(rows, LANES)
        dprelow_ref[...] = dpre.astype(BF16)
        lines_ref[states : states + 1, :] = jnp.sum(dpre, axis=0, keepdims=True)

        @pl.when(odd == 1)
        def _():
            pair = c // 2
            part = jnp.dot(normed_ref[...], dgated_scr[...], preferred_element_type=F32).astype(BF16)
            acc[2 * pair, :width, :] = part[:, :LANES]
            acc[2 * pair, width:, :] = part[:, LANES:]
            turned = gated_scr[...].T
            for b in range(width // (2 * LANES)):
                part = jnp.dot(
                    turned, upstream_ref[:, b * 2 * LANES : (b + 1) * 2 * LANES], preferred_element_type=F32
                ).astype(BF16)
                for side in range(2):
                    at = (2 * b + side) * 2 * LANES
                    acc[2 * pair + 1, at : at + 2 * LANES, :] = part[:, side * LANES : (side + 1) * LANES]

        take_turns(1)

    @pl.when(step < count)
    def _():
        tile = step
        spread_rates(tile)
        slot = lax.rem(step, lag)
        delta_scr, drive_scr, grad_scr = delta_ring.at[slot], drive_ring.at[slot], grad_ring.at[slot]
        lanes = pl.ds(pl.multiple_of(tile * LANES, LANES), LANES)
        pre = jnp.dot(select_ref[:, :rank], step_weight_ref[:, lanes], preferred_element_type=F32)
        pre = pre + step_bias_ref[:, lanes]
        small = jnp.exp(-jnp.abs(pre))
        delta = jnp.maximum(pre, 0.0) + jnp.log1p(small)
        slope_ring[slot] = flat(jnp.where(pre >= 0.0, 1.0, small) / (1.0 + small))
        delta_scr[...] = flat(delta)
        active = active_now[...].astype(F32)
        active_ring[slot] = flat(active)
        drive_scr[...] = flat(delta * active)
        gate = gate_now[...].astype(F32)
        sigma = jax.nn.sigmoid(gate)
        silu = gate * sigma
        silu_ring[slot] = flat(silu)
        graded = graded_now[...]
        grad_scr[...] = flat(graded * silu)
        sway_ring[slot] = flat(graded * (sigma * (1.0 + gate * (1.0 - sigma))))
        total = jnp.sum(delta_scr[...], axis=0)
        sums_scr[tile] = total
        whole = jnp.sum(total, axis=0, keepdims=True)
        totals[tile, 2 * states :] = jnp.broadcast_to(whole, (SUB, LANES))
        for h, part in enumerate(halves):

            def ends(i, carry):
                state, message, decay = carry
                for u in range(unroll):
                    j = i * unroll + u
                    factor = jnp.exp2(delta_scr[j][None] * rate_scr[part])
                    state = factor * state + drive_scr[j][None] * inject_scr[j, part]
                    decay = decay * factor
                    message = message + decay * (grad_scr[j][None] * readout_scr[j, part])
                return state, message, decay

            state, message, decay = lax.fori_loop(0, steps // unroll, ends, (zero, zero, zero + 1.0))
            for value, kept, at, reverse in (
                (state, ahead_scr, h * half, False), (message, behind_scr, states + h * half, True)
            ):
                factor = decay
                for by in (1, 2, 4):
                    value = value + factor * shift_up(value, by, 0.0, reverse)
                    factor = factor * shift_up(factor, by, 1.0, reverse)
                kept[tile, part] = shift_up(value, 1, 0.0, reverse)
                last = 0 if reverse else SUB - 1
                for n in range(half):
                    totals[tile, at + n : at + n + 1] = value[n, last : last + 1]

    for r in range(lag - 1, -1, -1):
        e = step - r

        @pl.when((e >= 0) & (e < count))
        def _():
            if r == 0:
                prefix.copy(e, 0).start()
            for done in range((r - 1) * per, min(r * per, rounds)) if r > 0 else ():
                prefix.advance(e, done + 1)

    @pl.when(step == count + lag - 1)
    def _():
        group = 4
        shape = (group * LANES, 2 * states)
        from_lane = lax.broadcasted_iota(jnp.int32, shape, 0) // LANES
        to_column = lax.broadcasted_iota(jnp.int32, shape, 1)
        whole = jnp.zeros((rows, 2 * states), F32)
        for first, scr in ((0, dinject_scr), (states, dread_scr)):
            for n in range(0, states, group):
                ones = (from_lane + (first + n) == to_column).astype(F32).astype(BF16)
                values = [scr[:, n + i].reshape(rows, LANES) for i in range(group)]
                highs = [value.astype(BF16) for value in values]
                lows = [(value - high.astype(F32)).astype(BF16) for value, high in zip(values, highs)]
                for parts in (highs, lows):
                    whole = whole + jnp.dot(jnp.concatenate(parts, axis=1), ones, preferred_element_type=F32)
        dselect_ref[...] = whole

        slots = 2 * count
        for k in range(count):
            for p in range(ex.phases):
                if slots - 2 <= slot_of(k, p) < slots:
                    ex.finish(k, p)
        sizes = []
        for k in range(early, count):
            sizes.append(0)
            for ref, base, size in ex.state(k, next_phase(k, count)):
                here = pl.ds(pl.multiple_of(base, 16), size)
                sizes[-1] += size
                pltpu.make_async_copy(ref.at[k, here, :], handed.at[k - early, here, :], store_sem.at[k]).start()
        for k in range(early):
            wait_rows(out.at[k], store_sem.at[k])
        for k in range(early, count):
            wait_rows(acc.at[k, pl.ds(0, sizes[k - early]), :], store_sem.at[k])


def run_scan(active, gate, graded, select, step_weight, step_bias, decay_log, skip, normed, upstream, seq):
    rows, inner = active.shape
    rank = step_weight.shape[0]
    states = decay_log.shape[0]
    width = upstream.shape[1]
    chunk = 2 * width
    tiles, steps = inner // LANES, rows // SUB
    rounds = seq.bit_length() - 1
    phases = 8 + max(rounds - 3, 0)
    early = begun(tiles, phases)
    gates, outs = (early + 1) // 2 * 2 * LANES, early // 2 * 2 * LANES
    lag = min(rounds, 3) + 1
    now = pl.BlockSpec((rows, LANES), lambda i: (0, lax.min(i, tiles - 1)))
    late = lambda shape: pl.BlockSpec(shape, lambda i: (0, lax.max(i - lag, 0)))
    whole = lambda a: pl.BlockSpec(a.shape, lambda i: (0, 0), pipeline_mode=pl.Buffered(1))
    hbm = pl.BlockSpec(memory_space=pltpu.HBM)
    wide = pltpu.VMEM((steps, states, SUB, LANES), F32)
    thin = pltpu.VMEM((steps, SUB, LANES), F32)
    cube = pltpu.VMEM((tiles, states, SUB, LANES), F32)
    small = pltpu.VMEM((tiles, states, LANES), F32)
    pair = pltpu.VMEM((rows, 2 * LANES), BF16)
    buffers = scratch(tiles, chunk, tiles // 2, seq)
    buffers[1] = pltpu.VMEM((begun(tiles, phases - 5), chunk, LANES), BF16)
    ring = pltpu.VMEM((lag, steps, SUB, LANES), F32)
    return pl.pallas_call(
        functools.partial(scan_kernel, rank, states, chunk, rounds, seq),
        grid=(tiles + lag,),
        in_specs=[
            now, now, now, whole(select), whole(step_weight), whole(step_bias), whole(decay_log), whole(skip),
            hbm, hbm,
        ],
        out_specs=[
            late((rows, LANES)), late((rows, LANES)), late((rows, LANES)), late((rows, LANES)),
            late((states + SUB, LANES)), pl.BlockSpec((rows, 2 * states), lambda i: (0, 0)), hbm, hbm, hbm,
        ],
        out_shape=[
            jax.ShapeDtypeStruct((rows, inner), BF16),
            jax.ShapeDtypeStruct((rows, inner), BF16),
            jax.ShapeDtypeStruct((rows, inner), BF16),
            jax.ShapeDtypeStruct((rows, inner), F32),
            jax.ShapeDtypeStruct((states + SUB, inner), F32),
            jax.ShapeDtypeStruct((rows, 2 * states), F32),
            jax.ShapeDtypeStruct((width, gates), BF16),
            jax.ShapeDtypeStruct((outs, width), BF16),
            jax.ShapeDtypeStruct((tiles - early, chunk, LANES), BF16),
        ],
        scratch_shapes=[
            wide, wide, wide, wide,
            pltpu.VMEM((steps + 1, states, SUB, LANES), F32), wide,
            small, pltpu.VMEM((states, SUB, LANES), F32), ring, ring, ring, ring, ring, ring, ring, thin, thin,
            cube, cube, pltpu.VMEM((tiles, SUB, LANES), F32), pair, pair,
            pltpu.VMEM((tiles, 2 * states + SUB, LANES), F32),
            pltpu.VMEM((tiles, rounds, 2 * states + SUB, LANES), F32),
            small, small, pltpu.VMEM((tiles, SUB, LANES), F32),
            pltpu.SemaphoreType.DMA((tiles, rounds)), pltpu.SemaphoreType.DMA((tiles, rounds)),
            pltpu.VMEM(normed.shape, BF16), pltpu.VMEM(upstream.shape, BF16), pltpu.SemaphoreType.DMA((2,)),
        ]
        + buffers
        + [pltpu.SemaphoreType.DMA((tiles,))],
        compiler_params=pltpu.CompilerParams(
            collective_id=1, has_side_effects=True, vmem_limit_bytes=62 << 20
        ),
        name="span_scan",
    )(
        active, gate, graded, select, step_weight, step_bias, decay_log, skip, normed, upstream
    )


def bit_of(index, step):
    return (index // step) % 2

def other(axis, step):
    place = lax.axis_index(axis)
    place = place + step * (1 - 2 * bit_of(place, step))
    if axis == "dp":
        return (place, lax.axis_index("seq"))
    return (lax.axis_index("dp"), place)

CORE, X, Y = ("seq", 1), ("dp", 1), ("dp", 2)

def wait_rows(rows, sem):
    pltpu.make_async_copy(rows, rows, sem).wait()


def store_lanes(source, target, pair, sem):
    width = target.shape[0]
    for side in range(2):
        lanes = pl.ds(pl.multiple_of((2 * pair + side) * LANES, LANES), LANES)
        pltpu.make_async_copy(source.at[pl.ds(side * width, width), :], target.at[:, lanes], sem).start()


def store_rows(source, target, pair, sem):
    tall = 2 * LANES
    rows = pl.ds(pl.multiple_of(pair * tall, tall), tall)
    for b in range(target.shape[1] // LANES):
        pltpu.make_async_copy(
            source.at[pl.ds(b * tall, tall), :], target.at[rows, pl.ds(b * LANES, LANES)], sem
        ).start()


class Exchange:
    levels = 4

    def __init__(self, acc, out, landing, extra, send_sem, recv_sem, rows, window, seq):
        self.acc, self.out, self.landing, self.extra = acc, out, landing, extra
        self.send_sem, self.recv_sem = send_sem, recv_sem
        self.rows, self.window = rows, window
        self.more = [("seq", 8 << i) for i in range(12) if (8 << i) < seq]
        self.orders = ((CORE, X, Y), (CORE, Y, X))
        self.back = self.levels + len(self.more)
        self.phases = self.back + self.levels
        place = lax.axis_index("seq")
        self.quarter = (place // 2) % 4
        self.core_base = bit_of(place, 1) * (rows // 2)
        self.kept = []
        for s, order in enumerate(self.orders):
            base, size = self.core_base + s * (rows // 4), rows // 4
            spans = [(base, size)]
            for axis, step in order[1:]:
                size = size // 2
                base = base + bit_of(lax.axis_index(axis), step) * size
                spans.append((base, size))
            size = size // 4
            spans.append((base + self.quarter * size, size))
            self.kept.append(spans)

    def partners(self):
        links = [CORE, X, Y] + self.more
        return [other(*link) for link in links] + [self.along(i) for i in range(1, 4)]

    def greet(self):
        for device in self.partners():
            pl.semaphore_signal(pltpu.get_barrier_semaphore(), inc=1, device_id=device, device_id_type=MESH)

    def welcome(self):
        pl.semaphore_wait(pltpu.get_barrier_semaphore(), len(self.partners()))

    def along(self, i):
        place = lax.axis_index("seq")
        return (lax.axis_index("dp"), place + 2 * (lax.rem(self.quarter + i, 4) - self.quarter))

    def span(self, ref, k, base, size):
        return ref.at[k, pl.ds(pl.multiple_of(base, 16), size), :]

    def land(self, p):
        rows = self.rows
        return [0, rows // 2, rows // 2 + rows // 4, rows // 2 + rows // 4 + rows // 8][p]

    def rows_of(self, p):
        rows, last = self.rows, self.phases - 1
        if self.levels <= p < self.back:
            return rows // 32
        return [rows // 2, rows // 4, rows // 8, 6 * rows // 64][min(p, last - p)]

    def copies(self, k, p):
        w = lax.rem(k, self.window)
        rows = self.rows
        if p == 0:
            return [(self.span(self.acc, k, rows // 2 - self.core_base, rows // 2),
                     self.landing.at[w, pl.ds(0, rows // 2), :], other(*CORE))]
        if p == self.phases - 1:
            half = self.span(self.out, k, self.core_base, rows // 2)
            return [(half, half, other(*CORE))]
        found = []
        for s in range(2):
            if p < self.levels - 1:
                size = self.kept[s][p][1]
                axis, step = self.orders[s][p]
                base = self.kept[s][p - 1][0] + (1 - bit_of(lax.axis_index(axis), step)) * size
                target = self.landing.at[w, pl.ds(self.land(p) + s * size, size), :]
                found.append((self.span(self.acc, k, base, size), target, other(axis, step)))
            elif p == self.levels - 1:
                first, size = self.kept[s][p - 1][0], self.kept[s][p][1]
                for i in range(1, 4):
                    base = first + lax.rem(self.quarter + i, 4) * size
                    target = self.landing.at[w, pl.ds(self.land(p) + (3 * s + i - 1) * size, size), :]
                    found.append((self.span(self.acc, k, base, size), target, self.along(i)))
            elif p < self.back:
                base, size = self.kept[s][-1]
                target = self.extra.at[w, p - self.levels, pl.ds(s * size, size), :]
                found.append((self.span(self.acc, k, base, size), target, other(*self.more[p - self.levels])))
            else:
                level = self.phases - 1 - p
                piece = self.span(self.out, k, *self.kept[s][level])
                devices = [self.along(i) for i in range(1, 4)] if level == 3 else [other(*self.orders[s][level])]
                found += [(piece, piece, device) for device in devices]
        return found

    def add(self, k, base, size, sources, target):
        step = min(size, 256)

        def body(i, _):
            here = pl.ds(pl.multiple_of(base + i * step, 16), step)
            total = self.acc[k, here, :].astype(F32)
            for ref, index, first in sources:
                there = pl.ds(pl.multiple_of(first + i * step, 16), step)
                total = total + ref[index + (there,)].astype(F32)
            target[k, here, :] = total.astype(BF16)
            return 0

        lax.fori_loop(0, size // step, body, 0)

    def finish(self, k, p):
        w = lax.rem(k, self.window)
        rows = self.acc.at[k, pl.ds(0, self.rows_of(p)), :]
        copy = pltpu.make_async_remote_copy(
            src_ref=rows, dst_ref=rows, send_sem=self.send_sem.at[w, p], recv_sem=self.recv_sem.at[w, p],
            device_id=other(*CORE), device_id_type=MESH,
        )
        copy.wait_send()
        copy.wait_recv()
        target = self.out if p == self.back - 1 else self.acc
        if p == 0:
            self.add(k, self.core_base, self.rows // 2, [(self.landing, (w,), 0)], target)
        elif p < self.back:
            for s in range(2):
                base, size = self.kept[s][min(p, self.levels - 1)]
                if p < self.levels - 1:
                    sources = [(self.landing, (w,), self.land(p) + s * size)]
                elif p < self.levels:
                    sources = [(self.landing, (w,), self.land(p) + (3 * s + i) * size) for i in range(3)]
                else:
                    sources = [(self.extra, (w, p - self.levels), s * size)]
                self.add(k, base, size, sources, target)

    def start(self, k, p):
        w = lax.rem(k, self.window)
        for source, target, device in self.copies(k, p):
            pltpu.make_async_remote_copy(
                src_ref=source, dst_ref=target, send_sem=self.send_sem.at[w, p], recv_sem=self.recv_sem.at[w, p],
                device_id=device, device_id_type=MESH,
            ).start()

    def advance(self, k, p):
        if p > 0:
            self.finish(k, p - 1)
        if p < self.phases:
            self.start(k, p)

    def state(self, k, p):
        rows = self.rows
        if p == 0:
            return [(self.acc, 0, rows)]
        if p == self.phases:
            return [(self.out, 0, rows)]
        level = min(p - 1, self.levels - 1) if p < self.back else self.phases - 1 - p
        spans = [(self.core_base, rows // 2)] if level == 0 else [self.kept[s][level] for s in range(2)]
        return [(self.acc if p < self.back else self.out, base, size) for base, size in spans]


def scratch(chunks, rows, window, seq):
    more = len([1 for i in range(12) if (8 << i) < seq])
    return [
        pltpu.VMEM((chunks, rows, LANES), BF16),
        pltpu.VMEM((chunks, rows, LANES), BF16),
        pltpu.VMEM((window, rows, LANES), BF16),
        pltpu.VMEM((window, max(more, 1), rows // 32, LANES), BF16),
        pltpu.SemaphoreType.DMA((window, 8 + more)),
        pltpu.SemaphoreType.DMA((window, 8 + more)),
    ]


def tail_kernel(
    rank, states, chunk, seq,
    dprelow_ref, select_ref, dpair_ref, step_weight_ref, normed_ref, upstream_hbm, inputs_hbm, scale_ref, hot_hbm,
    gain_ref, dactive_first_ref, mixed_first_ref, select_weight_ref, halo_ref, lines_ref,
    dactive_ref, mixed_ref, front_ref, active_ref, select_tile_ref, conv_ref, front_weight_ref, gate_weight_ref,
    dgate_ref, gated_ref, out_weight_ref, handed,
    output_ref, dinputs_ref, front_sum, gate_rest, out_rest, embedding_sum, wide_sum, mixed_sum,
    upstream_ref, inputs_ref, hot_ref, late_sem, dselect_scr, first_scr, after_scr, spread_scr, extended_scr, dnormed_scr, result_scr, misc_scr, gain_scr,
    acc, out, landing, extra, send_sem, recv_sem, load_sem, store_sem, first_send, first_recv,
):
    step = pl.program_id(0)
    rows, width = upstream_ref.shape
    across = width // LANES
    inner = dprelow_ref.shape[1]
    tiles, pairs = inner // LANES, inner // (2 * LANES)
    tall = 2 * LANES
    kernel = conv_ref.shape[0]
    halo = kernel - 1
    vocab = embedding_sum.shape[0]
    ex = Exchange(acc, out, landing, extra, send_sem, recv_sem, chunk, landing.shape[0], seq)
    early = begun(tiles, ex.phases)
    old = tiles - early
    embedding_at, wide_at, mixed_at = (old + pairs + i for i in range(3))
    count = old + pairs + 3
    place = lax.axis_index("seq")
    here_dp = lax.axis_index("dp")

    def add(scr, value):
        for b in range(across):
            scr[b] += value[:, b * LANES : (b + 1) * LANES]

    def put(scr, here, value):
        for b in range(across):
            scr[b, here, :] = value[:, b * LANES : (b + 1) * LANES]

    def take(scr, here):
        return jnp.concatenate([scr[b, here, :] for b in range(across)], axis=1)

    def first_copy():
        return pltpu.make_async_remote_copy(
            src_ref=first_scr, dst_ref=after_scr, send_sem=first_send, recv_sem=first_recv,
            device_id=(here_dp, lax.rem(place + seq - 1, seq)), device_id_type=MESH,
        )

    late_loads = [
        pltpu.make_async_copy(source, target, late_sem.at[i])
        for i, (source, target) in enumerate(
            ((upstream_hbm, upstream_ref), (inputs_hbm, inputs_ref), (hot_hbm, hot_ref))
        )
    ]

    def greet():
        barrier = pltpu.get_barrier_semaphore()
        ex.greet()
        for there, by in ((place > 0, -1), (place < seq - 1, 1)):

            @pl.when(there)
            def _():
                pl.semaphore_signal(barrier, inc=1, device_id=(here_dp, place + by), device_id_type=MESH)

    def welcome():
        barrier = pltpu.get_barrier_semaphore()
        neighbours = 2 - (place == 0).astype(jnp.int32) - (place == seq - 1).astype(jnp.int32)
        pl.semaphore_wait(barrier, len(ex.partners()) + neighbours)

    def store(k):
        pair = (k + early) // 2

        @pl.when((k < old) & (lax.rem(k + early, 2) == 0))
        def _():
            store_lanes(out.at[k], gate_rest, pair - (early + 1) // 2, store_sem.at[k])

        @pl.when((k < old) & (lax.rem(k + early, 2) == 1))
        def _():
            store_rows(out.at[k], out_rest, pair - early // 2, store_sem.at[k])

        @pl.when((k >= old) & (k < embedding_at))
        def _():
            store_lanes(out.at[k], front_sum, k - old, store_sem.at[k])

        @pl.when(k == embedding_at)
        def _():
            for b in range(width // LANES):
                pltpu.make_async_copy(
                    out.at[k, pl.ds(b * vocab, vocab), :], embedding_sum.at[:, pl.ds(b * LANES, LANES)], store_sem.at[k]
                ).start()

        @pl.when(k == wide_at)
        def _():
            pltpu.make_async_copy(out.at[k], wide_sum, store_sem.at[k]).start()

        @pl.when(k == mixed_at)
        def _():
            pltpu.make_async_copy(out.at[k], mixed_sum, store_sem.at[k]).start()

    def old_turns(spot):
        for k, p, now in turns(ex.phases, tiles + step, spot):
            k = k - early

            @pl.when(now & (k >= 0) & (k < old))
            def _():
                if p > 0:

                    @pl.when(step > 0)
                    def _():
                        ex.finish(k, p - 1)

                if p < ex.phases:
                    ex.start(k, p)
                else:
                    store(k)

    def new_turns(turn):
        for p in range(ex.phases, -1, -1):
            k = old + turn - 2 * p

            @pl.when((k >= old) & (k < count))
            def _():
                ex.advance(k, p)
                if p == ex.phases:
                    store(k)

    @pl.when(step == 0)
    def _():
        greet()
        sizes = []
        for k in range(old):
            sizes.append(0)
            for ref, base, size in ex.state(k, next_phase(k + early, tiles)):
                here = pl.ds(pl.multiple_of(base, 16), size)
                sizes[-1] += size
                pltpu.make_async_copy(handed.at[k, here, :], ref.at[k, here, :], load_sem.at[k]).start()
        for copy in late_loads:
            copy.start()
        dlow = contract_cols(dprelow_ref[...], step_weight_ref[...])
        dselect_scr[...] = jnp.concatenate([dlow, dpair_ref[...]], axis=1).astype(BF16)
        some = jnp.dot(dselect_scr[: (halo + 1) * SUB], select_weight_ref[...], preferred_element_type=F32)
        some = (dactive_first_ref[...] + some[: halo * SUB]) * silu_slope(mixed_first_ref[...])
        for i in range(halo):
            first_scr[i : i + 1, :] = some[i * SUB : i * SUB + 1, :]
        first_scr[halo:, :] = jnp.zeros((SUB - halo, inner), F32)
        welcome()

        @pl.when(place > 0)
        def _():
            first_copy().start()

        dnormed_scr[...] = jnp.zeros_like(dnormed_scr)
        result_scr[...] = jnp.zeros_like(result_scr)
        misc_scr[...] = jnp.zeros_like(misc_scr)
        misc_scr[kernel + 1 : kernel + 3, :] = lines_ref[states : states + 2, :]
        acc[wide_at] = jnp.zeros_like(acc[wide_at])
        acc[mixed_at] = jnp.zeros_like(acc[mixed_at])
        for b in range(tiles):
            at = rank * tiles + b * states
            acc[mixed_at, at : at + states, :] = lines_ref[:states, b * LANES : (b + 1) * LANES].astype(BF16)
        for k in range(old):
            wait_rows(acc.at[k, pl.ds(0, sizes[k]), :], load_sem.at[k])

    old_turns(0)

    @pl.when(step < pairs)
    def _():
        add(result_scr, jnp.dot(gated_ref[...], out_weight_ref[...], preferred_element_type=F32))
        add(dnormed_scr, contract_cols(dgate_ref[...], gate_weight_ref[...]))

    old_turns(1)

    @pl.when(step < pairs)
    def _():
        lanes = pl.ds(pl.multiple_of(step * tall, tall), tall)
        mixed = mixed_ref[...]
        back = jnp.dot(dselect_scr[...], select_tile_ref[...], preferred_element_type=F32)
        dmixed = (dactive_ref[...] + back) * silu_slope(mixed)
        spread_scr[:rows] = dmixed
        extended_scr[: halo * SUB] = halo_ref[...]
        extended_scr[halo * SUB :] = front_ref[...].astype(F32)
        misc_scr[kernel : kernel + 1, lanes] = jnp.sum(dmixed, axis=0, keepdims=True)
        for i in range(kernel):
            misc_scr[i : i + 1, lanes] = jnp.sum(
                dmixed * extended_scr[i * SUB : i * SUB + rows], axis=0, keepdims=True
            )
        wide = contract_rows(dselect_scr[...], active_ref[...]).astype(BF16)
        columns = wide.shape[0]
        for side in range(2):
            at = pl.ds(pl.multiple_of((2 * step + side) * columns, columns), columns)
            acc[wide_at, at, :] = wide[:, side * LANES : (side + 1) * LANES]
        part = contract_rows(select_ref[:, :rank], dprelow_ref[:, lanes]).astype(BF16)
        for side in range(2):
            at = pl.ds(pl.multiple_of((2 * step + side) * rank, rank), rank)
            acc[mixed_at, at, :] = part[:, side * LANES : (side + 1) * LANES]

        @pl.when(step == 0)
        def _():
            @pl.when(place > 0)
            def _():
                first_copy().wait_send()

            @pl.when(place < seq - 1)
            def _():
                first_copy().wait_recv()

            @pl.when(place == seq - 1)
            def _():
                after_scr[...] = jnp.zeros_like(after_scr)

        sub = lax.broadcasted_iota(jnp.int32, (SUB, tall), 0)
        for i in range(halo):
            own = pltpu.roll(spread_scr[i * SUB : (i + 1) * SUB, :], SUB - 1, 0)
            spread_scr[rows + i * SUB : rows + (i + 1) * SUB] = jnp.where(
                sub < SUB - 1, own, after_scr[i : i + 1, lanes]
            )
        dfront = conv_ref[halo : halo + 1] * spread_scr[:rows]
        for i in range(1, kernel):
            dfront = dfront + conv_ref[halo - i : halo - i + 1] * spread_scr[i * SUB : i * SUB + rows]
        dfront = dfront.astype(BF16)
        part = jnp.dot(normed_ref[...], dfront, preferred_element_type=F32).astype(BF16)
        acc[old + step, :width, :] = part[:, :LANES]
        acc[old + step, width:, :] = part[:, LANES:]
        add(dnormed_scr, contract_cols(dfront, front_weight_ref[...]))

    @pl.when(step == pairs)
    def _():
        for copy in late_loads:
            copy.wait()
        part = rows // SUB

        def norms(i, total):
            here = pl.ds(pl.multiple_of(i * part, part), part)
            dnormed, inputs, scale = take(dnormed_scr, here), inputs_ref[here, :], scale_ref[here, :]
            scaled = gain_ref[...] * dnormed
            mean = jnp.sum(scaled * inputs, axis=1, keepdims=True) * (1.0 / width)
            put(
                dnormed_scr, here,
                upstream_ref[here, :].astype(F32) + scale * scaled - inputs * (scale * scale * scale * mean),
            )
            put(result_scr, here, take(result_scr, here) + inputs)
            return total + jnp.sum((dnormed * inputs * scale).reshape(-1, SUB, width), axis=0)

        total = lax.fori_loop(0, SUB, norms, jnp.zeros((SUB, width), F32))
        gain_scr[...] = jnp.sum(total, axis=0, keepdims=True)
        for b in range(width // tall):
            value = jnp.concatenate([dnormed_scr[2 * b], dnormed_scr[2 * b + 1]], axis=1)
            high = value.astype(BF16)
            low = (value - high.astype(F32)).astype(BF16)
            whole = jnp.dot(hot_ref[...], high, preferred_element_type=F32)
            whole = (whole + jnp.dot(hot_ref[...], low, preferred_element_type=F32)).astype(BF16)
            for side in range(2):
                at = (2 * b + side) * vocab
                acc[embedding_at, at : at + vocab, :] = whole[:, side * LANES : (side + 1) * LANES]
        at = (rank + states) * tiles
        for b in range(tiles):
            acc[mixed_at, at + b * 16 : at + (b + 1) * 16, :] = misc_scr[:, b * LANES : (b + 1) * LANES].astype(BF16)
        at = (rank + states + 16) * tiles
        for b in range(width // LANES):
            acc[mixed_at, at + b * 16 : at + (b + 1) * 16, :] = jnp.broadcast_to(
                gain_scr[:, b * LANES : (b + 1) * LANES], (16, LANES)
            ).astype(BF16)

    @pl.when(step == pairs + 1)
    def _():
        span = rows // SUB
        for i in range(SUB):
            for b in range(across):
                lanes, every = slice(b * LANES, (b + 1) * LANES), pl.ds(i, span, stride=SUB)
                dinputs_ref[i * span : (i + 1) * span, lanes] = dnormed_scr[b, every, :]
                output_ref[i * span : (i + 1) * span, lanes] = result_scr[b, every, :].astype(BF16)

    new_turns(step)

    @pl.when(step == pl.num_programs(0) - 1)
    def _():
        def rest(turn, _):
            new_turns(turn)
            return 0

        lax.fori_loop(pairs + 3, pairs + 3 + 2 * ex.phases, rest, 0)
        for k in range(count):
            wait_rows(out.at[k], store_sem.at[k])


def run_tail(
    d_pre_low, select, d_pair, step_weight, normed, upstream, inputs, scale, hot, gain, d_active, mixed, select_weight,
    halo, lines, front, active, conv_weight, input_weight, d_gate, gated, output_weight, handed, vocab, seq,
):
    rows, inner = front.shape
    width = inputs.shape[1]
    rank, states = step_weight.shape[0], lines.shape[0] - SUB
    chunk = 2 * width
    tiles, pairs, tall = inner // LANES, inner // (2 * LANES), 2 * LANES
    phases = 8 + max(seq.bit_length() - 4, 0)
    early = begun(tiles, phases)
    count = tiles - early + pairs + 3
    some = halo.shape[0]
    at = lambda i: lax.min(i, pairs - 1)
    whole = lambda a: pl.BlockSpec(a.shape, lambda i: (0, 0), pipeline_mode=pl.Buffered(1))
    first = pl.BlockSpec((some, inner), lambda i: (0, 0), pipeline_mode=pl.Buffered(1))
    tile = lambda height: pl.BlockSpec((height, tall), lambda i: (0, at(i)))
    high = lambda wide: pl.BlockSpec((tall, wide), lambda i: (at(i), 0))
    hbm = pl.BlockSpec(memory_space=pltpu.HBM)
    fixed = pl.BlockSpec((rows, width), lambda i: (0, 0))
    gates, outs = inner - (early + 1) // 2 * tall, inner - early // 2 * tall
    return pl.pallas_call(
        functools.partial(tail_kernel, rank, states, chunk, seq),
        grid=(pairs + 3,),
        in_specs=[
            whole(d_pre_low), whole(select), whole(d_pair), whole(step_weight), whole(normed), hbm,
            hbm, whole(scale), hbm, whole(gain), first, first, whole(select_weight), tile(some),
            whole(lines), tile(rows), tile(rows), tile(rows), tile(rows),
            tile(select_weight.shape[0]), tile(conv_weight.shape[0]), tile(width),
            pl.BlockSpec((width, tall), lambda i: (0, at(i) + pairs)), tile(rows), tile(rows), high(width), hbm,
        ],
        out_specs=[fixed, fixed, hbm, hbm, hbm, hbm, hbm, hbm],
        out_shape=[
            jax.ShapeDtypeStruct((rows, width), BF16),
            jax.ShapeDtypeStruct((rows, width), F32),
            jax.ShapeDtypeStruct((width, inner), BF16),
            jax.ShapeDtypeStruct((width, gates), BF16),
            jax.ShapeDtypeStruct((outs, width), BF16),
            jax.ShapeDtypeStruct((vocab, width), BF16),
            jax.ShapeDtypeStruct((chunk, LANES), BF16),
            jax.ShapeDtypeStruct((chunk, LANES), BF16),
        ],
        scratch_shapes=[
            pltpu.VMEM(upstream.shape, BF16), pltpu.VMEM(inputs.shape, F32), pltpu.VMEM(hot.shape, BF16),
            pltpu.SemaphoreType.DMA((3,)),
            pltpu.VMEM(select.shape, BF16),
            pltpu.VMEM((SUB, inner), F32), pltpu.VMEM((SUB, inner), F32),
            pltpu.VMEM((rows + some, tall), F32), pltpu.VMEM((rows + some, tall), F32),
            pltpu.VMEM((width // LANES, rows, LANES), F32), pltpu.VMEM((width // LANES, rows, LANES), F32),
            pltpu.VMEM((16, inner), F32), pltpu.VMEM((1, width), F32),
        ]
        + scratch(count, chunk, 8, seq)
        + [
            pltpu.SemaphoreType.DMA((count,)), pltpu.SemaphoreType.DMA((count,)),
            pltpu.SemaphoreType.DMA, pltpu.SemaphoreType.DMA,
        ],
        compiler_params=pltpu.CompilerParams(
            collective_id=2, has_side_effects=True, vmem_limit_bytes=62 << 20
        ),
        name="span_tail",
    )(
        d_pre_low, select, d_pair, step_weight, normed, upstream, inputs, scale, hot, gain, d_active, mixed,
        select_weight, halo, lines, d_active, mixed, front, active, select_weight, conv_weight,
        input_weight, input_weight, d_gate, gated, output_weight, handed,
    )


def widen_kernel(
    rank, states, columns, parts, slots,
    front, gate, gate_rest, outs, outs_rest, output, dinputs, embedding, wide_sum, mixed_sum,
    input_to, output_weight_to, output_to, dinputs_to, *rest,
):
    small_to, scratches = rest[:9], rest[9:]
    (
        input_scr, outs_scr, wide_input, wide_outs, output_scr, dinputs_scr, embedding_ref, wide_ref, mixed_ref,
        load_sem, outs_load, store_sem, outs_store, pass_sem, small_load, small_store,
    ) = scratches[:16]
    small_scr = scratches[16:]
    small = [
        pltpu.make_async_copy(source, scr, small_load.at[i])
        for i, (source, scr) in enumerate(((embedding, embedding_ref), (wide_sum, wide_ref), (mixed_sum, mixed_ref)))
    ]
    small_out = [
        pltpu.make_async_copy(scr, to, small_store.at[i]) for i, (scr, to) in enumerate(zip(small_scr, small_to))
    ]
    passed = [
        (pltpu.make_async_copy(source, scr, pass_sem.at[i]), pltpu.make_async_copy(scr, to, pass_sem.at[i]))
        for i, (source, scr, to) in enumerate(((output, output_scr, output_to), (dinputs, dinputs_scr, dinputs_to)))
    ]
    thick, tall = input_scr.shape[0] // parts, outs_scr.shape[0] // parts
    early = outs.shape[0] // tall
    for i in range(parts):
        here, lane = pl.ds(i * thick, thick), 0
        for source in (front, gate, gate_rest):
            lanes = pl.ds(lane, source.shape[1])
            pltpu.make_async_copy(source.at[here, :], input_scr.at[here, lanes], load_sem.at[i]).start()
            lane += source.shape[1]
        source, at = (outs, i) if i < early else (outs_rest, i - early)
        there = pl.ds(i * tall, tall)
        pltpu.make_async_copy(source.at[pl.ds(at * tall, tall), :], outs_scr.at[there, :], outs_load.at[i]).start()
    for copy, unused in passed:
        copy.start()
    for copy in small:
        copy.start()

    def unpack():
        embedding_to, select_to, step_to, decay_to, conv_to, gain_to, *line_to = small_scr
        for copy in small:
            copy.wait()
        embedding_to[...] = embedding_ref[...].astype(F32)
        for source, whole in (
            (wide_ref, ((select_to, columns),)),
            (mixed_ref, ((step_to, rank), (decay_to, states), (conv_to, 16), (gain_to, 16))),
        ):
            at = 0
            for to, height in whole:
                for b in range(to.shape[1] // LANES):
                    part = source[at : at + height, :].astype(F32)
                    lanes = slice(b * LANES, (b + 1) * LANES)
                    to[:, lanes] = part[: to.shape[0]]
                    if to is conv_to:
                        for i, line in enumerate(line_to):
                            line[:, lanes] = part[to.shape[0] + i : to.shape[0] + i + 1]
                    at += height
        for copy in small_out:
            copy.start()

    for i in range(parts):
        if i == parts // 2:
            for first, second in passed:
                first.wait()
                second.start()
            unpack()
        slot = i % slots
        for narrow, wide, to, size, load, store in (
            (input_scr, wide_input, input_to, thick, load_sem, store_sem),
            (outs_scr, wide_outs, output_weight_to, tall, outs_load, outs_store),
        ):
            here, half = pl.ds(i * size, size), size // 2
            wait_rows(narrow.at[here, :], load.at[i])
            if i >= slots:
                wait_rows(wide.at[slot], store.at[slot])
            wide[slot] = narrow[here, :].astype(F32)
            for j in range(2):
                pltpu.make_async_copy(
                    wide.at[slot, pl.ds(j * half, half), :], to.at[pl.ds(i * size + j * half, half), :], store.at[slot]
                ).start()
    for slot in range(slots):
        wait_rows(wide_input.at[slot], store_sem.at[slot])
        wait_rows(wide_outs.at[slot], outs_store.at[slot])
    for unused, copy in passed:
        copy.wait()
    for copy in small_out:
        copy.wait()


def run_widen(
    front, gate, gate_rest, out, out_rest, output, d_inputs, embedding, wide, mixed, rank, states, columns, kernel
):
    width, inner = front.shape
    vocab = embedding.shape[0]
    parts = slots = inner // (2 * LANES)
    hbm = pl.BlockSpec(memory_space=pltpu.HBM)
    shapes = [
        (width, 2 * inner), (inner, width), output.shape, d_inputs.shape, (vocab, width), (columns, inner), (rank, inner),
        (states, inner), (kernel, inner), (1, width), (1, inner), (1, inner), (1, inner),
    ]
    return pl.pallas_call(
        functools.partial(widen_kernel, rank, states, columns, parts, slots),
        in_specs=[hbm] * 10,
        out_specs=[hbm] * len(shapes),
        out_shape=[
            jax.ShapeDtypeStruct(shape, output.dtype if i == 2 else F32) for i, shape in enumerate(shapes)
        ],
        scratch_shapes=[
            pltpu.VMEM((width, 2 * inner), BF16), pltpu.VMEM((inner, width), BF16),
            pltpu.VMEM((slots, width // parts, 2 * inner), F32), pltpu.VMEM((slots, inner // parts, width), F32),
            pltpu.VMEM(output.shape, output.dtype), pltpu.VMEM(d_inputs.shape, F32),
            pltpu.VMEM(embedding.shape, BF16), pltpu.VMEM(wide.shape, BF16), pltpu.VMEM(mixed.shape, BF16),
            pltpu.SemaphoreType.DMA((parts,)), pltpu.SemaphoreType.DMA((parts,)),
            pltpu.SemaphoreType.DMA((slots,)), pltpu.SemaphoreType.DMA((slots,)), pltpu.SemaphoreType.DMA((2,)),
            pltpu.SemaphoreType.DMA((3,)), pltpu.SemaphoreType.DMA((len(shapes) - 4,)),
        ]
        + [pltpu.VMEM(shape, F32) for shape in shapes[4:]],
        compiler_params=pltpu.CompilerParams(vmem_limit_bytes=62 << 20),
        name="sums_to_float32",
    )(front, gate, gate_rest, out, out_rest, output, d_inputs, embedding, wide, mixed)


def on_device(
    byte_ids,
    embedding,
    cotangent,
    norm_gain,
    input_projection_weight,
    conv_weight,
    conv_bias,
    select_weight,
    step_weight,
    step_bias,
    decay_log,
    skip_gain,
    output_projection_weight,
):
    count, stretch = byte_ids.shape
    vocab, width = embedding.shape
    kernel, inner = conv_weight.shape
    states = decay_log.shape[0]
    rank = step_weight.shape[0]
    rows = count * stretch
    seq = lax.axis_size("seq")
    gain, turned_select = norm_gain.reshape(1, width), select_weight.T
    (
        block_inputs, scale, unused, turned, upstream, hot, front, earlier, mixed, active, gate, graded, select
    ) = run_front(
        byte_ids.reshape(1, rows), embedding, cotangent.reshape(rows, width), gain, input_projection_weight,
        output_projection_weight, conv_weight, conv_bias.reshape(1, inner), turned_select, seq,
    )
    (
        gated, d_gate, d_pre_low, d_active, lines, d_pair, gate_sum, out_sum, handed
    ) = run_scan(
        active, gate, graded, select, step_weight, step_bias.reshape(1, inner), decay_log, skip_gain.reshape(1, inner),
        turned, upstream, seq,
    )
    output, d_inputs, front_sum, gate_rest, out_rest, embedding_sum, wide_sum, mixed_sum = run_tail(
        d_pre_low, select, d_pair, step_weight, turned, upstream, block_inputs, scale, hot, gain,
        d_active, mixed, turned_select, earlier, lines, front, active, conv_weight,
        input_projection_weight, d_gate, gated, output_projection_weight, handed, vocab, seq,
    )
    (
        d_input_weight, d_output_weight, output, d_inputs, d_embedding, d_select_weight, d_step_weight, d_decay_log, d_conv_weight,
        d_norm_gain, d_conv_bias, d_step_bias, d_skip_gain,
    ) = run_widen(
        front_sum, gate_sum, gate_rest, out_sum, out_rest, output, d_inputs, embedding_sum, wide_sum, mixed_sum, rank, states,
        select_weight.shape[1], kernel,
    )
    return (
        output.reshape(count, stretch, width),
        d_inputs.reshape(count, stretch, width),
        d_embedding,
        d_norm_gain[0],
        d_input_weight,
        d_conv_weight,
        d_conv_bias[0],
        d_select_weight.T,
        d_step_weight,
        d_step_bias[0],
        d_decay_log,
        d_skip_gain[0],
        d_output_weight,
    )


def solution(mesh):
    placed = (P("dp", "seq"), P(), P("dp", "seq", None)) + (P(),) * 10
    return jax.shard_map(
        on_device,
        mesh=mesh,
        in_specs=placed,
        out_specs=(P("dp", "seq", None), P("dp", "seq", None)) + (P(),) * 11,
        check_vma=False,
    )
```
